32 devices in a mesh: hx: 2 (over x), hy: 4 (over y, core), vz: 4 (over z).
Axes of the slice: x: 2, y: 2, z: 4, core: 2. Of those that a mesh axis runs over, the one named last changes fastest.
Arguments:
- prognostic: float32 [5, 80, 4, 4, 4, 256], P(None, 'vz', None, None, 'hy', 'hx'), may hold values from -6 to 6
- metric: float32 [4, 4, 4, 256], P(None, None, 'hy', 'hx'), may hold values from 0.5 to 2
- first_flux: float32 [5, 5], replicated, may hold values from -2.5 to 2.5
- second_flux: float32 [5, 5], replicated, may hold values from -2.5 to 2.5
- neighbour_face: int32 [4, 4, 256], P(None, 'hy', 'hx'), may hold values from 0 to 3
- orientation: int32 [4, 4, 256], P(None, 'hy', 'hx'), may hold values from 0 to 1
- coupling: float32 [4, 80, 4, 4, 4, 256], P(None, None, 'vz', None, 'hy', 'hx'), may hold values from 0.1 to 1
- damping: float32 [4, 4, 4, 256], P('vz', None, 'hy', 'hx'), may hold values from 0.005 to 0.05
Outputs:
- updated: float32 [5, 80, 4, 4, 4, 256], P(None, 'vz', None, None, 'hy', 'hx')
The draws below stay inside these ranges and needn't reach their ends.
All inputs are finite; a program needn't handle non-finite values.
Results may differ from the reference program's by a relative error of at most 0.0003.
Values sent between devices are 32-bit elements; how exact they have to be, the bound alone decides.
No kernel may reach another device: no remote copies, remote signals or barrier semaphores. Data moves between devices by JAX's collectives and lax.ppermute only.
A program may use at most 64 MiB of HBM per device.

```python
import math
import jax
import jax.numpy as jnp
import numpy as np
from jax import lax

FIELDS = 5
NODES = 4
FACES = 4
L = 80
NEX = 4
NEY = 256


def place_ends(entries, rng, smallest, top_value):
    dims = entries.shape
    index_at = [jax.random.randint(jax.random.fold_in(rng, axis), (), 0, dims[axis]) for axis in range(len(dims))]
    entries = entries.at[tuple(index_at)].set(smallest)
    longest = dims.index(max(dims))
    index_at[longest] = (index_at[longest] + 1) % dims[longest]
    return entries.at[tuple(index_at)].set(top_value)


def levels(stream_key, extent, shards, least, largest):
    def one(position, blocks):
        draws = jax.random.uniform(jax.random.fold_in(jax.random.fold_in(stream_key, 6), position), (blocks,), jnp.float32, least / len(shards), largest / len(shards))
        return jnp.repeat(jnp.exp(draws), extent[position] // blocks).reshape((-1,) + (1,) * (len(extent) - position - 1))

    level = one(*shards[0])
    for cut in shards[1:]:
        level = level * one(*cut)
    return level


def noise(own_key, shape, spread, limit, cuts=(), kind=jnp.bfloat16):
    loudness = levels(own_key, shape, cuts, -0.22, 0.18) if cuts else 1.0
    entries = jax.random.normal(own_key, shape, jnp.float32) * spread * loudness
    return jnp.minimum(jnp.maximum(entries, -limit), limit).astype(kind)


def setup_inputs(seed: int = 0) -> dict:
    keys = jax.random.split(jax.random.key(seed), 9)
    return {
        "prognostic": noise(keys[0], (FIELDS, L, NODES, NODES, NEX, NEY), 1.0, 6.0, ((1, 4), (4, 4), (5, 2)), jnp.float32),
        "metric": jnp.clip(jnp.exp(math.log(2.0) - 1.3862944 * jax.random.uniform(keys[1], (NODES, NODES, NEX, NEY), jnp.float32) ** levels(keys[1], (NODES, NODES, NEX, NEY), ((2, 4), (3, 2)), -0.2, 0.2)), 0.5, 2.0),
        "first_flux": noise(keys[2], (FIELDS, FIELDS), FIELDS ** -0.5, 2.5, (), jnp.float32),
        "second_flux": noise(keys[3], (FIELDS, FIELDS), FIELDS ** -0.5, 2.5, (), jnp.float32),
        "neighbour_face": place_ends(jax.random.randint(keys[4], (FACES, NEX, NEY), 0, FACES), jax.random.fold_in(keys[4], 1), 0, FACES - 1).astype(jnp.int32),
        "orientation": place_ends(jax.random.randint(keys[5], (FACES, NEX, NEY), 0, 2), jax.random.fold_in(keys[5], 1), 0, 1).astype(jnp.int32),
        "coupling": jnp.clip(0.1 + 0.9 * jax.random.uniform(keys[6], (4, L, NODES, NODES, NEX, NEY), jnp.float32) ** levels(keys[6], (4, L, NODES, NODES, NEX, NEY), ((2, 4), (4, 4), (5, 2)), -0.2, 0.2), 0.1, 1.0),
        "damping": jnp.clip(jnp.exp(math.log(0.05) - 2.3025851 * jax.random.uniform(keys[7], (NODES, NODES, NEX, NEY), jnp.float32) ** levels(keys[7], (NODES, NODES, NEX, NEY), ((0, 4), (2, 4), (3, 2)), -0.2, 0.2)), 0.005, 0.05),
    }


step_size = 0.05
rusanov_speed = 1.0
lift_weight = 6.0
gravity_couple = 0.5
density_couple = 0.3
theta_couple = 0.4

def derivative_table():
    points = np.array([-1.0, -1.0 / np.sqrt(5.0), 1.0 / np.sqrt(5.0), 1.0])
    number = points.shape[0]
    barycentric = np.ones(number)
    for source in range(number):
        for another in range(number):
            if another != source:
                barycentric[source] = barycentric[source] / (points[source] - points[another])
    matrix = np.zeros((number, number))
    for target in range(number):
        for source in range(number):
            if target != source:
                matrix[target, source] = barycentric[source] / barycentric[target] / (points[target] - points[source])
        matrix[target, target] = -np.sum(matrix[target])
    return jnp.asarray(matrix, dtype=jnp.float32)

def face_traces(fields):
    west_face = fields[:, :, :, 0]
    east_face = fields[:, :, :, -1]
    south_face = fields[:, :, 0, :]
    north_face = fields[:, :, -1, :]
    return jnp.stack([west_face, east_face, south_face, north_face], axis=2)

def pick_face(candidates, table_row, flip_row):
    chosen = jnp.zeros(candidates.shape[:2] + candidates.shape[3:], candidates.dtype)
    for option in range(candidates.shape[2]):
        chosen = chosen + jnp.where(table_row == option, candidates[:, :, option], 0.0)
    reverse = chosen[:, :, ::-1]
    return jnp.where(flip_row == 1, reverse, chosen)

def section_values(fields, outer_traces, metric, first_flux, second_flux):
    derivative = derivative_table()
    highest = lax.Precision.HIGHEST
    flux_first = jnp.einsum('fg,gljiab->fljiab', first_flux, fields, precision=highest)
    flux_second = jnp.einsum('fg,gljiab->fljiab', second_flux, fields, precision=highest)
    divergence = jnp.einsum('ci,fljiab->fljcab', derivative, flux_first, precision=highest)
    divergence = divergence + jnp.einsum('cj,fljiab->flciab', derivative, flux_second, precision=highest)
    own_traces = face_traces(fields)
    own_first = face_traces(flux_first)
    own_second = face_traces(flux_second)
    own_normal = jnp.stack([-own_first[:, :, 0], own_first[:, :, 1], -own_second[:, :, 2], own_second[:, :, 3]], axis=2)
    outer_first = jnp.einsum('fg,glhkab->flhkab', first_flux, outer_traces[:, :, 0:2], precision=highest)
    outer_second = jnp.einsum('fg,glhkab->flhkab', second_flux, outer_traces[:, :, 2:4], precision=highest)
    outer_normal = jnp.concatenate([-outer_first[:, :, 0:1], outer_first[:, :, 1:2], -outer_second[:, :, 0:1], outer_second[:, :, 1:2]], axis=2)
    correction = 0.5 * (own_normal - outer_normal) + 0.5 * rusanov_speed * (outer_traces - own_traces)
    blank_face = jnp.zeros_like(correction[:, :, 0])
    middle_blanks = [blank_face] * (fields.shape[3] - 2)
    across_first = jnp.stack([correction[:, :, 0]] + middle_blanks + [correction[:, :, 1]], axis=3)
    across_second = jnp.stack([correction[:, :, 2]] + middle_blanks + [correction[:, :, 3]], axis=2)
    tendency = metric * (lift_weight * (across_first + across_second) - divergence)
    return fields + step_size * tendency

def level_difference(column_values):
    upper_part = jnp.concatenate([column_values[1:], jnp.zeros_like(column_values[:1])], axis=0)
    lower_part = jnp.concatenate([jnp.zeros_like(column_values[:1]), column_values[:-1]], axis=0)
    return upper_part - lower_part

def column_solve(entry_a, entry_b, centre, entry_d, entry_e, source):
    empty_row = jnp.zeros_like(source[0])

    def forward(carried, level_row):
        far_ratio, far_second, far_value, near_ratio, near_second, near_value = carried
        lower_two, lower_one, middle, upper_one, upper_two, given_value = level_row
        reduced = lower_one - lower_two * far_ratio
        pivot_entry = middle - lower_two * far_second - reduced * near_ratio
        upper_ratio = (upper_one - reduced * near_second) / pivot_entry
        second_ratio = upper_two / pivot_entry
        scaled_value = (given_value - lower_two * far_value - reduced * near_value) / pivot_entry
        return ((near_ratio, near_second, near_value, upper_ratio, second_ratio, scaled_value), (upper_ratio, second_ratio, scaled_value))
    initial = (empty_row, empty_row, empty_row, empty_row, empty_row, empty_row)
    unused, (ratios, seconds, scaled) = lax.scan(forward, initial, (entry_a, entry_b, centre, entry_d, entry_e, source))

    def backward(carried, level_row):
        next_one, next_two = carried
        upper_ratio, second_ratio, scaled_value = level_row
        solved = scaled_value - upper_ratio * next_one - second_ratio * next_two
        return ((solved, next_one), solved)
    unused, solution = lax.scan(backward, (empty_row, empty_row), (ratios, seconds, scaled), reverse=True)
    return solution

def reference(prognostic, metric, first_flux, second_flux, neighbour_face, orientation, coupling, damping):

    def one_level(level_fields):
        fields = level_fields[:, None]
        own_traces = face_traces(fields)
        candidates = [jnp.roll(own_traces, 1, axis=4), jnp.roll(own_traces, -1, axis=4), jnp.roll(own_traces, 1, axis=5), jnp.roll(own_traces, -1, axis=5)]
        outer_traces = jnp.stack([pick_face(candidates[face_index], neighbour_face[face_index], orientation[face_index]) for face_index in range(4)], axis=2)
        return section_values(fields, outer_traces, metric, first_flux, second_flux)[:, 0]
    section_state = jnp.moveaxis(lax.map(one_level, jnp.moveaxis(prognostic, 1, 0)), 0, 1)
    source = section_state[3] - gravity_couple * level_difference(section_state[4])
    centre = coupling[0] + coupling[1] + coupling[2] + coupling[3] + damping[None]
    vertical_speed = column_solve(-coupling[0], -coupling[1], centre, -coupling[2], -coupling[3], source)
    speed_jump = level_difference(vertical_speed)
    return jnp.stack([section_state[0] - density_couple * speed_jump, section_state[1], section_state[2], vertical_speed, section_state[4] - theta_couple * speed_jump])
```

```python
import functools

import jax
import jax.numpy as jnp
import numpy as np
from jax import lax
from jax.experimental import pallas as pl
from jax.experimental.pallas import tpu as pltpu
from jax.sharding import PartitionSpec as P

step_size = 0.05
lift_weight = 6.0
gravity_couple = 0.5
density_couple = 0.3
theta_couple = 0.4

NODES = 4
POINTS = NODES * NODES
FIELDS = 5
FACE_POINTS = ((0, 4, 8, 12), (3, 7, 11, 15), (0, 1, 2, 3), (12, 13, 14, 15))
RIM_POINTS = tuple(sorted(set(sum(FACE_POINTS, ()))))
ROWS = 8


def derivative_table():
    points = np.array([-1.0, -1.0 / np.sqrt(5.0), 1.0 / np.sqrt(5.0), 1.0])
    number = points.shape[0]
    barycentric = np.ones(number)
    for source in range(number):
        for another in range(number):
            if another != source:
                barycentric[source] = barycentric[source] / (points[source] - points[another])
    matrix = np.zeros((number, number))
    for target in range(number):
        for source in range(number):
            if target != source:
                matrix[target, source] = (
                    barycentric[source] / barycentric[target] / (points[target] - points[source])
                )
        matrix[target, target] = -np.sum(matrix[target])
    return matrix


def operator_tables(lanes):
    weight = 0.5 * lift_weight
    table = derivative_table()
    table[0, 0] += weight
    table[-1, -1] -= weight
    eye = np.eye(NODES)
    along_first = np.kron(eye, table)
    along_second = np.kron(table, eye)
    ends = np.zeros(NODES)
    ends[0] = ends[-1] = 1.0
    faces = np.diag(np.kron(np.ones(NODES), ends) + np.kron(ends, np.ones(NODES)))
    first = np.zeros((POINTS, lanes))
    second = np.zeros((POINTS, lanes))
    same = np.zeros((FIELDS, POINTS, lanes))
    owner = np.full((lanes,), -1)
    for g in range(FIELDS):
        own = slice(POINTS * g, POINTS * (g + 1))
        first[:, own] = -along_first
        second[:, own] = -along_second
        same[g, :, own] = -weight * faces
        owner[own] = g
        for k in range(NODES):
            south = FIELDS * POINTS + 2 * NODES * g + k
            north = south + NODES
            second[FACE_POINTS[2][k], south] = weight
            second[FACE_POINTS[3][k], north] = -weight
            same[g, FACE_POINTS[2][k], south] = weight
            same[g, FACE_POINTS[3][k], north] = weight
            owner[south] = owner[north] = g
    tables = np.concatenate([first, second, same.reshape(FIELDS * POINTS, lanes)])
    return tables.astype(np.float32), owner


def chunks(total):
    return [min(start, total - ROWS) for start in range(0, total, ROWS)]


def pick(values, masks, flip):
    chosen = []
    for k in range(NODES):
        row = values[FACE_POINTS[0][k]]
        for option in range(1, 4):
            row = jnp.where(masks[option], values[FACE_POINTS[option][k]], row)
        chosen.append(row)
    return [jnp.where(flip, chosen[NODES - 1 - k], chosen[k]) for k in range(NODES)]


def table_masks(face_row, flip_row, lanes):
    face = jnp.broadcast_to(face_row, (ROWS, lanes))
    flip = jnp.broadcast_to(flip_row, (ROWS, lanes))
    return [face == option for option in range(4)], flip == 1


def edge_kernel(state, to_up, to_down):
    count, lanes = to_up.shape
    lane = lax.broadcasted_iota(jnp.int32, (ROWS, lanes), 1)
    for q in chunks(count):
        last = jnp.zeros((ROWS, lanes), jnp.float32)
        initial = last
        for point in RIM_POINTS:
            plane = state[pl.ds(q * POINTS + point, ROWS, stride=POINTS), :]
            moved = pltpu.roll(plane, point + 1, 1)
            last = jnp.where(lane == point, moved, last)
            initial = jnp.where(lane == point + 1, moved, initial)
        to_up[pl.ds(q, ROWS), :] = last
        to_down[pl.ds(q, ROWS), :] = initial


def face_kernel(state, table_west, table_east, to_west, to_east):
    count, lanes = state.shape
    sides = []
    for table, out in ((table_west, to_west), (table_east, to_east)):
        masks, flip = table_masks(table[0:1, :], table[1:2, :], lanes)
        sides.append((masks, flip, out))
    for q in chunks(count // POINTS):
        values = {
            point: state[pl.ds(q * POINTS + point, ROWS, stride=POINTS), :] for point in RIM_POINTS
        }
        for masks, flip, out in sides:
            for k, row in enumerate(pick(values, masks, flip)):
                out[pl.ds(q * NODES + k, ROWS, stride=NODES), :] = row


def element_kernel(
    state,
    from_down,
    from_up,
    neighbour_face,
    orientation,
    metric,
    first_flux,
    second_flux,
    tables,
    part,
    outer,
    operator_high,
    operator_low,
):
    levels = state.shape[0] // (FIELDS * POINTS)
    lanes = state.shape[1]
    lane = lax.broadcasted_iota(jnp.int32, (ROWS, lanes), 1)
    for side, (face, received, edge) in enumerate(((2, from_down, 0), (3, from_up, lanes - 1))):
        shift = 1 if side == 0 else lanes - 1
        row = neighbour_face[face : face + 1, :]
        way = orientation[face : face + 1, :]
        here, here_flip = table_masks(row, way, lanes)
        face_rows = jnp.broadcast_to(row, (ROWS, lanes))
        way_rows = jnp.broadcast_to(way, (ROWS, lanes))
        moved_face = pltpu.roll(face_rows, lanes - shift, 1)
        moved_way = pltpu.roll(way_rows, lanes - shift, 1)
        there = [moved_face == option for option in range(4)]
        there_flip = moved_way == 1
        for f in range(FIELDS):
            for start in chunks(levels):
                q = f * levels + start
                values = {
                    point: state[pl.ds(q * POINTS + point, ROWS, stride=POINTS), :]
                    for point in RIM_POINTS
                }
                packed = received[pl.ds(q, ROWS), :]
                beyond = {}
                for point in RIM_POINTS:
                    source = point if side == 0 else point + 1
                    beyond[point] = pltpu.roll(packed, (edge - source) % lanes, 1)
                inner = pick(values, there, there_flip)
                rim = pick(beyond, here, here_flip)
                for k in range(NODES):
                    row_k = jnp.where(lane == edge, rim[k], pltpu.roll(inner[k], shift, 1))
                    at = start * 8 * FIELDS + 8 * f + NODES * side + k
                    outer[pl.ds(at, ROWS, stride=8 * FIELDS), :] = row_k
    column = lax.broadcasted_iota(jnp.int32, (1, lanes), 1)
    own_columns = FIELDS * POINTS
    owner = jnp.where(column < own_columns, column // POINTS, (column - own_columns) // 8)
    for f in range(FIELDS):
        first_row = jnp.zeros((1, lanes), jnp.float32)
        second_row = first_row
        for g in range(FIELDS):
            first_row = jnp.where(owner == g, first_flux[f, g], first_row)
            second_row = jnp.where(owner == g, second_flux[f, g], second_row)
        block = (
            first_row * tables[0:POINTS, :]
            + second_row * tables[POINTS : 2 * POINTS, :]
            + tables[(2 + f) * POINTS : (3 + f) * POINTS, :]
        )
        high = block.astype(jnp.bfloat16)
        operator_high[f * POINTS : (f + 1) * POINTS, :] = high
        operator_low[f * POINTS : (f + 1) * POINTS, :] = (
            block - high.astype(jnp.float32)
        ).astype(jnp.bfloat16)
    high = operator_high[...]
    low = operator_low[...]
    scale = step_size * metric[...]
    blank = jnp.zeros((lanes - own_columns - 8 * FIELDS, lanes), jnp.float32)
    for pair in range(0, levels, 2):
        sides = []
        for level in (pair, pair + 1):
            rows = [
                state[pl.ds((f * levels + level) * POINTS, POINTS), :] for f in range(FIELDS)
            ]
            rows.append(outer[pl.ds(level * 8 * FIELDS, 8 * FIELDS), :])
            rows.append(blank)
            sides.append(jnp.concatenate(rows, axis=0))
        values = jnp.concatenate(sides, axis=1)
        top = values.astype(jnp.bfloat16)
        rest = (values - top.astype(jnp.float32)).astype(jnp.bfloat16)
        change = (
            jnp.dot(high, top, preferred_element_type=jnp.float32)
            + jnp.dot(high, rest, preferred_element_type=jnp.float32)
            + jnp.dot(low, top, preferred_element_type=jnp.float32)
        )
        for place, level in enumerate((pair, pair + 1)):
            for f in range(FIELDS):
                at = pl.ds((f * levels + level) * POINTS, POINTS)
                part[at, :] = (
                    state[at, :]
                    + scale
                    * change[
                        f * POINTS : (f + 1) * POINTS, place * lanes : (place + 1) * lanes
                    ]
                )


def first_side(part, from_west, from_east, flux, scale, f, start, j, i, levels):
    point = NODES * j + i
    value = part[pl.ds((f * levels + start) * POINTS + point, ROWS, stride=POINTS), :]
    if i in (0, NODES - 1):
        outer = from_west if i == 0 else from_east
        sign = 1.0 if i == 0 else -1.0
        total = None
        for g in range(FIELDS):
            rows = outer[pl.ds((g * levels + start) * NODES + j, ROWS, stride=NODES), :]
            factor = sign * flux[f, g] + (1.0 if f == g else 0.0)
            term = factor * rows
            total = term if total is None else total + term
        value = value + scale[point : point + 1, :] * total
    return value


def pack_kernel(
    nodes, part, from_west, from_east, metric, flux, theta, *rest
):
    ways = NODES
    sends, (blocks, column) = rest[:ways], rest[ways:]
    levels = part.shape[0] // (FIELDS * POINTS)
    lanes = part.shape[1]
    count = len(nodes)
    me = lax.axis_index("vz")
    scale = (0.5 * lift_weight * step_size) * metric[...]
    column[...] = jnp.zeros_like(column)
    for j in range(NODES):
        for place, i in enumerate(nodes):
            slot = j * count + place
            vertical = []
            for start in chunks(levels):
                args = (start, j, i, levels)
                vertical.append(first_side(part, from_west, from_east, flux, scale, 3, *args))
                heat = first_side(part, from_west, from_east, flux, scale, 4, *args)
                column[slot, pl.ds(ROWS + start, ROWS), :] = heat
                theta[pl.ds(start * POINTS + NODES * j + i, ROWS, stride=POINTS), :] = heat
            for start, speed in zip(chunks(levels), vertical):
                upper = column[slot, pl.ds(ROWS + start + 1, ROWS), :]
                lower = column[slot, pl.ds(ROWS + start - 1, ROWS), :]
                blocks[j, pl.ds(start * count + place, ROWS, stride=count), :] = (
                    speed - gravity_couple * (upper - lower)
                )
            for extra, level in ((0, 0), (1, levels - 1)):
                at = (levels + extra) * count + place
                blocks[j, at : at + 1, :] = column[slot, ROWS + level : ROWS + level + 1, :]
    for way in range(ways):
        sends[way][...] = blocks[me ^ way]


def finish_section_kernel(part, from_west, from_east, metric, flux, done):
    levels = part.shape[0] // (FIELDS * POINTS)
    scale = (0.5 * lift_weight * step_size) * metric[...]
    rows = 3 * levels * POINTS
    done[...] = part[0:rows, :]
    for f in range(3):
        for j in range(NODES):
            for i in (0, NODES - 1):
                for start in chunks(levels):
                    value = first_side(
                        part, from_west, from_east, flux, scale, f, start, j, i, levels
                    )
                    at = (f * levels + start) * POINTS + NODES * j + i
                    done[pl.ds(at, ROWS, stride=POINTS), :] = value


def factor_kernel(coupling, damping, far, near, inverse, ratio, second):
    levels = coupling.shape[1]
    shape = coupling.shape[2:]
    blank = jnp.zeros(shape, jnp.float32)
    far_ratio, far_second, near_ratio, near_second = (blank,) * 4
    extra = damping[...]
    for level in range(levels):
        a, b, d, e = (coupling[entry, level] for entry in range(4))
        centre = a + b + d + e + extra
        reduced = -b + a * far_ratio
        pivot = centre + a * far_second - reduced * near_ratio
        scaled = 1.0 / pivot
        upper_ratio = (-d - reduced * near_second) * scaled
        second_ratio = -e * scaled
        far[level] = a * scaled
        near[level] = reduced * scaled
        inverse[level] = scaled
        ratio[level] = upper_ratio
        second[level] = second_ratio
        far_ratio, far_second = near_ratio, near_second
        near_ratio, near_second = upper_ratio, second_ratio


def solve_kernel(far, near, inverse, ratio, second, *rest):
    ways = NODES
    received, sends, (source, heat, speed) = rest[:ways], rest[ways : 2 * ways], rest[2 * ways :]
    levels = far.shape[0]
    here = levels // ways
    me = lax.axis_index("vz")
    for way in range(ways):
        block = me ^ way
        source[pl.ds(block * here, here)] = received[way][0:here]
        heat[block] = received[way][here : here + 2]
    for block in range(ways - 1):
        last = block * here + here - 1
        source[last] = source[last] - gravity_couple * heat[block + 1, 0]
        source[last + 1] = source[last + 1] + gravity_couple * heat[block, 1]
    blank = jnp.zeros(far.shape[1:], jnp.float32)
    before_two, before_one = blank, blank
    for level in range(levels):
        value = source[level] * inverse[level]
        value = value + far[level] * before_two
        value = value - near[level] * before_one
        source[level] = value
        before_two, before_one = before_one, value
    speed[0] = blank
    speed[levels + 1] = blank
    next_one, next_two = blank, blank
    for level in range(levels - 1, -1, -1):
        value = source[level] - second[level] * next_two
        value = value - ratio[level] * next_one
        speed[level + 1] = value
        next_two, next_one = next_one, value
    for way in range(ways):
        sends[way][...] = speed[pl.ds((me ^ way) * here, here + 2)]


def update_kernel(nodes, done, theta, *rest):
    ways = NODES
    received, (out, speed) = rest[:ways], rest[ways:]
    levels = theta.shape[0] // POINTS
    size = levels * POINTS
    count = len(nodes)
    me = lax.axis_index("vz")
    for way in range(ways):
        speed[me ^ way] = received[way][...]
    out[size : 3 * size, :] = done[size : 3 * size, :]
    for j in range(NODES):
        for place, i in enumerate(nodes):
            point = NODES * j + i
            for start in chunks(levels):
                lower, value, upper = (
                    speed[j, pl.ds((start + k) * count + place, ROWS, stride=count), :]
                    for k in range(3)
                )
                jump = upper - lower
                at = pl.ds(start * POINTS + point, ROWS, stride=POINTS)
                out[pl.ds(start * POINTS + point, ROWS, stride=POINTS), :] = (
                    done[at, :] - density_couple * jump
                )
                out[pl.ds(3 * size + start * POINTS + point, ROWS, stride=POINTS), :] = value
                out[pl.ds(4 * size + start * POINTS + point, ROWS, stride=POINTS), :] = (
                    theta[at, :] - theta_couple * jump
                )


VMEM = pl.BlockSpec(memory_space=pltpu.VMEM)
SMEM = pl.BlockSpec(memory_space=pltpu.SMEM)


def call(kernel, outs, in_specs, scratch=(), cost=0, name=None):
    kinds = [pltpu.VMEM(shape, jnp.float32) for shape in outs]
    return pl.pallas_call(
        kernel,
        out_shape=kinds,
        in_specs=in_specs,
        out_specs=[VMEM] * len(outs),
        scratch_shapes=list(scratch),
        compiler_params=pltpu.CompilerParams(vmem_limit_bytes=24 * 1024 * 1024),
        cost_estimate=pl.CostEstimate(flops=cost, bytes_accessed=cost, transcendentals=0),
        name=name,
    )


def per_device(
    prognostic, metric, first_flux, second_flux, neighbour_face, orientation, coupling, damping
):
    fields, levels = prognostic.shape[:2]
    lanes = prognostic.shape[-1]
    state = prognostic.reshape(fields * levels * POINTS, lanes)
    metric = metric.reshape(POINTS, lanes)
    neighbour_face = neighbour_face.reshape(4, lanes)
    orientation = orientation.reshape(4, lanes)
    coupling = coupling.reshape(4, coupling.shape[1], NODES, lanes)
    damping = damping.reshape(NODES, lanes)
    tables, _ = operator_tables(lanes)

    def shifts(axis):
        size = lax.axis_size(axis)
        up = [(i, (i + 1) % size) for i in range(size)]
        return up, [(j, i) for i, j in up]

    def exchange(arrays):
        size = lax.axis_size("vz")
        moved = [arrays[0]]
        for way in range(1, size):
            moved.append(lax.ppermute(arrays[way], "vz", [(i, i ^ way) for i in range(size)]))
        return moved

    first_up, first_down = shifts("hy")
    second_up, second_down = shifts("hx")
    east_table = jnp.stack([neighbour_face[1], orientation[1]])
    west_table = jnp.stack([neighbour_face[0], orientation[0]])
    table_west = lax.ppermute(east_table, "hy", first_up)
    table_east = lax.ppermute(west_table, "hy", first_down)

    rows = fields * levels
    edge = (rows, lanes)
    to_up, to_down = call(edge_kernel, [edge, edge], [VMEM], cost=1000, name="edge")(state)
    from_down = lax.ppermute(to_up, "hx", second_up)
    from_up = lax.ppermute(to_down, "hx", second_down)

    face = (rows * NODES, lanes)
    to_west, to_east = call(face_kernel, [face, face], [VMEM] * 3, cost=1000, name="face")(
        state, table_west, table_east
    )
    from_east = lax.ppermute(to_west, "hy", first_down)
    from_west = lax.ppermute(to_east, "hy", first_up)

    (part,) = call(
        element_kernel,
        [state.shape],
        [VMEM] * 6 + [SMEM] * 2 + [VMEM],
        [
            pltpu.VMEM((levels * 8 * fields, lanes), jnp.float32),
            pltpu.VMEM((fields * POINTS, lanes), jnp.bfloat16),
            pltpu.VMEM((fields * POINTS, lanes), jnp.bfloat16),
        ],
        cost=4000000,
        name="element",
    )(
        state,
        from_down,
        from_up,
        neighbour_face,
        orientation,
        metric,
        first_flux,
        second_flux,
        jnp.asarray(tables),
    )
    column = (coupling.shape[1], NODES, lanes)
    factors = call(factor_kernel, [column] * 5, [VMEM] * 2, cost=4000000, name="factor")(
        coupling, damping
    )

    nodes = (0, 1, 2, 3)
    count = len(nodes)
    block = ((levels + 2) * count, lanes)
    theta, *sends = call(
        functools.partial(pack_kernel, nodes),
        [(levels * POINTS, lanes)] + [block] * NODES,
        [VMEM] * 4 + [SMEM],
        [
            pltpu.VMEM((NODES,) + block, jnp.float32),
            pltpu.VMEM((NODES * count, levels + 2 * ROWS + 4, lanes), jnp.float32),
        ],
        cost=1000,
        name="pack",
    )(part, from_west, from_east, metric, first_flux)
    cube = (levels + 2, count, lanes)
    received = [x.reshape(cube) for x in exchange(sends)]
    (done,) = call(
        finish_section_kernel,
        [(3 * levels * POINTS, lanes)],
        [VMEM] * 4 + [SMEM],
        cost=4000000,
        name="finish",
    )(part, from_west, from_east, metric, first_flux)
    speeds = call(
        solve_kernel,
        [cube] * NODES,
        [VMEM] * (5 + NODES),
        [
            pltpu.VMEM(column, jnp.float32),
            pltpu.VMEM((NODES, 2, count, lanes), jnp.float32),
            pltpu.VMEM((column[0] + 2,) + column[1:], jnp.float32),
        ],
        cost=1000,
        name="solve",
    )(*factors, *received)
    returned = exchange([x.reshape(block) for x in speeds])
    updated = pl.pallas_call(
        functools.partial(update_kernel, nodes),
        out_shape=jax.ShapeDtypeStruct(state.shape, jnp.float32),
        in_specs=[VMEM] * (2 + NODES),
        out_specs=VMEM,
        scratch_shapes=[pltpu.VMEM((NODES,) + block, jnp.float32)],
        compiler_params=pltpu.CompilerParams(vmem_limit_bytes=24 * 1024 * 1024),
        name="update",
    )(done, theta, *returned)
    return updated.reshape(prognostic.shape)


def solution(mesh):
    placed = (
        P(None, "vz", None, None, "hy", "hx"),
        P(None, None, "hy", "hx"),
        P(),
        P(),
        P(None, "hy", "hx"),
        P(None, "hy", "hx"),
        P(None, None, "vz", None, "hy", "hx"),
        P("vz", None, "hy", "hx"),
    )
    return jax.shard_map(
        per_device,
        mesh=mesh,
        in_specs=placed,
        out_specs=P(None, "vz", None, None, "hy", "hx"),
        check_vma=False,
    )
```

```python
import jax
import jax.numpy as jnp
import numpy as np
from jax import lax
from jax.experimental import pallas as pl
from jax.experimental.pallas import tpu as pltpu
from jax.sharding import PartitionSpec as P

step_size = 0.05
lift_weight = 6.0
gravity_couple = 0.5
density_couple = 0.3
theta_couple = 0.4

NODES = 4
POINTS = NODES * NODES
FIELDS = 5
FACE_POINTS = ((0, 4, 8, 12), (3, 7, 11, 15), (0, 1, 2, 3), (12, 13, 14, 15))
RIM_POINTS = tuple(sorted(set(sum(FACE_POINTS, ()))))
ROWS = 8
LATE_FIELDS = (0, 1, 2, 4)


def derivative_table():
    points = np.array([-1.0, -1.0 / np.sqrt(5.0), 1.0 / np.sqrt(5.0), 1.0])
    number = points.shape[0]
    barycentric = np.ones(number)
    for source in range(number):
        for another in range(number):
            if another != source:
                barycentric[source] = barycentric[source] / (points[source] - points[another])
    matrix = np.zeros((number, number))
    for target in range(number):
        for source in range(number):
            if target != source:
                matrix[target, source] = (
                    barycentric[source] / barycentric[target] / (points[target] - points[source])
                )
        matrix[target, target] = -np.sum(matrix[target])
    return matrix


def operator_tables(lanes):
    weight = 0.5 * lift_weight
    table = derivative_table()
    table[0, 0] += weight
    table[-1, -1] -= weight
    eye = np.eye(NODES)
    along_first = np.kron(eye, table)
    along_second = np.kron(table, eye)
    ends = np.zeros(NODES)
    ends[0] = ends[-1] = 1.0
    faces = np.diag(np.kron(np.ones(NODES), ends) + np.kron(ends, np.ones(NODES)))
    first = np.zeros((POINTS, lanes))
    second = np.zeros((POINTS, lanes))
    same = np.zeros((FIELDS, POINTS, lanes))
    owner = np.full((lanes,), -1)
    for g in range(FIELDS):
        own = slice(POINTS * g, POINTS * (g + 1))
        first[:, own] = -along_first
        second[:, own] = -along_second
        same[g, :, own] = -weight * faces
        owner[own] = g
        for k in range(NODES):
            south = FIELDS * POINTS + 2 * NODES * g + k
            north = south + NODES
            second[FACE_POINTS[2][k], south] = weight
            second[FACE_POINTS[3][k], north] = -weight
            same[g, FACE_POINTS[2][k], south] = weight
            same[g, FACE_POINTS[3][k], north] = weight
            owner[south] = owner[north] = g
    tables = np.concatenate([first, second, same.reshape(FIELDS * POINTS, lanes)])
    return tables.astype(np.float32), owner


def chunks(total):
    return [min(start, total - ROWS) for start in range(0, total, ROWS)]


def pick(values, masks, flip):
    chosen = []
    for k in range(NODES):
        row = values[FACE_POINTS[0][k]]
        for option in range(1, 4):
            row = jnp.where(masks[option], values[FACE_POINTS[option][k]], row)
        chosen.append(row)
    return [jnp.where(flip, chosen[NODES - 1 - k], chosen[k]) for k in range(NODES)]


def table_masks(face_row, flip_row, lanes):
    face = jnp.broadcast_to(face_row, (ROWS, lanes))
    flip = jnp.broadcast_to(flip_row, (ROWS, lanes))
    return [face == option for option in range(4)], flip == 1


def rim_kernel(state, neighbour_face, orientation, flux, to_east, to_west, to_sides, column):
    count, lanes = state.shape[0] // POINTS, state.shape[1]
    levels = count // FIELDS
    width = len(RIM_POINTS)
    column[...] = jnp.zeros_like(column)
    for place, point in enumerate(RIM_POINTS):
        speeds = []
        for start in chunks(levels):
            rows = [
                state[pl.ds((g * levels + start) * POINTS + point, ROWS, stride=POINTS), :]
                for g in range(FIELDS)
            ]
            pair = []
            for f in (3, 4):
                normal = flux[f, 0] * rows[0]
                for g in range(1, FIELDS):
                    normal = normal + flux[f, g] * rows[g]
                pair.append((rows[f] + normal, rows[f] - normal))
            speeds.append(pair[0])
            for side in range(2):
                column[side, pl.ds(ROWS + start, ROWS), :] = pair[1][side]
        for side, out in enumerate((to_east, to_west)):
            for start, speed in zip(chunks(levels), speeds):
                upper = column[side, pl.ds(ROWS + start + 1, ROWS), :]
                lower = column[side, pl.ds(ROWS + start - 1, ROWS), :]
                out[pl.ds(start * width + place, ROWS, stride=width), :] = speed[
                    side
                ] - gravity_couple * (upper - lower)
            for extra, level in ((0, 0), (1, levels - 1)):
                at = (levels + extra) * width + place
                out[at : at + 1, :] = column[side, ROWS + level : ROWS + level + 1, :]
    end = (levels + 2) * width
    for out, face in ((to_east, 1), (to_west, 0)):
        out[end : end + 1, :] = neighbour_face[face : face + 1, :].astype(jnp.float32)
        out[end + 1 : end + 2, :] = orientation[face : face + 1, :].astype(jnp.float32)
        left = out.shape[0] - end - 2
        out[end + 2 :, :] = jnp.zeros((left, lanes), jnp.float32)
    lane = lax.broadcasted_iota(jnp.int32, (ROWS, lanes), 1)
    for q in chunks(count):
        last = jnp.zeros((ROWS, lanes), jnp.float32)
        initial = last
        for point in RIM_POINTS:
            plane = state[pl.ds(q * POINTS + point, ROWS, stride=POINTS), :]
            moved = pltpu.roll(plane, point + 1, 1)
            last = jnp.where(lane == point, moved, last)
            initial = jnp.where(lane == point + 1, moved, initial)
        to_sides[pl.ds(q, ROWS), :] = last
        to_sides[pl.ds(count + q, ROWS), :] = initial


def face_kernel(state, from_west, from_east, flux, to_west, to_east):
    count, lanes = state.shape[0] // POINTS, state.shape[1]
    levels = count // FIELDS
    at = (levels + 2) * len(RIM_POINTS)
    sides = []
    for source, out, sign in ((from_west, to_west, -1.0), (from_east, to_east, 1.0)):
        face = source[at : at + 1, :].astype(jnp.int32)
        flip = source[at + 1 : at + 2, :].astype(jnp.int32)
        sides.append((*table_masks(face, flip, lanes), out, sign))
    for start in chunks(levels):
        values = []
        for g in range(FIELDS):
            values.append(
                {
                    point: state[
                        pl.ds((g * levels + start) * POINTS + point, ROWS, stride=POINTS), :
                    ]
                    for point in RIM_POINTS
                }
            )
        for masks, flip, out, sign in sides:
            picked = [pick(values[g], masks, flip) for g in range(FIELDS)]
            for place, f in enumerate(LATE_FIELDS):
                for k in range(NODES):
                    normal = flux[f, 0] * picked[0][k]
                    for g in range(1, FIELDS):
                        normal = normal + flux[f, g] * picked[g][k]
                    out[pl.ds((place * levels + start) * NODES + k, ROWS, stride=NODES), :] = (
                        picked[f][k] + sign * normal
                    )


def element_kernel(
    state,
    from_sides,
    neighbour_face,
    orientation,
    metric,
    first_flux,
    second_flux,
    tables,
    part,
    base,
    outer,
    column,
    operator_high,
    operator_low,
):
    levels = state.shape[0] // (FIELDS * POINTS)
    lanes = state.shape[1]
    lane = lax.broadcasted_iota(jnp.int32, (ROWS, lanes), 1)
    for side, (face, edge) in enumerate(((2, 0), (3, lanes - 1))):
        shift = 1 if side == 0 else lanes - 1
        row = neighbour_face[face : face + 1, :]
        way = orientation[face : face + 1, :]
        here, here_flip = table_masks(row, way, lanes)
        face_rows = jnp.broadcast_to(row, (ROWS, lanes))
        way_rows = jnp.broadcast_to(way, (ROWS, lanes))
        moved_face = pltpu.roll(face_rows, lanes - shift, 1)
        moved_way = pltpu.roll(way_rows, lanes - shift, 1)
        there = [moved_face == option for option in range(4)]
        there_flip = moved_way == 1
        for f in range(FIELDS):
            for start in chunks(levels):
                q = f * levels + start
                values = {
                    point: state[pl.ds(q * POINTS + point, ROWS, stride=POINTS), :]
                    for point in RIM_POINTS
                }
                packed = from_sides[pl.ds(side * FIELDS * levels + q, ROWS), :]
                beyond = {}
                for point in RIM_POINTS:
                    source = point if side == 0 else point + 1
                    beyond[point] = pltpu.roll(packed, (edge - source) % lanes, 1)
                inner = pick(values, there, there_flip)
                rim = pick(beyond, here, here_flip)
                for k in range(NODES):
                    row_k = jnp.where(lane == edge, rim[k], pltpu.roll(inner[k], shift, 1))
                    at = start * 8 * FIELDS + 8 * f + NODES * side + k
                    outer[pl.ds(at, ROWS, stride=8 * FIELDS), :] = row_k
    index = lax.broadcasted_iota(jnp.int32, (1, lanes), 1)
    own_columns = FIELDS * POINTS
    owner = jnp.where(index < own_columns, index // POINTS, (index - own_columns) // 8)
    for f in range(FIELDS):
        first_row = jnp.zeros((1, lanes), jnp.float32)
        second_row = first_row
        for g in range(FIELDS):
            first_row = jnp.where(owner == g, first_flux[f, g], first_row)
            second_row = jnp.where(owner == g, second_flux[f, g], second_row)
        block = (
            first_row * tables[0:POINTS, :]
            + second_row * tables[POINTS : 2 * POINTS, :]
            + tables[(2 + f) * POINTS : (3 + f) * POINTS, :]
        )
        high = block.astype(jnp.bfloat16)
        operator_high[f * POINTS : (f + 1) * POINTS, :] = high
        operator_low[f * POINTS : (f + 1) * POINTS, :] = (
            block - high.astype(jnp.float32)
        ).astype(jnp.bfloat16)
    high = operator_high[...]
    low = operator_low[...]
    scale = step_size * metric[...]
    blank = jnp.zeros((lanes - own_columns - 8 * FIELDS, lanes), jnp.float32)
    for pair in range(0, levels, 2):
        sides = []
        for level in (pair, pair + 1):
            rows = [
                state[pl.ds((f * levels + level) * POINTS, POINTS), :] for f in range(FIELDS)
            ]
            rows.append(outer[pl.ds(level * 8 * FIELDS, 8 * FIELDS), :])
            rows.append(blank)
            sides.append(jnp.concatenate(rows, axis=0))
        values = jnp.concatenate(sides, axis=1)
        top = values.astype(jnp.bfloat16)
        rest = (values - top.astype(jnp.float32)).astype(jnp.bfloat16)
        change = (
            jnp.dot(high, top, preferred_element_type=jnp.float32)
            + jnp.dot(high, rest, preferred_element_type=jnp.float32)
            + jnp.dot(low, top, preferred_element_type=jnp.float32)
        )
        for place, level in enumerate((pair, pair + 1)):
            for f in range(FIELDS):
                at = pl.ds((f * levels + level) * POINTS, POINTS)
                part[at, :] = (
                    state[at, :]
                    + scale
                    * change[
                        f * POINTS : (f + 1) * POINTS, place * lanes : (place + 1) * lanes
                    ]
                )
    column[...] = jnp.zeros_like(column)
    for j in range(NODES):
        for i in range(NODES):
            point = NODES * j + i
            for start in chunks(levels):
                column[point, pl.ds(ROWS + start, ROWS), :] = part[
                    pl.ds((4 * levels + start) * POINTS + point, ROWS, stride=POINTS), :
                ]
            for start in chunks(levels):
                upper = column[point, pl.ds(ROWS + start + 1, ROWS), :]
                lower = column[point, pl.ds(ROWS + start - 1, ROWS), :]
                speed = part[pl.ds((3 * levels + start) * POINTS + point, ROWS, stride=POINTS), :]
                base[j, pl.ds(start * NODES + i, ROWS, stride=NODES), :] = speed - gravity_couple * (
                    upper - lower
                )
            for extra, level in ((0, 0), (1, levels - 1)):
                at = (levels + extra) * NODES + i
                base[j, at : at + 1, :] = column[point, ROWS + level : ROWS + level + 1, :]


def pack_kernel(base, from_west, from_east, neighbour_face, orientation, metric, send):
    lanes = base.shape[2]
    width = len(RIM_POINTS)
    scale = (0.5 * lift_weight * step_size) * metric[...]
    send[...] = base[...]
    for face, source, i in ((0, from_west, 0), (1, from_east, NODES - 1)):
        masks, flip = table_masks(
            neighbour_face[face : face + 1, :], orientation[face : face + 1, :], lanes
        )
        for start in chunks(base.shape[1] // NODES):
            values = {
                point: source[pl.ds(start * width + place, ROWS, stride=width), :]
                for place, point in enumerate(RIM_POINTS)
            }
            for j, row in enumerate(pick(values, masks, flip)):
                point = NODES * j + i
                at = pl.ds(start * NODES + i, ROWS, stride=NODES)
                send[j, at, :] = base[j, at, :] + scale[point : point + 1, :] * row


def finish_section_kernel(part, from_west, from_east, metric, done):
    levels = part.shape[0] // (FIELDS * POINTS)
    size = levels * POINTS
    scale = (0.5 * lift_weight * step_size) * metric[...]
    for place, f in enumerate(LATE_FIELDS):
        done[place * size : (place + 1) * size, :] = part[f * size : (f + 1) * size, :]
        for j in range(NODES):
            for source, i in ((from_west, 0), (from_east, NODES - 1)):
                point = NODES * j + i
                for start in chunks(levels):
                    rows = source[
                        pl.ds((place * levels + start) * NODES + j, ROWS, stride=NODES), :
                    ]
                    done[pl.ds(place * size + start * POINTS + point, ROWS, stride=POINTS), :] = (
                        part[pl.ds(f * size + start * POINTS + point, ROWS, stride=POINTS), :]
                        + scale[point : point + 1, :] * rows
                    )


def factor_kernel(coupling, damping, far, near, inverse, ratio, second):
    levels = coupling.shape[1]
    shape = coupling.shape[2:]
    blank = jnp.zeros(shape, jnp.float32)
    far_ratio, far_second, near_ratio, near_second = (blank,) * 4
    extra = damping[...]
    for level in range(levels):
        a, b, d, e = (coupling[entry, level] for entry in range(4))
        centre = a + b + d + e + extra
        reduced = -b + a * far_ratio
        pivot = centre + a * far_second - reduced * near_ratio
        scaled = 1.0 / pivot
        upper_ratio = (-d - reduced * near_second) * scaled
        second_ratio = -e * scaled
        far[level] = a * scaled
        near[level] = reduced * scaled
        inverse[level] = scaled
        ratio[level] = upper_ratio
        second[level] = second_ratio
        far_ratio, far_second = near_ratio, near_second
        near_ratio, near_second = upper_ratio, second_ratio


def solve_kernel(far, near, inverse, ratio, second, *rest):
    ways = NODES
    received, sends, (source, heat, speed) = rest[0], rest[1 : 1 + ways], rest[1 + ways :]
    levels = far.shape[0]
    here = levels // ways
    me = lax.axis_index("vz")
    for block in range(ways):
        source[block * here : (block + 1) * here] = received[block, 0:here]
        heat[block] = received[block, here : here + 2]
    for block in range(ways - 1):
        last = block * here + here - 1
        source[last] = source[last] - gravity_couple * heat[block + 1, 0]
        source[last + 1] = source[last + 1] + gravity_couple * heat[block, 1]
    blank = jnp.zeros(far.shape[1:], jnp.float32)
    before_two, before_one = blank, blank
    for level in range(levels):
        value = source[level] * inverse[level]
        value = value + far[level] * before_two
        value = value - near[level] * before_one
        source[level] = value
        before_two, before_one = before_one, value
    speed[0] = blank
    speed[levels + 1] = blank
    next_one, next_two = blank, blank
    for level in range(levels - 1, -1, -1):
        value = source[level] - second[level] * next_two
        value = value - ratio[level] * next_one
        speed[level + 1] = value
        next_two, next_one = next_one, value
    for way in range(ways):
        sends[way][...] = speed[pl.ds((me ^ way) * here, here + 2)]


def update_kernel(done, *rest):
    ways = NODES
    received, (out, speed) = rest[:ways], rest[ways:]
    size = done.shape[0] // len(LATE_FIELDS)
    levels = size // POINTS
    me = lax.axis_index("vz")
    for way in range(ways):
        speed[me ^ way] = received[way][...]
    out[size : 3 * size, :] = done[size : 3 * size, :]
    for j in range(NODES):
        for i in range(NODES):
            for start in chunks(levels):
                lower, value, upper = (
                    speed[j, pl.ds((start + k) * NODES + i, ROWS, stride=NODES), :]
                    for k in range(3)
                )
                jump = upper - lower
                at = start * POINTS + NODES * j + i
                out[pl.ds(at, ROWS, stride=POINTS), :] = (
                    done[pl.ds(at, ROWS, stride=POINTS), :] - density_couple * jump
                )
                out[pl.ds(3 * size + at, ROWS, stride=POINTS), :] = value
                out[pl.ds(4 * size + at, ROWS, stride=POINTS), :] = (
                    done[pl.ds(3 * size + at, ROWS, stride=POINTS), :] - theta_couple * jump
                )


VMEM = pl.BlockSpec(memory_space=pltpu.VMEM)
SMEM = pl.BlockSpec(memory_space=pltpu.SMEM)


def call(kernel, outs, in_specs, scratch=(), cost=0, name=None):
    kinds = [pltpu.VMEM(shape, jnp.float32) for shape in outs]
    return pl.pallas_call(
        kernel,
        out_shape=kinds,
        in_specs=in_specs,
        out_specs=[VMEM] * len(outs),
        scratch_shapes=list(scratch),
        compiler_params=pltpu.CompilerParams(vmem_limit_bytes=24 * 1024 * 1024),
        cost_estimate=pl.CostEstimate(flops=cost, bytes_accessed=cost, transcendentals=0),
        name=name,
    )


def per_device(
    prognostic, metric, first_flux, second_flux, neighbour_face, orientation, coupling, damping
):
    fields, levels = prognostic.shape[:2]
    lanes = prognostic.shape[-1]
    state = prognostic.reshape(fields * levels * POINTS, lanes)
    metric = metric.reshape(POINTS, lanes)
    neighbour_face = neighbour_face.reshape(4, lanes)
    orientation = orientation.reshape(4, lanes)
    coupling = coupling.reshape(4, coupling.shape[1], NODES, lanes)
    damping = damping.reshape(NODES, lanes)
    tables, _ = operator_tables(lanes)

    def shifts(axis):
        size = lax.axis_size(axis)
        up = [(i, (i + 1) % size) for i in range(size)]
        return up, [(j, i) for i, j in up]

    def exchange(arrays):
        size = lax.axis_size("vz")
        moved = [arrays[0]]
        for way in range(1, size):
            moved.append(lax.ppermute(arrays[way], "vz", [(i, i ^ way) for i in range(size)]))
        return moved

    first_up, first_down = shifts("hy")
    second_up, second_down = shifts("hx")
    rows = fields * levels
    message = (-(-((levels + 2) * len(RIM_POINTS) + 2) // ROWS) * ROWS, lanes)
    padded = levels + 2 * ROWS + 4
    to_east, to_west, to_sides = call(
        rim_kernel,
        [message, message, (2 * rows, lanes)],
        [VMEM] * 3 + [SMEM],
        [pltpu.VMEM((2, padded, lanes), jnp.float32)],
        cost=1000,
        name="rim",
    )(state, neighbour_face, orientation, first_flux)
    from_east = lax.ppermute(to_west, "hy", first_down)
    from_west = lax.ppermute(to_east, "hy", first_up)
    if lax.axis_size("hx") == 2:
        from_sides = lax.ppermute(to_sides, "hx", second_up)
    else:
        from_sides = jnp.concatenate(
            [
                lax.ppermute(to_sides[:rows], "hx", second_up),
                lax.ppermute(to_sides[rows:], "hx", second_down),
            ]
        )

    column = (coupling.shape[1], NODES, lanes)
    factors = call(factor_kernel, [column] * 5, [VMEM] * 2, cost=4000000, name="factor")(
        coupling, damping
    )
    block = ((levels + 2) * NODES, lanes)
    part, base = call(
        element_kernel,
        [state.shape, (NODES,) + block],
        [VMEM] * 5 + [SMEM] * 2 + [VMEM],
        [
            pltpu.VMEM((levels * 8 * fields, lanes), jnp.float32),
            pltpu.VMEM((POINTS, padded, lanes), jnp.float32),
            pltpu.VMEM((fields * POINTS, lanes), jnp.bfloat16),
            pltpu.VMEM((fields * POINTS, lanes), jnp.bfloat16),
        ],
        cost=4000000,
        name="element",
    )(
        state,
        from_sides,
        neighbour_face,
        orientation,
        metric,
        first_flux,
        second_flux,
        jnp.asarray(tables),
    )
    (send,) = call(pack_kernel, [(NODES,) + block], [VMEM] * 6, cost=1000, name="pack")(
        base, from_west, from_east, neighbour_face, orientation, metric
    )
    received = lax.all_to_all(send, "vz", split_axis=0, concat_axis=0, tiled=True)

    late = (len(LATE_FIELDS) * levels * NODES, lanes)
    late_west, late_east = call(
        face_kernel, [late, late], [VMEM] * 3 + [SMEM], cost=1000, name="face"
    )(state, from_west, from_east, first_flux)
    late_from_east = lax.ppermute(late_west, "hy", first_down)
    late_from_west = lax.ppermute(late_east, "hy", first_up)

    cube = (levels + 2, NODES, lanes)
    speeds = call(
        solve_kernel,
        [cube] * NODES,
        [VMEM] * 6,
        [
            pltpu.VMEM(column, jnp.float32),
            pltpu.VMEM((NODES, 2, NODES, lanes), jnp.float32),
            pltpu.VMEM((column[0] + 2,) + column[1:], jnp.float32),
        ],
        cost=1000,
        name="solve",
    )(*factors, received.reshape((NODES,) + cube))
    returned = exchange([x.reshape(block) for x in speeds])
    (done,) = call(
        finish_section_kernel,
        [(len(LATE_FIELDS) * levels * POINTS, lanes)],
        [VMEM] * 4,
        cost=4000000,
        name="finish",
    )(part, late_from_west, late_from_east, metric)
    updated = pl.pallas_call(
        update_kernel,
        out_shape=jax.ShapeDtypeStruct(state.shape, jnp.float32),
        in_specs=[VMEM] * (1 + NODES),
        out_specs=VMEM,
        scratch_shapes=[pltpu.VMEM((NODES,) + block, jnp.float32)],
        compiler_params=pltpu.CompilerParams(vmem_limit_bytes=24 * 1024 * 1024),
        name="update",
    )(done, *returned)
    return updated.reshape(prognostic.shape)


def solution(mesh):
    placed = (
        P(None, "vz", None, None, "hy", "hx"),
        P(None, None, "hy", "hx"),
        P(),
        P(),
        P(None, "hy", "hx"),
        P(None, "hy", "hx"),
        P(None, None, "vz", None, "hy", "hx"),
        P("vz", None, "hy", "hx"),
    )
    return jax.shard_map(
        per_device,
        mesh=mesh,
        in_specs=placed,
        out_specs=P(None, "vz", None, None, "hy", "hx"),
        check_vma=False,
    )
```

```python
import jax
import jax.numpy as jnp
import numpy as np
from jax import lax
from jax.experimental import pallas as pl
from jax.experimental.pallas import tpu as pltpu
from jax.sharding import PartitionSpec as P

step_size = 0.05
lift_weight = 6.0
gravity_couple = 0.5
density_couple = 0.3
theta_couple = 0.4

NODES = 4
POINTS = NODES * NODES
FIELDS = 5
FACE_POINTS = ((0, 4, 8, 12), (3, 7, 11, 15), (0, 1, 2, 3), (12, 13, 14, 15))
RIM_POINTS = tuple(sorted(set(sum(FACE_POINTS, ()))))
ROWS = 8
LATE_FIELDS = (0, 1, 2, 4)


def derivative_table():
    points = np.array([-1.0, -1.0 / np.sqrt(5.0), 1.0 / np.sqrt(5.0), 1.0])
    number = points.shape[0]
    barycentric = np.ones(number)
    for source in range(number):
        for another in range(number):
            if another != source:
                barycentric[source] = barycentric[source] / (points[source] - points[another])
    matrix = np.zeros((number, number))
    for target in range(number):
        for source in range(number):
            if target != source:
                matrix[target, source] = (
                    barycentric[source] / barycentric[target] / (points[target] - points[source])
                )
        matrix[target, target] = -np.sum(matrix[target])
    return matrix


def operator_tables(lanes):
    weight = 0.5 * lift_weight
    table = derivative_table()
    table[0, 0] += weight
    table[-1, -1] -= weight
    eye = np.eye(NODES)
    along_first = np.kron(eye, table)
    along_second = np.kron(table, eye)
    ends = np.zeros(NODES)
    ends[0] = ends[-1] = 1.0
    faces = np.diag(np.kron(np.ones(NODES), ends) + np.kron(ends, np.ones(NODES)))
    first = np.zeros((POINTS, lanes))
    second = np.zeros((POINTS, lanes))
    same = np.zeros((FIELDS, POINTS, lanes))
    owner = np.full((lanes,), -1)
    for g in range(FIELDS):
        own = slice(POINTS * g, POINTS * (g + 1))
        first[:, own] = -along_first
        second[:, own] = -along_second
        same[g, :, own] = -weight * faces
        owner[own] = g
        for k in range(NODES):
            south = FIELDS * POINTS + 2 * NODES * g + k
            north = south + NODES
            second[FACE_POINTS[2][k], south] = weight
            second[FACE_POINTS[3][k], north] = -weight
            same[g, FACE_POINTS[2][k], south] = weight
            same[g, FACE_POINTS[3][k], north] = weight
            owner[south] = owner[north] = g
    tables = np.concatenate([first, second, same.reshape(FIELDS * POINTS, lanes)])
    return tables.astype(np.float32), owner


def chunks(total):
    return [min(start, total - ROWS) for start in range(0, total, ROWS)]


def pick(values, masks, flip):
    chosen = []
    for k in range(NODES):
        row = values[FACE_POINTS[0][k]]
        for option in range(1, 4):
            row = jnp.where(masks[option], values[FACE_POINTS[option][k]], row)
        chosen.append(row)
    return [jnp.where(flip, chosen[NODES - 1 - k], chosen[k]) for k in range(NODES)]


def table_masks(face_row, flip_row, lanes):
    face = jnp.broadcast_to(face_row, (ROWS, lanes))
    flip = jnp.broadcast_to(flip_row, (ROWS, lanes))
    return [face == option for option in range(4)], flip == 1


def side_lanes(f, piece, point):
    number = 3 * f + piece
    return number // 4, 32 * (number % 4) + point, 32 * (number % 4) + POINTS + point


def rim_kernel(
    state_hbm,
    face_hbm,
    way_hbm,
    flux_hbm,
    to_east,
    to_west,
    to_sides,
    state,
    column,
    speed,
    neighbour_face,
    orientation,
    flux,
    semaphores,
):
    levels = state.shape[1] // POINTS
    lanes = state.shape[2]
    width = len(RIM_POINTS)
    groups = [(start, min(start + ROWS, levels)) for start in range(0, levels, ROWS)]
    small = [
        pltpu.make_async_copy(source, target, semaphores.at[place])
        for place, (source, target) in enumerate(
            ((flux_hbm, flux), (face_hbm, neighbour_face), (way_hbm, orientation))
        )
    ]
    large = []
    for place, (low, high) in enumerate(groups):
        rows = pl.ds(low * POINTS, (high - low) * POINTS)
        large.append(
            pltpu.make_async_copy(
                state_hbm.at[:, rows, :], state.at[:, rows, :], semaphores.at[len(small) + place]
            )
        )
    for copy in small[:1] + large + small[1:]:
        copy.start()
    column[...] = jnp.zeros_like(column)
    lane = lax.broadcasted_iota(jnp.int32, (ROWS, lanes), 1)
    small[0].wait()
    packed = [jnp.zeros((ROWS, lanes), jnp.float32) for _ in range(to_sides.shape[0] // ROWS)]
    arrived = 0
    for piece, start in enumerate(chunks(levels)):
        while arrived < len(groups) and groups[arrived][0] < start + ROWS:
            large[arrived].wait()
            arrived += 1
        for place, point in enumerate(RIM_POINTS):
            rows = [
                state[g, pl.ds(start * POINTS + point, ROWS, stride=POINTS), :]
                for g in range(FIELDS)
            ]
            for f, out in ((3, speed), (4, column)):
                normal = flux[f, 0] * rows[0]
                for g in range(1, FIELDS):
                    normal = normal + flux[f, g] * rows[g]
                out[2 * place, pl.ds(ROWS + start, ROWS), :] = rows[f] + normal
                out[2 * place + 1, pl.ds(ROWS + start, ROWS), :] = rows[f] - normal
            for f in range(FIELDS):
                block, last, initial = side_lanes(f, piece, point)
                packed[block] = jnp.where(
                    lane == last, pltpu.roll(rows[f], last + 1, 1), packed[block]
                )
                packed[block] = jnp.where(
                    lane == initial, pltpu.roll(rows[f], initial, 1), packed[block]
                )
    for block, value in enumerate(packed):
        to_sides[block * ROWS : (block + 1) * ROWS, :] = value
    small[1].wait()
    small[2].wait()
    end = (levels + 2) * width
    for side, (out, face) in enumerate(((to_east, 1), (to_west, 0))):
        for place in range(width):
            slot = 2 * place + side
            for start in chunks(levels):
                upper = column[slot, pl.ds(ROWS + start + 1, ROWS), :]
                lower = column[slot, pl.ds(ROWS + start - 1, ROWS), :]
                out[pl.ds(start * width + place, ROWS, stride=width), :] = speed[
                    slot, pl.ds(ROWS + start, ROWS), :
                ] - gravity_couple * (upper - lower)
            for extra, level in ((0, 0), (1, levels - 1)):
                at = (levels + extra) * width + place
                out[at : at + 1, :] = column[slot, ROWS + level : ROWS + level + 1, :]
        out[end : end + 1, :] = neighbour_face[face : face + 1, :].astype(jnp.float32)
        out[end + 1 : end + 2, :] = orientation[face : face + 1, :].astype(jnp.float32)
        left = out.shape[0] - end - 2
        out[end + 2 :, :] = jnp.zeros((left, lanes), jnp.float32)


def face_kernel(state, from_west, from_east, flux, packed, to_west, to_east):
    count, lanes = state.shape[0] // POINTS, state.shape[1]
    levels = count // FIELDS
    at = (levels + 2) * len(RIM_POINTS)
    sides = []
    for source, out, sign in ((from_west, to_west, -1.0), (from_east, to_east, 1.0)):
        face = source[at : at + 1, :].astype(jnp.int32)
        flip = source[at + 1 : at + 2, :].astype(jnp.int32)
        sides.append((*table_masks(face, flip, lanes), out, sign))
    for start in chunks(levels):
        values = []
        for g in range(FIELDS):
            values.append(
                {
                    point: state[
                        pl.ds((g * levels + start) * POINTS + point, ROWS, stride=POINTS), :
                    ]
                    for point in RIM_POINTS
                }
            )
        for masks, flip, out, sign in sides:
            picked = [pick(values[g], masks, flip) for g in range(FIELDS)]
            for place, f in enumerate(LATE_FIELDS):
                for k in range(NODES):
                    normal = flux[f, 0] * picked[0][k]
                    for g in range(1, FIELDS):
                        normal = normal + flux[f, g] * picked[g][k]
                    out[pl.ds((place * levels + start) * NODES + k, ROWS, stride=NODES), :] = (
                        picked[f][k] + sign * normal
                    )


def element_kernel(
    state,
    from_down,
    from_up,
    neighbour_face,
    orientation,
    metric,
    first_flux,
    second_flux,
    tables,
    part,
    base,
    outer,
    operator_high,
    operator_low,
):
    levels = state.shape[0] // (FIELDS * POINTS)
    lanes = state.shape[1]
    lane = lax.broadcasted_iota(jnp.int32, (ROWS, lanes), 1)
    sides = []
    for side, (face, edge, received) in enumerate(((2, 0, from_down), (3, lanes - 1, from_up))):
        shift = 1 if side == 0 else lanes - 1
        row = neighbour_face[face : face + 1, :]
        way = orientation[face : face + 1, :]
        here, here_flip = table_masks(row, way, lanes)
        moved_face = pltpu.roll(jnp.broadcast_to(row, (ROWS, lanes)), lanes - shift, 1)
        moved_way = pltpu.roll(jnp.broadcast_to(way, (ROWS, lanes)), lanes - shift, 1)
        there = [moved_face == option for option in range(4)]
        sides.append((shift, edge, received, here, here_flip, there, moved_way == 1))
    for f in range(FIELDS):
        for piece, start in enumerate(chunks(levels)):
            q = f * levels + start
            values = {
                point: state[pl.ds(q * POINTS + point, ROWS, stride=POINTS), :]
                for point in RIM_POINTS
            }
            for side, (shift, edge, received, here, here_flip, there, flip) in enumerate(sides):
                beyond = {}
                for point in RIM_POINTS:
                    block, *places = side_lanes(f, piece, point)
                    beyond[point] = pltpu.roll(
                        received[block * ROWS : (block + 1) * ROWS, :],
                        (edge - places[side]) % lanes,
                        1,
                    )
                inner = pick(values, there, flip)
                rim = pick(beyond, here, here_flip)
                for k in range(NODES):
                    row_k = jnp.where(lane == edge, rim[k], pltpu.roll(inner[k], shift, 1))
                    at = start * 8 * FIELDS + 8 * f + NODES * side + k
                    outer[pl.ds(at, ROWS, stride=8 * FIELDS), :] = row_k
    index = lax.broadcasted_iota(jnp.int32, (1, lanes), 1)
    own_columns = FIELDS * POINTS
    owner = jnp.where(index < own_columns, index // POINTS, (index - own_columns) // 8)
    for f in range(FIELDS):
        first_row = jnp.zeros((1, lanes), jnp.float32)
        second_row = first_row
        for g in range(FIELDS):
            first_row = jnp.where(owner == g, first_flux[f, g], first_row)
            second_row = jnp.where(owner == g, second_flux[f, g], second_row)
        block = (
            first_row * tables[0:POINTS, :]
            + second_row * tables[POINTS : 2 * POINTS, :]
            + tables[(2 + f) * POINTS : (3 + f) * POINTS, :]
        )
        high = block.astype(jnp.bfloat16)
        operator_high[f * POINTS : (f + 1) * POINTS, :] = high
        operator_low[f * POINTS : (f + 1) * POINTS, :] = (
            block - high.astype(jnp.float32)
        ).astype(jnp.bfloat16)
    high = operator_high[...]
    low = operator_low[...]
    scale = step_size * metric[...]
    blank = jnp.zeros((lanes - own_columns - 8 * FIELDS, lanes), jnp.float32)
    for pair in range(0, levels, 2):
        sides = []
        for level in (pair, pair + 1):
            rows = [
                state[pl.ds((f * levels + level) * POINTS, POINTS), :] for f in range(FIELDS)
            ]
            rows.append(outer[pl.ds(level * 8 * FIELDS, 8 * FIELDS), :])
            rows.append(blank)
            sides.append(jnp.concatenate(rows, axis=0))
        values = jnp.concatenate(sides, axis=1)
        top = values.astype(jnp.bfloat16)
        rest = (values - top.astype(jnp.float32)).astype(jnp.bfloat16)
        change = (
            jnp.dot(high, top, preferred_element_type=jnp.float32)
            + jnp.dot(high, rest, preferred_element_type=jnp.float32)
            + jnp.dot(low, top, preferred_element_type=jnp.float32)
        )
        for place, level in enumerate((pair, pair + 1)):
            for f in range(FIELDS):
                at = pl.ds((f * levels + level) * POINTS, POINTS)
                part[at, :] = (
                    state[at, :]
                    + scale
                    * change[
                        f * POINTS : (f + 1) * POINTS, place * lanes : (place + 1) * lanes
                    ]
                )
    for level in range(levels):
        speed = part[pl.ds((3 * levels + level) * POINTS, POINTS), :]
        upper = part[pl.ds((4 * levels + level + 1) * POINTS, POINTS), :] if level < levels - 1 else 0.0
        lower = part[pl.ds((4 * levels + level - 1) * POINTS, POINTS), :] if level else 0.0
        value = speed - gravity_couple * (upper - lower)
        for j in range(NODES):
            base[j, level * NODES : (level + 1) * NODES, :] = value[NODES * j : NODES * (j + 1)]
    for extra, level in ((0, 0), (1, levels - 1)):
        value = part[pl.ds((4 * levels + level) * POINTS, POINTS), :]
        at = (levels + extra) * NODES
        for j in range(NODES):
            base[j, at : at + NODES, :] = value[NODES * j : NODES * (j + 1)]


def pack_kernel(base, from_west, from_east, neighbour_face, orientation, metric, *rest):
    sends, (send,) = rest[:NODES], rest[NODES:]
    me = lax.axis_index("vz")
    lanes = base.shape[2]
    width = len(RIM_POINTS)
    scale = (0.5 * lift_weight * step_size) * metric[...]
    send[...] = base[...]
    for face, source, i in ((0, from_west, 0), (1, from_east, NODES - 1)):
        masks, flip = table_masks(
            neighbour_face[face : face + 1, :], orientation[face : face + 1, :], lanes
        )
        for start in chunks(base.shape[1] // NODES):
            values = {
                point: source[pl.ds(start * width + place, ROWS, stride=width), :]
                for place, point in enumerate(RIM_POINTS)
            }
            for j, row in enumerate(pick(values, masks, flip)):
                point = NODES * j + i
                at = pl.ds(start * NODES + i, ROWS, stride=NODES)
                send[j, at, :] = base[j, at, :] + scale[point : point + 1, :] * row
    for way in range(NODES):
        sends[way][...] = send[me ^ way]


def finish_section_kernel(part, from_west, from_east, metric, out, done, final, semaphore):
    levels = part.shape[0] // (FIELDS * POINTS)
    size = levels * POINTS
    scale = (0.5 * lift_weight * step_size) * metric[...]
    copy = pltpu.make_async_copy(final, out.at[1:3], semaphore)
    for place, f in ((1, 1), (2, 2), (0, 0), (3, 4)):
        target = final.at[f - 1] if f in (1, 2) else done.at[min(f, 1)]
        target[...] = part[f * size : (f + 1) * size, :]
        for j in range(NODES):
            for source, i in ((from_west, 0), (from_east, NODES - 1)):
                point = NODES * j + i
                for start in chunks(levels):
                    rows = source[
                        pl.ds((place * levels + start) * NODES + j, ROWS, stride=NODES), :
                    ]
                    target[pl.ds(start * POINTS + point, ROWS, stride=POINTS), :] = (
                        part[pl.ds(f * size + start * POINTS + point, ROWS, stride=POINTS), :]
                        + scale[point : point + 1, :] * rows
                    )
        if f == 2:
            copy.start()
    copy.wait()


def factor_kernel(coupling, damping, far, near, inverse, ratio, second):
    levels = coupling.shape[1]
    shape = coupling.shape[2:]
    blank = jnp.zeros(shape, jnp.float32)
    far_ratio, far_second, near_ratio, near_second = (blank,) * 4
    extra = damping[...]
    for level in range(levels):
        a, b, d, e = (coupling[entry, level] for entry in range(4))
        centre = a + b + d + e + extra
        reduced = -b + a * far_ratio
        pivot = centre + a * far_second - reduced * near_ratio
        scaled = 1.0 / pivot
        upper_ratio = (-d - reduced * near_second) * scaled
        second_ratio = -e * scaled
        far[level] = a * scaled
        near[level] = reduced * scaled
        inverse[level] = scaled
        ratio[level] = upper_ratio
        second[level] = second_ratio
        far_ratio, far_second = near_ratio, near_second
        near_ratio, near_second = upper_ratio, second_ratio


def solve_kernel(far, near, inverse, ratio, second, *rest):
    ways = NODES
    received, sends, (source, heat, speed) = rest[:ways], rest[ways : 2 * ways], rest[2 * ways :]
    levels = far.shape[0]
    here = levels // ways
    me = lax.axis_index("vz")
    for way in range(ways):
        block = me ^ way
        source[pl.ds(block * here, here)] = received[way][0:here]
        heat[block] = received[way][here : here + 2]
    for block in range(ways - 1):
        last = block * here + here - 1
        source[last] = source[last] - gravity_couple * heat[block + 1, 0]
        source[last + 1] = source[last + 1] + gravity_couple * heat[block, 1]
    blank = jnp.zeros(far.shape[1:], jnp.float32)
    before_two, before_one = blank, blank
    for level in range(levels):
        value = source[level] * inverse[level]
        value = value + far[level] * before_two
        value = value - near[level] * before_one
        source[level] = value
        before_two, before_one = before_one, value
    speed[0] = blank
    speed[levels + 1] = blank
    next_one, next_two = blank, blank
    for level in range(levels - 1, -1, -1):
        value = source[level] - second[level] * next_two
        value = value - ratio[level] * next_one
        speed[level + 1] = value
        next_two, next_one = next_one, value
    for way in range(ways):
        sends[way][...] = speed[pl.ds((me ^ way) * here, here + 2)]


def update_kernel(*refs):
    ways = NODES
    received, (done, earlier, out, speed, final, semaphores) = refs[:ways], refs[ways:]
    levels = done.shape[1] // POINTS
    me = lax.axis_index("vz")
    for way in range(ways):
        speed[me ^ way] = received[way][...]
    copies = [
        pltpu.make_async_copy(final.at[place], out.at[f], semaphores.at[place])
        for place, f in enumerate((0, 3, 4))
    ]
    for place in (1, 0, 2):
        for j in range(NODES):
            for i in range(NODES):
                for start in chunks(levels):
                    lower, value, upper = (
                        speed[j, pl.ds((start + k) * NODES + i, ROWS, stride=NODES), :]
                        for k in range(3)
                    )
                    at = pl.ds(start * POINTS + NODES * j + i, ROWS, stride=POINTS)
                    if place == 1:
                        final[1, at, :] = value
                    elif place == 0:
                        final[0, at, :] = done[0, at, :] - density_couple * (upper - lower)
                    else:
                        final[2, at, :] = done[1, at, :] - theta_couple * (upper - lower)
        copies[place].start()
    for copy in copies:
        copy.wait()


VMEM = pl.BlockSpec(memory_space=pltpu.VMEM)
SMEM = pl.BlockSpec(memory_space=pltpu.SMEM)
HBM = pl.BlockSpec(memory_space=pltpu.HBM)
ANY = pl.BlockSpec(memory_space=pl.ANY)


def call(kernel, outs, in_specs, scratch=(), cost=0, name=None):
    kinds = [pltpu.VMEM(shape, jnp.float32) for shape in outs]
    return pl.pallas_call(
        kernel,
        out_shape=kinds,
        in_specs=in_specs,
        out_specs=[VMEM] * len(outs),
        scratch_shapes=list(scratch),
        compiler_params=pltpu.CompilerParams(vmem_limit_bytes=24 * 1024 * 1024),
        cost_estimate=pl.CostEstimate(flops=cost, bytes_accessed=cost, transcendentals=0),
        name=name,
    )


def per_device(
    prognostic, metric, first_flux, second_flux, neighbour_face, orientation, coupling, damping
):
    fields, levels = prognostic.shape[:2]
    lanes = prognostic.shape[-1]
    whole = (fields, levels * POINTS, lanes)
    metric = metric.reshape(POINTS, lanes)
    neighbour_face = neighbour_face.reshape(4, lanes)
    orientation = orientation.reshape(4, lanes)
    coupling = coupling.reshape(4, coupling.shape[1], NODES, lanes)
    damping = damping.reshape(NODES, lanes)
    tables, _ = operator_tables(lanes)

    def shifts(axis):
        size = lax.axis_size(axis)
        up = [(i, (i + 1) % size) for i in range(size)]
        return up, [(j, i) for i, j in up]

    def exchange(arrays):
        size = lax.axis_size("vz")
        moved = [arrays[0]] + [None] * (size - 1)
        for way in (3, 1, 2):
            moved[way] = lax.ppermute(arrays[way], "vz", [(i, i ^ way) for i in range(size)])
        return moved

    first_up, first_down = shifts("hy")
    second_up, second_down = shifts("hx")
    width = len(RIM_POINTS)
    message = (-(-((levels + 2) * width + 2) // ROWS) * ROWS, lanes)
    sides = (-(-fields * len(chunks(levels)) // 4) * ROWS, lanes)
    padded = levels + 2 * ROWS
    to_east, to_west, to_sides, state = call(
        rim_kernel,
        [message, message, sides, whole],
        [HBM] * 4,
        [
            pltpu.VMEM((2 * width, padded, lanes), jnp.float32),
            pltpu.VMEM((2 * width, padded, lanes), jnp.float32),
            pltpu.VMEM((4, lanes), jnp.int32),
            pltpu.VMEM((4, lanes), jnp.int32),
            pltpu.SMEM((fields, fields), jnp.float32),
            pltpu.SemaphoreType.DMA((3 + -(-levels // ROWS),)),
        ],
        cost=1000,
        name="rim",
    )(
        *(
            pltpu.with_memory_space_constraint(x, pltpu.HBM)
            for x in (prognostic.reshape(whole), neighbour_face, orientation, first_flux)
        )
    )
    state = state.reshape(fields * levels * POINTS, lanes)
    from_east = lax.ppermute(to_west, "hy", first_down)
    from_west = lax.ppermute(to_east, "hy", first_up)
    from_down = lax.ppermute(to_sides, "hx", second_up)
    from_up = from_down
    if lax.axis_size("hx") > 2:
        from_up = lax.ppermute(to_sides, "hx", second_down)

    column = (coupling.shape[1], NODES, lanes)
    factors = call(factor_kernel, [column] * 5, [VMEM] * 2, cost=4000000, name="factor")(
        coupling, damping
    )
    block = ((levels + 2) * NODES, lanes)
    part, base = call(
        element_kernel,
        [state.shape, (NODES,) + block],
        [VMEM] * 6 + [SMEM] * 2 + [VMEM],
        [
            pltpu.VMEM((levels * 8 * fields, lanes), jnp.float32),
            pltpu.VMEM((fields * POINTS, lanes), jnp.bfloat16),
            pltpu.VMEM((fields * POINTS, lanes), jnp.bfloat16),
        ],
        cost=4000000,
        name="element",
    )(
        state,
        from_down,
        from_up,
        neighbour_face,
        orientation,
        metric,
        first_flux,
        second_flux,
        jnp.asarray(tables),
    )
    sends = call(
        pack_kernel,
        [block] * NODES,
        [VMEM] * 6,
        [pltpu.VMEM((NODES,) + block, jnp.float32)],
        cost=1000,
        name="pack",
    )(base, from_west, from_east, neighbour_face, orientation, metric)
    received = exchange(sends)

    late = (len(LATE_FIELDS) * levels * NODES, lanes)
    late_west, late_east = call(
        face_kernel, [late, late], [VMEM] * 3 + [SMEM, ANY], cost=4000000, name="face"
    )(state, from_west, from_east, first_flux, sends[0])
    late_from_east = lax.ppermute(late_west, "hy", first_down)
    late_from_west = lax.ppermute(late_east, "hy", first_up)

    cube = (levels + 2, NODES, lanes)
    speeds = call(
        solve_kernel,
        [cube] * NODES,
        [VMEM] * (5 + NODES),
        [
            pltpu.VMEM(column, jnp.float32),
            pltpu.VMEM((NODES, 2, NODES, lanes), jnp.float32),
            pltpu.VMEM((column[0] + 2,) + column[1:], jnp.float32),
        ],
        cost=1000,
        name="solve",
    )(*factors, *[x.reshape(cube) for x in received])
    returned = exchange([x.reshape(block) for x in speeds])
    size = levels * POINTS
    limits = pltpu.CompilerParams(vmem_limit_bytes=24 * 1024 * 1024)
    earlier, done = pl.pallas_call(
        finish_section_kernel,
        out_shape=[
            jax.ShapeDtypeStruct(whole, jnp.float32),
            pltpu.VMEM((2, size, lanes), jnp.float32),
        ],
        in_specs=[VMEM] * 4,
        out_specs=[HBM, VMEM],
        scratch_shapes=[pltpu.VMEM((2, size, lanes), jnp.float32), pltpu.SemaphoreType.DMA],
        compiler_params=limits,
        cost_estimate=pl.CostEstimate(flops=4000000, bytes_accessed=4000000, transcendentals=0),
        name="finish",
    )(part, late_from_west, late_from_east, metric)
    updated = pl.pallas_call(
        update_kernel,
        out_shape=jax.ShapeDtypeStruct(whole, jnp.float32),
        in_specs=[VMEM] * (1 + NODES) + [HBM],
        out_specs=HBM,
        input_output_aliases={1 + NODES: 0},
        scratch_shapes=[
            pltpu.VMEM((NODES,) + block, jnp.float32),
            pltpu.VMEM((3, size, lanes), jnp.float32),
            pltpu.SemaphoreType.DMA((3,)),
        ],
        compiler_params=limits,
        name="update",
    )(*returned, done, earlier)
    return updated.reshape(prognostic.shape)


def solution(mesh):
    placed = (
        P(None, "vz", None, None, "hy", "hx"),
        P(None, None, "hy", "hx"),
        P(),
        P(),
        P(None, "hy", "hx"),
        P(None, "hy", "hx"),
        P(None, None, "vz", None, "hy", "hx"),
        P("vz", None, "hy", "hx"),
    )
    return jax.shard_map(
        per_device,
        mesh=mesh,
        in_specs=placed,
        out_specs=P(None, "vz", None, None, "hy", "hx"),
        check_vma=False,
    )
```

```python
import jax
import jax.numpy as jnp
import numpy as np
from jax import lax
from jax.experimental import pallas as pl
from jax.experimental.pallas import tpu as pltpu
from jax.sharding import PartitionSpec as P

step_size = 0.05
lift_weight = 6.0
gravity_couple = 0.5
density_couple = 0.3
theta_couple = 0.4

NODES = 4
POINTS = NODES * NODES
FIELDS = 5
FACE_POINTS = ((0, 4, 8, 12), (3, 7, 11, 15), (0, 1, 2, 3), (12, 13, 14, 15))
RIM_POINTS = tuple(sorted(set(sum(FACE_POINTS, ()))))
ROWS = 8
LATE_FIELDS = (0, 1, 2, 4)


def derivative_table():
    points = np.array([-1.0, -1.0 / np.sqrt(5.0), 1.0 / np.sqrt(5.0), 1.0])
    number = points.shape[0]
    barycentric = np.ones(number)
    for source in range(number):
        for another in range(number):
            if another != source:
                barycentric[source] = barycentric[source] / (points[source] - points[another])
    matrix = np.zeros((number, number))
    for target in range(number):
        for source in range(number):
            if target != source:
                matrix[target, source] = (
                    barycentric[source] / barycentric[target] / (points[target] - points[source])
                )
        matrix[target, target] = -np.sum(matrix[target])
    return matrix


def operator_tables(lanes):
    weight = 0.5 * lift_weight
    table = derivative_table()
    table[0, 0] += weight
    table[-1, -1] -= weight
    eye = np.eye(NODES)
    along_first = np.kron(eye, table)
    along_second = np.kron(table, eye)
    ends = np.zeros(NODES)
    ends[0] = ends[-1] = 1.0
    faces = np.diag(np.kron(np.ones(NODES), ends) + np.kron(ends, np.ones(NODES)))
    first = np.zeros((POINTS, lanes))
    second = np.zeros((POINTS, lanes))
    same = np.zeros((FIELDS, POINTS, lanes))
    owner = np.full((lanes,), -1)
    for g in range(FIELDS):
        own = slice(POINTS * g, POINTS * (g + 1))
        first[:, own] = -along_first
        second[:, own] = -along_second
        same[g, :, own] = -weight * faces
        owner[own] = g
        for k in range(NODES):
            south = FIELDS * POINTS + 2 * NODES * g + k
            north = south + NODES
            second[FACE_POINTS[2][k], south] = weight
            second[FACE_POINTS[3][k], north] = -weight
            same[g, FACE_POINTS[2][k], south] = weight
            same[g, FACE_POINTS[3][k], north] = weight
            owner[south] = owner[north] = g
    tables = np.concatenate([first, second, same.reshape(FIELDS * POINTS, lanes)])
    return tables.astype(np.float32), owner


def chunks(total):
    return [min(start, total - ROWS) for start in range(0, total, ROWS)]


def ends(total):
    return list(range(0, total, ROWS))


def pick(values, masks, flip):
    chosen = []
    for k in range(NODES):
        row = values[FACE_POINTS[0][k]]
        for option in range(1, 4):
            row = jnp.where(masks[option], values[FACE_POINTS[option][k]], row)
        chosen.append(row)
    return [jnp.where(flip, chosen[NODES - 1 - k], chosen[k]) for k in range(NODES)]


def table_masks(face_row, flip_row, lanes):
    face = jnp.broadcast_to(face_row, (ROWS, lanes))
    flip = jnp.broadcast_to(flip_row, (ROWS, lanes))
    return [face == option for option in range(4)], flip == 1


def flux_row(f, g, matrix):
    return (matrix * FIELDS + f) * FIELDS + g


def along(fluxes, matrix, f, rows):
    total = None
    for g in range(FIELDS):
        at = flux_row(f, g, matrix)
        term = fluxes[at : at + 1, :] * rows[g]
        total = term if total is None else total + term
    return total


def side_lanes(f, piece, point):
    number = 3 * f + piece
    return number // 4, 32 * (number % 4) + point, 32 * (number % 4) + POINTS + point


def rim_kernel(
    state_hbm,
    face_hbm,
    way_hbm,
    metric_hbm,
    tables_hbm,
    flux_hbm,
    second_hbm,
    to_east,
    to_west,
    to_sides,
    state,
    neighbour_face,
    orientation,
    metric,
    tables,
    fluxes,
    column,
    speed,
    flux,
    second_flux,
    semaphores,
):
    levels = state.shape[1] // POINTS
    lanes = state.shape[2]
    width = len(RIM_POINTS)
    groups = [(start, min(start + ROWS, levels)) for start in range(0, levels, ROWS)]
    small = [
        pltpu.make_async_copy(source, target, semaphores.at[place])
        for place, (source, target) in enumerate(
            (
                (flux_hbm, flux),
                (face_hbm, neighbour_face),
                (way_hbm, orientation),
                (metric_hbm, metric),
                (tables_hbm, tables),
                (second_hbm, second_flux),
            )
        )
    ]
    large = []
    for place, (low, high) in enumerate(groups):
        rows = pl.ds(low * POINTS, (high - low) * POINTS)
        large.append(
            pltpu.make_async_copy(
                state_hbm.at[:, rows, :], state.at[:, rows, :], semaphores.at[len(small) + place]
            )
        )
    for copy in small[:1] + large + small[1:]:
        copy.start()
    column[...] = jnp.zeros_like(column)
    lane = lax.broadcasted_iota(jnp.int32, (ROWS, lanes), 1)
    small[0].wait()
    packed = [jnp.zeros((ROWS, lanes), jnp.float32) for _ in range(to_sides.shape[0] // ROWS)]
    arrived = 0
    for piece, start in enumerate(chunks(levels)):
        while arrived < len(groups) and groups[arrived][0] < start + ROWS:
            large[arrived].wait()
            arrived += 1
        for place, point in enumerate(RIM_POINTS):
            rows = [
                state[g, pl.ds(start * POINTS + point, ROWS, stride=POINTS), :]
                for g in range(FIELDS)
            ]
            for f, out in ((3, speed), (4, column)):
                normal = flux[f, 0] * rows[0]
                for g in range(1, FIELDS):
                    normal = normal + flux[f, g] * rows[g]
                out[2 * place, pl.ds(ROWS + start, ROWS), :] = rows[f] + normal
                out[2 * place + 1, pl.ds(ROWS + start, ROWS), :] = rows[f] - normal
            for f in range(FIELDS):
                block, last, initial = side_lanes(f, piece, point)
                packed[block] = jnp.where(
                    lane == last, pltpu.roll(rows[f], last + 1, 1), packed[block]
                )
                packed[block] = jnp.where(
                    lane == initial, pltpu.roll(rows[f], initial, 1), packed[block]
                )
    for block, value in enumerate(packed):
        to_sides[block * ROWS : (block + 1) * ROWS, :] = value
    small[1].wait()
    small[2].wait()
    end = (levels + 2) * width
    for side, (out, face) in enumerate(((to_east, 1), (to_west, 0))):
        for place in range(width):
            slot = 2 * place + side
            for start in chunks(levels):
                upper = column[slot, pl.ds(ROWS + start + 1, ROWS), :]
                lower = column[slot, pl.ds(ROWS + start - 1, ROWS), :]
                out[pl.ds(start * width + place, ROWS, stride=width), :] = speed[
                    slot, pl.ds(ROWS + start, ROWS), :
                ] - gravity_couple * (upper - lower)
            for extra, level in ((0, 0), (1, levels - 1)):
                at = (levels + extra) * width + place
                out[at : at + 1, :] = column[slot, ROWS + level : ROWS + level + 1, :]
        out[end : end + 1, :] = neighbour_face[face : face + 1, :].astype(jnp.float32)
        out[end + 1 : end + 2, :] = orientation[face : face + 1, :].astype(jnp.float32)
        left = out.shape[0] - end - 2
        out[end + 2 :, :] = jnp.zeros((left, lanes), jnp.float32)
    small[3].wait()
    small[4].wait()
    small[5].wait()
    for place, source in enumerate((flux, second_flux)):
        for f in range(FIELDS):
            for g in range(FIELDS):
                at = flux_row(f, g, place)
                fluxes[at : at + 1, :] = jnp.full((1, lanes), source[f, g])


def face_kernel(state, from_west, from_east, fluxes, packed, faces):
    count, lanes = state.shape[0] // POINTS, state.shape[1]
    levels = count // FIELDS
    at = (levels + 2) * len(RIM_POINTS)
    sides = []
    for source, out, sign in ((from_west, faces.at[0], -1.0), (from_east, faces.at[1], 1.0)):
        face = source[at : at + 1, :].astype(jnp.int32)
        flip = source[at + 1 : at + 2, :].astype(jnp.int32)
        sides.append((*table_masks(face, flip, lanes), out, sign))
    for start in chunks(levels):
        values = []
        for g in range(FIELDS):
            values.append(
                {
                    point: state[
                        pl.ds((g * levels + start) * POINTS + point, ROWS, stride=POINTS), :
                    ]
                    for point in RIM_POINTS
                }
            )
        for masks, flip, out, sign in sides:
            picked = [pick(values[g], masks, flip) for g in range(FIELDS)]
            for place, f in enumerate(LATE_FIELDS):
                for k in range(NODES):
                    normal = along(fluxes, 0, f, [picked[g][k] for g in range(FIELDS)])
                    out[pl.ds((place * levels + start) * NODES + k, ROWS, stride=NODES), :] = (
                        picked[f][k] + sign * normal
                    )


def element_kernel(
    state,
    neighbour_face,
    orientation,
    metric,
    fluxes,
    tables,
    part,
    base,
    outer,
    operator_high,
    operator_low,
):
    levels = state.shape[0] // (FIELDS * POINTS)
    lanes = state.shape[1]
    lane = lax.broadcasted_iota(jnp.int32, (ROWS, lanes), 1)
    sides = []
    for side, (face, edge) in enumerate(((2, 0), (3, lanes - 1))):
        shift = 1 if side == 0 else lanes - 1
        row = jnp.broadcast_to(neighbour_face[face : face + 1, :], (ROWS, lanes))
        way = jnp.broadcast_to(orientation[face : face + 1, :], (ROWS, lanes))
        masks, flip = table_masks(
            pltpu.roll(row, lanes - shift, 1), pltpu.roll(way, lanes - shift, 1), lanes
        )
        sides.append((shift, edge, masks, flip))
    for f in range(FIELDS):
        for start in chunks(levels):
            q = f * levels + start
            values = {
                point: state[pl.ds(q * POINTS + point, ROWS, stride=POINTS), :]
                for point in RIM_POINTS
            }
            for side, (shift, edge, masks, flip) in enumerate(sides):
                for k, row in enumerate(pick(values, masks, flip)):
                    at = start * 8 * FIELDS + 8 * f + NODES * side + k
                    outer[pl.ds(at, ROWS, stride=8 * FIELDS), :] = jnp.where(
                        lane == edge, 0.0, pltpu.roll(row, shift, 1)
                    )
    index = lax.broadcasted_iota(jnp.int32, (1, lanes), 1)
    own_columns = FIELDS * POINTS
    owner = jnp.where(index < own_columns, index // POINTS, (index - own_columns) // 8)
    for f in range(FIELDS):
        first_row = jnp.zeros((1, lanes), jnp.float32)
        second_row = first_row
        for g in range(FIELDS):
            first, second = (flux_row(f, g, matrix) for matrix in range(2))
            first_row = jnp.where(owner == g, fluxes[first : first + 1, :], first_row)
            second_row = jnp.where(owner == g, fluxes[second : second + 1, :], second_row)
        block = (
            first_row * tables[0:POINTS, :]
            + second_row * tables[POINTS : 2 * POINTS, :]
            + tables[(2 + f) * POINTS : (3 + f) * POINTS, :]
        )
        high = block.astype(jnp.bfloat16)
        operator_high[f * POINTS : (f + 1) * POINTS, :] = high
        operator_low[f * POINTS : (f + 1) * POINTS, :] = (
            block - high.astype(jnp.float32)
        ).astype(jnp.bfloat16)
    high = operator_high[...]
    low = operator_low[...]
    scale = step_size * metric[...]
    blank = jnp.zeros((lanes - own_columns - 8 * FIELDS, lanes), jnp.float32)
    for pair in range(0, levels, 2):
        sides = []
        for level in (pair, pair + 1):
            rows = [
                state[pl.ds((f * levels + level) * POINTS, POINTS), :] for f in range(FIELDS)
            ]
            rows.append(outer[pl.ds(level * 8 * FIELDS, 8 * FIELDS), :])
            rows.append(blank)
            sides.append(jnp.concatenate(rows, axis=0))
        values = jnp.concatenate(sides, axis=1)
        top = values.astype(jnp.bfloat16)
        rest = (values - top.astype(jnp.float32)).astype(jnp.bfloat16)
        change = (
            jnp.dot(high, top, preferred_element_type=jnp.float32)
            + jnp.dot(high, rest, preferred_element_type=jnp.float32)
            + jnp.dot(low, top, preferred_element_type=jnp.float32)
        )
        for place, level in enumerate((pair, pair + 1)):
            for f in range(FIELDS):
                at = pl.ds((f * levels + level) * POINTS, POINTS)
                part[at, :] = (
                    state[at, :]
                    + scale
                    * change[
                        f * POINTS : (f + 1) * POINTS, place * lanes : (place + 1) * lanes
                    ]
                )
    for level in range(levels):
        speed = part[pl.ds((3 * levels + level) * POINTS, POINTS), :]
        upper = part[pl.ds((4 * levels + level + 1) * POINTS, POINTS), :] if level < levels - 1 else 0.0
        lower = part[pl.ds((4 * levels + level - 1) * POINTS, POINTS), :] if level else 0.0
        value = speed - gravity_couple * (upper - lower)
        for j in range(NODES):
            base[j, level * NODES : (level + 1) * NODES, :] = value[NODES * j : NODES * (j + 1)]
    for extra, level in ((0, 0), (1, levels - 1)):
        value = part[pl.ds((4 * levels + level) * POINTS, POINTS), :]
        at = (levels + extra) * NODES
        for j in range(NODES):
            base[j, at : at + NODES, :] = value[NODES * j : NODES * (j + 1)]


def side_corrections(received, side, fluxes, fields, pieces):
    lanes = received.shape[1]
    sign = 1.0 if side == 0 else -1.0
    result = [[] for _ in fields]
    for piece in range(pieces):
        rows = []
        for g in range(FIELDS):
            block, *places = side_lanes(g, piece, 0)
            rows.append(
                pltpu.roll(
                    received[block * ROWS : (block + 1) * ROWS, :], (lanes - places[side]) % lanes, 1
                )
            )
        for place, f in enumerate(fields):
            result[place].append(rows[f] + sign * along(fluxes, 1, f, rows))
    return result


def spread(value, edge, masks, flip):
    lanes = value.shape[1]
    return pick(
        {point: pltpu.roll(value, (edge - point) % lanes, 1) for point in RIM_POINTS}, masks, flip
    )


def pack_kernel(
    base,
    from_west,
    from_east,
    from_down,
    from_up,
    neighbour_face,
    orientation,
    metric,
    fluxes,
    *rest,
):
    sends, (send, column, mixed) = rest[:NODES], rest[NODES:]
    me = lax.axis_index("vz")
    rows, lanes = base.shape[1:]
    levels = rows // NODES - 2
    width = len(RIM_POINTS)
    scale = (0.5 * lift_weight * step_size) * metric[...]
    send[:, 0:rows, :] = base[...]
    send[:, rows:, :] = jnp.zeros((NODES, send.shape[1] - rows, lanes), jnp.float32)
    column[...] = jnp.zeros_like(column)
    mixed[...] = jnp.zeros_like(mixed)
    for face, source, i in ((0, from_west, 0), (1, from_east, NODES - 1)):
        masks, flip = table_masks(
            neighbour_face[face : face + 1, :], orientation[face : face + 1, :], lanes
        )
        for start in chunks(levels + 2):
            values = {
                point: source[pl.ds(start * width + place, ROWS, stride=width), :]
                for place, point in enumerate(RIM_POINTS)
            }
            for j, row in enumerate(pick(values, masks, flip)):
                point = NODES * j + i
                at = pl.ds(start * NODES + i, ROWS, stride=NODES)
                send[j, at, :] = base[j, at, :] + scale[point : point + 1, :] * row
    lane = lax.broadcasted_iota(jnp.int32, (ROWS, lanes), 1)
    for side, (received, edge, j) in enumerate(
        ((from_down, 0, 0), (from_up, lanes - 1, NODES - 1))
    ):
        face = 2 + side
        masks, flip = table_masks(
            neighbour_face[face : face + 1, :], orientation[face : face + 1, :], lanes
        )
        speed, heat = side_corrections(received, side, fluxes, (3, 4), len(chunks(levels)))
        for start, value in zip(chunks(levels), heat):
            column[pl.ds(ROWS + start, ROWS), :] = value
        for start, value in zip(chunks(levels), speed):
            upper = column[pl.ds(ROWS + start + 1, ROWS), :]
            lower = column[pl.ds(ROWS + start - 1, ROWS), :]
            mixed[pl.ds(start, ROWS), :] = value - gravity_couple * (upper - lower)
        mixed[levels : levels + 1, :] = column[ROWS : ROWS + 1, :]
        mixed[levels + 1 : levels + 2, :] = column[ROWS + levels - 1 : ROWS + levels, :]
        for start in ends(levels + 2):
            picked = spread(mixed[start : start + ROWS, :], edge, masks, flip)
            for k, row in enumerate(picked):
                point = NODES * j + k
                at = pl.ds(start * NODES + k, ROWS, stride=NODES)
                send[j, at, :] += jnp.where(lane == edge, scale[point : point + 1, :] * row, 0.0)
    for way in range(NODES):
        sends[way][...] = send[me ^ way, 0:rows, :]


def finish_section_kernel(
    part,
    faces,
    from_down,
    from_up,
    neighbour_face,
    orientation,
    metric,
    fluxes,
    out,
    done,
    final,
    beside,
    semaphores,
):
    levels = part.shape[0] // (FIELDS * POINTS)
    lanes = part.shape[1]
    size = levels * POINTS
    devices = faces.shape[0]
    me = lax.axis_index("hy")
    west = lax.rem(me + devices - 1, devices)
    east = lax.rem(me + 1, devices)
    loads = [
        pltpu.make_async_copy(faces.at[device, way], beside.at[side], semaphores.at[1 + side])
        for side, (device, way) in enumerate(((west, 1), (east, 0)))
    ]
    for load in loads:
        load.start()
    scale = (0.5 * lift_weight * step_size) * metric[...]
    lane = lax.broadcasted_iota(jnp.int32, (ROWS, lanes), 1)
    tables = []
    edges = []
    for side, received in enumerate((from_down, from_up)):
        face = 2 + side
        tables.append(
            table_masks(
                neighbour_face[face : face + 1, :], orientation[face : face + 1, :], lanes
            )
        )
        edges.append(
            side_corrections(received, side, fluxes, LATE_FIELDS, len(chunks(levels)))
        )
    copy = pltpu.make_async_copy(final, out.at[1:3], semaphores.at[0])
    for load in loads:
        load.wait()
    for place, f in ((1, 1), (2, 2), (0, 0), (3, 4)):
        target = final.at[f - 1] if f in (1, 2) else done.at[min(f, 1)]
        target[...] = part[f * size : (f + 1) * size, :]
        for piece, start in enumerate(chunks(levels)):
            for j in range(NODES):
                for source, i in ((beside.at[0], 0), (beside.at[1], NODES - 1)):
                    point = NODES * j + i
                    rows = source[
                        pl.ds((place * levels + start) * NODES + j, ROWS, stride=NODES), :
                    ]
                    at = pl.ds(start * POINTS + point, ROWS, stride=POINTS)
                    target[at, :] = (
                        part[pl.ds(f * size + start * POINTS + point, ROWS, stride=POINTS), :]
                        + scale[point : point + 1, :] * rows
                    )
        for piece, start in enumerate(chunks(levels)):
            row_index = lax.broadcasted_iota(jnp.int32, (ROWS, lanes), 0)
            fresh = row_index >= (-start) % ROWS
            for side, (edge, j) in enumerate(((0, 0), (lanes - 1, NODES - 1))):
                picked = spread(edges[side][place][piece], edge, *tables[side])
                for k, row in enumerate(picked):
                    point = NODES * j + k
                    at = pl.ds(start * POINTS + point, ROWS, stride=POINTS)
                    target[at, :] += jnp.where(
                        (lane == edge) & fresh, scale[point : point + 1, :] * row, 0.0
                    )
        if f == 2:
            copy.start()
    copy.wait()


def factor_kernel(coupling, damping, far, near, inverse, ratio, second):
    levels = coupling.shape[1]
    shape = coupling.shape[2:]
    blank = jnp.zeros(shape, jnp.float32)
    far_ratio, far_second, near_ratio, near_second = (blank,) * 4
    extra = damping[...]
    for level in range(levels):
        a, b, d, e = (coupling[entry, level] for entry in range(4))
        centre = a + b + d + e + extra
        reduced = -b + a * far_ratio
        pivot = centre + a * far_second - reduced * near_ratio
        scaled = 1.0 / pivot
        upper_ratio = (-d - reduced * near_second) * scaled
        second_ratio = -e * scaled
        far[level] = a * scaled
        near[level] = reduced * scaled
        inverse[level] = scaled
        ratio[level] = upper_ratio
        second[level] = second_ratio
        far_ratio, far_second = near_ratio, near_second
        near_ratio, near_second = upper_ratio, second_ratio


def solve_kernel(far, near, inverse, ratio, second, *rest):
    ways = NODES
    received, sends, (source, heat, speed) = rest[:ways], rest[ways : 2 * ways], rest[2 * ways :]
    levels = far.shape[0]
    here = levels // ways
    me = lax.axis_index("vz")
    for way in range(ways):
        block = me ^ way
        source[pl.ds(block * here, here)] = received[way][0:here]
        heat[block] = received[way][here : here + 2]
    for block in range(ways - 1):
        last = block * here + here - 1
        source[last] = source[last] - gravity_couple * heat[block + 1, 0]
        source[last + 1] = source[last + 1] + gravity_couple * heat[block, 1]
    blank = jnp.zeros(far.shape[1:], jnp.float32)
    before_two, before_one = blank, blank
    for level in range(levels):
        value = source[level] * inverse[level]
        value = value + far[level] * before_two
        value = value - near[level] * before_one
        source[level] = value
        before_two, before_one = before_one, value
    speed[0] = blank
    speed[levels + 1] = blank
    next_one, next_two = blank, blank
    for level in range(levels - 1, -1, -1):
        value = source[level] - second[level] * next_two
        value = value - ratio[level] * next_one
        speed[level + 1] = value
        next_two, next_one = next_one, value
    for way in range(ways):
        sends[way][...] = speed[pl.ds((me ^ way) * here, here + 2)]


def update_kernel(*refs):
    ways = NODES
    received, (done, earlier, out, speed, final, semaphores) = refs[:ways], refs[ways:]
    levels = done.shape[1] // POINTS
    me = lax.axis_index("vz")
    for way in range(ways):
        speed[me ^ way] = received[way][...]
    copies = [
        pltpu.make_async_copy(final.at[place], out.at[f], semaphores.at[place])
        for place, f in enumerate((0, 3, 4))
    ]
    for place in (1, 0, 2):
        for j in range(NODES):
            for i in range(NODES):
                for start in chunks(levels):
                    lower, value, upper = (
                        speed[j, pl.ds((start + k) * NODES + i, ROWS, stride=NODES), :]
                        for k in range(3)
                    )
                    at = pl.ds(start * POINTS + NODES * j + i, ROWS, stride=POINTS)
                    if place == 1:
                        final[1, at, :] = value
                    elif place == 0:
                        final[0, at, :] = done[0, at, :] - density_couple * (upper - lower)
                    else:
                        final[2, at, :] = done[1, at, :] - theta_couple * (upper - lower)
        copies[place].start()
    for copy in copies:
        copy.wait()


VMEM = pl.BlockSpec(memory_space=pltpu.VMEM)
HBM = pl.BlockSpec(memory_space=pltpu.HBM)
ANY = pl.BlockSpec(memory_space=pl.ANY)


def call(kernel, outs, in_specs, scratch=(), cost=0, name=None):
    kinds = [x if hasattr(x, "dtype") else pltpu.VMEM(x, jnp.float32) for x in outs]
    return pl.pallas_call(
        kernel,
        out_shape=kinds,
        in_specs=in_specs,
        out_specs=[VMEM] * len(outs),
        scratch_shapes=list(scratch),
        compiler_params=pltpu.CompilerParams(vmem_limit_bytes=24 * 1024 * 1024),
        cost_estimate=pl.CostEstimate(flops=cost, bytes_accessed=cost, transcendentals=0),
        name=name,
    )


def per_device(
    prognostic, metric, first_flux, second_flux, neighbour_face, orientation, coupling, damping
):
    fields, levels = prognostic.shape[:2]
    lanes = prognostic.shape[-1]
    whole = (fields, levels * POINTS, lanes)
    metric = metric.reshape(POINTS, lanes)
    neighbour_face = neighbour_face.reshape(4, lanes)
    orientation = orientation.reshape(4, lanes)
    coupling = coupling.reshape(4, coupling.shape[1], NODES, lanes)
    damping = damping.reshape(NODES, lanes)
    tables, _ = operator_tables(lanes)

    def shifts(axis):
        size = lax.axis_size(axis)
        up = [(i, (i + 1) % size) for i in range(size)]
        return up, [(j, i) for i, j in up]

    def exchange(arrays):
        size = lax.axis_size("vz")
        moved = [arrays[0]] + [None] * (size - 1)
        for way in (3, 1, 2):
            moved[way] = lax.ppermute(arrays[way], "vz", [(i, i ^ way) for i in range(size)])
        return moved

    first_up, first_down = shifts("hy")
    second_up, second_down = shifts("hx")
    width = len(RIM_POINTS)
    message = (-(-((levels + 2) * width + 2) // ROWS) * ROWS, lanes)
    sides = (-(-fields * len(chunks(levels)) // 4) * ROWS, lanes)
    padded = levels + 2 * ROWS
    table = pltpu.VMEM((4, lanes), jnp.int32)
    inputs = (
        prognostic.reshape(whole),
        neighbour_face,
        orientation,
        metric,
        jnp.asarray(tables),
        first_flux,
        second_flux,
    )
    (
        to_east,
        to_west,
        to_sides,
        state,
        neighbour_face,
        orientation,
        metric,
        tables,
        fluxes,
    ) = call(
        rim_kernel,
        [
            message,
            message,
            sides,
            whole,
            table,
            table,
            (POINTS, lanes),
            tables.shape,
            (-(-2 * fields * fields // ROWS) * ROWS, lanes),
        ],
        [HBM] * len(inputs),
        [
            pltpu.VMEM((2 * width, padded, lanes), jnp.float32),
            pltpu.VMEM((2 * width, padded, lanes), jnp.float32),
            pltpu.SMEM((fields, fields), jnp.float32),
            pltpu.SMEM((fields, fields), jnp.float32),
            pltpu.SemaphoreType.DMA((6 + -(-levels // ROWS),)),
        ],
        cost=1000,
        name="rim",
    )(*(pltpu.with_memory_space_constraint(x, pltpu.HBM) for x in inputs))
    state = state.reshape(fields * levels * POINTS, lanes)
    from_east = lax.ppermute(to_west, "hy", first_down)
    from_west = lax.ppermute(to_east, "hy", first_up)
    from_down = lax.ppermute(to_sides, "hx", second_up)
    from_up = from_down
    if lax.axis_size("hx") > 2:
        from_up = lax.ppermute(to_sides, "hx", second_down)

    column = (coupling.shape[1], NODES, lanes)
    factors = call(factor_kernel, [column] * 5, [VMEM] * 2, cost=4000000, name="factor")(
        coupling, damping
    )
    block = ((levels + 2) * NODES, lanes)
    part, base = call(
        element_kernel,
        [state.shape, (NODES,) + block],
        [VMEM] * 6,
        [
            pltpu.VMEM((levels * 8 * fields, lanes), jnp.float32),
            pltpu.VMEM((fields * POINTS, lanes), jnp.bfloat16),
            pltpu.VMEM((fields * POINTS, lanes), jnp.bfloat16),
        ],
        cost=4000000,
        name="element",
    )(
        state,
        neighbour_face,
        orientation,
        metric,
        fluxes,
        tables,
    )
    sends = call(
        pack_kernel,
        [block] * NODES,
        [VMEM] * 9,
        [
            pltpu.VMEM((NODES, -(-(levels + 2) // ROWS) * ROWS * NODES, lanes), jnp.float32),
            pltpu.VMEM((padded, lanes), jnp.float32),
            pltpu.VMEM((-(-(levels + 2) // ROWS) * ROWS, lanes), jnp.float32),
        ],
        cost=1000,
        name="pack",
    )(
        base,
        from_west,
        from_east,
        from_down,
        from_up,
        neighbour_face,
        orientation,
        metric,
        fluxes,
    )
    received = exchange(sends)

    (faces,) = call(
        face_kernel,
        [(2, len(LATE_FIELDS) * levels * NODES, lanes)],
        [VMEM] * 4 + [ANY],
        cost=4000000,
        name="face",
    )(state, from_west, from_east, fluxes, sends[0])
    faces = pltpu.with_memory_space_constraint(lax.all_gather(faces, "hy"), pltpu.HBM)

    cube = (levels + 2, NODES, lanes)
    speeds = call(
        solve_kernel,
        [cube] * NODES,
        [VMEM] * (5 + NODES),
        [
            pltpu.VMEM(column, jnp.float32),
            pltpu.VMEM((NODES, 2, NODES, lanes), jnp.float32),
            pltpu.VMEM((column[0] + 2,) + column[1:], jnp.float32),
        ],
        cost=1000,
        name="solve",
    )(*factors, *[x.reshape(cube) for x in received])
    returned = exchange([x.reshape(block) for x in speeds])
    size = levels * POINTS
    limits = pltpu.CompilerParams(vmem_limit_bytes=24 * 1024 * 1024)
    earlier, done = pl.pallas_call(
        finish_section_kernel,
        out_shape=[
            jax.ShapeDtypeStruct(whole, jnp.float32),
            pltpu.VMEM((2, size, lanes), jnp.float32),
        ],
        in_specs=[VMEM, HBM] + [VMEM] * 6,
        out_specs=[HBM, VMEM],
        scratch_shapes=[
            pltpu.VMEM((2, size, lanes), jnp.float32),
            pltpu.VMEM(faces.shape[1:], jnp.float32),
            pltpu.SemaphoreType.DMA((3,)),
        ],
        compiler_params=limits,
        cost_estimate=pl.CostEstimate(flops=4000000, bytes_accessed=4000000, transcendentals=0),
        name="finish",
    )(
        part, faces, from_down, from_up, neighbour_face, orientation, metric, fluxes
    )
    updated = pl.pallas_call(
        update_kernel,
        out_shape=jax.ShapeDtypeStruct(whole, jnp.float32),
        in_specs=[VMEM] * (1 + NODES) + [HBM],
        out_specs=HBM,
        input_output_aliases={1 + NODES: 0},
        scratch_shapes=[
            pltpu.VMEM((NODES,) + block, jnp.float32),
            pltpu.VMEM((3, size, lanes), jnp.float32),
            pltpu.SemaphoreType.DMA((3,)),
        ],
        compiler_params=limits,
        name="update",
    )(*returned, done, earlier)
    return updated.reshape(prognostic.shape)


def solution(mesh):
    placed = (
        P(None, "vz", None, None, "hy", "hx"),
        P(None, None, "hy", "hx"),
        P(),
        P(),
        P(None, "hy", "hx"),
        P(None, "hy", "hx"),
        P(None, None, "vz", None, "hy", "hx"),
        P("vz", None, "hy", "hx"),
    )
    return jax.shard_map(
        per_device,
        mesh=mesh,
        in_specs=placed,
        out_specs=P(None, "vz", None, None, "hy", "hx"),
        check_vma=False,
    )
```

```python
import jax
import jax.numpy as jnp
import numpy as np
from jax import lax
from jax.experimental import pallas as pl
from jax.experimental.pallas import tpu as pltpu
from jax.sharding import PartitionSpec as P

step_size = 0.05
lift_weight = 6.0
gravity_couple = 0.5
density_couple = 0.3
theta_couple = 0.4

NODES = 4
POINTS = NODES * NODES
FIELDS = 5
FACE_POINTS = ((0, 4, 8, 12), (3, 7, 11, 15), (0, 1, 2, 3), (12, 13, 14, 15))
RIM_POINTS = tuple(sorted(set(sum(FACE_POINTS, ()))))
ROWS = 8
LATE_FIELDS = (0, 1, 2, 4)
WAYS = (3, 2, 1, 0)


def derivative_table():
    points = np.array([-1.0, -1.0 / np.sqrt(5.0), 1.0 / np.sqrt(5.0), 1.0])
    number = points.shape[0]
    barycentric = np.ones(number)
    for source in range(number):
        for another in range(number):
            if another != source:
                barycentric[source] = barycentric[source] / (points[source] - points[another])
    matrix = np.zeros((number, number))
    for target in range(number):
        for source in range(number):
            if target != source:
                matrix[target, source] = (
                    barycentric[source] / barycentric[target] / (points[target] - points[source])
                )
        matrix[target, target] = -np.sum(matrix[target])
    return matrix


def operator_tables(lanes):
    weight = 0.5 * lift_weight
    table = derivative_table()
    table[0, 0] += weight
    table[-1, -1] -= weight
    eye = np.eye(NODES)
    along_first = np.kron(eye, table)
    along_second = np.kron(table, eye)
    ends = np.zeros(NODES)
    ends[0] = ends[-1] = 1.0
    faces = np.diag(np.kron(np.ones(NODES), ends) + np.kron(ends, np.ones(NODES)))
    first = np.zeros((POINTS, lanes))
    second = np.zeros((POINTS, lanes))
    same = np.zeros((FIELDS, POINTS, lanes))
    owner = np.full((lanes,), -1)
    for g in range(FIELDS):
        own = slice(POINTS * g, POINTS * (g + 1))
        first[:, own] = -along_first
        second[:, own] = -along_second
        same[g, :, own] = -weight * faces
        owner[own] = g
        for k in range(NODES):
            south = FIELDS * POINTS + 2 * NODES * g + k
            north = south + NODES
            second[FACE_POINTS[2][k], south] = weight
            second[FACE_POINTS[3][k], north] = -weight
            same[g, FACE_POINTS[2][k], south] = weight
            same[g, FACE_POINTS[3][k], north] = weight
            owner[south] = owner[north] = g
    tables = np.concatenate([first, second, same.reshape(FIELDS * POINTS, lanes)])
    return tables.astype(np.float32), owner


def chunks(total):
    return [min(start, total - ROWS) for start in range(0, total, ROWS)]


def ends(total):
    return list(range(0, total, ROWS))


def pick(values, masks, flip):
    chosen = []
    for k in range(NODES):
        row = values[FACE_POINTS[0][k]]
        for option in range(1, 4):
            row = jnp.where(masks[option], values[FACE_POINTS[option][k]], row)
        chosen.append(row)
    return [jnp.where(flip, chosen[NODES - 1 - k], chosen[k]) for k in range(NODES)]


def table_masks(face_row, flip_row, lanes):
    face = jnp.broadcast_to(face_row, (ROWS, lanes))
    flip = jnp.broadcast_to(flip_row, (ROWS, lanes))
    return [face == option for option in range(4)], flip == 1


def flux_row(f, g, matrix):
    return (matrix * FIELDS + f) * FIELDS + g


def along(fluxes, matrix, f, rows):
    total = None
    for g in range(FIELDS):
        at = flux_row(f, g, matrix)
        term = fluxes[at : at + 1, :] * rows[g]
        total = term if total is None else total + term
    return total


def side_lanes(f, piece, point):
    number = 3 * f + piece
    return number // 4, 32 * (number % 4) + point, 32 * (number % 4) + POINTS + point


def rim_kernel(
    state_hbm,
    face_hbm,
    way_hbm,
    metric_hbm,
    tables_hbm,
    flux_hbm,
    second_hbm,
    to_east,
    to_west,
    to_sides,
    state,
    neighbour_face,
    orientation,
    metric,
    tables,
    fluxes,
    column,
    speed,
    flux,
    second_flux,
    semaphores,
):
    levels = state.shape[1] // POINTS
    lanes = state.shape[2]
    width = len(RIM_POINTS)
    groups = [(start, min(start + ROWS, levels)) for start in range(0, levels, ROWS)]
    small = [
        pltpu.make_async_copy(source, target, semaphores.at[place])
        for place, (source, target) in enumerate(
            (
                (flux_hbm, flux),
                (face_hbm, neighbour_face),
                (way_hbm, orientation),
                (metric_hbm, metric),
                (tables_hbm, tables),
                (second_hbm, second_flux),
            )
        )
    ]
    large = []
    for place, (low, high) in enumerate(groups):
        rows = pl.ds(low * POINTS, (high - low) * POINTS)
        large.append(
            pltpu.make_async_copy(
                state_hbm.at[:, rows, :], state.at[:, rows, :], semaphores.at[len(small) + place]
            )
        )
    for copy in small[:1] + large + small[1:]:
        copy.start()
    column[...] = jnp.zeros_like(column)
    lane = lax.broadcasted_iota(jnp.int32, (ROWS, lanes), 1)
    small[0].wait()
    packed = [jnp.zeros((ROWS, lanes), jnp.float32) for _ in range(to_sides.shape[0] // ROWS)]
    arrived = 0
    for piece, start in enumerate(chunks(levels)):
        while arrived < len(groups) and groups[arrived][0] < start + ROWS:
            large[arrived].wait()
            arrived += 1
        for place, point in enumerate(RIM_POINTS):
            rows = [
                state[g, pl.ds(start * POINTS + point, ROWS, stride=POINTS), :]
                for g in range(FIELDS)
            ]
            for f, out in ((3, speed), (4, column)):
                normal = flux[f, 0] * rows[0]
                for g in range(1, FIELDS):
                    normal = normal + flux[f, g] * rows[g]
                out[2 * place, pl.ds(ROWS + start, ROWS), :] = rows[f] + normal
                out[2 * place + 1, pl.ds(ROWS + start, ROWS), :] = rows[f] - normal
            for f in range(FIELDS):
                block, last, initial = side_lanes(f, piece, point)
                packed[block] = jnp.where(
                    lane == last, pltpu.roll(rows[f], last + 1, 1), packed[block]
                )
                packed[block] = jnp.where(
                    lane == initial, pltpu.roll(rows[f], initial, 1), packed[block]
                )
    for block, value in enumerate(packed):
        to_sides[block * ROWS : (block + 1) * ROWS, :] = value
    small[1].wait()
    small[2].wait()
    end = (levels + 2) * width
    for side, (out, face) in enumerate(((to_east, 1), (to_west, 0))):
        for place in range(width):
            slot = 2 * place + side
            for start in chunks(levels):
                upper = column[slot, pl.ds(ROWS + start + 1, ROWS), :]
                lower = column[slot, pl.ds(ROWS + start - 1, ROWS), :]
                out[pl.ds(start * width + place, ROWS, stride=width), :] = speed[
                    slot, pl.ds(ROWS + start, ROWS), :
                ] - gravity_couple * (upper - lower)
            for extra, level in ((0, 0), (1, levels - 1)):
                at = (levels + extra) * width + place
                out[at : at + 1, :] = column[slot, ROWS + level : ROWS + level + 1, :]
        out[end : end + 1, :] = neighbour_face[face : face + 1, :].astype(jnp.float32)
        out[end + 1 : end + 2, :] = orientation[face : face + 1, :].astype(jnp.float32)
        left = out.shape[0] - end - 2
        out[end + 2 :, :] = jnp.zeros((left, lanes), jnp.float32)
    small[3].wait()
    small[4].wait()
    small[5].wait()
    for place, source in enumerate((flux, second_flux)):
        for f in range(FIELDS):
            for g in range(FIELDS):
                at = flux_row(f, g, place)
                fluxes[at : at + 1, :] = jnp.full((1, lanes), source[f, g])


def face_kernel(state, from_west, from_east, fluxes, packed, *outs):
    count, lanes = state.shape[0] // POINTS, state.shape[1]
    levels = count // FIELDS
    at = (levels + 2) * len(RIM_POINTS)
    sides = []
    for source, out, sign in ((from_west, outs[0::2], -1.0), (from_east, outs[1::2], 1.0)):
        face = source[at : at + 1, :].astype(jnp.int32)
        flip = source[at + 1 : at + 2, :].astype(jnp.int32)
        sides.append((*table_masks(face, flip, lanes), out, sign))
    for start in chunks(levels):
        values = []
        for g in range(FIELDS):
            values.append(
                {
                    point: state[
                        pl.ds((g * levels + start) * POINTS + point, ROWS, stride=POINTS), :
                    ]
                    for point in RIM_POINTS
                }
            )
        for masks, flip, out, sign in sides:
            picked = [pick(values[g], masks, flip) for g in range(FIELDS)]
            for place, f in enumerate(LATE_FIELDS):
                for k in range(NODES):
                    normal = along(fluxes, 0, f, [picked[g][k] for g in range(FIELDS)])
                    at = ((place % 2) * levels + start) * NODES + k
                    out[place // 2][pl.ds(at, ROWS, stride=NODES), :] = picked[f][k] + sign * normal


def element_kernel(
    state,
    neighbour_face,
    orientation,
    metric,
    fluxes,
    tables,
    part,
    base,
    outer,
    operator_high,
    operator_low,
):
    levels = state.shape[0] // (FIELDS * POINTS)
    lanes = state.shape[1]
    lane = lax.broadcasted_iota(jnp.int32, (ROWS, lanes), 1)
    sides = []
    for side, (face, edge) in enumerate(((2, 0), (3, lanes - 1))):
        shift = 1 if side == 0 else lanes - 1
        row = jnp.broadcast_to(neighbour_face[face : face + 1, :], (ROWS, lanes))
        way = jnp.broadcast_to(orientation[face : face + 1, :], (ROWS, lanes))
        masks, flip = table_masks(
            pltpu.roll(row, lanes - shift, 1), pltpu.roll(way, lanes - shift, 1), lanes
        )
        sides.append((shift, edge, masks, flip))
    for f in range(FIELDS):
        for start in chunks(levels):
            q = f * levels + start
            values = {
                point: state[pl.ds(q * POINTS + point, ROWS, stride=POINTS), :]
                for point in RIM_POINTS
            }
            for side, (shift, edge, masks, flip) in enumerate(sides):
                for k, row in enumerate(pick(values, masks, flip)):
                    at = start * 8 * FIELDS + 8 * f + NODES * side + k
                    outer[pl.ds(at, ROWS, stride=8 * FIELDS), :] = jnp.where(
                        lane == edge, 0.0, pltpu.roll(row, shift, 1)
                    )
    index = lax.broadcasted_iota(jnp.int32, (1, lanes), 1)
    own_columns = FIELDS * POINTS
    owner = jnp.where(index < own_columns, index // POINTS, (index - own_columns) // 8)
    for f in range(FIELDS):
        first_row = jnp.zeros((1, lanes), jnp.float32)
        second_row = first_row
        for g in range(FIELDS):
            first, second = (flux_row(f, g, matrix) for matrix in range(2))
            first_row = jnp.where(owner == g, fluxes[first : first + 1, :], first_row)
            second_row = jnp.where(owner == g, fluxes[second : second + 1, :], second_row)
        block = (
            first_row * tables[0:POINTS, :]
            + second_row * tables[POINTS : 2 * POINTS, :]
            + tables[(2 + f) * POINTS : (3 + f) * POINTS, :]
        )
        high = block.astype(jnp.bfloat16)
        operator_high[f * POINTS : (f + 1) * POINTS, :] = high
        operator_low[f * POINTS : (f + 1) * POINTS, :] = (
            block - high.astype(jnp.float32)
        ).astype(jnp.bfloat16)
    high = operator_high[...]
    low = operator_low[...]
    scale = step_size * metric[...]
    blank = jnp.zeros((lanes - own_columns - 8 * FIELDS, lanes), jnp.float32)
    for pair in range(0, levels, 2):
        sides = []
        for level in (pair, pair + 1):
            rows = [
                state[pl.ds((f * levels + level) * POINTS, POINTS), :] for f in range(FIELDS)
            ]
            rows.append(outer[pl.ds(level * 8 * FIELDS, 8 * FIELDS), :])
            rows.append(blank)
            sides.append(jnp.concatenate(rows, axis=0))
        values = jnp.concatenate(sides, axis=1)
        top = values.astype(jnp.bfloat16)
        rest = (values - top.astype(jnp.float32)).astype(jnp.bfloat16)
        change = (
            jnp.dot(high, top, preferred_element_type=jnp.float32)
            + jnp.dot(high, rest, preferred_element_type=jnp.float32)
            + jnp.dot(low, top, preferred_element_type=jnp.float32)
        )
        for place, level in enumerate((pair, pair + 1)):
            for f in range(FIELDS):
                at = pl.ds((f * levels + level) * POINTS, POINTS)
                part[at, :] = (
                    state[at, :]
                    + scale
                    * change[
                        f * POINTS : (f + 1) * POINTS, place * lanes : (place + 1) * lanes
                    ]
                )
    for level in range(levels):
        speed = part[pl.ds((3 * levels + level) * POINTS, POINTS), :]
        upper = part[pl.ds((4 * levels + level + 1) * POINTS, POINTS), :] if level < levels - 1 else 0.0
        lower = part[pl.ds((4 * levels + level - 1) * POINTS, POINTS), :] if level else 0.0
        value = speed - gravity_couple * (upper - lower)
        for j in range(NODES):
            base[j, level * NODES : (level + 1) * NODES, :] = value[NODES * j : NODES * (j + 1)]
    for extra, level in ((0, 0), (1, levels - 1)):
        value = part[pl.ds((4 * levels + level) * POINTS, POINTS), :]
        at = (levels + extra) * NODES
        for j in range(NODES):
            base[j, at : at + NODES, :] = value[NODES * j : NODES * (j + 1)]


def side_corrections(received, side, fluxes, fields, pieces):
    lanes = received.shape[1]
    sign = 1.0 if side == 0 else -1.0
    result = [[] for _ in fields]
    for piece in range(pieces):
        rows = []
        for g in range(FIELDS):
            block, *places = side_lanes(g, piece, 0)
            rows.append(
                pltpu.roll(
                    received[block * ROWS : (block + 1) * ROWS, :], (lanes - places[side]) % lanes, 1
                )
            )
        for place, f in enumerate(fields):
            result[place].append(rows[f] + sign * along(fluxes, 1, f, rows))
    return result


def spread(value, edge, masks, flip):
    lanes = value.shape[1]
    return pick(
        {point: pltpu.roll(value, (edge - point) % lanes, 1) for point in RIM_POINTS}, masks, flip
    )


def pack_kernel(
    base,
    from_west,
    from_east,
    from_down,
    from_up,
    neighbour_face,
    orientation,
    metric,
    fluxes,
    factored,
    *rest,
):
    sends, (send, column, mixed) = rest[:NODES], rest[NODES:]
    me = lax.axis_index("vz")
    rows, lanes = base.shape[1:]
    levels = rows // NODES - 2
    width = len(RIM_POINTS)
    scale = (0.5 * lift_weight * step_size) * metric[...]
    send[:, 0:rows, :] = base[...]
    send[:, rows:, :] = jnp.zeros((NODES, send.shape[1] - rows, lanes), jnp.float32)
    column[...] = jnp.zeros_like(column)
    mixed[...] = jnp.zeros_like(mixed)
    for face, source, i in ((0, from_west, 0), (1, from_east, NODES - 1)):
        masks, flip = table_masks(
            neighbour_face[face : face + 1, :], orientation[face : face + 1, :], lanes
        )
        for start in chunks(levels + 2):
            values = {
                point: source[pl.ds(start * width + place, ROWS, stride=width), :]
                for place, point in enumerate(RIM_POINTS)
            }
            for j, row in enumerate(pick(values, masks, flip)):
                point = NODES * j + i
                at = pl.ds(start * NODES + i, ROWS, stride=NODES)
                send[j, at, :] = base[j, at, :] + scale[point : point + 1, :] * row
    lane = lax.broadcasted_iota(jnp.int32, (ROWS, lanes), 1)
    for side, (received, edge, j) in enumerate(
        ((from_down, 0, 0), (from_up, lanes - 1, NODES - 1))
    ):
        face = 2 + side
        masks, flip = table_masks(
            neighbour_face[face : face + 1, :], orientation[face : face + 1, :], lanes
        )
        speed, heat = side_corrections(received, side, fluxes, (3, 4), len(chunks(levels)))
        for start, value in zip(chunks(levels), heat):
            column[pl.ds(ROWS + start, ROWS), :] = value
        for start, value in zip(chunks(levels), speed):
            upper = column[pl.ds(ROWS + start + 1, ROWS), :]
            lower = column[pl.ds(ROWS + start - 1, ROWS), :]
            mixed[pl.ds(start, ROWS), :] = value - gravity_couple * (upper - lower)
        mixed[levels : levels + 1, :] = column[ROWS : ROWS + 1, :]
        mixed[levels + 1 : levels + 2, :] = column[ROWS + levels - 1 : ROWS + levels, :]
        for start in ends(levels + 2):
            picked = spread(mixed[start : start + ROWS, :], edge, masks, flip)
            for k, row in enumerate(picked):
                point = NODES * j + k
                at = pl.ds(start * NODES + k, ROWS, stride=NODES)
                send[j, at, :] += jnp.where(lane == edge, scale[point : point + 1, :] * row, 0.0)
    for out, way in zip(sends, WAYS):
        out[...] = send[me ^ way, 0:rows, :]


def finish_section_kernel(
    part,
    from_east_early,
    from_west_early,
    from_east_late,
    from_west_late,
    from_down,
    from_up,
    neighbour_face,
    orientation,
    metric,
    fluxes,
    out,
    done,
    final,
    semaphore,
):
    levels = part.shape[0] // (FIELDS * POINTS)
    lanes = part.shape[1]
    size = levels * POINTS
    scale = (0.5 * lift_weight * step_size) * metric[...]
    lane = lax.broadcasted_iota(jnp.int32, (ROWS, lanes), 1)
    tables = []
    edges = []
    for side, received in enumerate((from_down, from_up)):
        face = 2 + side
        tables.append(
            table_masks(
                neighbour_face[face : face + 1, :], orientation[face : face + 1, :], lanes
            )
        )
        edges.append(
            side_corrections(received, side, fluxes, LATE_FIELDS, len(chunks(levels)))
        )
    copy = pltpu.make_async_copy(final, out.at[1:3], semaphore)
    west = (from_west_early, from_west_late)
    east = (from_east_early, from_east_late)
    for place, f in ((1, 1), (2, 2), (0, 0), (3, 4)):
        target = final.at[f - 1] if f in (1, 2) else done.at[min(f, 1)]
        target[...] = part[f * size : (f + 1) * size, :]
        for piece, start in enumerate(chunks(levels)):
            for j in range(NODES):
                for source, i in ((west[place // 2], 0), (east[place // 2], NODES - 1)):
                    point = NODES * j + i
                    rows = source[
                        pl.ds(((place % 2) * levels + start) * NODES + j, ROWS, stride=NODES), :
                    ]
                    at = pl.ds(start * POINTS + point, ROWS, stride=POINTS)
                    target[at, :] = (
                        part[pl.ds(f * size + start * POINTS + point, ROWS, stride=POINTS), :]
                        + scale[point : point + 1, :] * rows
                    )
        for piece, start in enumerate(chunks(levels)):
            row_index = lax.broadcasted_iota(jnp.int32, (ROWS, lanes), 0)
            fresh = row_index >= (-start) % ROWS
            for side, (edge, j) in enumerate(((0, 0), (lanes - 1, NODES - 1))):
                picked = spread(edges[side][place][piece], edge, *tables[side])
                for k, row in enumerate(picked):
                    point = NODES * j + k
                    at = pl.ds(start * POINTS + point, ROWS, stride=POINTS)
                    target[at, :] += jnp.where(
                        (lane == edge) & fresh, scale[point : point + 1, :] * row, 0.0
                    )
        if f == 2:
            copy.start()
    copy.wait()


def factor_kernel(coupling, damping, far, near, inverse, ratio, second):
    levels = coupling.shape[1]
    shape = coupling.shape[2:]
    blank = jnp.zeros(shape, jnp.float32)
    far_ratio, far_second, near_ratio, near_second = (blank,) * 4
    extra = damping[...]
    for level in range(levels):
        a, b, d, e = (coupling[entry, level] for entry in range(4))
        centre = a + b + d + e + extra
        reduced = -b + a * far_ratio
        pivot = centre + a * far_second - reduced * near_ratio
        scaled = 1.0 / pivot
        upper_ratio = (-d - reduced * near_second) * scaled
        second_ratio = -e * scaled
        far[level] = a * scaled
        near[level] = reduced * scaled
        inverse[level] = scaled
        ratio[level] = upper_ratio
        second[level] = second_ratio
        far_ratio, far_second = near_ratio, near_second
        near_ratio, near_second = upper_ratio, second_ratio


def solve_kernel(far, near, inverse, ratio, second, *rest):
    ways = NODES
    received, sends, (source, heat, speed) = rest[:ways], rest[ways : 2 * ways], rest[2 * ways :]
    levels = far.shape[0]
    here = levels // ways
    me = lax.axis_index("vz")
    for values, way in zip(received, WAYS):
        block = me ^ way
        source[pl.ds(block * here, here)] = values[0:here]
        heat[block] = values[here : here + 2]
    for block in range(ways - 1):
        last = block * here + here - 1
        source[last] = source[last] - gravity_couple * heat[block + 1, 0]
        source[last + 1] = source[last + 1] + gravity_couple * heat[block, 1]
    blank = jnp.zeros(far.shape[1:], jnp.float32)
    before_two, before_one = blank, blank
    for level in range(levels):
        value = source[level] * inverse[level]
        value = value + far[level] * before_two
        value = value - near[level] * before_one
        source[level] = value
        before_two, before_one = before_one, value
    speed[0] = blank
    speed[levels + 1] = blank
    next_one, next_two = blank, blank
    for level in range(levels - 1, -1, -1):
        value = source[level] - second[level] * next_two
        value = value - ratio[level] * next_one
        speed[level + 1] = value
        next_two, next_one = next_one, value
    for send, way in zip(sends, WAYS):
        send[...] = speed[pl.ds((me ^ way) * here, here + 2)]


def update_kernel(*refs):
    ways = NODES
    received, (done, earlier, out, speed, final, semaphores) = refs[:ways], refs[ways:]
    levels = done.shape[1] // POINTS
    me = lax.axis_index("vz")
    for values, way in zip(received, WAYS):
        speed[me ^ way] = values[...]
    copies = [
        pltpu.make_async_copy(final.at[place], out.at[f], semaphores.at[place])
        for place, f in enumerate((0, 3, 4))
    ]
    for place in (1, 0, 2):
        for j in range(NODES):
            for i in range(NODES):
                for start in chunks(levels):
                    lower, value, upper = (
                        speed[j, pl.ds((start + k) * NODES + i, ROWS, stride=NODES), :]
                        for k in range(3)
                    )
                    at = pl.ds(start * POINTS + NODES * j + i, ROWS, stride=POINTS)
                    if place == 1:
                        final[1, at, :] = value
                    elif place == 0:
                        final[0, at, :] = done[0, at, :] - density_couple * (upper - lower)
                    else:
                        final[2, at, :] = done[1, at, :] - theta_couple * (upper - lower)
        copies[place].start()
    for copy in copies:
        copy.wait()


VMEM = pl.BlockSpec(memory_space=pltpu.VMEM)
HBM = pl.BlockSpec(memory_space=pltpu.HBM)
ANY = pl.BlockSpec(memory_space=pl.ANY)


def call(kernel, outs, in_specs, scratch=(), cost=0, name=None):
    kinds = [x if hasattr(x, "dtype") else pltpu.VMEM(x, jnp.float32) for x in outs]
    return pl.pallas_call(
        kernel,
        out_shape=kinds,
        in_specs=in_specs,
        out_specs=[VMEM] * len(outs),
        scratch_shapes=list(scratch),
        compiler_params=pltpu.CompilerParams(vmem_limit_bytes=24 * 1024 * 1024),
        cost_estimate=pl.CostEstimate(flops=cost, bytes_accessed=cost, transcendentals=0),
        name=name,
    )


def per_device(
    prognostic, metric, first_flux, second_flux, neighbour_face, orientation, coupling, damping
):
    fields, levels = prognostic.shape[:2]
    lanes = prognostic.shape[-1]
    whole = (fields, levels * POINTS, lanes)
    metric = metric.reshape(POINTS, lanes)
    neighbour_face = neighbour_face.reshape(4, lanes)
    orientation = orientation.reshape(4, lanes)
    coupling = coupling.reshape(4, coupling.shape[1], NODES, lanes)
    damping = damping.reshape(NODES, lanes)
    tables, _ = operator_tables(lanes)

    def shifts(axis):
        size = lax.axis_size(axis)
        up = [(i, (i + 1) % size) for i in range(size)]
        return up, [(j, i) for i, j in up]

    def exchange(arrays):
        size = lax.axis_size("vz")
        return [
            lax.ppermute(x, "vz", [(i, i ^ way) for i in range(size)]) if way else x
            for x, way in zip(arrays, WAYS)
        ]

    first_up, first_down = shifts("hy")
    second_up, second_down = shifts("hx")
    width = len(RIM_POINTS)
    message = (-(-((levels + 2) * width + 2) // ROWS) * ROWS, lanes)
    sides = (-(-fields * len(chunks(levels)) // 4) * ROWS, lanes)
    padded = levels + 2 * ROWS
    table = pltpu.VMEM((4, lanes), jnp.int32)
    inputs = (
        prognostic.reshape(whole),
        neighbour_face,
        orientation,
        metric,
        jnp.asarray(tables),
        first_flux,
        second_flux,
    )
    (
        to_east,
        to_west,
        to_sides,
        state,
        neighbour_face,
        orientation,
        metric,
        tables,
        fluxes,
    ) = call(
        rim_kernel,
        [
            message,
            message,
            sides,
            whole,
            table,
            table,
            (POINTS, lanes),
            tables.shape,
            (-(-2 * fields * fields // ROWS) * ROWS, lanes),
        ],
        [HBM] * len(inputs),
        [
            pltpu.VMEM((2 * width, padded, lanes), jnp.float32),
            pltpu.VMEM((2 * width, padded, lanes), jnp.float32),
            pltpu.SMEM((fields, fields), jnp.float32),
            pltpu.SMEM((fields, fields), jnp.float32),
            pltpu.SemaphoreType.DMA((6 + -(-levels // ROWS),)),
        ],
        cost=1000,
        name="rim",
    )(*(pltpu.with_memory_space_constraint(x, pltpu.HBM) for x in inputs))
    state = state.reshape(fields * levels * POINTS, lanes)
    from_east = lax.ppermute(to_west, "hy", first_down)
    from_west = lax.ppermute(to_east, "hy", first_up)
    from_down = lax.ppermute(to_sides, "hx", second_up)
    from_up = from_down
    if lax.axis_size("hx") > 2:
        from_up = lax.ppermute(to_sides, "hx", second_down)

    column = (coupling.shape[1], NODES, lanes)
    factors = call(factor_kernel, [column] * 5, [VMEM] * 2, cost=4000000, name="factor")(
        coupling, damping
    )
    block = ((levels + 2) * NODES, lanes)
    part, base = call(
        element_kernel,
        [state.shape, (NODES,) + block],
        [VMEM] * 6,
        [
            pltpu.VMEM((levels * 8 * fields, lanes), jnp.float32),
            pltpu.VMEM((fields * POINTS, lanes), jnp.bfloat16),
            pltpu.VMEM((fields * POINTS, lanes), jnp.bfloat16),
        ],
        cost=4000000,
        name="element",
    )(
        state,
        neighbour_face,
        orientation,
        metric,
        fluxes,
        tables,
    )
    sends = call(
        pack_kernel,
        [block] * NODES,
        [VMEM] * 9 + [ANY],
        [
            pltpu.VMEM((NODES, -(-(levels + 2) // ROWS) * ROWS * NODES, lanes), jnp.float32),
            pltpu.VMEM((padded, lanes), jnp.float32),
            pltpu.VMEM((-(-(levels + 2) // ROWS) * ROWS, lanes), jnp.float32),
        ],
        cost=1000,
        name="pack",
    )(
        base,
        from_west,
        from_east,
        from_down,
        from_up,
        neighbour_face,
        orientation,
        metric,
        fluxes,
        factors[0],
    )
    received = exchange(sends)

    late = (len(LATE_FIELDS) // 2 * levels * NODES, lanes)
    faces = call(
        face_kernel, [late] * 4, [VMEM] * 4 + [ANY], cost=4000000, name="face"
    )(state, from_west, from_east, fluxes, sends[-1])
    faces = [
        lax.ppermute(x, "hy", first_up if place % 2 else first_down)
        for place, x in enumerate(faces)
    ]

    cube = (levels + 2, NODES, lanes)
    speeds = call(
        solve_kernel,
        [cube] * NODES,
        [VMEM] * (5 + NODES),
        [
            pltpu.VMEM(column, jnp.float32),
            pltpu.VMEM((NODES, 2, NODES, lanes), jnp.float32),
            pltpu.VMEM((column[0] + 2,) + column[1:], jnp.float32),
        ],
        cost=1000,
        name="solve",
    )(*factors, *[x.reshape(cube) for x in received])
    returned = exchange([x.reshape(block) for x in speeds])
    size = levels * POINTS
    limits = pltpu.CompilerParams(vmem_limit_bytes=24 * 1024 * 1024)
    earlier, done = pl.pallas_call(
        finish_section_kernel,
        out_shape=[
            jax.ShapeDtypeStruct(whole, jnp.float32),
            pltpu.VMEM((2, size, lanes), jnp.float32),
        ],
        in_specs=[VMEM] * 11,
        out_specs=[HBM, VMEM],
        scratch_shapes=[pltpu.VMEM((2, size, lanes), jnp.float32), pltpu.SemaphoreType.DMA],
        compiler_params=limits,
        cost_estimate=pl.CostEstimate(flops=4000000, bytes_accessed=4000000, transcendentals=0),
        name="finish",
    )(
        part, *faces, from_down, from_up, neighbour_face, orientation, metric, fluxes
    )
    updated = pl.pallas_call(
        update_kernel,
        out_shape=jax.ShapeDtypeStruct(whole, jnp.float32),
        in_specs=[VMEM] * (1 + NODES) + [HBM],
        out_specs=HBM,
        input_output_aliases={1 + NODES: 0},
        scratch_shapes=[
            pltpu.VMEM((NODES,) + block, jnp.float32),
            pltpu.VMEM((3, size, lanes), jnp.float32),
            pltpu.SemaphoreType.DMA((3,)),
        ],
        compiler_params=limits,
        name="update",
    )(*returned, done, earlier)
    return updated.reshape(prognostic.shape)


def solution(mesh):
    placed = (
        P(None, "vz", None, None, "hy", "hx"),
        P(None, None, "hy", "hx"),
        P(),
        P(),
        P(None, "hy", "hx"),
        P(None, "hy", "hx"),
        P(None, None, "vz", None, "hy", "hx"),
        P("vz", None, "hy", "hx"),
    )
    return jax.shard_map(
        per_device,
        mesh=mesh,
        in_specs=placed,
        out_specs=P(None, "vz", None, None, "hy", "hx"),
        check_vma=False,
    )
```

```python
import jax
import jax.numpy as jnp
import numpy as np
from jax import lax
from jax.experimental import pallas as pl
from jax.experimental.pallas import tpu as pltpu
from jax.sharding import PartitionSpec as P

step_size = 0.05
lift_weight = 6.0
gravity_couple = 0.5
density_couple = 0.3
theta_couple = 0.4

NODES = 4
POINTS = NODES * NODES
FIELDS = 5
FACE_POINTS = ((0, 4, 8, 12), (3, 7, 11, 15), (0, 1, 2, 3), (12, 13, 14, 15))
RIM_POINTS = tuple(sorted(set(sum(FACE_POINTS, ()))))
ROWS = 8
LATE_FIELDS = (0, 1, 2, 4)
WAYS = (3, 2, 1, 0)


def derivative_table():
    points = np.array([-1.0, -1.0 / np.sqrt(5.0), 1.0 / np.sqrt(5.0), 1.0])
    number = points.shape[0]
    barycentric = np.ones(number)
    for source in range(number):
        for another in range(number):
            if another != source:
                barycentric[source] = barycentric[source] / (points[source] - points[another])
    matrix = np.zeros((number, number))
    for target in range(number):
        for source in range(number):
            if target != source:
                matrix[target, source] = (
                    barycentric[source] / barycentric[target] / (points[target] - points[source])
                )
        matrix[target, target] = -np.sum(matrix[target])
    return matrix


def operator_tables(lanes):
    weight = 0.5 * lift_weight
    table = derivative_table()
    table[0, 0] += weight
    table[-1, -1] -= weight
    eye = np.eye(NODES)
    along_first = np.kron(eye, table)
    along_second = np.kron(table, eye)
    ends = np.zeros(NODES)
    ends[0] = ends[-1] = 1.0
    faces = np.diag(np.kron(np.ones(NODES), ends) + np.kron(ends, np.ones(NODES)))
    first = np.zeros((POINTS, lanes))
    second = np.zeros((POINTS, lanes))
    same = np.zeros((FIELDS, POINTS, lanes))
    owner = np.full((lanes,), -1)
    for g in range(FIELDS):
        own = slice(POINTS * g, POINTS * (g + 1))
        first[:, own] = -along_first
        second[:, own] = -along_second
        same[g, :, own] = -weight * faces
        owner[own] = g
        for k in range(NODES):
            south = FIELDS * POINTS + 2 * NODES * g + k
            north = south + NODES
            second[FACE_POINTS[2][k], south] = weight
            second[FACE_POINTS[3][k], north] = -weight
            same[g, FACE_POINTS[2][k], south] = weight
            same[g, FACE_POINTS[3][k], north] = weight
            owner[south] = owner[north] = g
    tables = np.concatenate([first, second, same.reshape(FIELDS * POINTS, lanes)])
    return tables.astype(np.float32), owner


def chunks(total):
    return [min(start, total - ROWS) for start in range(0, total, ROWS)]


def partner_side(partner):
    odd = lax.rem(lax.axis_index("hy"), 2)
    return odd if partner else 1 - odd


def side_sign(side):
    return (2 * side - 1).astype(jnp.float32)


def ends(total):
    return list(range(0, total, ROWS))


def pick(values, masks, flip):
    chosen = []
    for k in range(NODES):
        row = values[FACE_POINTS[0][k]]
        for option in range(1, 4):
            row = jnp.where(masks[option], values[FACE_POINTS[option][k]], row)
        chosen.append(row)
    return [jnp.where(flip, chosen[NODES - 1 - k], chosen[k]) for k in range(NODES)]


def table_masks(face_row, flip_row, lanes):
    face = jnp.broadcast_to(face_row, (ROWS, lanes))
    flip = jnp.broadcast_to(flip_row, (ROWS, lanes))
    return [face == option for option in range(4)], flip == 1


def flux_row(f, g, matrix):
    return (matrix * FIELDS + f) * FIELDS + g


def along(fluxes, matrix, f, rows):
    total = None
    for g in range(FIELDS):
        at = flux_row(f, g, matrix)
        term = fluxes[at : at + 1, :] * rows[g]
        total = term if total is None else total + term
    return total


def side_lanes(f, piece, point):
    number = 3 * f + piece
    return number // 4, 32 * (number % 4) + point, 32 * (number % 4) + POINTS + point


def rim_kernel(
    state_hbm,
    face_hbm,
    way_hbm,
    metric_hbm,
    tables_hbm,
    flux_hbm,
    second_hbm,
    to_near,
    to_other,
    state,
    neighbour_face,
    orientation,
    metric,
    tables,
    fluxes,
    column,
    speed,
    flux,
    second_flux,
    semaphores,
):
    levels = state.shape[1] // POINTS
    sign = side_sign(partner_side(0))
    lanes = state.shape[2]
    width = len(RIM_POINTS)
    groups = [(start, min(start + ROWS, levels)) for start in range(0, levels, ROWS)]
    small = [
        pltpu.make_async_copy(source, target, semaphores.at[place])
        for place, (source, target) in enumerate(
            (
                (flux_hbm, flux),
                (face_hbm, neighbour_face),
                (way_hbm, orientation),
                (metric_hbm, metric),
                (tables_hbm, tables),
                (second_hbm, second_flux),
            )
        )
    ]
    large = []
    for place, (low, high) in enumerate(groups):
        rows = pl.ds(low * POINTS, (high - low) * POINTS)
        large.append(
            pltpu.make_async_copy(
                state_hbm.at[:, rows, :], state.at[:, rows, :], semaphores.at[len(small) + place]
            )
        )
    for copy in small[:1] + large + small[1:]:
        copy.start()
    column[...] = jnp.zeros_like(column)
    small[0].wait()
    arrived = 0
    for piece, start in enumerate(chunks(levels)):
        while arrived < len(groups) and groups[arrived][0] < start + ROWS:
            large[arrived].wait()
            arrived += 1
        for place, point in enumerate(RIM_POINTS):
            rows = [
                state[g, pl.ds(start * POINTS + point, ROWS, stride=POINTS), :]
                for g in range(FIELDS)
            ]
            for f, out in ((3, speed), (4, column)):
                normal = (sign * flux[f, 0]) * rows[0]
                for g in range(1, FIELDS):
                    normal = normal + (sign * flux[f, g]) * rows[g]
                out[2 * place, pl.ds(ROWS + start, ROWS), :] = rows[f] + normal
                out[2 * place + 1, pl.ds(ROWS + start, ROWS), :] = rows[f] - normal
    small[1].wait()
    small[2].wait()
    end = (levels + 2) * width
    for partner, out in enumerate((to_near, to_other)):
        face = partner_side(partner)
        for place in range(width):
            slot = 2 * place + partner
            for start in chunks(levels):
                upper = column[slot, pl.ds(ROWS + start + 1, ROWS), :]
                lower = column[slot, pl.ds(ROWS + start - 1, ROWS), :]
                out[pl.ds(start * width + place, ROWS, stride=width), :] = speed[
                    slot, pl.ds(ROWS + start, ROWS), :
                ] - gravity_couple * (upper - lower)
            for extra, level in ((0, 0), (1, levels - 1)):
                at = (levels + extra) * width + place
                out[at : at + 1, :] = column[slot, ROWS + level : ROWS + level + 1, :]
        out[end : end + 1, :] = neighbour_face[pl.ds(face, 1), :].astype(jnp.float32)
        out[end + 1 : end + 2, :] = orientation[pl.ds(face, 1), :].astype(jnp.float32)
        left = out.shape[0] - end - 2
        out[end + 2 :, :] = jnp.zeros((left, lanes), jnp.float32)
    small[3].wait()
    small[4].wait()
    small[5].wait()
    for place, source in enumerate((flux, second_flux)):
        for f in range(FIELDS):
            for g in range(FIELDS):
                at = flux_row(f, g, place)
                fluxes[at : at + 1, :] = jnp.full((1, lanes), source[f, g])


def edge_kernel(state, to_sides):
    lanes = state.shape[1]
    levels = state.shape[0] // (FIELDS * POINTS)
    lane = lax.broadcasted_iota(jnp.int32, (ROWS, lanes), 1)
    packed = [jnp.zeros((ROWS, lanes), jnp.float32) for _ in range(to_sides.shape[0] // ROWS)]
    for f in range(FIELDS):
        for piece, start in enumerate(chunks(levels)):
            for point in RIM_POINTS:
                row = state[pl.ds((f * levels + start) * POINTS + point, ROWS, stride=POINTS), :]
                block, last, initial = side_lanes(f, piece, point)
                packed[block] = jnp.where(lane == last, pltpu.roll(row, last + 1, 1), packed[block])
                packed[block] = jnp.where(lane == initial, pltpu.roll(row, initial, 1), packed[block])
    for block, value in enumerate(packed):
        to_sides[block * ROWS : (block + 1) * ROWS, :] = value


def face_kernel(state, from_near, from_other, fluxes, packed, *outs):
    count, lanes = state.shape[0] // POINTS, state.shape[1]
    levels = count // FIELDS
    at = (levels + 2) * len(RIM_POINTS)
    sides = []
    for partner, (source, out) in enumerate(((from_near, outs[:2]), (from_other, outs[2:]))):
        sign = side_sign(partner_side(partner))
        face = source[at : at + 1, :].astype(jnp.int32)
        flip = source[at + 1 : at + 2, :].astype(jnp.int32)
        sides.append((*table_masks(face, flip, lanes), out, sign))
    for start in chunks(levels):
        values = []
        for g in range(FIELDS):
            values.append(
                {
                    point: state[
                        pl.ds((g * levels + start) * POINTS + point, ROWS, stride=POINTS), :
                    ]
                    for point in RIM_POINTS
                }
            )
        for masks, flip, out, sign in sides:
            picked = [pick(values[g], masks, flip) for g in range(FIELDS)]
            for place, f in enumerate(LATE_FIELDS):
                for k in range(NODES):
                    normal = along(fluxes, 0, f, [picked[g][k] for g in range(FIELDS)])
                    at = ((place % 2) * levels + start) * NODES + k
                    out[place // 2][pl.ds(at, ROWS, stride=NODES), :] = picked[f][k] + sign * normal


def element_kernel(
    state,
    neighbour_face,
    orientation,
    metric,
    fluxes,
    tables,
    part,
    base,
    outer,
    operator_high,
    operator_low,
):
    levels = state.shape[0] // (FIELDS * POINTS)
    lanes = state.shape[1]
    lane = lax.broadcasted_iota(jnp.int32, (ROWS, lanes), 1)
    sides = []
    for side, (face, edge) in enumerate(((2, 0), (3, lanes - 1))):
        shift = 1 if side == 0 else lanes - 1
        row = jnp.broadcast_to(neighbour_face[face : face + 1, :], (ROWS, lanes))
        way = jnp.broadcast_to(orientation[face : face + 1, :], (ROWS, lanes))
        masks, flip = table_masks(
            pltpu.roll(row, lanes - shift, 1), pltpu.roll(way, lanes - shift, 1), lanes
        )
        sides.append((shift, edge, masks, flip))
    for f in range(FIELDS):
        for start in chunks(levels):
            q = f * levels + start
            values = {
                point: state[pl.ds(q * POINTS + point, ROWS, stride=POINTS), :]
                for point in RIM_POINTS
            }
            for side, (shift, edge, masks, flip) in enumerate(sides):
                for k, row in enumerate(pick(values, masks, flip)):
                    at = start * 8 * FIELDS + 8 * f + NODES * side + k
                    outer[pl.ds(at, ROWS, stride=8 * FIELDS), :] = jnp.where(
                        lane == edge, 0.0, pltpu.roll(row, shift, 1)
                    )
    index = lax.broadcasted_iota(jnp.int32, (1, lanes), 1)
    own_columns = FIELDS * POINTS
    owner = jnp.where(index < own_columns, index // POINTS, (index - own_columns) // 8)
    for f in range(FIELDS):
        first_row = jnp.zeros((1, lanes), jnp.float32)
        second_row = first_row
        for g in range(FIELDS):
            first, second = (flux_row(f, g, matrix) for matrix in range(2))
            first_row = jnp.where(owner == g, fluxes[first : first + 1, :], first_row)
            second_row = jnp.where(owner == g, fluxes[second : second + 1, :], second_row)
        block = (
            first_row * tables[0:POINTS, :]
            + second_row * tables[POINTS : 2 * POINTS, :]
            + tables[(2 + f) * POINTS : (3 + f) * POINTS, :]
        )
        high = block.astype(jnp.bfloat16)
        operator_high[f * POINTS : (f + 1) * POINTS, :] = high
        operator_low[f * POINTS : (f + 1) * POINTS, :] = (
            block - high.astype(jnp.float32)
        ).astype(jnp.bfloat16)
    high = operator_high[...]
    low = operator_low[...]
    scale = step_size * metric[...]
    blank = jnp.zeros((lanes - own_columns - 8 * FIELDS, lanes), jnp.float32)
    for pair in range(0, levels, 2):
        sides = []
        for level in (pair, pair + 1):
            rows = [
                state[pl.ds((f * levels + level) * POINTS, POINTS), :] for f in range(FIELDS)
            ]
            rows.append(outer[pl.ds(level * 8 * FIELDS, 8 * FIELDS), :])
            rows.append(blank)
            sides.append(jnp.concatenate(rows, axis=0))
        values = jnp.concatenate(sides, axis=1)
        top = values.astype(jnp.bfloat16)
        rest = (values - top.astype(jnp.float32)).astype(jnp.bfloat16)
        change = (
            jnp.dot(high, top, preferred_element_type=jnp.float32)
            + jnp.dot(high, rest, preferred_element_type=jnp.float32)
            + jnp.dot(low, top, preferred_element_type=jnp.float32)
        )
        for place, level in enumerate((pair, pair + 1)):
            for f in range(FIELDS):
                at = pl.ds((f * levels + level) * POINTS, POINTS)
                part[at, :] = (
                    state[at, :]
                    + scale
                    * change[
                        f * POINTS : (f + 1) * POINTS, place * lanes : (place + 1) * lanes
                    ]
                )
    for level in range(levels):
        speed = part[pl.ds((3 * levels + level) * POINTS, POINTS), :]
        upper = part[pl.ds((4 * levels + level + 1) * POINTS, POINTS), :] if level < levels - 1 else 0.0
        lower = part[pl.ds((4 * levels + level - 1) * POINTS, POINTS), :] if level else 0.0
        value = speed - gravity_couple * (upper - lower)
        for j in range(NODES):
            base[j, level * NODES : (level + 1) * NODES, :] = value[NODES * j : NODES * (j + 1)]
    for extra, level in ((0, 0), (1, levels - 1)):
        value = part[pl.ds((4 * levels + level) * POINTS, POINTS), :]
        at = (levels + extra) * NODES
        for j in range(NODES):
            base[j, at : at + NODES, :] = value[NODES * j : NODES * (j + 1)]


def side_corrections(received, side, fluxes, fields, pieces):
    lanes = received.shape[1]
    sign = 1.0 if side == 0 else -1.0
    result = [[] for _ in fields]
    for piece in range(pieces):
        rows = []
        for g in range(FIELDS):
            block, *places = side_lanes(g, piece, 0)
            rows.append(
                pltpu.roll(
                    received[block * ROWS : (block + 1) * ROWS, :], (lanes - places[side]) % lanes, 1
                )
            )
        for place, f in enumerate(fields):
            result[place].append(rows[f] + sign * along(fluxes, 1, f, rows))
    return result


def spread(value, edge, masks, flip):
    lanes = value.shape[1]
    return pick(
        {point: pltpu.roll(value, (edge - point) % lanes, 1) for point in RIM_POINTS}, masks, flip
    )


def pack_kernel(
    base,
    from_other,
    from_near,
    from_down,
    from_up,
    neighbour_face,
    orientation,
    metric,
    fluxes,
    factored,
    *rest,
):
    sends, (send, column, mixed) = rest[:NODES], rest[NODES:]
    me = lax.axis_index("vz")
    rows, lanes = base.shape[1:]
    levels = rows // NODES - 2
    width = len(RIM_POINTS)
    weight = 0.5 * lift_weight * step_size
    send[:, 0:rows, :] = base[...]
    send[:, rows:, :] = jnp.zeros((NODES, send.shape[1] - rows, lanes), jnp.float32)
    column[...] = jnp.zeros_like(column)
    mixed[...] = jnp.zeros_like(mixed)
    for partner, source in enumerate((from_near, from_other)):
        face = partner_side(partner)
        i = (NODES - 1) * face
        masks, flip = table_masks(
            neighbour_face[pl.ds(face, 1), :], orientation[pl.ds(face, 1), :], lanes
        )
        for start in chunks(levels + 2):
            values = {
                point: source[pl.ds(start * width + place, ROWS, stride=width), :]
                for place, point in enumerate(RIM_POINTS)
            }
            for j, row in enumerate(pick(values, masks, flip)):
                at = pl.ds(start * NODES + i, ROWS, stride=NODES)
                scale = weight * metric[pl.ds(NODES * j + i, 1), :]
                send[j, at, :] = base[j, at, :] + scale * row
    lane = lax.broadcasted_iota(jnp.int32, (ROWS, lanes), 1)
    for side, (received, edge, j) in enumerate(
        ((from_down, 0, 0), (from_up, lanes - 1, NODES - 1))
    ):
        face = 2 + side
        masks, flip = table_masks(
            neighbour_face[face : face + 1, :], orientation[face : face + 1, :], lanes
        )
        speed, heat = side_corrections(received, side, fluxes, (3, 4), len(chunks(levels)))
        for start, value in zip(chunks(levels), heat):
            column[pl.ds(ROWS + start, ROWS), :] = value
        for start, value in zip(chunks(levels), speed):
            upper = column[pl.ds(ROWS + start + 1, ROWS), :]
            lower = column[pl.ds(ROWS + start - 1, ROWS), :]
            mixed[pl.ds(start, ROWS), :] = value - gravity_couple * (upper - lower)
        mixed[levels : levels + 1, :] = column[ROWS : ROWS + 1, :]
        mixed[levels + 1 : levels + 2, :] = column[ROWS + levels - 1 : ROWS + levels, :]
        for start in ends(levels + 2):
            picked = spread(mixed[start : start + ROWS, :], edge, masks, flip)
            for k, row in enumerate(picked):
                point = NODES * j + k
                at = pl.ds(start * NODES + k, ROWS, stride=NODES)
                scale = weight * metric[point : point + 1, :]
                send[j, at, :] += jnp.where(lane == edge, scale * row, 0.0)
    for out, way in zip(sends, WAYS):
        out[...] = send[me ^ way, 0:rows, :]


def finish_section_kernel(
    part,
    near_early,
    near_late,
    other_early,
    other_late,
    from_down,
    from_up,
    neighbour_face,
    orientation,
    metric,
    fluxes,
    out,
    done,
    final,
    semaphore,
):
    levels = part.shape[0] // (FIELDS * POINTS)
    lanes = part.shape[1]
    size = levels * POINTS
    weight = 0.5 * lift_weight * step_size
    scale = weight * metric[...]
    lane = lax.broadcasted_iota(jnp.int32, (ROWS, lanes), 1)
    tables = []
    edges = []
    for side, received in enumerate((from_down, from_up)):
        face = 2 + side
        tables.append(
            table_masks(
                neighbour_face[face : face + 1, :], orientation[face : face + 1, :], lanes
            )
        )
        edges.append(
            side_corrections(received, side, fluxes, LATE_FIELDS, len(chunks(levels)))
        )
    copy = pltpu.make_async_copy(final, out.at[1:3], semaphore)
    sources = ((near_early, near_late), (other_early, other_late))
    for place, f in ((1, 1), (2, 2), (0, 0), (3, 4)):
        target = final.at[f - 1] if f in (1, 2) else done.at[min(f, 1)]
        target[...] = part[f * size : (f + 1) * size, :]
        for piece, start in enumerate(chunks(levels)):
            for j in range(NODES):
                for partner, source in enumerate(sources):
                    point = NODES * j + (NODES - 1) * partner_side(partner)
                    rows = source[place // 2][
                        pl.ds(((place % 2) * levels + start) * NODES + j, ROWS, stride=NODES), :
                    ]
                    at = pl.ds(start * POINTS + point, ROWS, stride=POINTS)
                    target[at, :] = (
                        part[pl.ds(f * size + start * POINTS + point, ROWS, stride=POINTS), :]
                        + weight * metric[pl.ds(point, 1), :] * rows
                    )
        for piece, start in enumerate(chunks(levels)):
            row_index = lax.broadcasted_iota(jnp.int32, (ROWS, lanes), 0)
            fresh = row_index >= (-start) % ROWS
            for side, (edge, j) in enumerate(((0, 0), (lanes - 1, NODES - 1))):
                picked = spread(edges[side][place][piece], edge, *tables[side])
                for k, row in enumerate(picked):
                    point = NODES * j + k
                    at = pl.ds(start * POINTS + point, ROWS, stride=POINTS)
                    target[at, :] += jnp.where(
                        (lane == edge) & fresh, scale[point : point + 1, :] * row, 0.0
                    )
        if f == 2:
            copy.start()
    copy.wait()


def factor_kernel(coupling, damping, far, near, inverse, ratio, second):
    levels = coupling.shape[1]
    shape = coupling.shape[2:]
    blank = jnp.zeros(shape, jnp.float32)
    far_ratio, far_second, near_ratio, near_second = (blank,) * 4
    extra = damping[...]
    for level in range(levels):
        a, b, d, e = (coupling[entry, level] for entry in range(4))
        centre = a + b + d + e + extra
        reduced = -b + a * far_ratio
        pivot = centre + a * far_second - reduced * near_ratio
        scaled = 1.0 / pivot
        upper_ratio = (-d - reduced * near_second) * scaled
        second_ratio = -e * scaled
        far[level] = a * scaled
        near[level] = reduced * scaled
        inverse[level] = scaled
        ratio[level] = upper_ratio
        second[level] = second_ratio
        far_ratio, far_second = near_ratio, near_second
        near_ratio, near_second = upper_ratio, second_ratio


def solve_kernel(far, near, inverse, ratio, second, *rest):
    ways = NODES
    received, sends, (source, heat, speed) = rest[:ways], rest[ways : 2 * ways], rest[2 * ways :]
    levels = far.shape[0]
    here = levels // ways
    me = lax.axis_index("vz")
    for values, way in zip(received, WAYS):
        block = me ^ way
        source[pl.ds(block * here, here)] = values[0:here]
        heat[block] = values[here : here + 2]
    for block in range(ways - 1):
        last = block * here + here - 1
        source[last] = source[last] - gravity_couple * heat[block + 1, 0]
        source[last + 1] = source[last + 1] + gravity_couple * heat[block, 1]
    blank = jnp.zeros(far.shape[1:], jnp.float32)
    before_two, before_one = blank, blank
    for level in range(levels):
        value = source[level] * inverse[level]
        value = value + far[level] * before_two
        value = value - near[level] * before_one
        source[level] = value
        before_two, before_one = before_one, value
    speed[0] = blank
    speed[levels + 1] = blank
    next_one, next_two = blank, blank
    for level in range(levels - 1, -1, -1):
        value = source[level] - second[level] * next_two
        value = value - ratio[level] * next_one
        speed[level + 1] = value
        next_two, next_one = next_one, value
    for send, way in zip(sends, WAYS):
        send[...] = speed[pl.ds((me ^ way) * here, here + 2)]


def update_kernel(*refs):
    ways = NODES
    received, (done, earlier, out, speed, final, semaphores) = refs[:ways], refs[ways:]
    levels = done.shape[1] // POINTS
    me = lax.axis_index("vz")
    for values, way in zip(received, WAYS):
        speed[me ^ way] = values[...]
    lanes = done.shape[2]
    half = levels // 2
    low = lax.broadcasted_iota(jnp.int32, (ROWS, lanes), 0) < NODES
    copies = []
    for pair in range(half):
        lower = [speed[j, pair * ROWS : (pair + 1) * ROWS, :] for j in range(NODES)]
        upper = [speed[j, (pair + 1) * ROWS : (pair + 2) * ROWS, :] for j in range(NODES)]
        jump = [above - below for above, below in zip(upper, lower)]
        value = [jnp.where(low, above, below) for above, below in zip(upper, lower)]
        for h in range(2):
            a, b = 2 * h, 2 * h + 1
            for odd in range(2):
                at = pl.ds((2 * pair + odd) * POINTS + ROWS * h, ROWS)
                jumps = side_by_side(jump[a], jump[b], odd, low)
                final[0, at, :] = done[0, at, :] - density_couple * jumps
                final[1, at, :] = side_by_side(value[a], value[b], 1 - odd, low)
                final[2, at, :] = done[1, at, :] - theta_couple * jumps
        if pair in (half // 2 - 1, half - 1):
            first = 0 if pair < half - 1 else half // 2
            rows = pl.ds(first * 2 * POINTS, (pair + 1 - first) * 2 * POINTS)
            for place, f in enumerate((0, 3, 4)):
                copies.append(
                    pltpu.make_async_copy(
                        final.at[place, rows, :], out.at[f, rows, :], semaphores.at[len(copies)]
                    )
                )
                copies[-1].start()
    for copy in copies:
        copy.wait()


def side_by_side(first, second, upper, low):
    if upper:
        return jnp.where(low, pltpu.roll(first, NODES, 0), second)
    return jnp.where(low, first, pltpu.roll(second, NODES, 0))


VMEM = pl.BlockSpec(memory_space=pltpu.VMEM)
HBM = pl.BlockSpec(memory_space=pltpu.HBM)
ANY = pl.BlockSpec(memory_space=pl.ANY)


def call(kernel, outs, in_specs, scratch=(), cost=0, name=None):
    kinds = [x if hasattr(x, "dtype") else pltpu.VMEM(x, jnp.float32) for x in outs]
    return pl.pallas_call(
        kernel,
        out_shape=kinds,
        in_specs=in_specs,
        out_specs=[VMEM] * len(outs),
        scratch_shapes=list(scratch),
        compiler_params=pltpu.CompilerParams(vmem_limit_bytes=24 * 1024 * 1024),
        cost_estimate=pl.CostEstimate(flops=cost, bytes_accessed=cost, transcendentals=0),
        name=name,
    )


def per_device(
    prognostic, metric, first_flux, second_flux, neighbour_face, orientation, coupling, damping
):
    fields, levels = prognostic.shape[:2]
    lanes = prognostic.shape[-1]
    whole = (fields, levels * POINTS, lanes)
    metric = metric.reshape(POINTS, lanes)
    neighbour_face = neighbour_face.reshape(4, lanes)
    orientation = orientation.reshape(4, lanes)
    coupling = coupling.reshape(4, coupling.shape[1], NODES, lanes)
    damping = damping.reshape(NODES, lanes)
    tables, _ = operator_tables(lanes)

    def shifts(axis):
        size = lax.axis_size(axis)
        up = [(i, (i + 1) % size) for i in range(size)]
        return up, [(j, i) for i, j in up]

    def exchange(arrays):
        size = lax.axis_size("vz")
        return [
            lax.ppermute(x, "vz", [(i, i ^ way) for i in range(size)]) if way else x
            for x, way in zip(arrays, WAYS)
        ]

    count = lax.axis_size("hy")
    near = [(i, i ^ 1) for i in range(count)]
    other = [(i, (i + 1 if i % 2 else i - 1) % count) for i in range(count)]
    second_up, second_down = shifts("hx")
    width = len(RIM_POINTS)
    message = (-(-((levels + 2) * width + 2) // ROWS) * ROWS, lanes)
    sides = (-(-fields * len(chunks(levels)) // 4) * ROWS, lanes)
    padded = levels + 2 * ROWS
    table = pltpu.VMEM((4, lanes), jnp.int32)
    inputs = (
        prognostic.reshape(whole),
        neighbour_face,
        orientation,
        metric,
        jnp.asarray(tables),
        first_flux,
        second_flux,
    )
    (
        to_near,
        to_other,
        state,
        neighbour_face,
        orientation,
        metric,
        tables,
        fluxes,
    ) = call(
        rim_kernel,
        [
            message,
            message,
            whole,
            table,
            table,
            (POINTS, lanes),
            tables.shape,
            (-(-2 * fields * fields // ROWS) * ROWS, lanes),
        ],
        [HBM] * len(inputs),
        [
            pltpu.VMEM((2 * width, padded, lanes), jnp.float32),
            pltpu.VMEM((2 * width, padded, lanes), jnp.float32),
            pltpu.SMEM((fields, fields), jnp.float32),
            pltpu.SMEM((fields, fields), jnp.float32),
            pltpu.SemaphoreType.DMA((6 + -(-levels // ROWS),)),
        ],
        cost=1000,
        name="rim",
    )(*(pltpu.with_memory_space_constraint(x, pltpu.HBM) for x in inputs))
    state = state.reshape(fields * levels * POINTS, lanes)
    from_other = lax.ppermute(to_other, "hy", other)
    from_near = lax.ppermute(to_near, "hy", near)
    (to_sides,) = call(edge_kernel, [sides], [VMEM], cost=1000, name="edge")(state)
    from_down = lax.ppermute(to_sides, "hx", second_up)
    from_up = from_down
    if lax.axis_size("hx") > 2:
        from_up = lax.ppermute(to_sides, "hx", second_down)

    column = (coupling.shape[1], NODES, lanes)
    factors = call(factor_kernel, [column] * 5, [VMEM] * 2, cost=4000000, name="factor")(
        coupling, damping
    )
    block = ((levels + 2) * NODES, lanes)
    part, base = call(
        element_kernel,
        [state.shape, (NODES,) + block],
        [VMEM] * 6,
        [
            pltpu.VMEM((levels * 8 * fields, lanes), jnp.float32),
            pltpu.VMEM((fields * POINTS, lanes), jnp.bfloat16),
            pltpu.VMEM((fields * POINTS, lanes), jnp.bfloat16),
        ],
        cost=4000000,
        name="element",
    )(
        state,
        neighbour_face,
        orientation,
        metric,
        fluxes,
        tables,
    )
    sends = call(
        pack_kernel,
        [block] * NODES,
        [VMEM] * 9 + [ANY],
        [
            pltpu.VMEM((NODES, -(-(levels + 2) // ROWS) * ROWS * NODES, lanes), jnp.float32),
            pltpu.VMEM((padded, lanes), jnp.float32),
            pltpu.VMEM((-(-(levels + 2) // ROWS) * ROWS, lanes), jnp.float32),
        ],
        cost=1000,
        name="pack",
    )(
        base,
        from_other,
        from_near,
        from_down,
        from_up,
        neighbour_face,
        orientation,
        metric,
        fluxes,
        factors[0],
    )
    received = exchange(sends)

    late = (len(LATE_FIELDS) // 2 * levels * NODES, lanes)
    faces = call(
        face_kernel, [late] * 4, [VMEM] * 4 + [ANY], cost=4000000, name="face"
    )(state, from_near, from_other, fluxes, sends[-1])
    faces = [
        lax.ppermute(x, "hy", near if place < 2 else other)
        for place, x in enumerate(faces)
    ]

    cube = (levels + 2, NODES, lanes)
    speeds = call(
        solve_kernel,
        [cube] * NODES,
        [VMEM] * (5 + NODES),
        [
            pltpu.VMEM(column, jnp.float32),
            pltpu.VMEM((NODES, 2, NODES, lanes), jnp.float32),
            pltpu.VMEM((column[0] + 2,) + column[1:], jnp.float32),
        ],
        cost=1000,
        name="solve",
    )(*factors, *[x.reshape(cube) for x in received])
    returned = exchange([x.reshape(block) for x in speeds])
    size = levels * POINTS
    limits = pltpu.CompilerParams(vmem_limit_bytes=24 * 1024 * 1024)
    earlier, done = pl.pallas_call(
        finish_section_kernel,
        out_shape=[
            jax.ShapeDtypeStruct(whole, jnp.float32),
            pltpu.VMEM((2, size, lanes), jnp.float32),
        ],
        in_specs=[VMEM] * 11,
        out_specs=[HBM, VMEM],
        scratch_shapes=[pltpu.VMEM((2, size, lanes), jnp.float32), pltpu.SemaphoreType.DMA],
        compiler_params=limits,
        cost_estimate=pl.CostEstimate(flops=4000000, bytes_accessed=4000000, transcendentals=0),
        name="finish",
    )(
        part, *faces, from_down, from_up, neighbour_face, orientation, metric, fluxes
    )
    updated = pl.pallas_call(
        update_kernel,
        out_shape=jax.ShapeDtypeStruct(whole, jnp.float32),
        in_specs=[VMEM] * (1 + NODES) + [HBM],
        out_specs=HBM,
        input_output_aliases={1 + NODES: 0},
        scratch_shapes=[
            pltpu.VMEM((NODES,) + block, jnp.float32),
            pltpu.VMEM((3, size, lanes), jnp.float32),
            pltpu.SemaphoreType.DMA((6,)),
        ],
        compiler_params=limits,
        name="update",
    )(*returned, done, earlier)
    return updated.reshape(prognostic.shape)


def solution(mesh):
    placed = (
        P(None, "vz", None, None, "hy", "hx"),
        P(None, None, "hy", "hx"),
        P(),
        P(),
        P(None, "hy", "hx"),
        P(None, "hy", "hx"),
        P(None, None, "vz", None, "hy", "hx"),
        P("vz", None, "hy", "hx"),
    )
    return jax.shard_map(
        per_device,
        mesh=mesh,
        in_specs=placed,
        out_specs=P(None, "vz", None, None, "hy", "hx"),
        check_vma=False,
    )
```

```python
import functools

import jax
import jax.numpy as jnp
import numpy as np
from jax import lax
from jax.experimental import pallas as pl
from jax.experimental.pallas import tpu as pltpu
from jax.sharding import PartitionSpec as P

step_size = 0.05
lift_weight = 6.0
gravity_couple = 0.5
density_couple = 0.3
theta_couple = 0.4

NODES = 4
POINTS = NODES * NODES
FIELDS = 5
FACE_POINTS = ((0, 4, 8, 12), (3, 7, 11, 15), (0, 1, 2, 3), (12, 13, 14, 15))
RIM_POINTS = tuple(sorted(set(sum(FACE_POINTS, ()))))
ROWS = 8
LATE_FIELDS = (0, 1, 2, 4)
WAYS = (3, 2, 1, 0)


def derivative_table():
    points = np.array([-1.0, -1.0 / np.sqrt(5.0), 1.0 / np.sqrt(5.0), 1.0])
    number = points.shape[0]
    barycentric = np.ones(number)
    for source in range(number):
        for another in range(number):
            if another != source:
                barycentric[source] = barycentric[source] / (points[source] - points[another])
    matrix = np.zeros((number, number))
    for target in range(number):
        for source in range(number):
            if target != source:
                matrix[target, source] = (
                    barycentric[source] / barycentric[target] / (points[target] - points[source])
                )
        matrix[target, target] = -np.sum(matrix[target])
    return matrix


def operator_tables(lanes):
    weight = 0.5 * lift_weight
    table = derivative_table()
    table[0, 0] += weight
    table[-1, -1] -= weight
    eye = np.eye(NODES)
    along_first = np.kron(eye, table)
    along_second = np.kron(table, eye)
    ends = np.zeros(NODES)
    ends[0] = ends[-1] = 1.0
    faces = np.diag(np.kron(np.ones(NODES), ends) + np.kron(ends, np.ones(NODES)))
    first = np.zeros((POINTS, lanes))
    second = np.zeros((POINTS, lanes))
    same = np.zeros((FIELDS, POINTS, lanes))
    owner = np.full((lanes,), -1)
    for g in range(FIELDS):
        own = slice(POINTS * g, POINTS * (g + 1))
        first[:, own] = -along_first
        second[:, own] = -along_second
        same[g, :, own] = -weight * faces
        owner[own] = g
        for k in range(NODES):
            south = FIELDS * POINTS + 2 * NODES * g + k
            north = south + NODES
            second[FACE_POINTS[2][k], south] = weight
            second[FACE_POINTS[3][k], north] = -weight
            same[g, FACE_POINTS[2][k], south] = weight
            same[g, FACE_POINTS[3][k], north] = weight
            owner[south] = owner[north] = g
    tables = np.concatenate([first, second, same.reshape(FIELDS * POINTS, lanes)])
    return tables.astype(np.float32), owner


def chunks(total):
    return [min(start, total - ROWS) for start in range(0, total, ROWS)]


def partner_side(partner):
    odd = lax.rem(lax.axis_index("hy"), 2)
    return odd if partner else 1 - odd


def side_sign(side):
    return (2 * side - 1).astype(jnp.float32)


def ends(total):
    return list(range(0, total, ROWS))


def pick(values, masks, flip):
    chosen = []
    for k in range(NODES):
        row = values[FACE_POINTS[0][k]]
        for option in range(1, 4):
            row = jnp.where(masks[option], values[FACE_POINTS[option][k]], row)
        chosen.append(row)
    return [jnp.where(flip, chosen[NODES - 1 - k], chosen[k]) for k in range(NODES)]


def table_masks(face_row, flip_row, lanes):
    face = jnp.broadcast_to(face_row, (ROWS, lanes))
    flip = jnp.broadcast_to(flip_row, (ROWS, lanes))
    return [face == option for option in range(4)], flip == 1


def flux_row(f, g, matrix):
    return (matrix * FIELDS + f) * FIELDS + g


def along(fluxes, matrix, f, rows):
    total = None
    for g in range(FIELDS):
        at = flux_row(f, g, matrix)
        term = fluxes[at : at + 1, :] * rows[g]
        total = term if total is None else total + term
    return total


def side_lanes(f, piece, point):
    number = 3 * f + piece
    return number // 4, 32 * (number % 4) + point, 32 * (number % 4) + POINTS + point


def rim_kernel(
    state_hbm,
    face_hbm,
    way_hbm,
    metric_hbm,
    tables_hbm,
    flux_hbm,
    second_hbm,
    to_near,
    to_other,
    state,
    neighbour_face,
    orientation,
    metric,
    tables,
    fluxes,
    column,
    speed,
    flux,
    second_flux,
    semaphores,
):
    levels = state.shape[1] // POINTS
    sign = side_sign(partner_side(0))
    lanes = state.shape[2]
    width = len(RIM_POINTS)
    groups = [(start, min(start + ROWS, levels)) for start in range(0, levels, ROWS)]
    small = [
        pltpu.make_async_copy(source, target, semaphores.at[place])
        for place, (source, target) in enumerate(
            (
                (flux_hbm, flux),
                (face_hbm, neighbour_face),
                (way_hbm, orientation),
                (metric_hbm, metric),
                (tables_hbm, tables),
                (second_hbm, second_flux),
            )
        )
    ]
    large = []
    for place, (low, high) in enumerate(groups):
        rows = pl.ds(low * POINTS, (high - low) * POINTS)
        large.append(
            pltpu.make_async_copy(
                state_hbm.at[:, rows, :], state.at[:, rows, :], semaphores.at[len(small) + place]
            )
        )
    for copy in small[:1] + large + small[1:]:
        copy.start()
    column[...] = jnp.zeros_like(column)
    small[0].wait()
    arrived = 0
    for piece, start in enumerate(chunks(levels)):
        while arrived < len(groups) and groups[arrived][0] < start + ROWS:
            large[arrived].wait()
            arrived += 1
        for place, point in enumerate(RIM_POINTS):
            rows = [
                state[g, pl.ds(start * POINTS + point, ROWS, stride=POINTS), :]
                for g in range(FIELDS)
            ]
            for f, out in ((3, speed), (4, column)):
                normal = (sign * flux[f, 0]) * rows[0]
                for g in range(1, FIELDS):
                    normal = normal + (sign * flux[f, g]) * rows[g]
                out[2 * place, pl.ds(ROWS + start, ROWS), :] = rows[f] + normal
                out[2 * place + 1, pl.ds(ROWS + start, ROWS), :] = rows[f] - normal
    small[1].wait()
    small[2].wait()
    end = (levels + 2) * width
    for partner, out in enumerate((to_near, to_other)):
        face = partner_side(partner)
        for place in range(width):
            slot = 2 * place + partner
            for start in chunks(levels):
                upper = column[slot, pl.ds(ROWS + start + 1, ROWS), :]
                lower = column[slot, pl.ds(ROWS + start - 1, ROWS), :]
                out[pl.ds(start * width + place, ROWS, stride=width), :] = speed[
                    slot, pl.ds(ROWS + start, ROWS), :
                ] - gravity_couple * (upper - lower)
            for extra, level in ((0, 0), (1, levels - 1)):
                at = (levels + extra) * width + place
                out[at : at + 1, :] = column[slot, ROWS + level : ROWS + level + 1, :]
        out[end : end + 1, :] = neighbour_face[pl.ds(face, 1), :].astype(jnp.float32)
        out[end + 1 : end + 2, :] = orientation[pl.ds(face, 1), :].astype(jnp.float32)
        left = out.shape[0] - end - 2
        out[end + 2 :, :] = jnp.zeros((left, lanes), jnp.float32)
    small[3].wait()
    small[4].wait()
    small[5].wait()
    for place, source in enumerate((flux, second_flux)):
        for f in range(FIELDS):
            for g in range(FIELDS):
                at = flux_row(f, g, place)
                fluxes[at : at + 1, :] = jnp.full((1, lanes), source[f, g])


def edge_kernel(state, to_sides):
    lanes = state.shape[1]
    levels = state.shape[0] // (FIELDS * POINTS)
    lane = lax.broadcasted_iota(jnp.int32, (ROWS, lanes), 1)
    packed = [jnp.zeros((ROWS, lanes), jnp.float32) for _ in range(to_sides.shape[0] // ROWS)]
    for f in range(FIELDS):
        for piece, start in enumerate(chunks(levels)):
            for point in RIM_POINTS:
                row = state[pl.ds((f * levels + start) * POINTS + point, ROWS, stride=POINTS), :]
                block, last, initial = side_lanes(f, piece, point)
                packed[block] = jnp.where(lane == last, pltpu.roll(row, last + 1, 1), packed[block])
                packed[block] = jnp.where(lane == initial, pltpu.roll(row, initial, 1), packed[block])
    for block, value in enumerate(packed):
        to_sides[block * ROWS : (block + 1) * ROWS, :] = value


def face_kernel(partner, state, received, fluxes, after, *outs):
    lanes = state.shape[1]
    levels = state.shape[0] // (FIELDS * POINTS)
    at = (levels + 2) * len(RIM_POINTS)
    share = len(LATE_FIELDS) // len(outs)
    sign = side_sign(partner_side(partner))
    masks, flip = table_masks(
        received[at : at + 1, :].astype(jnp.int32),
        received[at + 1 : at + 2, :].astype(jnp.int32),
        lanes,
    )
    for start in chunks(levels):
        picked = []
        for g in range(FIELDS):
            values = {
                point: state[pl.ds((g * levels + start) * POINTS + point, ROWS, stride=POINTS), :]
                for point in RIM_POINTS
            }
            picked.append(pick(values, masks, flip))
        for place, f in enumerate(LATE_FIELDS):
            for k in range(NODES):
                normal = along(fluxes, 0, f, [picked[g][k] for g in range(FIELDS)])
                at = ((place % share) * levels + start) * NODES + k
                outs[place // share][pl.ds(at, ROWS, stride=NODES), :] = (
                    picked[f][k] + sign * normal
                )


def element_kernel(
    state,
    neighbour_face,
    orientation,
    metric,
    fluxes,
    tables,
    part,
    base,
    outer,
    operator_high,
    operator_low,
):
    levels = state.shape[0] // (FIELDS * POINTS)
    lanes = state.shape[1]
    lane = lax.broadcasted_iota(jnp.int32, (ROWS, lanes), 1)
    sides = []
    for side, (face, edge) in enumerate(((2, 0), (3, lanes - 1))):
        shift = 1 if side == 0 else lanes - 1
        row = jnp.broadcast_to(neighbour_face[face : face + 1, :], (ROWS, lanes))
        way = jnp.broadcast_to(orientation[face : face + 1, :], (ROWS, lanes))
        masks, flip = table_masks(
            pltpu.roll(row, lanes - shift, 1), pltpu.roll(way, lanes - shift, 1), lanes
        )
        sides.append((shift, edge, masks, flip))
    for f in range(FIELDS):
        for start in chunks(levels):
            q = f * levels + start
            values = {
                point: state[pl.ds(q * POINTS + point, ROWS, stride=POINTS), :]
                for point in RIM_POINTS
            }
            for side, (shift, edge, masks, flip) in enumerate(sides):
                for k, row in enumerate(pick(values, masks, flip)):
                    at = start * 8 * FIELDS + 8 * f + NODES * side + k
                    outer[pl.ds(at, ROWS, stride=8 * FIELDS), :] = jnp.where(
                        lane == edge, 0.0, pltpu.roll(row, shift, 1)
                    )
    index = lax.broadcasted_iota(jnp.int32, (1, lanes), 1)
    own_columns = FIELDS * POINTS
    owner = jnp.where(index < own_columns, index // POINTS, (index - own_columns) // 8)
    for f in range(FIELDS):
        first_row = jnp.zeros((1, lanes), jnp.float32)
        second_row = first_row
        for g in range(FIELDS):
            first, second = (flux_row(f, g, matrix) for matrix in range(2))
            first_row = jnp.where(owner == g, fluxes[first : first + 1, :], first_row)
            second_row = jnp.where(owner == g, fluxes[second : second + 1, :], second_row)
        block = (
            first_row * tables[0:POINTS, :]
            + second_row * tables[POINTS : 2 * POINTS, :]
            + tables[(2 + f) * POINTS : (3 + f) * POINTS, :]
        )
        high = block.astype(jnp.bfloat16)
        operator_high[f * POINTS : (f + 1) * POINTS, :] = high
        operator_low[f * POINTS : (f + 1) * POINTS, :] = (
            block - high.astype(jnp.float32)
        ).astype(jnp.bfloat16)
    high = operator_high[...]
    low = operator_low[...]
    scale = step_size * metric[...]
    blank = jnp.zeros((lanes - own_columns - 8 * FIELDS, lanes), jnp.float32)
    for pair in range(0, levels, 2):
        sides = []
        for level in (pair, pair + 1):
            rows = [
                state[pl.ds((f * levels + level) * POINTS, POINTS), :] for f in range(FIELDS)
            ]
            rows.append(outer[pl.ds(level * 8 * FIELDS, 8 * FIELDS), :])
            rows.append(blank)
            sides.append(jnp.concatenate(rows, axis=0))
        values = jnp.concatenate(sides, axis=1)
        top = values.astype(jnp.bfloat16)
        rest = (values - top.astype(jnp.float32)).astype(jnp.bfloat16)
        change = (
            jnp.dot(high, top, preferred_element_type=jnp.float32)
            + jnp.dot(high, rest, preferred_element_type=jnp.float32)
            + jnp.dot(low, top, preferred_element_type=jnp.float32)
        )
        for place, level in enumerate((pair, pair + 1)):
            for f in range(FIELDS):
                at = pl.ds((f * levels + level) * POINTS, POINTS)
                part[at, :] = (
                    state[at, :]
                    + scale
                    * change[
                        f * POINTS : (f + 1) * POINTS, place * lanes : (place + 1) * lanes
                    ]
                )
    for level in range(levels):
        speed = part[pl.ds((3 * levels + level) * POINTS, POINTS), :]
        upper = part[pl.ds((4 * levels + level + 1) * POINTS, POINTS), :] if level < levels - 1 else 0.0
        lower = part[pl.ds((4 * levels + level - 1) * POINTS, POINTS), :] if level else 0.0
        value = speed - gravity_couple * (upper - lower)
        for j in range(NODES):
            base[j, level * NODES : (level + 1) * NODES, :] = value[NODES * j : NODES * (j + 1)]
    for extra, level in ((0, 0), (1, levels - 1)):
        value = part[pl.ds((4 * levels + level) * POINTS, POINTS), :]
        at = (levels + extra) * NODES
        for j in range(NODES):
            base[j, at : at + NODES, :] = value[NODES * j : NODES * (j + 1)]


def side_corrections(received, side, fluxes, fields, pieces):
    lanes = received.shape[1]
    sign = 1.0 if side == 0 else -1.0
    result = [[] for _ in fields]
    for piece in range(pieces):
        rows = []
        for g in range(FIELDS):
            block, *places = side_lanes(g, piece, 0)
            rows.append(
                pltpu.roll(
                    received[block * ROWS : (block + 1) * ROWS, :], (lanes - places[side]) % lanes, 1
                )
            )
        for place, f in enumerate(fields):
            result[place].append(rows[f] + sign * along(fluxes, 1, f, rows))
    return result


def spread(value, edge, masks, flip):
    lanes = value.shape[1]
    return pick(
        {point: pltpu.roll(value, (edge - point) % lanes, 1) for point in RIM_POINTS}, masks, flip
    )


def pack_kernel(
    base,
    from_other,
    from_near,
    from_down,
    from_up,
    neighbour_face,
    orientation,
    metric,
    fluxes,
    factored,
    *rest,
):
    sends, (send, column, mixed) = rest[:NODES], rest[NODES:]
    me = lax.axis_index("vz")
    rows, lanes = base.shape[1:]
    levels = rows // NODES - 2
    width = len(RIM_POINTS)
    weight = 0.5 * lift_weight * step_size
    send[:, 0:rows, :] = base[...]
    send[:, rows:, :] = jnp.zeros((NODES, send.shape[1] - rows, lanes), jnp.float32)
    column[...] = jnp.zeros_like(column)
    mixed[...] = jnp.zeros_like(mixed)
    for partner, source in enumerate((from_near, from_other)):
        face = partner_side(partner)
        i = (NODES - 1) * face
        masks, flip = table_masks(
            neighbour_face[pl.ds(face, 1), :], orientation[pl.ds(face, 1), :], lanes
        )
        for start in chunks(levels + 2):
            values = {
                point: source[pl.ds(start * width + place, ROWS, stride=width), :]
                for place, point in enumerate(RIM_POINTS)
            }
            for j, row in enumerate(pick(values, masks, flip)):
                at = pl.ds(start * NODES + i, ROWS, stride=NODES)
                scale = weight * metric[pl.ds(NODES * j + i, 1), :]
                send[j, at, :] = base[j, at, :] + scale * row
    lane = lax.broadcasted_iota(jnp.int32, (ROWS, lanes), 1)
    for side, (received, edge, j) in enumerate(
        ((from_down, 0, 0), (from_up, lanes - 1, NODES - 1))
    ):
        face = 2 + side
        masks, flip = table_masks(
            neighbour_face[face : face + 1, :], orientation[face : face + 1, :], lanes
        )
        speed, heat = side_corrections(received, side, fluxes, (3, 4), len(chunks(levels)))
        for start, value in zip(chunks(levels), heat):
            column[pl.ds(ROWS + start, ROWS), :] = value
        for start, value in zip(chunks(levels), speed):
            upper = column[pl.ds(ROWS + start + 1, ROWS), :]
            lower = column[pl.ds(ROWS + start - 1, ROWS), :]
            mixed[pl.ds(start, ROWS), :] = value - gravity_couple * (upper - lower)
        mixed[levels : levels + 1, :] = column[ROWS : ROWS + 1, :]
        mixed[levels + 1 : levels + 2, :] = column[ROWS + levels - 1 : ROWS + levels, :]
        for start in ends(levels + 2):
            picked = spread(mixed[start : start + ROWS, :], edge, masks, flip)
            for k, row in enumerate(picked):
                point = NODES * j + k
                at = pl.ds(start * NODES + k, ROWS, stride=NODES)
                scale = weight * metric[point : point + 1, :]
                send[j, at, :] += jnp.where(lane == edge, scale * row, 0.0)
    for out, way in zip(sends, WAYS):
        out[...] = send[me ^ way, 0:rows, :]


def finish_section_kernel(
    part,
    near,
    other_early,
    other_late,
    from_down,
    from_up,
    neighbour_face,
    orientation,
    metric,
    fluxes,
    out,
    done,
    final,
    semaphore,
):
    levels = part.shape[0] // (FIELDS * POINTS)
    lanes = part.shape[1]
    size = levels * POINTS
    weight = 0.5 * lift_weight * step_size
    scale = weight * metric[...]
    lane = lax.broadcasted_iota(jnp.int32, (ROWS, lanes), 1)
    tables = []
    edges = []
    for side, received in enumerate((from_down, from_up)):
        face = 2 + side
        tables.append(
            table_masks(
                neighbour_face[face : face + 1, :], orientation[face : face + 1, :], lanes
            )
        )
        edges.append(
            side_corrections(received, side, fluxes, LATE_FIELDS, len(chunks(levels)))
        )
    copy = pltpu.make_async_copy(final, out.at[1:3], semaphore)
    sources = ((near,), (other_early, other_late))
    for place, f in ((1, 1), (2, 2), (0, 0), (3, 4)):
        target = final.at[f - 1] if f in (1, 2) else done.at[min(f, 1)]
        target[...] = part[f * size : (f + 1) * size, :]
        for piece, start in enumerate(chunks(levels)):
            for j in range(NODES):
                for partner, source in enumerate(sources):
                    point = NODES * j + (NODES - 1) * partner_side(partner)
                    share = len(LATE_FIELDS) // len(source)
                    rows = source[place // share][
                        pl.ds(((place % share) * levels + start) * NODES + j, ROWS, stride=NODES),
                        :,
                    ]
                    at = pl.ds(start * POINTS + point, ROWS, stride=POINTS)
                    target[at, :] = (
                        part[pl.ds(f * size + start * POINTS + point, ROWS, stride=POINTS), :]
                        + weight * metric[pl.ds(point, 1), :] * rows
                    )
        for piece, start in enumerate(chunks(levels)):
            row_index = lax.broadcasted_iota(jnp.int32, (ROWS, lanes), 0)
            fresh = row_index >= (-start) % ROWS
            for side, (edge, j) in enumerate(((0, 0), (lanes - 1, NODES - 1))):
                picked = spread(edges[side][place][piece], edge, *tables[side])
                for k, row in enumerate(picked):
                    point = NODES * j + k
                    at = pl.ds(start * POINTS + point, ROWS, stride=POINTS)
                    target[at, :] += jnp.where(
                        (lane == edge) & fresh, scale[point : point + 1, :] * row, 0.0
                    )
        if f == 2:
            copy.start()
    copy.wait()


def factor_kernel(coupling, damping, far, near, inverse, ratio, second):
    levels = coupling.shape[1]
    shape = coupling.shape[2:]
    blank = jnp.zeros(shape, jnp.float32)
    far_ratio, far_second, near_ratio, near_second = (blank,) * 4
    extra = damping[...]
    for level in range(levels):
        a, b, d, e = (coupling[entry, level] for entry in range(4))
        centre = a + b + d + e + extra
        reduced = -b + a * far_ratio
        pivot = centre + a * far_second - reduced * near_ratio
        scaled = 1.0 / pivot
        upper_ratio = (-d - reduced * near_second) * scaled
        second_ratio = -e * scaled
        far[level] = a * scaled
        near[level] = reduced * scaled
        inverse[level] = scaled
        ratio[level] = upper_ratio
        second[level] = second_ratio
        far_ratio, far_second = near_ratio, near_second
        near_ratio, near_second = upper_ratio, second_ratio


def solve_kernel(far, near, inverse, ratio, second, *rest):
    ways = NODES
    received, sends, (source, heat, speed) = rest[:ways], rest[ways : 2 * ways], rest[2 * ways :]
    levels = far.shape[0]
    here = levels // ways
    me = lax.axis_index("vz")
    for values, way in zip(received, WAYS):
        block = me ^ way
        source[pl.ds(block * here, here)] = values[0:here]
        heat[block] = values[here : here + 2]
    for block in range(ways - 1):
        last = block * here + here - 1
        source[last] = source[last] - gravity_couple * heat[block + 1, 0]
        source[last + 1] = source[last + 1] + gravity_couple * heat[block, 1]
    blank = jnp.zeros(far.shape[1:], jnp.float32)
    before_two, before_one = blank, blank
    for level in range(levels):
        value = source[level] * inverse[level]
        value = value + far[level] * before_two
        value = value - near[level] * before_one
        source[level] = value
        before_two, before_one = before_one, value
    speed[0] = blank
    speed[levels + 1] = blank
    next_one, next_two = blank, blank
    for level in range(levels - 1, -1, -1):
        value = source[level] - second[level] * next_two
        value = value - ratio[level] * next_one
        speed[level + 1] = value
        next_two, next_one = next_one, value
    for send, way in zip(sends, WAYS):
        send[...] = speed[pl.ds((me ^ way) * here, here + 2)]


def update_kernel(*refs):
    ways = NODES
    received, (done, earlier, out, speed, final, semaphores) = refs[:ways], refs[ways:]
    levels = done.shape[1] // POINTS
    me = lax.axis_index("vz")
    for values, way in zip(received, WAYS):
        speed[me ^ way] = values[...]
    lanes = done.shape[2]
    half = levels // 2
    low = lax.broadcasted_iota(jnp.int32, (ROWS, lanes), 0) < NODES
    copies = []
    for pair in range(half):
        lower = [speed[j, pair * ROWS : (pair + 1) * ROWS, :] for j in range(NODES)]
        upper = [speed[j, (pair + 1) * ROWS : (pair + 2) * ROWS, :] for j in range(NODES)]
        jump = [above - below for above, below in zip(upper, lower)]
        value = [jnp.where(low, above, below) for above, below in zip(upper, lower)]
        for h in range(2):
            a, b = 2 * h, 2 * h + 1
            for odd in range(2):
                at = pl.ds((2 * pair + odd) * POINTS + ROWS * h, ROWS)
                jumps = side_by_side(jump[a], jump[b], odd, low)
                final[0, at, :] = done[0, at, :] - density_couple * jumps
                final[1, at, :] = side_by_side(value[a], value[b], 1 - odd, low)
                final[2, at, :] = done[1, at, :] - theta_couple * jumps
        if pair in (half // 2 - 1, half - 1):
            first = 0 if pair < half - 1 else half // 2
            rows = pl.ds(first * 2 * POINTS, (pair + 1 - first) * 2 * POINTS)
            for place, f in enumerate((0, 3, 4)):
                copies.append(
                    pltpu.make_async_copy(
                        final.at[place, rows, :], out.at[f, rows, :], semaphores.at[len(copies)]
                    )
                )
                copies[-1].start()
    for copy in copies:
        copy.wait()


def side_by_side(first, second, upper, low):
    if upper:
        return jnp.where(low, pltpu.roll(first, NODES, 0), second)
    return jnp.where(low, first, pltpu.roll(second, NODES, 0))


VMEM = pl.BlockSpec(memory_space=pltpu.VMEM)
HBM = pl.BlockSpec(memory_space=pltpu.HBM)
ANY = pl.BlockSpec(memory_space=pl.ANY)


def call(kernel, outs, in_specs, scratch=(), cost=0, name=None):
    kinds = [x if hasattr(x, "dtype") else pltpu.VMEM(x, jnp.float32) for x in outs]
    return pl.pallas_call(
        kernel,
        out_shape=kinds,
        in_specs=in_specs,
        out_specs=[VMEM] * len(outs),
        scratch_shapes=list(scratch),
        compiler_params=pltpu.CompilerParams(vmem_limit_bytes=24 * 1024 * 1024),
        cost_estimate=pl.CostEstimate(flops=cost, bytes_accessed=cost, transcendentals=0),
        name=name,
    )


def per_device(
    prognostic, metric, first_flux, second_flux, neighbour_face, orientation, coupling, damping
):
    fields, levels = prognostic.shape[:2]
    lanes = prognostic.shape[-1]
    whole = (fields, levels * POINTS, lanes)
    metric = metric.reshape(POINTS, lanes)
    neighbour_face = neighbour_face.reshape(4, lanes)
    orientation = orientation.reshape(4, lanes)
    coupling = coupling.reshape(4, coupling.shape[1], NODES, lanes)
    damping = damping.reshape(NODES, lanes)
    tables, _ = operator_tables(lanes)

    def shifts(axis):
        size = lax.axis_size(axis)
        up = [(i, (i + 1) % size) for i in range(size)]
        return up, [(j, i) for i, j in up]

    def exchange(arrays):
        size = lax.axis_size("vz")
        return [
            lax.ppermute(x, "vz", [(i, i ^ way) for i in range(size)]) if way else x
            for x, way in zip(arrays, WAYS)
        ]

    count = lax.axis_size("hy")
    near = [(i, i ^ 1) for i in range(count)]
    other = [(i, (i + 1 if i % 2 else i - 1) % count) for i in range(count)]
    second_up, second_down = shifts("hx")
    width = len(RIM_POINTS)
    message = (-(-((levels + 2) * width + 2) // ROWS) * ROWS, lanes)
    sides = (-(-fields * len(chunks(levels)) // 4) * ROWS, lanes)
    padded = levels + 2 * ROWS
    table = pltpu.VMEM((4, lanes), jnp.int32)
    inputs = (
        prognostic.reshape(whole),
        neighbour_face,
        orientation,
        metric,
        jnp.asarray(tables),
        first_flux,
        second_flux,
    )
    (
        to_near,
        to_other,
        state,
        neighbour_face,
        orientation,
        metric,
        tables,
        fluxes,
    ) = call(
        rim_kernel,
        [
            message,
            message,
            whole,
            table,
            table,
            (POINTS, lanes),
            tables.shape,
            (-(-2 * fields * fields // ROWS) * ROWS, lanes),
        ],
        [HBM] * len(inputs),
        [
            pltpu.VMEM((2 * width, padded, lanes), jnp.float32),
            pltpu.VMEM((2 * width, padded, lanes), jnp.float32),
            pltpu.SMEM((fields, fields), jnp.float32),
            pltpu.SMEM((fields, fields), jnp.float32),
            pltpu.SemaphoreType.DMA((6 + -(-levels // ROWS),)),
        ],
        cost=1000,
        name="rim",
    )(*(pltpu.with_memory_space_constraint(x, pltpu.HBM) for x in inputs))
    state = state.reshape(fields * levels * POINTS, lanes)
    from_other = lax.ppermute(to_other, "hy", other)
    from_near = lax.ppermute(to_near, "hy", near)
    (to_sides,) = call(edge_kernel, [sides], [VMEM], cost=1000, name="edge")(state)
    from_down = lax.ppermute(to_sides, "hx", second_up)
    from_up = from_down
    if lax.axis_size("hx") > 2:
        from_up = lax.ppermute(to_sides, "hx", second_down)

    column = (coupling.shape[1], NODES, lanes)
    factors = call(factor_kernel, [column] * 5, [VMEM] * 2, cost=4000000, name="factor")(
        coupling, damping
    )
    block = ((levels + 2) * NODES, lanes)
    part, base = call(
        element_kernel,
        [state.shape, (NODES,) + block],
        [VMEM] * 6,
        [
            pltpu.VMEM((levels * 8 * fields, lanes), jnp.float32),
            pltpu.VMEM((fields * POINTS, lanes), jnp.bfloat16),
            pltpu.VMEM((fields * POINTS, lanes), jnp.bfloat16),
        ],
        cost=4000000,
        name="element",
    )(
        state,
        neighbour_face,
        orientation,
        metric,
        fluxes,
        tables,
    )
    sends = call(
        pack_kernel,
        [block] * NODES,
        [VMEM] * 9 + [ANY],
        [
            pltpu.VMEM((NODES, -(-(levels + 2) // ROWS) * ROWS * NODES, lanes), jnp.float32),
            pltpu.VMEM((padded, lanes), jnp.float32),
            pltpu.VMEM((-(-(levels + 2) // ROWS) * ROWS, lanes), jnp.float32),
        ],
        cost=1000,
        name="pack",
    )(
        base,
        from_other,
        from_near,
        from_down,
        from_up,
        neighbour_face,
        orientation,
        metric,
        fluxes,
        factors[0],
    )
    late = levels * NODES * len(LATE_FIELDS)
    (near_face,) = call(
        functools.partial(face_kernel, 0),
        [(late, lanes)],
        [VMEM] * 3 + [ANY],
        cost=1000,
        name="near_face",
    )(state, from_near, fluxes, sends[-1])
    near_face = lax.ppermute(near_face, "hy", near)
    received = exchange(sends)

    other_face = call(
        functools.partial(face_kernel, 1),
        [(late // 2, lanes)] * 2,
        [VMEM] * 3 + [ANY],
        cost=1000,
        name="other_face",
    )(state, from_other, fluxes, near_face)
    other_face = [lax.ppermute(x, "hy", other) for x in other_face]

    cube = (levels + 2, NODES, lanes)
    speeds = call(
        solve_kernel,
        [cube] * NODES,
        [VMEM] * (5 + NODES),
        [
            pltpu.VMEM(column, jnp.float32),
            pltpu.VMEM((NODES, 2, NODES, lanes), jnp.float32),
            pltpu.VMEM((column[0] + 2,) + column[1:], jnp.float32),
        ],
        cost=1000,
        name="solve",
    )(*factors, *[x.reshape(cube) for x in received])
    returned = exchange([x.reshape(block) for x in speeds])
    size = levels * POINTS
    limits = pltpu.CompilerParams(vmem_limit_bytes=24 * 1024 * 1024)
    earlier, done = pl.pallas_call(
        finish_section_kernel,
        out_shape=[
            jax.ShapeDtypeStruct(whole, jnp.float32),
            pltpu.VMEM((2, size, lanes), jnp.float32),
        ],
        in_specs=[VMEM] * 10,
        out_specs=[HBM, VMEM],
        scratch_shapes=[pltpu.VMEM((2, size, lanes), jnp.float32), pltpu.SemaphoreType.DMA],
        compiler_params=limits,
        cost_estimate=pl.CostEstimate(flops=4000000, bytes_accessed=4000000, transcendentals=0),
        name="finish",
    )(
        part, near_face, *other_face, from_down, from_up, neighbour_face, orientation, metric, fluxes
    )
    updated = pl.pallas_call(
        update_kernel,
        out_shape=jax.ShapeDtypeStruct(whole, jnp.float32),
        in_specs=[VMEM] * (1 + NODES) + [HBM],
        out_specs=HBM,
        input_output_aliases={1 + NODES: 0},
        scratch_shapes=[
            pltpu.VMEM((NODES,) + block, jnp.float32),
            pltpu.VMEM((3, size, lanes), jnp.float32),
            pltpu.SemaphoreType.DMA((6,)),
        ],
        compiler_params=limits,
        name="update",
    )(*returned, done, earlier)
    return updated.reshape(prognostic.shape)


def solution(mesh):
    placed = (
        P(None, "vz", None, None, "hy", "hx"),
        P(None, None, "hy", "hx"),
        P(),
        P(),
        P(None, "hy", "hx"),
        P(None, "hy", "hx"),
        P(None, None, "vz", None, "hy", "hx"),
        P("vz", None, "hy", "hx"),
    )
    return jax.shard_map(
        per_device,
        mesh=mesh,
        in_specs=placed,
        out_specs=P(None, "vz", None, None, "hy", "hx"),
        check_vma=False,
    )
```

```python
import functools

import jax
import jax.numpy as jnp
import numpy as np
from jax import lax
from jax.experimental import pallas as pl
from jax.experimental.pallas import tpu as pltpu
from jax.sharding import PartitionSpec as P

step_size = 0.05
lift_weight = 6.0
gravity_couple = 0.5
density_couple = 0.3
theta_couple = 0.4

NODES = 4
POINTS = NODES * NODES
FIELDS = 5
FACE_POINTS = ((0, 4, 8, 12), (3, 7, 11, 15), (0, 1, 2, 3), (12, 13, 14, 15))
RIM_POINTS = tuple(sorted(set(sum(FACE_POINTS, ()))))
ROWS = 8
LATE_FIELDS = (0, 1, 2, 4)
WAYS = (3, 2, 1, 0)


def derivative_table():
    points = np.array([-1.0, -1.0 / np.sqrt(5.0), 1.0 / np.sqrt(5.0), 1.0])
    number = points.shape[0]
    barycentric = np.ones(number)
    for source in range(number):
        for another in range(number):
            if another != source:
                barycentric[source] = barycentric[source] / (points[source] - points[another])
    matrix = np.zeros((number, number))
    for target in range(number):
        for source in range(number):
            if target != source:
                matrix[target, source] = (
                    barycentric[source] / barycentric[target] / (points[target] - points[source])
                )
        matrix[target, target] = -np.sum(matrix[target])
    return matrix


def operator_tables(lanes):
    weight = 0.5 * lift_weight
    table = derivative_table()
    table[0, 0] += weight
    table[-1, -1] -= weight
    eye = np.eye(NODES)
    along_first = np.kron(eye, table)
    along_second = np.kron(table, eye)
    ends = np.zeros(NODES)
    ends[0] = ends[-1] = 1.0
    faces = np.diag(np.kron(np.ones(NODES), ends) + np.kron(ends, np.ones(NODES)))
    first = np.zeros((POINTS, lanes))
    second = np.zeros((POINTS, lanes))
    same = np.zeros((FIELDS, POINTS, lanes))
    owner = np.full((lanes,), -1)
    for g in range(FIELDS):
        own = slice(POINTS * g, POINTS * (g + 1))
        first[:, own] = -along_first
        second[:, own] = -along_second
        same[g, :, own] = -weight * faces
        owner[own] = g
        for k in range(NODES):
            south = FIELDS * POINTS + 2 * NODES * g + k
            north = south + NODES
            second[FACE_POINTS[2][k], south] = weight
            second[FACE_POINTS[3][k], north] = -weight
            same[g, FACE_POINTS[2][k], south] = weight
            same[g, FACE_POINTS[3][k], north] = weight
            owner[south] = owner[north] = g
    tables = np.concatenate([first, second, same.reshape(FIELDS * POINTS, lanes)])
    return tables.astype(np.float32), owner


def chunks(total):
    return [min(start, total - ROWS) for start in range(0, total, ROWS)]


def partner_side(partner):
    odd = lax.rem(lax.axis_index("hy"), 2)
    return odd if partner else 1 - odd


def side_sign(side):
    return (2 * side - 1).astype(jnp.float32)


def ends(total):
    return list(range(0, total, ROWS))


def pick(values, masks, flip):
    chosen = []
    for k in range(NODES):
        row = values[FACE_POINTS[0][k]]
        for option in range(1, 4):
            row = jnp.where(masks[option], values[FACE_POINTS[option][k]], row)
        chosen.append(row)
    return [jnp.where(flip, chosen[NODES - 1 - k], chosen[k]) for k in range(NODES)]


def table_masks(face_row, flip_row, lanes):
    face = jnp.broadcast_to(face_row, (ROWS, lanes))
    flip = jnp.broadcast_to(flip_row, (ROWS, lanes))
    return [face == option for option in range(4)], flip == 1


def flux_row(f, g, matrix):
    return (matrix * FIELDS + f) * FIELDS + g


def along(fluxes, matrix, f, rows):
    total = None
    for g in range(FIELDS):
        at = flux_row(f, g, matrix)
        term = fluxes[at : at + 1, :] * rows[g]
        total = term if total is None else total + term
    return total


def side_lanes(f, piece, point):
    number = 3 * f + piece
    return number // 4, 32 * (number % 4) + point, 32 * (number % 4) + POINTS + point


def rim_kernel(
    state_hbm,
    face_hbm,
    way_hbm,
    metric_hbm,
    tables_hbm,
    flux_hbm,
    second_hbm,
    to_near,
    to_other,
    state,
    neighbour_face,
    orientation,
    metric,
    tables,
    fluxes,
    column,
    speed,
    flux,
    second_flux,
    semaphores,
):
    levels = state.shape[1] // POINTS
    sign = side_sign(partner_side(0))
    lanes = state.shape[2]
    width = len(RIM_POINTS)
    groups = [(start, min(start + ROWS, levels)) for start in range(0, levels, ROWS)]
    small = [
        pltpu.make_async_copy(source, target, semaphores.at[place])
        for place, (source, target) in enumerate(
            (
                (flux_hbm, flux),
                (face_hbm, neighbour_face),
                (way_hbm, orientation),
                (metric_hbm, metric),
                (tables_hbm, tables),
                (second_hbm, second_flux),
            )
        )
    ]
    large = []
    for place, (low, high) in enumerate(groups):
        rows = pl.ds(low * POINTS, (high - low) * POINTS)
        large.append(
            pltpu.make_async_copy(
                state_hbm.at[:, rows, :], state.at[:, rows, :], semaphores.at[len(small) + place]
            )
        )
    for copy in small[:1] + large + small[1:]:
        copy.start()
    column[...] = jnp.zeros_like(column)
    small[0].wait()
    arrived = 0
    for piece, start in enumerate(chunks(levels)):
        while arrived < len(groups) and groups[arrived][0] < start + ROWS:
            large[arrived].wait()
            arrived += 1
        for place, point in enumerate(RIM_POINTS):
            rows = [
                state[g, pl.ds(start * POINTS + point, ROWS, stride=POINTS), :]
                for g in range(FIELDS)
            ]
            for f, out in ((3, speed), (4, column)):
                normal = (sign * flux[f, 0]) * rows[0]
                for g in range(1, FIELDS):
                    normal = normal + (sign * flux[f, g]) * rows[g]
                out[2 * place, pl.ds(ROWS + start, ROWS), :] = rows[f] + normal
                out[2 * place + 1, pl.ds(ROWS + start, ROWS), :] = rows[f] - normal
    small[1].wait()
    small[2].wait()
    end = (levels + 2) * width
    for partner, out in enumerate((to_near, to_other)):
        face = partner_side(partner)
        for place in range(width):
            slot = 2 * place + partner
            for start in chunks(levels):
                upper = column[slot, pl.ds(ROWS + start + 1, ROWS), :]
                lower = column[slot, pl.ds(ROWS + start - 1, ROWS), :]
                out[pl.ds(start * width + place, ROWS, stride=width), :] = speed[
                    slot, pl.ds(ROWS + start, ROWS), :
                ] - gravity_couple * (upper - lower)
            for extra, level in ((0, 0), (1, levels - 1)):
                at = (levels + extra) * width + place
                out[at : at + 1, :] = column[slot, ROWS + level : ROWS + level + 1, :]
        out[end : end + 1, :] = neighbour_face[pl.ds(face, 1), :].astype(jnp.float32)
        out[end + 1 : end + 2, :] = orientation[pl.ds(face, 1), :].astype(jnp.float32)
        left = out.shape[0] - end - 2
        out[end + 2 :, :] = jnp.zeros((left, lanes), jnp.float32)
    small[3].wait()
    small[4].wait()
    small[5].wait()
    for place, source in enumerate((flux, second_flux)):
        for f in range(FIELDS):
            for g in range(FIELDS):
                at = flux_row(f, g, place)
                fluxes[at : at + 1, :] = jnp.full((1, lanes), source[f, g])


def edge_kernel(state, to_sides):
    lanes = state.shape[1]
    levels = state.shape[0] // (FIELDS * POINTS)
    lane = lax.broadcasted_iota(jnp.int32, (ROWS, lanes), 1)
    packed = [jnp.zeros((ROWS, lanes), jnp.float32) for _ in range(to_sides.shape[0] // ROWS)]
    for f in range(FIELDS):
        for piece, start in enumerate(chunks(levels)):
            for point in RIM_POINTS:
                row = state[pl.ds((f * levels + start) * POINTS + point, ROWS, stride=POINTS), :]
                block, last, initial = side_lanes(f, piece, point)
                packed[block] = jnp.where(lane == last, pltpu.roll(row, last + 1, 1), packed[block])
                packed[block] = jnp.where(lane == initial, pltpu.roll(row, initial, 1), packed[block])
    for block, value in enumerate(packed):
        to_sides[block * ROWS : (block + 1) * ROWS, :] = value


def face_kernel(partner, state, received, fluxes, *rest):
    lanes = state.shape[1]
    levels = state.shape[0] // (FIELDS * POINTS)
    at = (levels + 2) * len(RIM_POINTS)
    outs = rest[-2:]
    share = len(LATE_FIELDS) // len(outs)
    sign = side_sign(partner_side(partner))
    masks, flip = table_masks(
        received[at : at + 1, :].astype(jnp.int32),
        received[at + 1 : at + 2, :].astype(jnp.int32),
        lanes,
    )
    for start in chunks(levels):
        picked = []
        for g in range(FIELDS):
            values = {
                point: state[pl.ds((g * levels + start) * POINTS + point, ROWS, stride=POINTS), :]
                for point in RIM_POINTS
            }
            picked.append(pick(values, masks, flip))
        for place, f in enumerate(LATE_FIELDS):
            for k in range(NODES):
                normal = along(fluxes, 0, f, [picked[g][k] for g in range(FIELDS)])
                at = ((place % share) * levels + start) * NODES + k
                outs[place // share][pl.ds(at, ROWS, stride=NODES), :] = (
                    picked[f][k] + sign * normal
                )


def element_kernel(
    state,
    neighbour_face,
    orientation,
    metric,
    fluxes,
    tables,
    part,
    base,
    outer,
    operator_high,
    operator_low,
):
    levels = state.shape[0] // (FIELDS * POINTS)
    lanes = state.shape[1]
    lane = lax.broadcasted_iota(jnp.int32, (ROWS, lanes), 1)
    sides = []
    for side, (face, edge) in enumerate(((2, 0), (3, lanes - 1))):
        shift = 1 if side == 0 else lanes - 1
        row = jnp.broadcast_to(neighbour_face[face : face + 1, :], (ROWS, lanes))
        way = jnp.broadcast_to(orientation[face : face + 1, :], (ROWS, lanes))
        masks, flip = table_masks(
            pltpu.roll(row, lanes - shift, 1), pltpu.roll(way, lanes - shift, 1), lanes
        )
        sides.append((shift, edge, masks, flip))
    for f in range(FIELDS):
        for start in chunks(levels):
            q = f * levels + start
            values = {
                point: state[pl.ds(q * POINTS + point, ROWS, stride=POINTS), :]
                for point in RIM_POINTS
            }
            for side, (shift, edge, masks, flip) in enumerate(sides):
                for k, row in enumerate(pick(values, masks, flip)):
                    at = start * 8 * FIELDS + 8 * f + NODES * side + k
                    outer[pl.ds(at, ROWS, stride=8 * FIELDS), :] = jnp.where(
                        lane == edge, 0.0, pltpu.roll(row, shift, 1)
                    )
    index = lax.broadcasted_iota(jnp.int32, (1, lanes), 1)
    own_columns = FIELDS * POINTS
    owner = jnp.where(index < own_columns, index // POINTS, (index - own_columns) // 8)
    for f in range(FIELDS):
        first_row = jnp.zeros((1, lanes), jnp.float32)
        second_row = first_row
        for g in range(FIELDS):
            first, second = (flux_row(f, g, matrix) for matrix in range(2))
            first_row = jnp.where(owner == g, fluxes[first : first + 1, :], first_row)
            second_row = jnp.where(owner == g, fluxes[second : second + 1, :], second_row)
        block = (
            first_row * tables[0:POINTS, :]
            + second_row * tables[POINTS : 2 * POINTS, :]
            + tables[(2 + f) * POINTS : (3 + f) * POINTS, :]
        )
        high = block.astype(jnp.bfloat16)
        operator_high[f * POINTS : (f + 1) * POINTS, :] = high
        operator_low[f * POINTS : (f + 1) * POINTS, :] = (
            block - high.astype(jnp.float32)
        ).astype(jnp.bfloat16)
    high = operator_high[...]
    low = operator_low[...]
    scale = step_size * metric[...]
    blank = jnp.zeros((lanes - own_columns - 8 * FIELDS, lanes), jnp.float32)
    for pair in range(0, levels, 2):
        sides = []
        for level in (pair, pair + 1):
            rows = [
                state[pl.ds((f * levels + level) * POINTS, POINTS), :] for f in range(FIELDS)
            ]
            rows.append(outer[pl.ds(level * 8 * FIELDS, 8 * FIELDS), :])
            rows.append(blank)
            sides.append(jnp.concatenate(rows, axis=0))
        values = jnp.concatenate(sides, axis=1)
        top = values.astype(jnp.bfloat16)
        rest = (values - top.astype(jnp.float32)).astype(jnp.bfloat16)
        change = (
            jnp.dot(high, top, preferred_element_type=jnp.float32)
            + jnp.dot(high, rest, preferred_element_type=jnp.float32)
            + jnp.dot(low, top, preferred_element_type=jnp.float32)
        )
        for place, level in enumerate((pair, pair + 1)):
            for f in range(FIELDS):
                at = pl.ds((f * levels + level) * POINTS, POINTS)
                part[at, :] = (
                    state[at, :]
                    + scale
                    * change[
                        f * POINTS : (f + 1) * POINTS, place * lanes : (place + 1) * lanes
                    ]
                )
    for level in range(levels):
        speed = part[pl.ds((3 * levels + level) * POINTS, POINTS), :]
        upper = part[pl.ds((4 * levels + level + 1) * POINTS, POINTS), :] if level < levels - 1 else 0.0
        lower = part[pl.ds((4 * levels + level - 1) * POINTS, POINTS), :] if level else 0.0
        value = speed - gravity_couple * (upper - lower)
        for j in range(NODES):
            base[j, level * NODES : (level + 1) * NODES, :] = value[NODES * j : NODES * (j + 1)]
    for extra, level in ((0, 0), (1, levels - 1)):
        value = part[pl.ds((4 * levels + level) * POINTS, POINTS), :]
        at = (levels + extra) * NODES
        for j in range(NODES):
            base[j, at : at + NODES, :] = value[NODES * j : NODES * (j + 1)]


def side_corrections(received, side, fluxes, fields, pieces):
    lanes = received.shape[1]
    sign = 1.0 if side == 0 else -1.0
    result = [[] for _ in fields]
    for piece in range(pieces):
        rows = []
        for g in range(FIELDS):
            block, *places = side_lanes(g, piece, 0)
            rows.append(
                pltpu.roll(
                    received[block * ROWS : (block + 1) * ROWS, :], (lanes - places[side]) % lanes, 1
                )
            )
        for place, f in enumerate(fields):
            result[place].append(rows[f] + sign * along(fluxes, 1, f, rows))
    return result


def spread(value, edge, masks, flip):
    lanes = value.shape[1]
    return pick(
        {point: pltpu.roll(value, (edge - point) % lanes, 1) for point in RIM_POINTS}, masks, flip
    )


def add_first_side(partner, source, send, base, neighbour_face, orientation, metric):
    rows, lanes = base.shape[1:]
    width = len(RIM_POINTS)
    weight = 0.5 * lift_weight * step_size
    face = partner_side(partner)
    i = (NODES - 1) * face
    masks, flip = table_masks(
        neighbour_face[pl.ds(face, 1), :], orientation[pl.ds(face, 1), :], lanes
    )
    for start in chunks(rows // NODES):
        values = {
            point: source[pl.ds(start * width + place, ROWS, stride=width), :]
            for place, point in enumerate(RIM_POINTS)
        }
        for j, row in enumerate(pick(values, masks, flip)):
            at = pl.ds(start * NODES + i, ROWS, stride=NODES)
            scale = weight * metric[pl.ds(NODES * j + i, 1), :]
            send[j, at, :] = base[j, at, :] + scale * row


def pack_kernel(half, from_other, neighbour_face, orientation, metric, *rest):
    sends, (send,) = rest[:NODES], rest[NODES:]
    me = lax.axis_index("vz")
    send[...] = half[...]
    add_first_side(1, from_other, send, half, neighbour_face, orientation, metric)
    for out, way in zip(sends, WAYS):
        out[...] = send[me ^ way]


def half_pack_kernel(
    base,
    from_near,
    from_down,
    from_up,
    neighbour_face,
    orientation,
    metric,
    fluxes,
    factored,
    half,
    send,
    column,
    mixed,
):
    rows, lanes = base.shape[1:]
    levels = rows // NODES - 2
    width = len(RIM_POINTS)
    weight = 0.5 * lift_weight * step_size
    send[:, 0:rows, :] = base[...]
    send[:, rows:, :] = jnp.zeros((NODES, send.shape[1] - rows, lanes), jnp.float32)
    column[...] = jnp.zeros_like(column)
    mixed[...] = jnp.zeros_like(mixed)
    add_first_side(0, from_near, send, base, neighbour_face, orientation, metric)
    lane = lax.broadcasted_iota(jnp.int32, (ROWS, lanes), 1)
    for side, (received, edge, j) in enumerate(
        ((from_down, 0, 0), (from_up, lanes - 1, NODES - 1))
    ):
        face = 2 + side
        masks, flip = table_masks(
            neighbour_face[face : face + 1, :], orientation[face : face + 1, :], lanes
        )
        speed, heat = side_corrections(received, side, fluxes, (3, 4), len(chunks(levels)))
        for start, value in zip(chunks(levels), heat):
            column[pl.ds(ROWS + start, ROWS), :] = value
        for start, value in zip(chunks(levels), speed):
            upper = column[pl.ds(ROWS + start + 1, ROWS), :]
            lower = column[pl.ds(ROWS + start - 1, ROWS), :]
            mixed[pl.ds(start, ROWS), :] = value - gravity_couple * (upper - lower)
        mixed[levels : levels + 1, :] = column[ROWS : ROWS + 1, :]
        mixed[levels + 1 : levels + 2, :] = column[ROWS + levels - 1 : ROWS + levels, :]
        for start in ends(levels + 2):
            picked = spread(mixed[start : start + ROWS, :], edge, masks, flip)
            for k, row in enumerate(picked):
                point = NODES * j + k
                at = pl.ds(start * NODES + k, ROWS, stride=NODES)
                scale = weight * metric[point : point + 1, :]
                send[j, at, :] += jnp.where(lane == edge, scale * row, 0.0)
    half[...] = send[:, 0:rows, :]


def finish_section_kernel(
    part,
    near_early,
    near_late,
    other_early,
    other_late,
    from_down,
    from_up,
    neighbour_face,
    orientation,
    metric,
    fluxes,
    out,
    done,
    final,
    mixed,
    semaphore,
):
    levels = part.shape[0] // (FIELDS * POINTS)
    lanes = part.shape[1]
    size = levels * POINTS
    weight = 0.5 * lift_weight * step_size
    scale = weight * metric[...]
    lane = lax.broadcasted_iota(jnp.int32, (ROWS, lanes), 1)
    tables = []
    edges = []
    for side, received in enumerate((from_down, from_up)):
        face = 2 + side
        tables.append(
            table_masks(
                neighbour_face[face : face + 1, :], orientation[face : face + 1, :], lanes
            )
        )
        edges.append(
            side_corrections(received, side, fluxes, LATE_FIELDS, len(chunks(levels)))
        )
    copy = pltpu.make_async_copy(final, out.at[1:3], semaphore)
    sources = ((near_early, near_late), (other_early, other_late))
    for place, f in ((1, 1), (2, 2), (0, 0), (3, 4)):
        target = final.at[f - 1] if f in (1, 2) else mixed
        target[...] = part[f * size : (f + 1) * size, :]
        for piece, start in enumerate(chunks(levels)):
            for j in range(NODES):
                for partner, source in enumerate(sources):
                    point = NODES * j + (NODES - 1) * partner_side(partner)
                    share = len(LATE_FIELDS) // len(source)
                    rows = source[place // share][
                        pl.ds(((place % share) * levels + start) * NODES + j, ROWS, stride=NODES),
                        :,
                    ]
                    at = pl.ds(start * POINTS + point, ROWS, stride=POINTS)
                    target[at, :] = (
                        part[pl.ds(f * size + start * POINTS + point, ROWS, stride=POINTS), :]
                        + weight * metric[pl.ds(point, 1), :] * rows
                    )
        for piece, start in enumerate(chunks(levels)):
            row_index = lax.broadcasted_iota(jnp.int32, (ROWS, lanes), 0)
            fresh = row_index >= (-start) % ROWS
            for side, (edge, j) in enumerate(((0, 0), (lanes - 1, NODES - 1))):
                picked = spread(edges[side][place][piece], edge, *tables[side])
                for k, row in enumerate(picked):
                    point = NODES * j + k
                    at = pl.ds(start * POINTS + point, ROWS, stride=POINTS)
                    target[at, :] += jnp.where(
                        (lane == edge) & fresh, scale[point : point + 1, :] * row, 0.0
                    )
        if f == 2:
            copy.start()
        if f in (0, 4):
            for level in range(levels):
                for j in range(NODES):
                    done[min(f, 1), j, level * NODES : (level + 1) * NODES, :] = mixed[
                        level * POINTS + j * NODES : level * POINTS + (j + 1) * NODES, :
                    ]
    copy.wait()


def factor_kernel(coupling, damping, far, near, inverse, ratio, second):
    levels = coupling.shape[1]
    shape = coupling.shape[2:]
    blank = jnp.zeros(shape, jnp.float32)
    far_ratio, far_second, near_ratio, near_second = (blank,) * 4
    extra = damping[...]
    for level in range(levels):
        a, b, d, e = (coupling[entry, level] for entry in range(4))
        centre = a + b + d + e + extra
        reduced = -b + a * far_ratio
        pivot = centre + a * far_second - reduced * near_ratio
        scaled = 1.0 / pivot
        upper_ratio = (-d - reduced * near_second) * scaled
        second_ratio = -e * scaled
        far[level] = a * scaled
        near[level] = reduced * scaled
        inverse[level] = scaled
        ratio[level] = upper_ratio
        second[level] = second_ratio
        far_ratio, far_second = near_ratio, near_second
        near_ratio, near_second = upper_ratio, second_ratio


def solve_kernel(far, near, inverse, ratio, second, *rest):
    ways = NODES
    received, sends, (source, heat, speed) = rest[:ways], rest[ways : 2 * ways], rest[2 * ways :]
    levels = far.shape[0]
    here = levels // ways
    me = lax.axis_index("vz")
    for values, way in zip(received, WAYS):
        block = me ^ way
        source[pl.ds(block * here, here)] = values[0:here]
        heat[block] = values[here : here + 2]
    for block in range(ways - 1):
        last = block * here + here - 1
        source[last] = source[last] - gravity_couple * heat[block + 1, 0]
        source[last + 1] = source[last + 1] + gravity_couple * heat[block, 1]
    blank = jnp.zeros(far.shape[1:], jnp.float32)
    before_two, before_one = blank, blank
    for level in range(levels):
        value = source[level] * inverse[level]
        value = value + far[level] * before_two
        value = value - near[level] * before_one
        source[level] = value
        before_two, before_one = before_one, value
    speed[0] = blank
    speed[levels + 1] = blank
    next_one, next_two = blank, blank
    for level in range(levels - 1, -1, -1):
        value = source[level] - second[level] * next_two
        value = value - ratio[level] * next_one
        speed[level + 1] = value
        next_two, next_one = next_one, value
    for send, way in zip(sends, WAYS):
        send[...] = speed[pl.ds((me ^ way) * here, here + 2)]


def update_kernel(ways, *refs):
    received, (done, earlier, out, final, semaphores) = refs[: len(ways)], refs[len(ways) :]
    levels = done.shape[2]
    me = lax.axis_index("vz")
    copies = []
    for place, (speed, way) in enumerate(zip(received, ways)):
        j = me ^ way
        jump = speed[2 : levels + 2] - speed[0:levels]
        final[place, 0] = speed[1 : levels + 1]
        final[place, 1] = done[0, j] - density_couple * jump
        final[place, 2] = done[1, j] - theta_couple * jump
        for k, f in enumerate((3, 0, 4)):
            copies.append(
                pltpu.make_async_copy(
                    final.at[place, k], out.at[f, :, j], semaphores.at[len(copies)]
                )
            )
            copies[-1].start()
    for copy in copies:
        copy.wait()


VMEM = pl.BlockSpec(memory_space=pltpu.VMEM)
HBM = pl.BlockSpec(memory_space=pltpu.HBM)
ANY = pl.BlockSpec(memory_space=pl.ANY)


def call(kernel, outs, in_specs, scratch=(), cost=0, name=None):
    kinds = [x if hasattr(x, "dtype") else pltpu.VMEM(x, jnp.float32) for x in outs]
    return pl.pallas_call(
        kernel,
        out_shape=kinds,
        in_specs=in_specs,
        out_specs=[VMEM] * len(outs),
        scratch_shapes=list(scratch),
        compiler_params=pltpu.CompilerParams(vmem_limit_bytes=24 * 1024 * 1024),
        cost_estimate=pl.CostEstimate(flops=cost, bytes_accessed=cost, transcendentals=0),
        name=name,
    )


def per_device(
    prognostic, metric, first_flux, second_flux, neighbour_face, orientation, coupling, damping
):
    fields, levels = prognostic.shape[:2]
    lanes = prognostic.shape[-1]
    whole = (fields, levels * POINTS, lanes)
    metric = metric.reshape(POINTS, lanes)
    neighbour_face = neighbour_face.reshape(4, lanes)
    orientation = orientation.reshape(4, lanes)
    coupling = coupling.reshape(4, coupling.shape[1], NODES, lanes)
    damping = damping.reshape(NODES, lanes)
    tables, _ = operator_tables(lanes)

    def shifts(axis):
        size = lax.axis_size(axis)
        up = [(i, (i + 1) % size) for i in range(size)]
        return up, [(j, i) for i, j in up]

    def exchange(arrays):
        size = lax.axis_size("vz")
        return [
            lax.ppermute(x, "vz", [(i, i ^ way) for i in range(size)]) if way else x
            for x, way in zip(arrays, WAYS)
        ]

    count = lax.axis_size("hy")
    near = [(i, i ^ 1) for i in range(count)]
    other = [(i, (i + 1 if i % 2 else i - 1) % count) for i in range(count)]
    second_up, second_down = shifts("hx")
    width = len(RIM_POINTS)
    message = (-(-((levels + 2) * width + 2) // ROWS) * ROWS, lanes)
    sides = (-(-fields * len(chunks(levels)) // 4) * ROWS, lanes)
    padded = levels + 2 * ROWS
    table = pltpu.VMEM((4, lanes), jnp.int32)
    inputs = (
        prognostic.reshape(whole),
        neighbour_face,
        orientation,
        metric,
        jnp.asarray(tables),
        first_flux,
        second_flux,
    )
    (
        to_near,
        to_other,
        state,
        neighbour_face,
        orientation,
        metric,
        tables,
        fluxes,
    ) = call(
        rim_kernel,
        [
            message,
            message,
            whole,
            table,
            table,
            (POINTS, lanes),
            tables.shape,
            (-(-2 * fields * fields // ROWS) * ROWS, lanes),
        ],
        [HBM] * len(inputs),
        [
            pltpu.VMEM((2 * width, padded, lanes), jnp.float32),
            pltpu.VMEM((2 * width, padded, lanes), jnp.float32),
            pltpu.SMEM((fields, fields), jnp.float32),
            pltpu.SMEM((fields, fields), jnp.float32),
            pltpu.SemaphoreType.DMA((6 + -(-levels // ROWS),)),
        ],
        cost=1000,
        name="rim",
    )(*(pltpu.with_memory_space_constraint(x, pltpu.HBM) for x in inputs))
    state = state.reshape(fields * levels * POINTS, lanes)
    from_other = lax.ppermute(to_other, "hy", other)
    from_near = lax.ppermute(to_near, "hy", near)
    (to_sides,) = call(edge_kernel, [sides], [VMEM], cost=1000, name="edge")(state)
    from_down = lax.ppermute(to_sides, "hx", second_up)
    from_up = from_down
    if lax.axis_size("hx") > 2:
        from_up = lax.ppermute(to_sides, "hx", second_down)

    column = (coupling.shape[1], NODES, lanes)
    factors = call(factor_kernel, [column] * 5, [VMEM] * 2, cost=4000000, name="factor")(
        coupling, damping
    )
    block = ((levels + 2) * NODES, lanes)
    part, base = call(
        element_kernel,
        [state.shape, (NODES,) + block],
        [VMEM] * 6,
        [
            pltpu.VMEM((levels * 8 * fields, lanes), jnp.float32),
            pltpu.VMEM((fields * POINTS, lanes), jnp.bfloat16),
            pltpu.VMEM((fields * POINTS, lanes), jnp.bfloat16),
        ],
        cost=4000000,
        name="element",
    )(
        state,
        neighbour_face,
        orientation,
        metric,
        fluxes,
        tables,
    )
    count = -(-(levels + 2) // ROWS) * ROWS
    (half,) = call(
        half_pack_kernel,
        [(NODES,) + block],
        [VMEM] * 8 + [ANY],
        [
            pltpu.VMEM((NODES, count * NODES, lanes), jnp.float32),
            pltpu.VMEM((padded, lanes), jnp.float32),
            pltpu.VMEM((count, lanes), jnp.float32),
        ],
        cost=1000,
        name="half_pack",
    )(
        base,
        from_near,
        from_down,
        from_up,
        neighbour_face,
        orientation,
        metric,
        fluxes,
        factors[0],
    )
    late = [(levels * NODES * len(LATE_FIELDS) // 2, lanes)] * 2
    near_face = call(
        functools.partial(face_kernel, 0), late, [VMEM] * 3 + [ANY], cost=1000, name="near_face"
    )(state, from_near, fluxes, half)
    near_face = [lax.ppermute(x, "hy", near) for x in near_face]
    sends = call(
        pack_kernel,
        [block] * NODES,
        [VMEM] * 5,
        [pltpu.VMEM((NODES,) + block, jnp.float32)],
        cost=1000,
        name="pack",
    )(half, from_other, neighbour_face, orientation, metric)
    received = exchange(sends)

    other_face = call(
        functools.partial(face_kernel, 1),
        late,
        [VMEM] * 3 + [ANY] * 2,
        cost=1000,
        name="other_face",
    )(state, from_other, fluxes, *near_face)
    other_face = [lax.ppermute(x, "hy", other) for x in other_face]

    cube = (levels + 2, NODES, lanes)
    speeds = call(
        solve_kernel,
        [cube] * NODES,
        [VMEM] * (5 + NODES),
        [
            pltpu.VMEM(column, jnp.float32),
            pltpu.VMEM((NODES, 2, NODES, lanes), jnp.float32),
            pltpu.VMEM((column[0] + 2,) + column[1:], jnp.float32),
        ],
        cost=1000,
        name="solve",
    )(*factors, *[x.reshape(cube) for x in received])
    returned = [x.reshape(cube) for x in exchange([x.reshape(block) for x in speeds])]
    size = levels * POINTS
    limits = pltpu.CompilerParams(vmem_limit_bytes=24 * 1024 * 1024)
    earlier, done = pl.pallas_call(
        finish_section_kernel,
        out_shape=[
            jax.ShapeDtypeStruct(whole, jnp.float32),
            pltpu.VMEM((2, NODES, levels * NODES, lanes), jnp.float32),
        ],
        in_specs=[VMEM] * 11,
        out_specs=[HBM, VMEM],
        scratch_shapes=[
            pltpu.VMEM((2, size, lanes), jnp.float32),
            pltpu.VMEM((size, lanes), jnp.float32),
            pltpu.SemaphoreType.DMA,
        ],
        compiler_params=limits,
        cost_estimate=pl.CostEstimate(flops=4000000, bytes_accessed=4000000, transcendentals=0),
        name="finish",
    )(
        part, *near_face, *other_face, from_down, from_up, neighbour_face, orientation, metric, fluxes
    )
    result = earlier.reshape(fields, levels, NODES, NODES, lanes)
    done = done.reshape(2, NODES, levels, NODES, lanes)
    for ways in ((3, 0), (1, 2)):
        result = pl.pallas_call(
            functools.partial(update_kernel, ways),
            out_shape=jax.ShapeDtypeStruct(result.shape, jnp.float32),
            in_specs=[VMEM] * (len(ways) + 1) + [HBM],
            out_specs=HBM,
            input_output_aliases={len(ways) + 1: 0},
            scratch_shapes=[
                pltpu.VMEM((len(ways), 3, levels, NODES, lanes), jnp.float32),
                pltpu.SemaphoreType.DMA((3 * len(ways),)),
            ],
            compiler_params=limits,
            name="update",
        )(*(returned[WAYS.index(way)] for way in ways), done, result)
    return result.reshape(prognostic.shape)


def solution(mesh):
    placed = (
        P(None, "vz", None, None, "hy", "hx"),
        P(None, None, "hy", "hx"),
        P(),
        P(),
        P(None, "hy", "hx"),
        P(None, "hy", "hx"),
        P(None, None, "vz", None, "hy", "hx"),
        P("vz", None, "hy", "hx"),
    )
    return jax.shard_map(
        per_device,
        mesh=mesh,
        in_specs=placed,
        out_specs=P(None, "vz", None, None, "hy", "hx"),
        check_vma=False,
    )
```

```python
import functools

import jax
import jax.numpy as jnp
import numpy as np
from jax import lax
from jax.experimental import pallas as pl
from jax.experimental.pallas import tpu as pltpu
from jax.sharding import PartitionSpec as P

step_size = 0.05
lift_weight = 6.0
gravity_couple = 0.5
density_couple = 0.3
theta_couple = 0.4

NODES = 4
POINTS = NODES * NODES
FIELDS = 5
FACE_POINTS = ((0, 4, 8, 12), (3, 7, 11, 15), (0, 1, 2, 3), (12, 13, 14, 15))
RIM_POINTS = tuple(sorted(set(sum(FACE_POINTS, ()))))
ROWS = 8
LATE_FIELDS = (0, 1, 2, 4)
WAYS = (3, 2, 1, 0)


def derivative_table():
    points = np.array([-1.0, -1.0 / np.sqrt(5.0), 1.0 / np.sqrt(5.0), 1.0])
    number = points.shape[0]
    barycentric = np.ones(number)
    for source in range(number):
        for another in range(number):
            if another != source:
                barycentric[source] = barycentric[source] / (points[source] - points[another])
    matrix = np.zeros((number, number))
    for target in range(number):
        for source in range(number):
            if target != source:
                matrix[target, source] = (
                    barycentric[source] / barycentric[target] / (points[target] - points[source])
                )
        matrix[target, target] = -np.sum(matrix[target])
    return matrix


def operator_tables(lanes):
    weight = 0.5 * lift_weight
    table = derivative_table()
    table[0, 0] += weight
    table[-1, -1] -= weight
    eye = np.eye(NODES)
    along_first = np.kron(eye, table)
    along_second = np.kron(table, eye)
    ends = np.zeros(NODES)
    ends[0] = ends[-1] = 1.0
    faces = np.diag(np.kron(np.ones(NODES), ends) + np.kron(ends, np.ones(NODES)))
    first = np.zeros((POINTS, lanes))
    second = np.zeros((POINTS, lanes))
    same = np.zeros((FIELDS, POINTS, lanes))
    owner = np.full((lanes,), -1)
    for g in range(FIELDS):
        own = slice(POINTS * g, POINTS * (g + 1))
        first[:, own] = -along_first
        second[:, own] = -along_second
        same[g, :, own] = -weight * faces
        owner[own] = g
        for k in range(NODES):
            south = FIELDS * POINTS + 2 * NODES * g + k
            north = south + NODES
            second[FACE_POINTS[2][k], south] = weight
            second[FACE_POINTS[3][k], north] = -weight
            same[g, FACE_POINTS[2][k], south] = weight
            same[g, FACE_POINTS[3][k], north] = weight
            owner[south] = owner[north] = g
    tables = np.concatenate([first, second, same.reshape(FIELDS * POINTS, lanes)])
    return tables.astype(np.float32), owner


def chunks(total):
    return [min(start, total - ROWS) for start in range(0, total, ROWS)]


def partner_side(partner):
    odd = lax.rem(lax.axis_index("hy"), 2)
    return odd if partner else 1 - odd


def side_sign(side):
    return (2 * side - 1).astype(jnp.float32)


def ends(total):
    return list(range(0, total, ROWS))


def pick(values, masks, flip):
    chosen = []
    for k in range(NODES):
        row = values[FACE_POINTS[0][k]]
        for option in range(1, 4):
            row = jnp.where(masks[option], values[FACE_POINTS[option][k]], row)
        chosen.append(row)
    return [jnp.where(flip, chosen[NODES - 1 - k], chosen[k]) for k in range(NODES)]


def table_masks(face_row, flip_row, lanes):
    face = jnp.broadcast_to(face_row, (ROWS, lanes))
    flip = jnp.broadcast_to(flip_row, (ROWS, lanes))
    return [face == option for option in range(4)], flip == 1


def flux_row(f, g, matrix):
    return (matrix * FIELDS + f) * FIELDS + g


def along(fluxes, matrix, f, rows):
    total = None
    for g in range(FIELDS):
        at = flux_row(f, g, matrix)
        term = fluxes[at : at + 1, :] * rows[g]
        total = term if total is None else total + term
    return total


def side_lanes(f, piece, point):
    number = 3 * f + piece
    return number // 4, 32 * (number % 4) + point, 32 * (number % 4) + POINTS + point


def rim_kernel(
    state_hbm,
    face_hbm,
    way_hbm,
    metric_hbm,
    tables_hbm,
    flux_hbm,
    second_hbm,
    to_other,
    state,
    neighbour_face,
    orientation,
    metric,
    tables,
    fluxes,
    column,
    speed,
    flux,
    second_flux,
    semaphores,
):
    levels = state.shape[1] // POINTS
    face = partner_side(1)
    sign = side_sign(face)
    lanes = state.shape[2]
    width = len(RIM_POINTS)
    groups = [(start, min(start + ROWS, levels)) for start in range(0, levels, ROWS)]
    small = [
        pltpu.make_async_copy(source, target, semaphores.at[place])
        for place, (source, target) in enumerate(
            (
                (flux_hbm, flux),
                (face_hbm, neighbour_face),
                (way_hbm, orientation),
                (metric_hbm, metric),
                (tables_hbm, tables),
                (second_hbm, second_flux),
            )
        )
    ]
    large = []
    for place, (low, high) in enumerate(groups):
        rows = pl.ds(low * POINTS, (high - low) * POINTS)
        large.append(
            pltpu.make_async_copy(
                state_hbm.at[:, rows, :], state.at[:, rows, :], semaphores.at[len(small) + place]
            )
        )
    for copy in small[:1] + large + small[1:]:
        copy.start()
    column[...] = jnp.zeros_like(column)
    small[0].wait()
    arrived = 0
    for piece, start in enumerate(chunks(levels)):
        while arrived < len(groups) and groups[arrived][0] < start + ROWS:
            large[arrived].wait()
            arrived += 1
        for place, point in enumerate(RIM_POINTS):
            rows = [
                state[g, pl.ds(start * POINTS + point, ROWS, stride=POINTS), :]
                for g in range(FIELDS)
            ]
            for f, out in ((3, speed), (4, column)):
                normal = (sign * flux[f, 0]) * rows[0]
                for g in range(1, FIELDS):
                    normal = normal + (sign * flux[f, g]) * rows[g]
                out[place, pl.ds(ROWS + start, ROWS), :] = rows[f] + normal
    small[1].wait()
    small[2].wait()
    end = (levels + 2) * width
    for place in range(width):
        for start in chunks(levels):
            upper = column[place, pl.ds(ROWS + start + 1, ROWS), :]
            lower = column[place, pl.ds(ROWS + start - 1, ROWS), :]
            to_other[pl.ds(start * width + place, ROWS, stride=width), :] = speed[
                place, pl.ds(ROWS + start, ROWS), :
            ] - gravity_couple * (upper - lower)
        for extra, level in ((0, 0), (1, levels - 1)):
            at = (levels + extra) * width + place
            to_other[at : at + 1, :] = column[place, ROWS + level : ROWS + level + 1, :]
    to_other[end : end + 1, :] = neighbour_face[pl.ds(face, 1), :].astype(jnp.float32)
    to_other[end + 1 : end + 2, :] = orientation[pl.ds(face, 1), :].astype(jnp.float32)
    left = to_other.shape[0] - end - 2
    to_other[end + 2 :, :] = jnp.zeros((left, lanes), jnp.float32)
    small[3].wait()
    small[4].wait()
    small[5].wait()
    for place, source in enumerate((flux, second_flux)):
        for f in range(FIELDS):
            for g in range(FIELDS):
                at = flux_row(f, g, place)
                fluxes[at : at + 1, :] = jnp.full((1, lanes), source[f, g])


def edge_kernel(state, to_sides):
    lanes = state.shape[1]
    levels = state.shape[0] // (FIELDS * POINTS)
    lane = lax.broadcasted_iota(jnp.int32, (ROWS, lanes), 1)
    packed = [jnp.zeros((ROWS, lanes), jnp.float32) for _ in range(to_sides.shape[0] // ROWS)]
    for f in range(FIELDS):
        for piece, start in enumerate(chunks(levels)):
            for point in RIM_POINTS:
                row = state[pl.ds((f * levels + start) * POINTS + point, ROWS, stride=POINTS), :]
                block, last, initial = side_lanes(f, piece, point)
                packed[block] = jnp.where(lane == last, pltpu.roll(row, last + 1, 1), packed[block])
                packed[block] = jnp.where(lane == initial, pltpu.roll(row, initial, 1), packed[block])
    for block, value in enumerate(packed):
        to_sides[block * ROWS : (block + 1) * ROWS, :] = value


def near_kernel(state, neighbour_face, orientation, fluxes, source, late, column):
    lanes = state.shape[1]
    levels = state.shape[0] // (FIELDS * POINTS)
    face = partner_side(0)
    sign = -side_sign(face)
    masks, flip = table_masks(
        neighbour_face[pl.ds(face, 1), :], orientation[pl.ds(face, 1), :], lanes
    )
    column[...] = jnp.zeros_like(column)
    speeds = []
    for start in chunks(levels):
        picked = []
        for g in range(FIELDS):
            values = {
                point: state[pl.ds((g * levels + start) * POINTS + point, ROWS, stride=POINTS), :]
                for point in RIM_POINTS
            }
            picked.append(pick(values, masks, flip))
        for k in range(NODES):
            rows = [picked[g][k] for g in range(FIELDS)]
            changed = [rows[f] + sign * along(fluxes, 0, f, rows) for f in range(FIELDS)]
            for place, f in enumerate(LATE_FIELDS):
                at = (place * levels + start) * NODES + k
                late[pl.ds(at, ROWS, stride=NODES), :] = changed[f]
            column[k, pl.ds(ROWS + start, ROWS), :] = changed[4]
            speeds.append(changed[3])
    for piece, start in enumerate(chunks(levels)):
        for k in range(NODES):
            upper = column[k, pl.ds(ROWS + start + 1, ROWS), :]
            lower = column[k, pl.ds(ROWS + start - 1, ROWS), :]
            source[pl.ds(start * NODES + k, ROWS, stride=NODES), :] = speeds[
                NODES * piece + k
            ] - gravity_couple * (upper - lower)
    for extra, level in ((0, 0), (1, levels - 1)):
        for k in range(NODES):
            at = (levels + extra) * NODES + k
            source[at : at + 1, :] = column[k, ROWS + level : ROWS + level + 1, :]


def face_kernel(partner, state, received, fluxes, *rest):
    lanes = state.shape[1]
    levels = state.shape[0] // (FIELDS * POINTS)
    at = (levels + 2) * len(RIM_POINTS)
    outs = rest[-2:]
    share = len(LATE_FIELDS) // len(outs)
    sign = side_sign(partner_side(partner))
    masks, flip = table_masks(
        received[at : at + 1, :].astype(jnp.int32),
        received[at + 1 : at + 2, :].astype(jnp.int32),
        lanes,
    )
    for start in chunks(levels):
        picked = []
        for g in range(FIELDS):
            values = {
                point: state[pl.ds((g * levels + start) * POINTS + point, ROWS, stride=POINTS), :]
                for point in RIM_POINTS
            }
            picked.append(pick(values, masks, flip))
        for place, f in enumerate(LATE_FIELDS):
            for k in range(NODES):
                normal = along(fluxes, 0, f, [picked[g][k] for g in range(FIELDS)])
                at = ((place % share) * levels + start) * NODES + k
                outs[place // share][pl.ds(at, ROWS, stride=NODES), :] = (
                    picked[f][k] + sign * normal
                )


def element_kernel(
    state,
    neighbour_face,
    orientation,
    metric,
    fluxes,
    tables,
    part,
    base,
    outer,
    operator_high,
    operator_low,
):
    levels = state.shape[0] // (FIELDS * POINTS)
    lanes = state.shape[1]
    lane = lax.broadcasted_iota(jnp.int32, (ROWS, lanes), 1)
    sides = []
    for side, (face, edge) in enumerate(((2, 0), (3, lanes - 1))):
        shift = 1 if side == 0 else lanes - 1
        row = jnp.broadcast_to(neighbour_face[face : face + 1, :], (ROWS, lanes))
        way = jnp.broadcast_to(orientation[face : face + 1, :], (ROWS, lanes))
        masks, flip = table_masks(
            pltpu.roll(row, lanes - shift, 1), pltpu.roll(way, lanes - shift, 1), lanes
        )
        sides.append((shift, edge, masks, flip))
    for f in range(FIELDS):
        for start in chunks(levels):
            q = f * levels + start
            values = {
                point: state[pl.ds(q * POINTS + point, ROWS, stride=POINTS), :]
                for point in RIM_POINTS
            }
            for side, (shift, edge, masks, flip) in enumerate(sides):
                for k, row in enumerate(pick(values, masks, flip)):
                    at = start * 8 * FIELDS + 8 * f + NODES * side + k
                    outer[pl.ds(at, ROWS, stride=8 * FIELDS), :] = jnp.where(
                        lane == edge, 0.0, pltpu.roll(row, shift, 1)
                    )
    index = lax.broadcasted_iota(jnp.int32, (1, lanes), 1)
    own_columns = FIELDS * POINTS
    owner = jnp.where(index < own_columns, index // POINTS, (index - own_columns) // 8)
    for f in range(FIELDS):
        first_row = jnp.zeros((1, lanes), jnp.float32)
        second_row = first_row
        for g in range(FIELDS):
            first, second = (flux_row(f, g, matrix) for matrix in range(2))
            first_row = jnp.where(owner == g, fluxes[first : first + 1, :], first_row)
            second_row = jnp.where(owner == g, fluxes[second : second + 1, :], second_row)
        block = (
            first_row * tables[0:POINTS, :]
            + second_row * tables[POINTS : 2 * POINTS, :]
            + tables[(2 + f) * POINTS : (3 + f) * POINTS, :]
        )
        high = block.astype(jnp.bfloat16)
        operator_high[f * POINTS : (f + 1) * POINTS, :] = high
        operator_low[f * POINTS : (f + 1) * POINTS, :] = (
            block - high.astype(jnp.float32)
        ).astype(jnp.bfloat16)
    high = operator_high[...]
    low = operator_low[...]
    scale = step_size * metric[...]
    blank = jnp.zeros((lanes - own_columns - 8 * FIELDS, lanes), jnp.float32)
    for pair in range(0, levels, 2):
        sides = []
        for level in (pair, pair + 1):
            rows = [
                state[pl.ds((f * levels + level) * POINTS, POINTS), :] for f in range(FIELDS)
            ]
            rows.append(outer[pl.ds(level * 8 * FIELDS, 8 * FIELDS), :])
            rows.append(blank)
            sides.append(jnp.concatenate(rows, axis=0))
        values = jnp.concatenate(sides, axis=1)
        top = values.astype(jnp.bfloat16)
        rest = (values - top.astype(jnp.float32)).astype(jnp.bfloat16)
        change = (
            jnp.dot(high, top, preferred_element_type=jnp.float32)
            + jnp.dot(high, rest, preferred_element_type=jnp.float32)
            + jnp.dot(low, top, preferred_element_type=jnp.float32)
        )
        for place, level in enumerate((pair, pair + 1)):
            for f in range(FIELDS):
                at = pl.ds((f * levels + level) * POINTS, POINTS)
                part[at, :] = (
                    state[at, :]
                    + scale
                    * change[
                        f * POINTS : (f + 1) * POINTS, place * lanes : (place + 1) * lanes
                    ]
                )
    for level in range(levels):
        speed = part[pl.ds((3 * levels + level) * POINTS, POINTS), :]
        upper = part[pl.ds((4 * levels + level + 1) * POINTS, POINTS), :] if level < levels - 1 else 0.0
        lower = part[pl.ds((4 * levels + level - 1) * POINTS, POINTS), :] if level else 0.0
        value = speed - gravity_couple * (upper - lower)
        for j in range(NODES):
            base[j, level * NODES : (level + 1) * NODES, :] = value[NODES * j : NODES * (j + 1)]
    for extra, level in ((0, 0), (1, levels - 1)):
        value = part[pl.ds((4 * levels + level) * POINTS, POINTS), :]
        at = (levels + extra) * NODES
        for j in range(NODES):
            base[j, at : at + NODES, :] = value[NODES * j : NODES * (j + 1)]


def side_corrections(received, side, fluxes, fields, pieces):
    lanes = received.shape[1]
    sign = 1.0 if side == 0 else -1.0
    result = [[] for _ in fields]
    for piece in range(pieces):
        rows = []
        for g in range(FIELDS):
            block, *places = side_lanes(g, piece, 0)
            rows.append(
                pltpu.roll(
                    received[block * ROWS : (block + 1) * ROWS, :], (lanes - places[side]) % lanes, 1
                )
            )
        for place, f in enumerate(fields):
            result[place].append(rows[f] + sign * along(fluxes, 1, f, rows))
    return result


def spread(value, edge, masks, flip):
    lanes = value.shape[1]
    return pick(
        {point: pltpu.roll(value, (edge - point) % lanes, 1) for point in RIM_POINTS}, masks, flip
    )


def add_first_side(partner, start, picked, send, base, metric):
    weight = 0.5 * lift_weight * step_size
    i = (NODES - 1) * partner_side(partner)
    for j, row in enumerate(picked):
        at = pl.ds(start * NODES + i, ROWS, stride=NODES)
        scale = weight * metric[pl.ds(NODES * j + i, 1), :]
        send[j, at, :] = base[j, at, :] + scale * row


def pack_kernel(half, from_other, neighbour_face, orientation, metric, *rest):
    sends, (send,) = rest[:NODES], rest[NODES:]
    me = lax.axis_index("vz")
    send[...] = half[...]
    rows, lanes = half.shape[1:]
    width = len(RIM_POINTS)
    face = partner_side(1)
    masks, flip = table_masks(
        neighbour_face[pl.ds(face, 1), :], orientation[pl.ds(face, 1), :], lanes
    )
    for start in chunks(rows // NODES):
        values = {
            point: from_other[pl.ds(start * width + place, ROWS, stride=width), :]
            for place, point in enumerate(RIM_POINTS)
        }
        add_first_side(1, start, pick(values, masks, flip), send, half, metric)
    for out, way in zip(sends, WAYS):
        out[...] = send[me ^ way]


def half_pack_kernel(
    base,
    from_near,
    from_down,
    from_up,
    neighbour_face,
    orientation,
    metric,
    fluxes,
    factored,
    half,
    send,
    column,
    mixed,
):
    rows, lanes = base.shape[1:]
    levels = rows // NODES - 2
    width = len(RIM_POINTS)
    weight = 0.5 * lift_weight * step_size
    send[:, 0:rows, :] = base[...]
    send[:, rows:, :] = jnp.zeros((NODES, send.shape[1] - rows, lanes), jnp.float32)
    column[...] = jnp.zeros_like(column)
    mixed[...] = jnp.zeros_like(mixed)
    for start in chunks(levels + 2):
        picked = [
            from_near[pl.ds(start * NODES + k, ROWS, stride=NODES), :] for k in range(NODES)
        ]
        add_first_side(0, start, picked, send, base, metric)
    lane = lax.broadcasted_iota(jnp.int32, (ROWS, lanes), 1)
    for side, (received, edge, j) in enumerate(
        ((from_down, 0, 0), (from_up, lanes - 1, NODES - 1))
    ):
        face = 2 + side
        masks, flip = table_masks(
            neighbour_face[face : face + 1, :], orientation[face : face + 1, :], lanes
        )
        speed, heat = side_corrections(received, side, fluxes, (3, 4), len(chunks(levels)))
        for start, value in zip(chunks(levels), heat):
            column[pl.ds(ROWS + start, ROWS), :] = value
        for start, value in zip(chunks(levels), speed):
            upper = column[pl.ds(ROWS + start + 1, ROWS), :]
            lower = column[pl.ds(ROWS + start - 1, ROWS), :]
            mixed[pl.ds(start, ROWS), :] = value - gravity_couple * (upper - lower)
        mixed[levels : levels + 1, :] = column[ROWS : ROWS + 1, :]
        mixed[levels + 1 : levels + 2, :] = column[ROWS + levels - 1 : ROWS + levels, :]
        for start in ends(levels + 2):
            picked = spread(mixed[start : start + ROWS, :], edge, masks, flip)
            for k, row in enumerate(picked):
                point = NODES * j + k
                at = pl.ds(start * NODES + k, ROWS, stride=NODES)
                scale = weight * metric[point : point + 1, :]
                send[j, at, :] += jnp.where(lane == edge, scale * row, 0.0)
    half[...] = send[:, 0:rows, :]


def finish_section_kernel(
    part,
    near,
    other_early,
    other_late,
    from_down,
    from_up,
    neighbour_face,
    orientation,
    metric,
    fluxes,
    out,
    done,
    final,
    semaphore,
):
    levels = part.shape[0] // (FIELDS * POINTS)
    lanes = part.shape[1]
    size = levels * POINTS
    weight = 0.5 * lift_weight * step_size
    scale = weight * metric[...]
    lane = lax.broadcasted_iota(jnp.int32, (ROWS, lanes), 1)
    tables = []
    edges = []
    for side, received in enumerate((from_down, from_up)):
        face = 2 + side
        tables.append(
            table_masks(
                neighbour_face[face : face + 1, :], orientation[face : face + 1, :], lanes
            )
        )
        edges.append(
            side_corrections(received, side, fluxes, LATE_FIELDS, len(chunks(levels)))
        )
    copy = pltpu.make_async_copy(final, out.at[1:3], semaphore)
    sources = ((near,), (other_early, other_late))
    for place, f in ((1, 1), (2, 2), (0, 0), (3, 4)):
        target = final.at[f - 1] if f in (1, 2) else done.at[min(f, 1)]
        target[...] = part[f * size : (f + 1) * size, :]
        for piece, start in enumerate(chunks(levels)):
            for j in range(NODES):
                for partner, source in enumerate(sources):
                    point = NODES * j + (NODES - 1) * partner_side(partner)
                    share = len(LATE_FIELDS) // len(source)
                    rows = source[place // share][
                        pl.ds(((place % share) * levels + start) * NODES + j, ROWS, stride=NODES),
                        :,
                    ]
                    at = pl.ds(start * POINTS + point, ROWS, stride=POINTS)
                    target[at, :] = (
                        part[pl.ds(f * size + start * POINTS + point, ROWS, stride=POINTS), :]
                        + weight * metric[pl.ds(point, 1), :] * rows
                    )
        for piece, start in enumerate(chunks(levels)):
            row_index = lax.broadcasted_iota(jnp.int32, (ROWS, lanes), 0)
            fresh = row_index >= (-start) % ROWS
            for side, (edge, j) in enumerate(((0, 0), (lanes - 1, NODES - 1))):
                picked = spread(edges[side][place][piece], edge, *tables[side])
                for k, row in enumerate(picked):
                    point = NODES * j + k
                    at = pl.ds(start * POINTS + point, ROWS, stride=POINTS)
                    target[at, :] += jnp.where(
                        (lane == edge) & fresh, scale[point : point + 1, :] * row, 0.0
                    )
        if f == 2:
            copy.start()
    copy.wait()


def factor_kernel(coupling, damping, far, near, inverse, ratio, second):
    levels = coupling.shape[1]
    shape = coupling.shape[2:]
    blank = jnp.zeros(shape, jnp.float32)
    far_ratio, far_second, near_ratio, near_second = (blank,) * 4
    extra = damping[...]
    for level in range(levels):
        a, b, d, e = (coupling[entry, level] for entry in range(4))
        centre = a + b + d + e + extra
        reduced = -b + a * far_ratio
        pivot = centre + a * far_second - reduced * near_ratio
        scaled = 1.0 / pivot
        upper_ratio = (-d - reduced * near_second) * scaled
        second_ratio = -e * scaled
        far[level] = a * scaled
        near[level] = reduced * scaled
        inverse[level] = scaled
        ratio[level] = upper_ratio
        second[level] = second_ratio
        far_ratio, far_second = near_ratio, near_second
        near_ratio, near_second = upper_ratio, second_ratio


def solve_kernel(far, near, inverse, ratio, second, *rest):
    ways = NODES
    received, sends, (source, heat, speed) = rest[:ways], rest[ways : 2 * ways], rest[2 * ways :]
    levels = far.shape[0]
    here = levels // ways
    me = lax.axis_index("vz")
    for values, way in zip(received, WAYS):
        block = me ^ way
        source[pl.ds(block * here, here)] = values[0:here]
        heat[block] = values[here : here + 2]
    for block in range(ways - 1):
        last = block * here + here - 1
        source[last] = source[last] - gravity_couple * heat[block + 1, 0]
        source[last + 1] = source[last + 1] + gravity_couple * heat[block, 1]
    blank = jnp.zeros(far.shape[1:], jnp.float32)
    before_two, before_one = blank, blank
    for level in range(levels):
        value = source[level] * inverse[level]
        value = value + far[level] * before_two
        value = value - near[level] * before_one
        source[level] = value
        before_two, before_one = before_one, value
    speed[0] = blank
    speed[levels + 1] = blank
    next_one, next_two = blank, blank
    for level in range(levels - 1, -1, -1):
        value = source[level] - second[level] * next_two
        value = value - ratio[level] * next_one
        speed[level + 1] = value
        next_two, next_one = next_one, value
    for send, way in zip(sends, WAYS):
        send[...] = speed[pl.ds((me ^ way) * here, here + 2)]


def update_kernel(*refs):
    ways = NODES
    received, (done, earlier, out, speed, final, semaphores) = refs[:ways], refs[ways:]
    levels = done.shape[1] // POINTS
    me = lax.axis_index("vz")
    for values, way in zip(received, WAYS):
        speed[me ^ way] = values[...]
    lanes = done.shape[2]
    half = levels // 2
    low = lax.broadcasted_iota(jnp.int32, (ROWS, lanes), 0) < NODES
    copies = []
    for pair in range(half):
        lower = [speed[j, pair * ROWS : (pair + 1) * ROWS, :] for j in range(NODES)]
        upper = [speed[j, (pair + 1) * ROWS : (pair + 2) * ROWS, :] for j in range(NODES)]
        jump = [above - below for above, below in zip(upper, lower)]
        value = [jnp.where(low, above, below) for above, below in zip(upper, lower)]
        for h in range(2):
            a, b = 2 * h, 2 * h + 1
            for odd in range(2):
                at = pl.ds((2 * pair + odd) * POINTS + ROWS * h, ROWS)
                jumps = side_by_side(jump[a], jump[b], odd, low)
                final[0, at, :] = done[0, at, :] - density_couple * jumps
                final[1, at, :] = side_by_side(value[a], value[b], 1 - odd, low)
                final[2, at, :] = done[1, at, :] - theta_couple * jumps
        if pair in (half // 2 - 1, half - 1):
            first = 0 if pair < half - 1 else half // 2
            rows = pl.ds(first * 2 * POINTS, (pair + 1 - first) * 2 * POINTS)
            for place, f in enumerate((0, 3, 4)):
                copies.append(
                    pltpu.make_async_copy(
                        final.at[place, rows, :], out.at[f, rows, :], semaphores.at[len(copies)]
                    )
                )
                copies[-1].start()
    for copy in copies:
        copy.wait()


def side_by_side(first, second, upper, low):
    if upper:
        return jnp.where(low, pltpu.roll(first, NODES, 0), second)
    return jnp.where(low, first, pltpu.roll(second, NODES, 0))


VMEM = pl.BlockSpec(memory_space=pltpu.VMEM)
HBM = pl.BlockSpec(memory_space=pltpu.HBM)
ANY = pl.BlockSpec(memory_space=pl.ANY)


def call(kernel, outs, in_specs, scratch=(), cost=0, name=None):
    kinds = [x if hasattr(x, "dtype") else pltpu.VMEM(x, jnp.float32) for x in outs]
    return pl.pallas_call(
        kernel,
        out_shape=kinds,
        in_specs=in_specs,
        out_specs=[VMEM] * len(outs),
        scratch_shapes=list(scratch),
        compiler_params=pltpu.CompilerParams(vmem_limit_bytes=24 * 1024 * 1024),
        cost_estimate=pl.CostEstimate(flops=cost, bytes_accessed=cost, transcendentals=0),
        name=name,
    )


def per_device(
    prognostic, metric, first_flux, second_flux, neighbour_face, orientation, coupling, damping
):
    fields, levels = prognostic.shape[:2]
    lanes = prognostic.shape[-1]
    whole = (fields, levels * POINTS, lanes)
    metric = metric.reshape(POINTS, lanes)
    neighbour_face = neighbour_face.reshape(4, lanes)
    orientation = orientation.reshape(4, lanes)
    coupling = coupling.reshape(4, coupling.shape[1], NODES, lanes)
    damping = damping.reshape(NODES, lanes)
    tables, _ = operator_tables(lanes)

    def shifts(axis):
        size = lax.axis_size(axis)
        up = [(i, (i + 1) % size) for i in range(size)]
        return up, [(j, i) for i, j in up]

    def exchange(arrays):
        size = lax.axis_size("vz")
        return [
            lax.ppermute(x, "vz", [(i, i ^ way) for i in range(size)]) if way else x
            for x, way in zip(arrays, WAYS)
        ]

    count = lax.axis_size("hy")
    near = [(i, i ^ 1) for i in range(count)]
    other = [(i, (i + 1 if i % 2 else i - 1) % count) for i in range(count)]
    second_up, second_down = shifts("hx")
    width = len(RIM_POINTS)
    message = (-(-((levels + 2) * width + 2) // ROWS) * ROWS, lanes)
    sides = (-(-fields * len(chunks(levels)) // 4) * ROWS, lanes)
    padded = levels + 2 * ROWS
    table = pltpu.VMEM((4, lanes), jnp.int32)
    inputs = (
        prognostic.reshape(whole),
        neighbour_face,
        orientation,
        metric,
        jnp.asarray(tables),
        first_flux,
        second_flux,
    )
    (
        to_other,
        state,
        neighbour_face,
        orientation,
        metric,
        tables,
        fluxes,
    ) = call(
        rim_kernel,
        [
            message,
            whole,
            table,
            table,
            (POINTS, lanes),
            tables.shape,
            (-(-2 * fields * fields // ROWS) * ROWS, lanes),
        ],
        [HBM] * len(inputs),
        [
            pltpu.VMEM((width, padded, lanes), jnp.float32),
            pltpu.VMEM((width, padded, lanes), jnp.float32),
            pltpu.SMEM((fields, fields), jnp.float32),
            pltpu.SMEM((fields, fields), jnp.float32),
            pltpu.SemaphoreType.DMA((6 + -(-levels // ROWS),)),
        ],
        cost=1000,
        name="rim",
    )(*(pltpu.with_memory_space_constraint(x, pltpu.HBM) for x in inputs))
    state = state.reshape(fields * levels * POINTS, lanes)
    from_other = lax.ppermute(to_other, "hy", other)
    from_near = lax.ppermute(state, "hy", near)
    (to_sides,) = call(edge_kernel, [sides], [VMEM], cost=1000, name="edge")(state)
    from_down = lax.ppermute(to_sides, "hx", second_up)
    from_up = from_down
    if lax.axis_size("hx") > 2:
        from_up = lax.ppermute(to_sides, "hx", second_down)

    column = (coupling.shape[1], NODES, lanes)
    factors = call(factor_kernel, [column] * 5, [VMEM] * 2, cost=4000000, name="factor")(
        coupling, damping
    )
    block = ((levels + 2) * NODES, lanes)
    part, base = call(
        element_kernel,
        [state.shape, (NODES,) + block],
        [VMEM] * 6,
        [
            pltpu.VMEM((levels * 8 * fields, lanes), jnp.float32),
            pltpu.VMEM((fields * POINTS, lanes), jnp.bfloat16),
            pltpu.VMEM((fields * POINTS, lanes), jnp.bfloat16),
        ],
        cost=4000000,
        name="element",
    )(
        state,
        neighbour_face,
        orientation,
        metric,
        fluxes,
        tables,
    )
    late = levels * NODES * len(LATE_FIELDS)
    near_source, near_late = call(
        near_kernel,
        [block, (late, lanes)],
        [VMEM] * 4,
        [pltpu.VMEM((NODES, padded, lanes), jnp.float32)],
        cost=1000,
        name="near",
    )(from_near, neighbour_face, orientation, fluxes)
    count = -(-(levels + 2) // ROWS) * ROWS
    (half,) = call(
        half_pack_kernel,
        [(NODES,) + block],
        [VMEM] * 8 + [ANY],
        [
            pltpu.VMEM((NODES, count * NODES, lanes), jnp.float32),
            pltpu.VMEM((padded, lanes), jnp.float32),
            pltpu.VMEM((count, lanes), jnp.float32),
        ],
        cost=1000,
        name="half_pack",
    )(
        base,
        near_source,
        from_down,
        from_up,
        neighbour_face,
        orientation,
        metric,
        fluxes,
        factors[0],
    )
    sends = call(
        pack_kernel,
        [block] * NODES,
        [VMEM] * 5,
        [pltpu.VMEM((NODES,) + block, jnp.float32)],
        cost=1000,
        name="pack",
    )(half, from_other, neighbour_face, orientation, metric)
    received = exchange(sends)

    other_face = call(
        functools.partial(face_kernel, 1),
        [(late // 2, lanes)] * 2,
        [VMEM] * 3 + [ANY],
        cost=1000,
        name="other_face",
    )(state, from_other, fluxes, sends[-1])
    other_face = [lax.ppermute(x, "hy", other) for x in other_face]

    cube = (levels + 2, NODES, lanes)
    speeds = call(
        solve_kernel,
        [cube] * NODES,
        [VMEM] * (5 + NODES),
        [
            pltpu.VMEM(column, jnp.float32),
            pltpu.VMEM((NODES, 2, NODES, lanes), jnp.float32),
            pltpu.VMEM((column[0] + 2,) + column[1:], jnp.float32),
        ],
        cost=1000,
        name="solve",
    )(*factors, *[x.reshape(cube) for x in received])
    returned = exchange([x.reshape(block) for x in speeds])
    size = levels * POINTS
    limits = pltpu.CompilerParams(vmem_limit_bytes=24 * 1024 * 1024)
    earlier, done = pl.pallas_call(
        finish_section_kernel,
        out_shape=[
            jax.ShapeDtypeStruct(whole, jnp.float32),
            pltpu.VMEM((2, size, lanes), jnp.float32),
        ],
        in_specs=[VMEM] * 10,
        out_specs=[HBM, VMEM],
        scratch_shapes=[
            pltpu.VMEM((2, size, lanes), jnp.float32),
            pltpu.SemaphoreType.DMA,
        ],
        compiler_params=limits,
        cost_estimate=pl.CostEstimate(flops=4000000, bytes_accessed=4000000, transcendentals=0),
        name="finish",
    )(
        part, near_late, *other_face, from_down, from_up, neighbour_face, orientation, metric, fluxes
    )
    updated = pl.pallas_call(
        update_kernel,
        out_shape=jax.ShapeDtypeStruct(whole, jnp.float32),
        in_specs=[VMEM] * (1 + NODES) + [HBM],
        out_specs=HBM,
        input_output_aliases={1 + NODES: 0},
        scratch_shapes=[
            pltpu.VMEM((NODES,) + block, jnp.float32),
            pltpu.VMEM((3, size, lanes), jnp.float32),
            pltpu.SemaphoreType.DMA((6,)),
        ],
        compiler_params=limits,
        name="update",
    )(*returned, done, earlier)
    return updated.reshape(prognostic.shape)


def solution(mesh):
    placed = (
        P(None, "vz", None, None, "hy", "hx"),
        P(None, None, "hy", "hx"),
        P(),
        P(),
        P(None, "hy", "hx"),
        P(None, "hy", "hx"),
        P(None, None, "vz", None, "hy", "hx"),
        P("vz", None, "hy", "hx"),
    )
    return jax.shard_map(
        per_device,
        mesh=mesh,
        in_specs=placed,
        out_specs=P(None, "vz", None, None, "hy", "hx"),
        check_vma=False,
    )
```

```python
import functools

import jax
import jax.numpy as jnp
import numpy as np
from jax import lax
from jax.experimental import pallas as pl
from jax.experimental.pallas import tpu as pltpu
from jax.sharding import PartitionSpec as P

step_size = 0.05
lift_weight = 6.0
gravity_couple = 0.5
density_couple = 0.3
theta_couple = 0.4

NODES = 4
POINTS = NODES * NODES
FIELDS = 5
FACE_POINTS = ((0, 4, 8, 12), (3, 7, 11, 15), (0, 1, 2, 3), (12, 13, 14, 15))
RIM_POINTS = tuple(sorted(set(sum(FACE_POINTS, ()))))
ROWS = 8
LATE_FIELDS = (0, 1, 2, 4)
WAYS = (3, 1, 2, 0)
BACK_WAYS = (3, 2, 1, 0)


def derivative_table():
    points = np.array([-1.0, -1.0 / np.sqrt(5.0), 1.0 / np.sqrt(5.0), 1.0])
    number = points.shape[0]
    barycentric = np.ones(number)
    for source in range(number):
        for another in range(number):
            if another != source:
                barycentric[source] = barycentric[source] / (points[source] - points[another])
    matrix = np.zeros((number, number))
    for target in range(number):
        for source in range(number):
            if target != source:
                matrix[target, source] = (
                    barycentric[source] / barycentric[target] / (points[target] - points[source])
                )
        matrix[target, target] = -np.sum(matrix[target])
    return matrix


def operator_tables(lanes):
    weight = 0.5 * lift_weight
    table = derivative_table()
    table[0, 0] += weight
    table[-1, -1] -= weight
    eye = np.eye(NODES)
    along_first = np.kron(eye, table)
    along_second = np.kron(table, eye)
    ends = np.zeros(NODES)
    ends[0] = ends[-1] = 1.0
    faces = np.diag(np.kron(np.ones(NODES), ends) + np.kron(ends, np.ones(NODES)))
    first = np.zeros((POINTS, lanes))
    second = np.zeros((POINTS, lanes))
    same = np.zeros((FIELDS, POINTS, lanes))
    owner = np.full((lanes,), -1)
    for g in range(FIELDS):
        own = slice(POINTS * g, POINTS * (g + 1))
        first[:, own] = -along_first
        second[:, own] = -along_second
        same[g, :, own] = -weight * faces
        owner[own] = g
        for k in range(NODES):
            south = FIELDS * POINTS + 2 * NODES * g + k
            north = south + NODES
            second[FACE_POINTS[2][k], south] = weight
            second[FACE_POINTS[3][k], north] = -weight
            same[g, FACE_POINTS[2][k], south] = weight
            same[g, FACE_POINTS[3][k], north] = weight
            owner[south] = owner[north] = g
    tables = np.concatenate([first, second, same.reshape(FIELDS * POINTS, lanes)])
    return tables.astype(np.float32), owner


def chunks(total):
    return [min(start, total - ROWS) for start in range(0, total, ROWS)]


def partner_side(partner):
    odd = lax.rem(lax.axis_index("hy"), 2)
    return odd if partner else 1 - odd


def side_sign(side):
    return (2 * side - 1).astype(jnp.float32)


def ends(total):
    return list(range(0, total, ROWS))


def pick(values, masks, flip):
    chosen = []
    for k in range(NODES):
        row = values[FACE_POINTS[0][k]]
        for option in range(1, 4):
            row = jnp.where(masks[option], values[FACE_POINTS[option][k]], row)
        chosen.append(row)
    return [jnp.where(flip, chosen[NODES - 1 - k], chosen[k]) for k in range(NODES)]


def table_masks(face_row, flip_row, lanes):
    face = jnp.broadcast_to(face_row, (ROWS, lanes))
    flip = jnp.broadcast_to(flip_row, (ROWS, lanes))
    return [face == option for option in range(4)], flip == 1


def flux_row(f, g, matrix):
    return (matrix * FIELDS + f) * FIELDS + g


def along(fluxes, matrix, f, rows):
    total = None
    for g in range(FIELDS):
        at = flux_row(f, g, matrix)
        term = fluxes[at : at + 1, :] * rows[g]
        total = term if total is None else total + term
    return total


def side_rows(f, piece):
    number = 3 * f + piece
    return number // 4, 32 * (number % 4)


def rim_kernel(
    state_hbm,
    face_hbm,
    way_hbm,
    metric_hbm,
    tables_hbm,
    flux_hbm,
    second_hbm,
    to_other,
    state,
    neighbour_face,
    orientation,
    metric,
    tables,
    fluxes,
    column,
    speed,
    flux,
    second_flux,
    semaphores,
):
    levels = state.shape[1] // POINTS
    face = partner_side(1)
    sign = side_sign(face)
    lanes = state.shape[2]
    width = len(RIM_POINTS)
    groups = [(start, min(start + ROWS, levels)) for start in range(0, levels, ROWS)]
    small = [
        pltpu.make_async_copy(source, target, semaphores.at[place])
        for place, (source, target) in enumerate(
            (
                (flux_hbm, flux),
                (face_hbm, neighbour_face),
                (way_hbm, orientation),
                (metric_hbm, metric),
                (tables_hbm, tables),
                (second_hbm, second_flux),
            )
        )
    ]
    large = []
    for place, (low, high) in enumerate(groups):
        rows = pl.ds(low * POINTS, (high - low) * POINTS)
        large.append(
            pltpu.make_async_copy(
                state_hbm.at[:, rows, :], state.at[:, rows, :], semaphores.at[len(small) + place]
            )
        )
    for copy in small[:1] + large + small[1:]:
        copy.start()
    column[...] = jnp.zeros_like(column)
    small[0].wait()
    arrived = 0
    for piece, start in enumerate(chunks(levels)):
        while arrived < len(groups) and groups[arrived][0] < start + ROWS:
            large[arrived].wait()
            arrived += 1
        for place, point in enumerate(RIM_POINTS):
            rows = [
                state[g, pl.ds(start * POINTS + point, ROWS, stride=POINTS), :]
                for g in range(FIELDS)
            ]
            for f, out in ((3, speed), (4, column)):
                normal = (sign * flux[f, 0]) * rows[0]
                for g in range(1, FIELDS):
                    normal = normal + (sign * flux[f, g]) * rows[g]
                out[place, pl.ds(ROWS + start, ROWS), :] = rows[f] + normal
    small[1].wait()
    small[2].wait()
    end = (levels + 2) * width
    for place in range(width):
        for start in chunks(levels):
            upper = column[place, pl.ds(ROWS + start + 1, ROWS), :]
            lower = column[place, pl.ds(ROWS + start - 1, ROWS), :]
            to_other[pl.ds(start * width + place, ROWS, stride=width), :] = speed[
                place, pl.ds(ROWS + start, ROWS), :
            ] - gravity_couple * (upper - lower)
        for extra, level in ((0, 0), (1, levels - 1)):
            at = (levels + extra) * width + place
            to_other[at : at + 1, :] = column[place, ROWS + level : ROWS + level + 1, :]
    to_other[end : end + 1, :] = neighbour_face[pl.ds(face, 1), :].astype(jnp.float32)
    to_other[end + 1 : end + 2, :] = orientation[pl.ds(face, 1), :].astype(jnp.float32)
    left = to_other.shape[0] - end - 2
    to_other[end + 2 :, :] = jnp.zeros((left, lanes), jnp.float32)
    small[3].wait()
    small[4].wait()
    small[5].wait()
    for place, source in enumerate((flux, second_flux)):
        for f in range(FIELDS):
            for g in range(FIELDS):
                at = flux_row(f, g, place)
                fluxes[at : at + 1, :] = jnp.full((1, lanes), source[f, g])


def edge_kernel(state, to_sides):
    lanes = state.shape[1]
    levels = state.shape[0] // (FIELDS * POINTS)
    lane = lax.broadcasted_iota(jnp.int32, (ROWS, lanes), 1)
    packed = [jnp.zeros((ROWS, lanes), jnp.float32) for _ in range(to_sides.shape[0] // ROWS)]
    for f in range(FIELDS):
        for piece, start in enumerate(chunks(levels)):
            block, at = side_rows(f, piece)
            for place, point in enumerate(RIM_POINTS):
                row = state[pl.ds((f * levels + start) * POINTS + point, ROWS, stride=POINTS), :]
                first = at + 2 * place
                packed[block] = jnp.where(
                    lane // 2 == first // 2, pltpu.roll(row, first + 1, 1), packed[block]
                )
    for block, value in enumerate(packed):
        to_sides[block * ROWS : (block + 1) * ROWS, :] = value


def near_kernel(
    state, neighbour_face, orientation, fluxes, base, metric, half, late, column, source
):
    lanes = state.shape[1]
    levels = state.shape[0] // (FIELDS * POINTS)
    face = partner_side(0)
    sign = -side_sign(face)
    masks, flip = table_masks(
        neighbour_face[pl.ds(face, 1), :], orientation[pl.ds(face, 1), :], lanes
    )
    column[...] = jnp.zeros_like(column)
    speeds = []
    for start in chunks(levels):
        picked = []
        for g in range(FIELDS):
            values = {
                point: state[pl.ds((g * levels + start) * POINTS + point, ROWS, stride=POINTS), :]
                for point in RIM_POINTS
            }
            picked.append(pick(values, masks, flip))
        for k in range(NODES):
            rows = [picked[g][k] for g in range(FIELDS)]
            changed = [rows[f] + sign * along(fluxes, 0, f, rows) for f in range(FIELDS)]
            for place, f in enumerate(LATE_FIELDS):
                at = (place * levels + start) * NODES + k
                late[pl.ds(at, ROWS, stride=NODES), :] = changed[f]
            column[k, pl.ds(ROWS + start, ROWS), :] = changed[4]
            speeds.append(changed[3])
    for piece, start in enumerate(chunks(levels)):
        for k in range(NODES):
            upper = column[k, pl.ds(ROWS + start + 1, ROWS), :]
            lower = column[k, pl.ds(ROWS + start - 1, ROWS), :]
            source[pl.ds(start * NODES + k, ROWS, stride=NODES), :] = speeds[
                NODES * piece + k
            ] - gravity_couple * (upper - lower)
    for extra, level in ((0, 0), (1, levels - 1)):
        for k in range(NODES):
            at = (levels + extra) * NODES + k
            source[at : at + 1, :] = column[k, ROWS + level : ROWS + level + 1, :]
    half[...] = base[...]
    for start in chunks(levels + 2):
        picked = [source[pl.ds(start * NODES + k, ROWS, stride=NODES), :] for k in range(NODES)]
        add_first_side(0, start, picked, half, base, metric)


def face_kernel(partner, state, received, fluxes, *rest):
    lanes = state.shape[1]
    levels = state.shape[0] // (FIELDS * POINTS)
    at = (levels + 2) * len(RIM_POINTS)
    outs = rest[-2:]
    share = len(LATE_FIELDS) // len(outs)
    sign = side_sign(partner_side(partner))
    masks, flip = table_masks(
        received[at : at + 1, :].astype(jnp.int32),
        received[at + 1 : at + 2, :].astype(jnp.int32),
        lanes,
    )
    for start in chunks(levels):
        picked = []
        for g in range(FIELDS):
            values = {
                point: state[pl.ds((g * levels + start) * POINTS + point, ROWS, stride=POINTS), :]
                for point in RIM_POINTS
            }
            picked.append(pick(values, masks, flip))
        for place, f in enumerate(LATE_FIELDS):
            for k in range(NODES):
                normal = along(fluxes, 0, f, [picked[g][k] for g in range(FIELDS)])
                at = ((place % share) * levels + start) * NODES + k
                outs[place // share][pl.ds(at, ROWS, stride=NODES), :] = (
                    picked[f][k] + sign * normal
                )


def element_kernel(
    state,
    neighbour_face,
    orientation,
    metric,
    fluxes,
    tables,
    part,
    base,
    outer,
    operator_high,
    operator_low,
):
    levels = state.shape[0] // (FIELDS * POINTS)
    lanes = state.shape[1]
    lane = lax.broadcasted_iota(jnp.int32, (ROWS, lanes), 1)
    sides = []
    for side, (face, edge) in enumerate(((2, 0), (3, lanes - 1))):
        shift = 1 if side == 0 else lanes - 1
        row = jnp.broadcast_to(neighbour_face[face : face + 1, :], (ROWS, lanes))
        way = jnp.broadcast_to(orientation[face : face + 1, :], (ROWS, lanes))
        masks, flip = table_masks(
            pltpu.roll(row, lanes - shift, 1), pltpu.roll(way, lanes - shift, 1), lanes
        )
        sides.append((shift, edge, masks, flip))
    for f in range(FIELDS):
        for start in chunks(levels):
            q = f * levels + start
            values = {
                point: state[pl.ds(q * POINTS + point, ROWS, stride=POINTS), :]
                for point in RIM_POINTS
            }
            for side, (shift, edge, masks, flip) in enumerate(sides):
                for k, row in enumerate(pick(values, masks, flip)):
                    at = start * 8 * FIELDS + 8 * f + NODES * side + k
                    outer[pl.ds(at, ROWS, stride=8 * FIELDS), :] = jnp.where(
                        lane == edge, 0.0, pltpu.roll(row, shift, 1)
                    )
    index = lax.broadcasted_iota(jnp.int32, (1, lanes), 1)
    own_columns = FIELDS * POINTS
    owner = jnp.where(index < own_columns, index // POINTS, (index - own_columns) // 8)
    for f in range(FIELDS):
        first_row = jnp.zeros((1, lanes), jnp.float32)
        second_row = first_row
        for g in range(FIELDS):
            first, second = (flux_row(f, g, matrix) for matrix in range(2))
            first_row = jnp.where(owner == g, fluxes[first : first + 1, :], first_row)
            second_row = jnp.where(owner == g, fluxes[second : second + 1, :], second_row)
        block = (
            first_row * tables[0:POINTS, :]
            + second_row * tables[POINTS : 2 * POINTS, :]
            + tables[(2 + f) * POINTS : (3 + f) * POINTS, :]
        )
        high = block.astype(jnp.bfloat16)
        operator_high[f * POINTS : (f + 1) * POINTS, :] = high
        operator_low[f * POINTS : (f + 1) * POINTS, :] = (
            block - high.astype(jnp.float32)
        ).astype(jnp.bfloat16)
    high = operator_high[...]
    low = operator_low[...]
    scale = step_size * metric[...]
    blank = jnp.zeros((lanes - own_columns - 8 * FIELDS, lanes), jnp.float32)
    for pair in range(0, levels, 2):
        sides = []
        for level in (pair, pair + 1):
            rows = [
                state[pl.ds((f * levels + level) * POINTS, POINTS), :] for f in range(FIELDS)
            ]
            rows.append(outer[pl.ds(level * 8 * FIELDS, 8 * FIELDS), :])
            rows.append(blank)
            sides.append(jnp.concatenate(rows, axis=0))
        values = jnp.concatenate(sides, axis=1)
        top = values.astype(jnp.bfloat16)
        rest = (values - top.astype(jnp.float32)).astype(jnp.bfloat16)
        change = (
            jnp.dot(high, top, preferred_element_type=jnp.float32)
            + jnp.dot(high, rest, preferred_element_type=jnp.float32)
            + jnp.dot(low, top, preferred_element_type=jnp.float32)
        )
        for place, level in enumerate((pair, pair + 1)):
            for f in range(FIELDS):
                at = pl.ds((f * levels + level) * POINTS, POINTS)
                part[at, :] = (
                    state[at, :]
                    + scale
                    * change[
                        f * POINTS : (f + 1) * POINTS, place * lanes : (place + 1) * lanes
                    ]
                )
    for level in range(levels):
        speed = part[pl.ds((3 * levels + level) * POINTS, POINTS), :]
        upper = part[pl.ds((4 * levels + level + 1) * POINTS, POINTS), :] if level < levels - 1 else 0.0
        lower = part[pl.ds((4 * levels + level - 1) * POINTS, POINTS), :] if level else 0.0
        value = speed - gravity_couple * (upper - lower)
        for j in range(NODES):
            base[j, level * NODES : (level + 1) * NODES, :] = value[NODES * j : NODES * (j + 1)]
    for extra, level in ((0, 0), (1, levels - 1)):
        value = part[pl.ds((4 * levels + level) * POINTS, POINTS), :]
        at = (levels + extra) * NODES
        for j in range(NODES):
            base[j, at : at + NODES, :] = value[NODES * j : NODES * (j + 1)]


def side_corrections(received, side, fluxes, fields, pieces):
    lanes = received.shape[1]
    sign = 1.0 if side == 0 else -1.0
    result = [[] for _ in fields]
    for piece in range(pieces):
        rows = []
        for g in range(FIELDS):
            block, at = side_rows(g, piece)
            rows.append(
                pltpu.roll(
                    received[block * ROWS : (block + 1) * ROWS, :], (lanes - at - side) % lanes, 1
                )
            )
        for place, f in enumerate(fields):
            result[place].append(rows[f] + sign * along(fluxes, 1, f, rows))
    return result


def spread(value, edge, masks, flip):
    lanes = value.shape[1]
    values = {
        point: pltpu.roll(value, (edge - 2 * place) % lanes, 1)
        for place, point in enumerate(RIM_POINTS)
    }
    return pick(values, masks, flip)


def add_first_side(partner, start, picked, send, base, metric):
    weight = 0.5 * lift_weight * step_size
    i = (NODES - 1) * partner_side(partner)
    for j, row in enumerate(picked):
        at = pl.ds(start * NODES + i, ROWS, stride=NODES)
        scale = weight * metric[pl.ds(NODES * j + i, 1), :]
        send[j, at, :] = base[j, at, :] + scale * row


def pack_kernel(half, from_other, neighbour_face, orientation, metric, *rest):
    sends, (send,) = rest[:NODES], rest[NODES:]
    me = lax.axis_index("vz")
    send[...] = half[...]
    rows, lanes = half.shape[1:]
    width = len(RIM_POINTS)
    face = partner_side(1)
    masks, flip = table_masks(
        neighbour_face[pl.ds(face, 1), :], orientation[pl.ds(face, 1), :], lanes
    )
    for start in chunks(rows // NODES):
        values = {
            point: from_other[pl.ds(start * width + place, ROWS, stride=width), :]
            for place, point in enumerate(RIM_POINTS)
        }
        add_first_side(1, start, pick(values, masks, flip), send, half, metric)
    for out, way in zip(sends, WAYS):
        out[...] = send[me ^ way]


def half_pack_kernel(
    base,
    from_down,
    from_up,
    neighbour_face,
    orientation,
    metric,
    fluxes,
    factored,
    half,
    send,
    column,
    mixed,
):
    rows, lanes = base.shape[1:]
    levels = rows // NODES - 2
    width = len(RIM_POINTS)
    weight = 0.5 * lift_weight * step_size
    send[:, 0:rows, :] = base[...]
    send[:, rows:, :] = jnp.zeros((NODES, send.shape[1] - rows, lanes), jnp.float32)
    column[...] = jnp.zeros_like(column)
    mixed[...] = jnp.zeros_like(mixed)
    lane = lax.broadcasted_iota(jnp.int32, (ROWS, lanes), 1)
    for side, (received, edge, j) in enumerate(
        ((from_down, 0, 0), (from_up, lanes - 1, NODES - 1))
    ):
        face = 2 + side
        masks, flip = table_masks(
            neighbour_face[face : face + 1, :], orientation[face : face + 1, :], lanes
        )
        speed, heat = side_corrections(received, side, fluxes, (3, 4), len(chunks(levels)))
        for start, value in zip(chunks(levels), heat):
            column[pl.ds(ROWS + start, ROWS), :] = value
        for start, value in zip(chunks(levels), speed):
            upper = column[pl.ds(ROWS + start + 1, ROWS), :]
            lower = column[pl.ds(ROWS + start - 1, ROWS), :]
            mixed[pl.ds(start, ROWS), :] = value - gravity_couple * (upper - lower)
        mixed[levels : levels + 1, :] = column[ROWS : ROWS + 1, :]
        mixed[levels + 1 : levels + 2, :] = column[ROWS + levels - 1 : ROWS + levels, :]
        for start in ends(levels + 2):
            picked = spread(mixed[start : start + ROWS, :], edge, masks, flip)
            for k, row in enumerate(picked):
                point = NODES * j + k
                at = pl.ds(start * NODES + k, ROWS, stride=NODES)
                scale = weight * metric[point : point + 1, :]
                send[j, at, :] += jnp.where(lane == edge, scale * row, 0.0)
    half[...] = send[:, 0:rows, :]


def finish_section_kernel(
    part,
    near,
    other_early,
    other_late,
    from_down,
    from_up,
    neighbour_face,
    orientation,
    metric,
    fluxes,
    out,
    done,
    final,
    semaphore,
):
    levels = part.shape[0] // (FIELDS * POINTS)
    lanes = part.shape[1]
    size = levels * POINTS
    weight = 0.5 * lift_weight * step_size
    scale = weight * metric[...]
    lane = lax.broadcasted_iota(jnp.int32, (ROWS, lanes), 1)
    tables = []
    edges = []
    for side, received in enumerate((from_down, from_up)):
        face = 2 + side
        tables.append(
            table_masks(
                neighbour_face[face : face + 1, :], orientation[face : face + 1, :], lanes
            )
        )
        edges.append(
            side_corrections(received, side, fluxes, LATE_FIELDS, len(chunks(levels)))
        )
    copy = pltpu.make_async_copy(final, out.at[1:3], semaphore)
    sources = ((near,), (other_early, other_late))
    for place, f in ((1, 1), (2, 2), (0, 0), (3, 4)):
        target = final.at[f - 1] if f in (1, 2) else done.at[min(f, 1)]
        target[...] = part[f * size : (f + 1) * size, :]
        for piece, start in enumerate(chunks(levels)):
            for j in range(NODES):
                for partner, source in enumerate(sources):
                    point = NODES * j + (NODES - 1) * partner_side(partner)
                    share = len(LATE_FIELDS) // len(source)
                    rows = source[place // share][
                        pl.ds(((place % share) * levels + start) * NODES + j, ROWS, stride=NODES),
                        :,
                    ]
                    at = pl.ds(start * POINTS + point, ROWS, stride=POINTS)
                    target[at, :] = (
                        part[pl.ds(f * size + start * POINTS + point, ROWS, stride=POINTS), :]
                        + weight * metric[pl.ds(point, 1), :] * rows
                    )
        for piece, start in enumerate(chunks(levels)):
            row_index = lax.broadcasted_iota(jnp.int32, (ROWS, lanes), 0)
            fresh = row_index >= (-start) % ROWS
            for side, (edge, j) in enumerate(((0, 0), (lanes - 1, NODES - 1))):
                picked = spread(edges[side][place][piece], edge, *tables[side])
                for k, row in enumerate(picked):
                    point = NODES * j + k
                    at = pl.ds(start * POINTS + point, ROWS, stride=POINTS)
                    target[at, :] += jnp.where(
                        (lane == edge) & fresh, scale[point : point + 1, :] * row, 0.0
                    )
        if f == 2:
            copy.start()
    copy.wait()


def factor_kernel(coupling, damping, far, near, inverse, ratio, second):
    levels = coupling.shape[1]
    shape = coupling.shape[2:]
    blank = jnp.zeros(shape, jnp.float32)
    far_ratio, far_second, near_ratio, near_second = (blank,) * 4
    extra = damping[...]
    for level in range(levels):
        a, b, d, e = (coupling[entry, level] for entry in range(4))
        centre = a + b + d + e + extra
        reduced = -b + a * far_ratio
        pivot = centre + a * far_second - reduced * near_ratio
        scaled = 1.0 / pivot
        upper_ratio = (-d - reduced * near_second) * scaled
        second_ratio = -e * scaled
        far[level] = a * scaled
        near[level] = reduced * scaled
        inverse[level] = scaled
        ratio[level] = upper_ratio
        second[level] = second_ratio
        far_ratio, far_second = near_ratio, near_second
        near_ratio, near_second = upper_ratio, second_ratio


def solve_kernel(far, near, inverse, ratio, second, *rest):
    ways = NODES
    received, sends, (source, heat, speed) = rest[:ways], rest[ways : 2 * ways], rest[2 * ways :]
    levels = far.shape[0]
    here = levels // ways
    me = lax.axis_index("vz")
    for values, way in zip(received, WAYS):
        block = me ^ way
        source[pl.ds(block * here, here)] = values[0:here]
        heat[block] = values[here : here + 2]
    for block in range(ways - 1):
        last = block * here + here - 1
        source[last] = source[last] - gravity_couple * heat[block + 1, 0]
        source[last + 1] = source[last + 1] + gravity_couple * heat[block, 1]
    blank = jnp.zeros(far.shape[1:], jnp.float32)
    before_two, before_one = blank, blank
    for level in range(levels):
        value = source[level] * inverse[level]
        value = value + far[level] * before_two
        value = value - near[level] * before_one
        source[level] = value
        before_two, before_one = before_one, value
    speed[0] = blank
    speed[levels + 1] = blank
    next_one, next_two = blank, blank
    for level in range(levels - 1, -1, -1):
        value = source[level] - second[level] * next_two
        value = value - ratio[level] * next_one
        speed[level + 1] = value
        next_two, next_one = next_one, value
    for send, way in zip(sends, BACK_WAYS):
        send[...] = speed[pl.ds((me ^ way) * here, here + 2)]


def update_kernel(*refs):
    ways = NODES
    received, (done, earlier, out, speed, final, semaphores) = refs[:ways], refs[ways:]
    levels = done.shape[1] // POINTS
    me = lax.axis_index("vz")
    for values, way in zip(received, BACK_WAYS):
        speed[me ^ way] = values[...]
    lanes = done.shape[2]
    half = levels // 2
    low = lax.broadcasted_iota(jnp.int32, (ROWS, lanes), 0) < NODES
    copies = []
    for pair in range(half):
        lower = [speed[j, pair * ROWS : (pair + 1) * ROWS, :] for j in range(NODES)]
        upper = [speed[j, (pair + 1) * ROWS : (pair + 2) * ROWS, :] for j in range(NODES)]
        jump = [above - below for above, below in zip(upper, lower)]
        value = [jnp.where(low, above, below) for above, below in zip(upper, lower)]
        for h in range(2):
            a, b = 2 * h, 2 * h + 1
            for odd in range(2):
                at = pl.ds((2 * pair + odd) * POINTS + ROWS * h, ROWS)
                jumps = side_by_side(jump[a], jump[b], odd, low)
                final[0, at, :] = done[0, at, :] - density_couple * jumps
                final[1, at, :] = side_by_side(value[a], value[b], 1 - odd, low)
                final[2, at, :] = done[1, at, :] - theta_couple * jumps
        if pair in (half // 2 - 1, half - 1):
            first = 0 if pair < half - 1 else half // 2
            rows = pl.ds(first * 2 * POINTS, (pair + 1 - first) * 2 * POINTS)
            for place, f in enumerate((0, 3, 4)):
                copies.append(
                    pltpu.make_async_copy(
                        final.at[place, rows, :], out.at[f, rows, :], semaphores.at[len(copies)]
                    )
                )
                copies[-1].start()
    for copy in copies:
        copy.wait()


def side_by_side(first, second, upper, low):
    if upper:
        return jnp.where(low, pltpu.roll(first, NODES, 0), second)
    return jnp.where(low, first, pltpu.roll(second, NODES, 0))


VMEM = pl.BlockSpec(memory_space=pltpu.VMEM)
HBM = pl.BlockSpec(memory_space=pltpu.HBM)
ANY = pl.BlockSpec(memory_space=pl.ANY)


def call(kernel, outs, in_specs, scratch=(), cost=0, name=None):
    kinds = [x if hasattr(x, "dtype") else pltpu.VMEM(x, jnp.float32) for x in outs]
    return pl.pallas_call(
        kernel,
        out_shape=kinds,
        in_specs=in_specs,
        out_specs=[VMEM] * len(outs),
        scratch_shapes=list(scratch),
        compiler_params=pltpu.CompilerParams(vmem_limit_bytes=24 * 1024 * 1024),
        cost_estimate=pl.CostEstimate(flops=cost, bytes_accessed=cost, transcendentals=0),
        name=name,
    )


def per_device(
    prognostic, metric, first_flux, second_flux, neighbour_face, orientation, coupling, damping
):
    fields, levels = prognostic.shape[:2]
    lanes = prognostic.shape[-1]
    whole = (fields, levels * POINTS, lanes)
    metric = metric.reshape(POINTS, lanes)
    neighbour_face = neighbour_face.reshape(4, lanes)
    orientation = orientation.reshape(4, lanes)
    coupling = coupling.reshape(4, coupling.shape[1], NODES, lanes)
    damping = damping.reshape(NODES, lanes)
    tables, _ = operator_tables(lanes)

    def shifts(axis):
        size = lax.axis_size(axis)
        up = [(i, (i + 1) % size) for i in range(size)]
        return up, [(j, i) for i, j in up]

    def exchange(arrays, ways):
        size = lax.axis_size("vz")
        return [
            lax.ppermute(x, "vz", [(i, i ^ way) for i in range(size)]) if way else x
            for x, way in zip(arrays, ways)
        ]

    count = lax.axis_size("hy")
    near = [(i, i ^ 1) for i in range(count)]
    other = [(i, (i + 1 if i % 2 else i - 1) % count) for i in range(count)]
    second_up, second_down = shifts("hx")
    width = len(RIM_POINTS)
    message = (-(-((levels + 2) * width + 2) // ROWS) * ROWS, lanes)
    sides = (-(-fields * len(chunks(levels)) // 4) * ROWS, lanes)
    padded = levels + 2 * ROWS
    table = pltpu.VMEM((4, lanes), jnp.int32)
    inputs = (
        prognostic.reshape(whole),
        neighbour_face,
        orientation,
        metric,
        jnp.asarray(tables),
        first_flux,
        second_flux,
    )
    (
        to_other,
        state,
        neighbour_face,
        orientation,
        metric,
        tables,
        fluxes,
    ) = call(
        rim_kernel,
        [
            message,
            whole,
            table,
            table,
            (POINTS, lanes),
            tables.shape,
            (-(-2 * fields * fields // ROWS) * ROWS, lanes),
        ],
        [HBM] * len(inputs),
        [
            pltpu.VMEM((width, padded, lanes), jnp.float32),
            pltpu.VMEM((width, padded, lanes), jnp.float32),
            pltpu.SMEM((fields, fields), jnp.float32),
            pltpu.SMEM((fields, fields), jnp.float32),
            pltpu.SemaphoreType.DMA((6 + -(-levels // ROWS),)),
        ],
        cost=1000,
        name="rim",
    )(*(pltpu.with_memory_space_constraint(x, pltpu.HBM) for x in inputs))
    state = state.reshape(fields * levels * POINTS, lanes)
    from_other = lax.ppermute(to_other, "hy", other)
    from_near = lax.ppermute(state, "hy", near)
    (to_sides,) = call(edge_kernel, [sides], [VMEM], cost=1000, name="edge")(state)
    from_down = lax.ppermute(to_sides, "hx", second_up)
    from_up = from_down
    if lax.axis_size("hx") > 2:
        from_up = lax.ppermute(to_sides, "hx", second_down)

    column = (coupling.shape[1], NODES, lanes)
    factors = call(factor_kernel, [column] * 5, [VMEM] * 2, cost=4000000, name="factor")(
        coupling, damping
    )
    block = ((levels + 2) * NODES, lanes)
    part, base = call(
        element_kernel,
        [state.shape, (NODES,) + block],
        [VMEM] * 6,
        [
            pltpu.VMEM((levels * 8 * fields, lanes), jnp.float32),
            pltpu.VMEM((fields * POINTS, lanes), jnp.bfloat16),
            pltpu.VMEM((fields * POINTS, lanes), jnp.bfloat16),
        ],
        cost=4000000,
        name="element",
    )(
        state,
        neighbour_face,
        orientation,
        metric,
        fluxes,
        tables,
    )
    late = levels * NODES * len(LATE_FIELDS)
    base, near_late = call(
        near_kernel,
        [(NODES,) + block, (late, lanes)],
        [VMEM] * 6,
        [pltpu.VMEM((NODES, padded, lanes), jnp.float32), pltpu.VMEM(block, jnp.float32)],
        cost=1000,
        name="near",
    )(from_near, neighbour_face, orientation, fluxes, base, metric)
    count = -(-(levels + 2) // ROWS) * ROWS
    (half,) = call(
        half_pack_kernel,
        [(NODES,) + block],
        [VMEM] * 7 + [ANY],
        [
            pltpu.VMEM((NODES, count * NODES, lanes), jnp.float32),
            pltpu.VMEM((padded, lanes), jnp.float32),
            pltpu.VMEM((count, lanes), jnp.float32),
        ],
        cost=1000,
        name="half_pack",
    )(
        base,
        from_down,
        from_up,
        neighbour_face,
        orientation,
        metric,
        fluxes,
        factors[0],
    )
    sends = call(
        pack_kernel,
        [block] * NODES,
        [VMEM] * 5,
        [pltpu.VMEM((NODES,) + block, jnp.float32)],
        cost=1000,
        name="pack",
    )(half, from_other, neighbour_face, orientation, metric)
    received = exchange(sends, WAYS)

    other_face = call(
        functools.partial(face_kernel, 1),
        [(late // 2, lanes)] * 2,
        [VMEM] * 3 + [ANY],
        cost=1000,
        name="other_face",
    )(state, from_other, fluxes, sends[-1])
    other_face = [lax.ppermute(x, "hy", other) for x in other_face]

    cube = (levels + 2, NODES, lanes)
    speeds = call(
        solve_kernel,
        [cube] * NODES,
        [VMEM] * (5 + NODES),
        [
            pltpu.VMEM(column, jnp.float32),
            pltpu.VMEM((NODES, 2, NODES, lanes), jnp.float32),
            pltpu.VMEM((column[0] + 2,) + column[1:], jnp.float32),
        ],
        cost=1000,
        name="solve",
    )(*factors, *[x.reshape(cube) for x in received])
    returned = exchange([x.reshape(block) for x in speeds], BACK_WAYS)
    size = levels * POINTS
    limits = pltpu.CompilerParams(vmem_limit_bytes=24 * 1024 * 1024)
    earlier, done = pl.pallas_call(
        finish_section_kernel,
        out_shape=[
            jax.ShapeDtypeStruct(whole, jnp.float32),
            pltpu.VMEM((2, size, lanes), jnp.float32),
        ],
        in_specs=[VMEM] * 10,
        out_specs=[HBM, VMEM],
        scratch_shapes=[
            pltpu.VMEM((2, size, lanes), jnp.float32),
            pltpu.SemaphoreType.DMA,
        ],
        compiler_params=limits,
        cost_estimate=pl.CostEstimate(flops=4000000, bytes_accessed=4000000, transcendentals=0),
        name="finish",
    )(
        part, near_late, *other_face, from_down, from_up, neighbour_face, orientation, metric, fluxes
    )
    updated = pl.pallas_call(
        update_kernel,
        out_shape=jax.ShapeDtypeStruct(whole, jnp.float32),
        in_specs=[VMEM] * (1 + NODES) + [HBM],
        out_specs=HBM,
        input_output_aliases={1 + NODES: 0},
        scratch_shapes=[
            pltpu.VMEM((NODES,) + block, jnp.float32),
            pltpu.VMEM((3, size, lanes), jnp.float32),
            pltpu.SemaphoreType.DMA((6,)),
        ],
        compiler_params=limits,
        name="update",
    )(*returned, done, earlier)
    return updated.reshape(prognostic.shape)


def solution(mesh):
    placed = (
        P(None, "vz", None, None, "hy", "hx"),
        P(None, None, "hy", "hx"),
        P(),
        P(),
        P(None, "hy", "hx"),
        P(None, "hy", "hx"),
        P(None, None, "vz", None, "hy", "hx"),
        P("vz", None, "hy", "hx"),
    )
    return jax.shard_map(
        per_device,
        mesh=mesh,
        in_specs=placed,
        out_specs=P(None, "vz", None, None, "hy", "hx"),
        check_vma=False,
    )
```

```python
import functools

import jax
import jax.numpy as jnp
import numpy as np
from jax import lax
from jax.experimental import pallas as pl
from jax.experimental.pallas import tpu as pltpu
from jax.sharding import PartitionSpec as P

step_size = 0.05
lift_weight = 6.0
gravity_couple = 0.5
density_couple = 0.3
theta_couple = 0.4

NODES = 4
POINTS = NODES * NODES
FIELDS = 5
FACE_POINTS = ((0, 4, 8, 12), (3, 7, 11, 15), (0, 1, 2, 3), (12, 13, 14, 15))
RIM_POINTS = tuple(sorted(set(sum(FACE_POINTS, ()))))
ROWS = 8
LATE_FIELDS = (0, 1, 2, 4)
WAYS = (2, 3, 1, 0)
BACK_WAYS = (3, 2, 1, 0)


def derivative_table():
    points = np.array([-1.0, -1.0 / np.sqrt(5.0), 1.0 / np.sqrt(5.0), 1.0])
    number = points.shape[0]
    barycentric = np.ones(number)
    for source in range(number):
        for another in range(number):
            if another != source:
                barycentric[source] = barycentric[source] / (points[source] - points[another])
    matrix = np.zeros((number, number))
    for target in range(number):
        for source in range(number):
            if target != source:
                matrix[target, source] = (
                    barycentric[source] / barycentric[target] / (points[target] - points[source])
                )
        matrix[target, target] = -np.sum(matrix[target])
    return matrix


def operator_tables(lanes):
    weight = 0.5 * lift_weight
    table = derivative_table()
    table[0, 0] += weight
    table[-1, -1] -= weight
    eye = np.eye(NODES)
    along_first = np.kron(eye, table)
    along_second = np.kron(table, eye)
    ends = np.zeros(NODES)
    ends[0] = ends[-1] = 1.0
    faces = np.diag(np.kron(np.ones(NODES), ends) + np.kron(ends, np.ones(NODES)))
    first = np.zeros((POINTS, lanes))
    second = np.zeros((POINTS, lanes))
    same = np.zeros((FIELDS, POINTS, lanes))
    owner = np.full((lanes,), -1)
    for g in range(FIELDS):
        own = slice(POINTS * g, POINTS * (g + 1))
        first[:, own] = -along_first
        second[:, own] = -along_second
        same[g, :, own] = -weight * faces
        owner[own] = g
        for k in range(NODES):
            south = FIELDS * POINTS + 2 * NODES * g + k
            north = south + NODES
            second[FACE_POINTS[2][k], south] = weight
            second[FACE_POINTS[3][k], north] = -weight
            same[g, FACE_POINTS[2][k], south] = weight
            same[g, FACE_POINTS[3][k], north] = weight
            owner[south] = owner[north] = g
    tables = np.concatenate([first, second, same.reshape(FIELDS * POINTS, lanes)])
    return tables.astype(np.float32), owner


def chunks(total):
    return [min(start, total - ROWS) for start in range(0, total, ROWS)]


def partner_side(partner):
    odd = lax.rem(lax.axis_index("hy"), 2)
    return odd if partner else 1 - odd


def side_sign(side):
    return (2 * side - 1).astype(jnp.float32)


def ends(total):
    return list(range(0, total, ROWS))


def pick(values, masks, flip):
    chosen = []
    for k in range(NODES):
        row = values[FACE_POINTS[0][k]]
        for option in range(1, 4):
            row = jnp.where(masks[option], values[FACE_POINTS[option][k]], row)
        chosen.append(row)
    return [jnp.where(flip, chosen[NODES - 1 - k], chosen[k]) for k in range(NODES)]


def table_masks(face_row, flip_row, lanes):
    face = jnp.broadcast_to(face_row, (ROWS, lanes))
    flip = jnp.broadcast_to(flip_row, (ROWS, lanes))
    return [face == option for option in range(4)], flip == 1


def flux_row(f, g, matrix):
    return (matrix * FIELDS + f) * FIELDS + g


def along(fluxes, matrix, f, rows):
    total = None
    for g in range(FIELDS):
        at = flux_row(f, g, matrix)
        term = fluxes[at : at + 1, :] * rows[g]
        total = term if total is None else total + term
    return total


def side_rows(f, piece):
    number = 3 * f + piece
    return number // 4, 32 * (number % 4)


def rim_kernel(
    state_hbm,
    face_hbm,
    way_hbm,
    metric_hbm,
    tables_hbm,
    flux_hbm,
    second_hbm,
    to_other,
    state,
    neighbour_face,
    orientation,
    metric,
    tables,
    fluxes,
    column,
    speed,
    flux,
    second_flux,
    semaphores,
):
    levels = state.shape[1] // POINTS
    face = partner_side(1)
    sign = side_sign(face)
    lanes = state.shape[2]
    width = len(RIM_POINTS)
    groups = [(start, min(start + ROWS, levels)) for start in range(0, levels, ROWS)]
    small = [
        pltpu.make_async_copy(source, target, semaphores.at[place])
        for place, (source, target) in enumerate(
            (
                (flux_hbm, flux),
                (face_hbm, neighbour_face),
                (way_hbm, orientation),
                (metric_hbm, metric),
                (tables_hbm, tables),
                (second_hbm, second_flux),
            )
        )
    ]
    large = []
    for place, (low, high) in enumerate(groups):
        rows = pl.ds(low * POINTS, (high - low) * POINTS)
        large.append(
            pltpu.make_async_copy(
                state_hbm.at[:, rows, :], state.at[:, rows, :], semaphores.at[len(small) + place]
            )
        )
    for copy in small[:1] + large + small[1:]:
        copy.start()
    column[...] = jnp.zeros_like(column)
    small[0].wait()
    arrived = 0
    for piece, start in enumerate(chunks(levels)):
        while arrived < len(groups) and groups[arrived][0] < start + ROWS:
            large[arrived].wait()
            arrived += 1
        for place, point in enumerate(RIM_POINTS):
            rows = [
                state[g, pl.ds(start * POINTS + point, ROWS, stride=POINTS), :]
                for g in range(FIELDS)
            ]
            for f, out in ((3, speed), (4, column)):
                normal = (sign * flux[f, 0]) * rows[0]
                for g in range(1, FIELDS):
                    normal = normal + (sign * flux[f, g]) * rows[g]
                out[place, pl.ds(ROWS + start, ROWS), :] = rows[f] + normal
    small[1].wait()
    small[2].wait()
    end = (levels + 2) * width
    for place in range(width):
        for start in chunks(levels):
            upper = column[place, pl.ds(ROWS + start + 1, ROWS), :]
            lower = column[place, pl.ds(ROWS + start - 1, ROWS), :]
            to_other[pl.ds(start * width + place, ROWS, stride=width), :] = speed[
                place, pl.ds(ROWS + start, ROWS), :
            ] - gravity_couple * (upper - lower)
        for extra, level in ((0, 0), (1, levels - 1)):
            at = (levels + extra) * width + place
            to_other[at : at + 1, :] = column[place, ROWS + level : ROWS + level + 1, :]
    to_other[end : end + 1, :] = neighbour_face[pl.ds(face, 1), :].astype(jnp.float32)
    to_other[end + 1 : end + 2, :] = orientation[pl.ds(face, 1), :].astype(jnp.float32)
    left = to_other.shape[0] - end - 2
    to_other[end + 2 :, :] = jnp.zeros((left, lanes), jnp.float32)
    small[3].wait()
    small[4].wait()
    small[5].wait()
    for place, source in enumerate((flux, second_flux)):
        for f in range(FIELDS):
            for g in range(FIELDS):
                at = flux_row(f, g, place)
                fluxes[at : at + 1, :] = jnp.full((1, lanes), source[f, g])


def edge_kernel(state, to_sides):
    lanes = state.shape[1]
    levels = state.shape[0] // (FIELDS * POINTS)
    lane = lax.broadcasted_iota(jnp.int32, (ROWS, lanes), 1)
    packed = [jnp.zeros((ROWS, lanes), jnp.float32) for _ in range(to_sides.shape[0] // ROWS)]
    for f in range(FIELDS):
        for piece, start in enumerate(chunks(levels)):
            block, at = side_rows(f, piece)
            for place, point in enumerate(RIM_POINTS):
                row = state[pl.ds((f * levels + start) * POINTS + point, ROWS, stride=POINTS), :]
                first = at + 2 * place
                packed[block] = jnp.where(
                    lane // 2 == first // 2, pltpu.roll(row, first + 1, 1), packed[block]
                )
    for block, value in enumerate(packed):
        to_sides[block * ROWS : (block + 1) * ROWS, :] = value


def near_kernel(
    state, neighbour_face, orientation, fluxes, base, metric, half, late, column, source
):
    lanes = state.shape[1]
    levels = state.shape[0] // (FIELDS * POINTS)
    face = partner_side(0)
    sign = -side_sign(face)
    masks, flip = table_masks(
        neighbour_face[pl.ds(face, 1), :], orientation[pl.ds(face, 1), :], lanes
    )
    column[...] = jnp.zeros_like(column)
    speeds = []
    for start in chunks(levels):
        picked = []
        for g in range(FIELDS):
            values = {
                point: state[pl.ds((g * levels + start) * POINTS + point, ROWS, stride=POINTS), :]
                for point in RIM_POINTS
            }
            picked.append(pick(values, masks, flip))
        for k in range(NODES):
            rows = [picked[g][k] for g in range(FIELDS)]
            changed = [rows[f] + sign * along(fluxes, 0, f, rows) for f in range(FIELDS)]
            for place, f in enumerate(LATE_FIELDS):
                at = (place * levels + start) * NODES + k
                late[pl.ds(at, ROWS, stride=NODES), :] = changed[f]
            column[k, pl.ds(ROWS + start, ROWS), :] = changed[4]
            speeds.append(changed[3])
    for piece, start in enumerate(chunks(levels)):
        for k in range(NODES):
            upper = column[k, pl.ds(ROWS + start + 1, ROWS), :]
            lower = column[k, pl.ds(ROWS + start - 1, ROWS), :]
            source[pl.ds(start * NODES + k, ROWS, stride=NODES), :] = speeds[
                NODES * piece + k
            ] - gravity_couple * (upper - lower)
    for extra, level in ((0, 0), (1, levels - 1)):
        for k in range(NODES):
            at = (levels + extra) * NODES + k
            source[at : at + 1, :] = column[k, ROWS + level : ROWS + level + 1, :]
    half[...] = base[...]
    for start in chunks(levels + 2):
        picked = [source[pl.ds(start * NODES + k, ROWS, stride=NODES), :] for k in range(NODES)]
        add_first_side(0, start, picked, half, base, metric)


def face_kernel(partner, state, received, fluxes, *rest):
    lanes = state.shape[1]
    levels = state.shape[0] // (FIELDS * POINTS)
    at = (levels + 2) * len(RIM_POINTS)
    outs = rest[-2:]
    share = len(LATE_FIELDS) // len(outs)
    sign = side_sign(partner_side(partner))
    masks, flip = table_masks(
        received[at : at + 1, :].astype(jnp.int32),
        received[at + 1 : at + 2, :].astype(jnp.int32),
        lanes,
    )
    for start in chunks(levels):
        picked = []
        for g in range(FIELDS):
            values = {
                point: state[pl.ds((g * levels + start) * POINTS + point, ROWS, stride=POINTS), :]
                for point in RIM_POINTS
            }
            picked.append(pick(values, masks, flip))
        for place, f in enumerate(LATE_FIELDS):
            for k in range(NODES):
                normal = along(fluxes, 0, f, [picked[g][k] for g in range(FIELDS)])
                at = ((place % share) * levels + start) * NODES + k
                outs[place // share][pl.ds(at, ROWS, stride=NODES), :] = (
                    picked[f][k] + sign * normal
                )


def element_kernel(
    state,
    neighbour_face,
    orientation,
    metric,
    fluxes,
    tables,
    part,
    base,
    outer,
    operator_high,
    operator_low,
):
    levels = state.shape[0] // (FIELDS * POINTS)
    lanes = state.shape[1]
    lane = lax.broadcasted_iota(jnp.int32, (ROWS, lanes), 1)
    sides = []
    for side, (face, edge) in enumerate(((2, 0), (3, lanes - 1))):
        shift = 1 if side == 0 else lanes - 1
        row = jnp.broadcast_to(neighbour_face[face : face + 1, :], (ROWS, lanes))
        way = jnp.broadcast_to(orientation[face : face + 1, :], (ROWS, lanes))
        masks, flip = table_masks(
            pltpu.roll(row, lanes - shift, 1), pltpu.roll(way, lanes - shift, 1), lanes
        )
        sides.append((shift, edge, masks, flip))
    for f in range(FIELDS):
        for start in chunks(levels):
            q = f * levels + start
            values = {
                point: state[pl.ds(q * POINTS + point, ROWS, stride=POINTS), :]
                for point in RIM_POINTS
            }
            for side, (shift, edge, masks, flip) in enumerate(sides):
                for k, row in enumerate(pick(values, masks, flip)):
                    at = start * 8 * FIELDS + 8 * f + NODES * side + k
                    outer[pl.ds(at, ROWS, stride=8 * FIELDS), :] = jnp.where(
                        lane == edge, 0.0, pltpu.roll(row, shift, 1)
                    )
    index = lax.broadcasted_iota(jnp.int32, (1, lanes), 1)
    own_columns = FIELDS * POINTS
    owner = jnp.where(index < own_columns, index // POINTS, (index - own_columns) // 8)
    for f in range(FIELDS):
        first_row = jnp.zeros((1, lanes), jnp.float32)
        second_row = first_row
        for g in range(FIELDS):
            first, second = (flux_row(f, g, matrix) for matrix in range(2))
            first_row = jnp.where(owner == g, fluxes[first : first + 1, :], first_row)
            second_row = jnp.where(owner == g, fluxes[second : second + 1, :], second_row)
        block = (
            first_row * tables[0:POINTS, :]
            + second_row * tables[POINTS : 2 * POINTS, :]
            + tables[(2 + f) * POINTS : (3 + f) * POINTS, :]
        )
        high = block.astype(jnp.bfloat16)
        operator_high[f * POINTS : (f + 1) * POINTS, :] = high
        operator_low[f * POINTS : (f + 1) * POINTS, :] = (
            block - high.astype(jnp.float32)
        ).astype(jnp.bfloat16)
    high = operator_high[...]
    low = operator_low[...]
    scale = step_size * metric[...]
    blank = jnp.zeros((lanes - own_columns - 8 * FIELDS, lanes), jnp.float32)
    for pair in range(0, levels, 2):
        sides = []
        for level in (pair, pair + 1):
            rows = [
                state[pl.ds((f * levels + level) * POINTS, POINTS), :] for f in range(FIELDS)
            ]
            rows.append(outer[pl.ds(level * 8 * FIELDS, 8 * FIELDS), :])
            rows.append(blank)
            sides.append(jnp.concatenate(rows, axis=0))
        values = jnp.concatenate(sides, axis=1)
        top = values.astype(jnp.bfloat16)
        rest = (values - top.astype(jnp.float32)).astype(jnp.bfloat16)
        change = (
            jnp.dot(high, top, preferred_element_type=jnp.float32)
            + jnp.dot(high, rest, preferred_element_type=jnp.float32)
            + jnp.dot(low, top, preferred_element_type=jnp.float32)
        )
        for place, level in enumerate((pair, pair + 1)):
            for f in range(FIELDS):
                at = pl.ds((f * levels + level) * POINTS, POINTS)
                part[at, :] = (
                    state[at, :]
                    + scale
                    * change[
                        f * POINTS : (f + 1) * POINTS, place * lanes : (place + 1) * lanes
                    ]
                )
    for level in range(levels):
        speed = part[pl.ds((3 * levels + level) * POINTS, POINTS), :]
        upper = part[pl.ds((4 * levels + level + 1) * POINTS, POINTS), :] if level < levels - 1 else 0.0
        lower = part[pl.ds((4 * levels + level - 1) * POINTS, POINTS), :] if level else 0.0
        value = speed - gravity_couple * (upper - lower)
        for j in range(NODES):
            base[j, level * NODES : (level + 1) * NODES, :] = value[NODES * j : NODES * (j + 1)]
    for extra, level in ((0, 0), (1, levels - 1)):
        value = part[pl.ds((4 * levels + level) * POINTS, POINTS), :]
        at = (levels + extra) * NODES
        for j in range(NODES):
            base[j, at : at + NODES, :] = value[NODES * j : NODES * (j + 1)]


def side_corrections(received, side, fluxes, fields, pieces):
    lanes = received.shape[1]
    sign = 1.0 if side == 0 else -1.0
    result = [[] for _ in fields]
    for piece in range(pieces):
        rows = []
        for g in range(FIELDS):
            block, at = side_rows(g, piece)
            rows.append(
                pltpu.roll(
                    received[block * ROWS : (block + 1) * ROWS, :], (lanes - at - side) % lanes, 1
                )
            )
        for place, f in enumerate(fields):
            result[place].append(rows[f] + sign * along(fluxes, 1, f, rows))
    return result


def spread(value, edge, masks, flip):
    lanes = value.shape[1]
    values = {
        point: pltpu.roll(value, (edge - 2 * place) % lanes, 1)
        for place, point in enumerate(RIM_POINTS)
    }
    return pick(values, masks, flip)


def add_first_side(partner, start, picked, send, base, metric):
    weight = 0.5 * lift_weight * step_size
    i = (NODES - 1) * partner_side(partner)
    for j, row in enumerate(picked):
        at = pl.ds(start * NODES + i, ROWS, stride=NODES)
        scale = weight * metric[pl.ds(NODES * j + i, 1), :]
        send[j, at, :] = base[j, at, :] + scale * row


def pack_kernel(half, from_other, neighbour_face, orientation, metric, *rest):
    sends, (send,) = rest[:NODES], rest[NODES:]
    me = lax.axis_index("vz")
    send[...] = half[...]
    rows, lanes = half.shape[1:]
    width = len(RIM_POINTS)
    face = partner_side(1)
    masks, flip = table_masks(
        neighbour_face[pl.ds(face, 1), :], orientation[pl.ds(face, 1), :], lanes
    )
    for start in chunks(rows // NODES):
        values = {
            point: from_other[pl.ds(start * width + place, ROWS, stride=width), :]
            for place, point in enumerate(RIM_POINTS)
        }
        add_first_side(1, start, pick(values, masks, flip), send, half, metric)
    for out, way in zip(sends, WAYS):
        out[...] = send[me ^ way]


def half_pack_kernel(
    base,
    from_down,
    from_up,
    neighbour_face,
    orientation,
    metric,
    fluxes,
    factored,
    half,
    send,
    column,
    mixed,
):
    rows, lanes = base.shape[1:]
    levels = rows // NODES - 2
    width = len(RIM_POINTS)
    weight = 0.5 * lift_weight * step_size
    send[:, 0:rows, :] = base[...]
    send[:, rows:, :] = jnp.zeros((NODES, send.shape[1] - rows, lanes), jnp.float32)
    column[...] = jnp.zeros_like(column)
    mixed[...] = jnp.zeros_like(mixed)
    lane = lax.broadcasted_iota(jnp.int32, (ROWS, lanes), 1)
    for side, (received, edge, j) in enumerate(
        ((from_down, 0, 0), (from_up, lanes - 1, NODES - 1))
    ):
        face = 2 + side
        masks, flip = table_masks(
            neighbour_face[face : face + 1, :], orientation[face : face + 1, :], lanes
        )
        speed, heat = side_corrections(received, side, fluxes, (3, 4), len(chunks(levels)))
        for start, value in zip(chunks(levels), heat):
            column[pl.ds(ROWS + start, ROWS), :] = value
        for start, value in zip(chunks(levels), speed):
            upper = column[pl.ds(ROWS + start + 1, ROWS), :]
            lower = column[pl.ds(ROWS + start - 1, ROWS), :]
            mixed[pl.ds(start, ROWS), :] = value - gravity_couple * (upper - lower)
        mixed[levels : levels + 1, :] = column[ROWS : ROWS + 1, :]
        mixed[levels + 1 : levels + 2, :] = column[ROWS + levels - 1 : ROWS + levels, :]
        for start in ends(levels + 2):
            picked = spread(mixed[start : start + ROWS, :], edge, masks, flip)
            for k, row in enumerate(picked):
                point = NODES * j + k
                at = pl.ds(start * NODES + k, ROWS, stride=NODES)
                scale = weight * metric[point : point + 1, :]
                send[j, at, :] += jnp.where(lane == edge, scale * row, 0.0)
    half[...] = send[:, 0:rows, :]


def finish_section_kernel(
    part,
    near,
    other_early,
    other_late,
    from_down,
    from_up,
    neighbour_face,
    orientation,
    metric,
    fluxes,
    out,
    done,
    final,
    semaphore,
):
    levels = part.shape[0] // (FIELDS * POINTS)
    lanes = part.shape[1]
    size = levels * POINTS
    weight = 0.5 * lift_weight * step_size
    scale = weight * metric[...]
    lane = lax.broadcasted_iota(jnp.int32, (ROWS, lanes), 1)
    tables = []
    edges = []
    for side, received in enumerate((from_down, from_up)):
        face = 2 + side
        tables.append(
            table_masks(
                neighbour_face[face : face + 1, :], orientation[face : face + 1, :], lanes
            )
        )
        edges.append(
            side_corrections(received, side, fluxes, LATE_FIELDS, len(chunks(levels)))
        )
    copy = pltpu.make_async_copy(final, out.at[1:3], semaphore)
    sources = ((near,), (other_early, other_late))
    for place, f in ((1, 1), (2, 2), (0, 0), (3, 4)):
        target = final.at[f - 1] if f in (1, 2) else done.at[min(f, 1)]
        target[...] = part[f * size : (f + 1) * size, :]
        for piece, start in enumerate(chunks(levels)):
            for j in range(NODES):
                for partner, source in enumerate(sources):
                    point = NODES * j + (NODES - 1) * partner_side(partner)
                    share = len(LATE_FIELDS) // len(source)
                    rows = source[place // share][
                        pl.ds(((place % share) * levels + start) * NODES + j, ROWS, stride=NODES),
                        :,
                    ]
                    at = pl.ds(start * POINTS + point, ROWS, stride=POINTS)
                    target[at, :] = (
                        part[pl.ds(f * size + start * POINTS + point, ROWS, stride=POINTS), :]
                        + weight * metric[pl.ds(point, 1), :] * rows
                    )
        for piece, start in enumerate(chunks(levels)):
            row_index = lax.broadcasted_iota(jnp.int32, (ROWS, lanes), 0)
            fresh = row_index >= (-start) % ROWS
            for side, (edge, j) in enumerate(((0, 0), (lanes - 1, NODES - 1))):
                picked = spread(edges[side][place][piece], edge, *tables[side])
                for k, row in enumerate(picked):
                    point = NODES * j + k
                    at = pl.ds(start * POINTS + point, ROWS, stride=POINTS)
                    target[at, :] += jnp.where(
                        (lane == edge) & fresh, scale[point : point + 1, :] * row, 0.0
                    )
        if f == 2:
            copy.start()
    copy.wait()


def factor_kernel(coupling, damping, far, near, inverse, ratio, second):
    levels = coupling.shape[1]
    shape = coupling.shape[2:]
    blank = jnp.zeros(shape, jnp.float32)
    far_ratio, far_second, near_ratio, near_second = (blank,) * 4
    extra = damping[...]
    for level in range(levels):
        a, b, d, e = (coupling[entry, level] for entry in range(4))
        centre = a + b + d + e + extra
        reduced = -b + a * far_ratio
        pivot = centre + a * far_second - reduced * near_ratio
        scaled = 1.0 / pivot
        upper_ratio = (-d - reduced * near_second) * scaled
        second_ratio = -e * scaled
        far[level] = a * scaled
        near[level] = reduced * scaled
        inverse[level] = scaled
        ratio[level] = upper_ratio
        second[level] = second_ratio
        far_ratio, far_second = near_ratio, near_second
        near_ratio, near_second = upper_ratio, second_ratio


def solve_kernel(far, near, inverse, ratio, second, *rest):
    ways = NODES
    received, sends, (source, heat, speed) = rest[:ways], rest[ways : 2 * ways], rest[2 * ways :]
    levels = far.shape[0]
    here = levels // ways
    me = lax.axis_index("vz")
    for values, way in zip(received, WAYS):
        block = me ^ way
        source[pl.ds(block * here, here)] = values[0:here]
        heat[block] = values[here : here + 2]
    for block in range(ways - 1):
        last = block * here + here - 1
        source[last] = source[last] - gravity_couple * heat[block + 1, 0]
        source[last + 1] = source[last + 1] + gravity_couple * heat[block, 1]
    blank = jnp.zeros(far.shape[1:], jnp.float32)
    before_two, before_one = blank, blank
    for level in range(levels):
        value = source[level] * inverse[level]
        value = value + far[level] * before_two
        value = value - near[level] * before_one
        source[level] = value
        before_two, before_one = before_one, value
    speed[0] = blank
    speed[levels + 1] = blank
    next_one, next_two = blank, blank
    for level in range(levels - 1, -1, -1):
        value = source[level] - second[level] * next_two
        value = value - ratio[level] * next_one
        speed[level + 1] = value
        next_two, next_one = next_one, value
    for send, way in zip(sends, BACK_WAYS):
        send[...] = speed[pl.ds((me ^ way) * here, here + 2)]


def update_kernel(*refs):
    ways = NODES
    received, (done, earlier, out, speed, final, semaphores) = refs[:ways], refs[ways:]
    levels = done.shape[1] // POINTS
    me = lax.axis_index("vz")
    for values, way in zip(received, BACK_WAYS):
        speed[me ^ way] = values[...]
    lanes = done.shape[2]
    half = levels // 2
    low = lax.broadcasted_iota(jnp.int32, (ROWS, lanes), 0) < NODES
    copies = []
    for pair in range(half):
        lower = [speed[j, pair * ROWS : (pair + 1) * ROWS, :] for j in range(NODES)]
        upper = [speed[j, (pair + 1) * ROWS : (pair + 2) * ROWS, :] for j in range(NODES)]
        jump = [above - below for above, below in zip(upper, lower)]
        value = [jnp.where(low, above, below) for above, below in zip(upper, lower)]
        for h in range(2):
            a, b = 2 * h, 2 * h + 1
            for odd in range(2):
                at = pl.ds((2 * pair + odd) * POINTS + ROWS * h, ROWS)
                jumps = side_by_side(jump[a], jump[b], odd, low)
                final[0, at, :] = done[0, at, :] - density_couple * jumps
                final[1, at, :] = side_by_side(value[a], value[b], 1 - odd, low)
                final[2, at, :] = done[1, at, :] - theta_couple * jumps
        if pair in (half // 2 - 1, half - 1):
            first = 0 if pair < half - 1 else half // 2
            rows = pl.ds(first * 2 * POINTS, (pair + 1 - first) * 2 * POINTS)
            for place, f in enumerate((0, 3, 4)):
                copies.append(
                    pltpu.make_async_copy(
                        final.at[place, rows, :], out.at[f, rows, :], semaphores.at[len(copies)]
                    )
                )
                copies[-1].start()
    for copy in copies:
        copy.wait()


def side_by_side(first, second, upper, low):
    if upper:
        return jnp.where(low, pltpu.roll(first, NODES, 0), second)
    return jnp.where(low, first, pltpu.roll(second, NODES, 0))


VMEM = pl.BlockSpec(memory_space=pltpu.VMEM)
HBM = pl.BlockSpec(memory_space=pltpu.HBM)
ANY = pl.BlockSpec(memory_space=pl.ANY)


def call(kernel, outs, in_specs, scratch=(), cost=0, name=None):
    kinds = [x if hasattr(x, "dtype") else pltpu.VMEM(x, jnp.float32) for x in outs]
    return pl.pallas_call(
        kernel,
        out_shape=kinds,
        in_specs=in_specs,
        out_specs=[VMEM] * len(outs),
        scratch_shapes=list(scratch),
        compiler_params=pltpu.CompilerParams(vmem_limit_bytes=24 * 1024 * 1024),
        cost_estimate=pl.CostEstimate(flops=cost, bytes_accessed=cost, transcendentals=0),
        name=name,
    )


def per_device(
    prognostic, metric, first_flux, second_flux, neighbour_face, orientation, coupling, damping
):
    fields, levels = prognostic.shape[:2]
    lanes = prognostic.shape[-1]
    whole = (fields, levels * POINTS, lanes)
    metric = metric.reshape(POINTS, lanes)
    neighbour_face = neighbour_face.reshape(4, lanes)
    orientation = orientation.reshape(4, lanes)
    coupling = coupling.reshape(4, coupling.shape[1], NODES, lanes)
    damping = damping.reshape(NODES, lanes)
    tables, _ = operator_tables(lanes)

    def shifts(axis):
        size = lax.axis_size(axis)
        up = [(i, (i + 1) % size) for i in range(size)]
        return up, [(j, i) for i, j in up]

    def exchange(arrays, ways):
        size = lax.axis_size("vz")
        return [
            lax.ppermute(x, "vz", [(i, i ^ way) for i in range(size)]) if way else x
            for x, way in zip(arrays, ways)
        ]

    count = lax.axis_size("hy")
    near = [(i, i ^ 1) for i in range(count)]
    other = [(i, (i + 1 if i % 2 else i - 1) % count) for i in range(count)]
    second_up, second_down = shifts("hx")
    width = len(RIM_POINTS)
    message = (-(-((levels + 2) * width + 2) // ROWS) * ROWS, lanes)
    sides = (-(-fields * len(chunks(levels)) // 4) * ROWS, lanes)
    padded = levels + 2 * ROWS
    table = pltpu.VMEM((4, lanes), jnp.int32)
    inputs = (
        prognostic.reshape(whole),
        neighbour_face,
        orientation,
        metric,
        jnp.asarray(tables),
        first_flux,
        second_flux,
    )
    (
        to_other,
        state,
        neighbour_face,
        orientation,
        metric,
        tables,
        fluxes,
    ) = call(
        rim_kernel,
        [
            message,
            whole,
            table,
            table,
            (POINTS, lanes),
            tables.shape,
            (-(-2 * fields * fields // ROWS) * ROWS, lanes),
        ],
        [HBM] * len(inputs),
        [
            pltpu.VMEM((width, padded, lanes), jnp.float32),
            pltpu.VMEM((width, padded, lanes), jnp.float32),
            pltpu.SMEM((fields, fields), jnp.float32),
            pltpu.SMEM((fields, fields), jnp.float32),
            pltpu.SemaphoreType.DMA((6 + -(-levels // ROWS),)),
        ],
        cost=1000,
        name="rim",
    )(*(pltpu.with_memory_space_constraint(x, pltpu.HBM) for x in inputs))
    state = state.reshape(fields * levels * POINTS, lanes)
    from_other = lax.ppermute(to_other, "hy", other)
    from_near = lax.ppermute(state, "hy", near)
    (to_sides,) = call(edge_kernel, [sides], [VMEM], cost=1000, name="edge")(state)
    from_down = lax.ppermute(to_sides, "hx", second_up)
    from_up = from_down
    if lax.axis_size("hx") > 2:
        from_up = lax.ppermute(to_sides, "hx", second_down)

    column = (coupling.shape[1], NODES, lanes)
    factors = call(factor_kernel, [column] * 5, [VMEM] * 2, cost=4000000, name="factor")(
        coupling, damping
    )
    block = ((levels + 2) * NODES, lanes)
    part, base = call(
        element_kernel,
        [state.shape, (NODES,) + block],
        [VMEM] * 6,
        [
            pltpu.VMEM((levels * 8 * fields, lanes), jnp.float32),
            pltpu.VMEM((fields * POINTS, lanes), jnp.bfloat16),
            pltpu.VMEM((fields * POINTS, lanes), jnp.bfloat16),
        ],
        cost=4000000,
        name="element",
    )(
        state,
        neighbour_face,
        orientation,
        metric,
        fluxes,
        tables,
    )
    late = levels * NODES * len(LATE_FIELDS)
    base, near_late = call(
        near_kernel,
        [(NODES,) + block, (late, lanes)],
        [VMEM] * 6,
        [pltpu.VMEM((NODES, padded, lanes), jnp.float32), pltpu.VMEM(block, jnp.float32)],
        cost=1000,
        name="near",
    )(from_near, neighbour_face, orientation, fluxes, base, metric)
    count = -(-(levels + 2) // ROWS) * ROWS
    (half,) = call(
        half_pack_kernel,
        [(NODES,) + block],
        [VMEM] * 7 + [ANY],
        [
            pltpu.VMEM((NODES, count * NODES, lanes), jnp.float32),
            pltpu.VMEM((padded, lanes), jnp.float32),
            pltpu.VMEM((count, lanes), jnp.float32),
        ],
        cost=1000,
        name="half_pack",
    )(
        base,
        from_down,
        from_up,
        neighbour_face,
        orientation,
        metric,
        fluxes,
        factors[0],
    )
    sends = call(
        pack_kernel,
        [block] * NODES,
        [VMEM] * 5,
        [pltpu.VMEM((NODES,) + block, jnp.float32)],
        cost=1000,
        name="pack",
    )(half, from_other, neighbour_face, orientation, metric)
    received = exchange(sends, WAYS)

    other_face = call(
        functools.partial(face_kernel, 1),
        [(late // 2, lanes)] * 2,
        [VMEM] * 3 + [ANY],
        cost=1000,
        name="other_face",
    )(state, from_other, fluxes, sends[-1])
    other_face = [lax.ppermute(x, "hy", other) for x in other_face]

    cube = (levels + 2, NODES, lanes)
    speeds = call(
        solve_kernel,
        [cube] * NODES,
        [VMEM] * (5 + NODES),
        [
            pltpu.VMEM(column, jnp.float32),
            pltpu.VMEM((NODES, 2, NODES, lanes), jnp.float32),
            pltpu.VMEM((column[0] + 2,) + column[1:], jnp.float32),
        ],
        cost=1000,
        name="solve",
    )(*factors, *[x.reshape(cube) for x in received])
    returned = exchange([x.reshape(block) for x in speeds], BACK_WAYS)
    size = levels * POINTS
    limits = pltpu.CompilerParams(vmem_limit_bytes=24 * 1024 * 1024)
    earlier, done = pl.pallas_call(
        finish_section_kernel,
        out_shape=[
            jax.ShapeDtypeStruct(whole, jnp.float32),
            pltpu.VMEM((2, size, lanes), jnp.float32),
        ],
        in_specs=[VMEM] * 10,
        out_specs=[HBM, VMEM],
        scratch_shapes=[
            pltpu.VMEM((2, size, lanes), jnp.float32),
            pltpu.SemaphoreType.DMA,
        ],
        compiler_params=limits,
        cost_estimate=pl.CostEstimate(flops=4000000, bytes_accessed=4000000, transcendentals=0),
        name="finish",
    )(
        part, near_late, *other_face, from_down, from_up, neighbour_face, orientation, metric, fluxes
    )
    updated = pl.pallas_call(
        update_kernel,
        out_shape=jax.ShapeDtypeStruct(whole, jnp.float32),
        in_specs=[VMEM] * (1 + NODES) + [HBM],
        out_specs=HBM,
        input_output_aliases={1 + NODES: 0},
        scratch_shapes=[
            pltpu.VMEM((NODES,) + block, jnp.float32),
            pltpu.VMEM((3, size, lanes), jnp.float32),
            pltpu.SemaphoreType.DMA((6,)),
        ],
        compiler_params=limits,
        name="update",
    )(*returned, done, earlier)
    return updated.reshape(prognostic.shape)


def solution(mesh):
    placed = (
        P(None, "vz", None, None, "hy", "hx"),
        P(None, None, "hy", "hx"),
        P(),
        P(),
        P(None, "hy", "hx"),
        P(None, "hy", "hx"),
        P(None, None, "vz", None, "hy", "hx"),
        P("vz", None, "hy", "hx"),
    )
    return jax.shard_map(
        per_device,
        mesh=mesh,
        in_specs=placed,
        out_specs=P(None, "vz", None, None, "hy", "hx"),
        check_vma=False,
    )
```

```python
import functools

import jax
import jax.numpy as jnp
import numpy as np
from jax import lax
from jax.experimental import pallas as pl
from jax.experimental.pallas import tpu as pltpu
from jax.sharding import PartitionSpec as P

step_size = 0.05
lift_weight = 6.0
gravity_couple = 0.5
density_couple = 0.3
theta_couple = 0.4

NODES = 4
POINTS = NODES * NODES
FIELDS = 5
FACE_POINTS = ((0, 4, 8, 12), (3, 7, 11, 15), (0, 1, 2, 3), (12, 13, 14, 15))
RIM_POINTS = tuple(sorted(set(sum(FACE_POINTS, ()))))
ROWS = 8
LATE_FIELDS = (0, 1, 2, 4)
WAYS = (2, 3, 1, 0)
BACK_WAYS = (2, 3, 1, 0)


def derivative_table():
    points = np.array([-1.0, -1.0 / np.sqrt(5.0), 1.0 / np.sqrt(5.0), 1.0])
    number = points.shape[0]
    barycentric = np.ones(number)
    for source in range(number):
        for another in range(number):
            if another != source:
                barycentric[source] = barycentric[source] / (points[source] - points[another])
    matrix = np.zeros((number, number))
    for target in range(number):
        for source in range(number):
            if target != source:
                matrix[target, source] = (
                    barycentric[source] / barycentric[target] / (points[target] - points[source])
                )
        matrix[target, target] = -np.sum(matrix[target])
    return matrix


def operator_tables(lanes):
    weight = 0.5 * lift_weight
    table = derivative_table()
    table[0, 0] += weight
    table[-1, -1] -= weight
    eye = np.eye(NODES)
    along_first = np.kron(eye, table)
    along_second = np.kron(table, eye)
    ends = np.zeros(NODES)
    ends[0] = ends[-1] = 1.0
    faces = np.diag(np.kron(np.ones(NODES), ends) + np.kron(ends, np.ones(NODES)))
    first = np.zeros((POINTS, lanes))
    second = np.zeros((POINTS, lanes))
    same = np.zeros((FIELDS, POINTS, lanes))
    owner = np.full((lanes,), -1)
    for g in range(FIELDS):
        own = slice(POINTS * g, POINTS * (g + 1))
        first[:, own] = -along_first
        second[:, own] = -along_second
        same[g, :, own] = -weight * faces
        owner[own] = g
        for k in range(NODES):
            south = FIELDS * POINTS + 2 * NODES * g + k
            north = south + NODES
            second[FACE_POINTS[2][k], south] = weight
            second[FACE_POINTS[3][k], north] = -weight
            same[g, FACE_POINTS[2][k], south] = weight
            same[g, FACE_POINTS[3][k], north] = weight
            owner[south] = owner[north] = g
    tables = np.concatenate([first, second, same.reshape(FIELDS * POINTS, lanes)])
    return tables.astype(np.float32), owner


def chunks(total):
    return [min(start, total - ROWS) for start in range(0, total, ROWS)]


def partner_side(partner):
    odd = lax.rem(lax.axis_index("hy"), 2)
    return odd if partner else 1 - odd


def side_sign(side):
    return (2 * side - 1).astype(jnp.float32)


def ends(total):
    return list(range(0, total, ROWS))


def pick(values, masks, flip):
    chosen = []
    for k in range(NODES):
        row = values[FACE_POINTS[0][k]]
        for option in range(1, 4):
            row = jnp.where(masks[option], values[FACE_POINTS[option][k]], row)
        chosen.append(row)
    return [jnp.where(flip, chosen[NODES - 1 - k], chosen[k]) for k in range(NODES)]


def table_masks(face_row, flip_row, lanes):
    face = jnp.broadcast_to(face_row, (ROWS, lanes))
    flip = jnp.broadcast_to(flip_row, (ROWS, lanes))
    return [face == option for option in range(4)], flip == 1


def flux_row(f, g, matrix):
    return (matrix * FIELDS + f) * FIELDS + g


def along(fluxes, matrix, f, rows):
    total = None
    for g in range(FIELDS):
        at = flux_row(f, g, matrix)
        term = fluxes[at : at + 1, :] * rows[g]
        total = term if total is None else total + term
    return total


def side_rows(f, piece):
    number = 3 * f + piece
    return number // 4, 32 * (number % 4)


def rim_kernel(
    state_hbm,
    face_hbm,
    way_hbm,
    metric_hbm,
    tables_hbm,
    flux_hbm,
    second_hbm,
    to_other,
    state,
    neighbour_face,
    orientation,
    metric,
    tables,
    fluxes,
    column,
    speed,
    flux,
    second_flux,
    semaphores,
):
    levels = state.shape[1] // POINTS
    face = partner_side(1)
    sign = side_sign(face)
    lanes = state.shape[2]
    width = len(RIM_POINTS)
    groups = [(start, min(start + ROWS, levels)) for start in range(0, levels, ROWS)]
    small = [
        pltpu.make_async_copy(source, target, semaphores.at[place])
        for place, (source, target) in enumerate(
            (
                (flux_hbm, flux),
                (face_hbm, neighbour_face),
                (way_hbm, orientation),
                (metric_hbm, metric),
                (tables_hbm, tables),
                (second_hbm, second_flux),
            )
        )
    ]
    large = []
    for place, (low, high) in enumerate(groups):
        rows = pl.ds(low * POINTS, (high - low) * POINTS)
        large.append(
            [
                pltpu.make_async_copy(
                    state_hbm.at[f, rows, :],
                    state.at[f, rows, :],
                    semaphores.at[len(small) + place * FIELDS + f],
                )
                for f in range(FIELDS)
            ]
        )
    for copy in small[:1] + sum(large, []) + small[1:]:
        copy.start()
    column[...] = jnp.zeros_like(column)
    small[0].wait()
    arrived = 0
    for piece, start in enumerate(chunks(levels)):
        while arrived < len(groups) and groups[arrived][0] < start + ROWS:
            for copy in large[arrived]:
                copy.wait()
            arrived += 1
        for place, point in enumerate(RIM_POINTS):
            rows = [
                state[g, pl.ds(start * POINTS + point, ROWS, stride=POINTS), :]
                for g in range(FIELDS)
            ]
            for f, out in ((3, speed), (4, column)):
                normal = (sign * flux[f, 0]) * rows[0]
                for g in range(1, FIELDS):
                    normal = normal + (sign * flux[f, g]) * rows[g]
                out[place, pl.ds(ROWS + start, ROWS), :] = rows[f] + normal
    small[1].wait()
    small[2].wait()
    end = (levels + 2) * width
    for place in range(width):
        for start in chunks(levels):
            upper = column[place, pl.ds(ROWS + start + 1, ROWS), :]
            lower = column[place, pl.ds(ROWS + start - 1, ROWS), :]
            to_other[pl.ds(start * width + place, ROWS, stride=width), :] = speed[
                place, pl.ds(ROWS + start, ROWS), :
            ] - gravity_couple * (upper - lower)
        for extra, level in ((0, 0), (1, levels - 1)):
            at = (levels + extra) * width + place
            to_other[at : at + 1, :] = column[place, ROWS + level : ROWS + level + 1, :]
    to_other[end : end + 1, :] = neighbour_face[pl.ds(face, 1), :].astype(jnp.float32)
    to_other[end + 1 : end + 2, :] = orientation[pl.ds(face, 1), :].astype(jnp.float32)
    left = to_other.shape[0] - end - 2
    to_other[end + 2 :, :] = jnp.zeros((left, lanes), jnp.float32)
    small[3].wait()
    small[4].wait()
    small[5].wait()
    for place, source in enumerate((flux, second_flux)):
        for f in range(FIELDS):
            for g in range(FIELDS):
                at = flux_row(f, g, place)
                fluxes[at : at + 1, :] = jnp.full((1, lanes), source[f, g])


def edge_kernel(state, to_sides):
    lanes = state.shape[1]
    levels = state.shape[0] // (FIELDS * POINTS)
    lane = lax.broadcasted_iota(jnp.int32, (ROWS, lanes), 1)
    packed = [jnp.zeros((ROWS, lanes), jnp.float32) for _ in range(to_sides.shape[0] // ROWS)]
    for f in range(FIELDS):
        for piece, start in enumerate(chunks(levels)):
            block, at = side_rows(f, piece)
            for place, point in enumerate(RIM_POINTS):
                row = state[pl.ds((f * levels + start) * POINTS + point, ROWS, stride=POINTS), :]
                first = at + 2 * place
                packed[block] = jnp.where(
                    lane // 2 == first // 2, pltpu.roll(row, first + 1, 1), packed[block]
                )
    for block, value in enumerate(packed):
        to_sides[block * ROWS : (block + 1) * ROWS, :] = value


def near_kernel(
    state, neighbour_face, orientation, fluxes, base, metric, half, late, column, source
):
    lanes = state.shape[1]
    levels = state.shape[0] // (FIELDS * POINTS)
    face = partner_side(0)
    sign = -side_sign(face)
    masks, flip = table_masks(
        neighbour_face[pl.ds(face, 1), :], orientation[pl.ds(face, 1), :], lanes
    )
    column[...] = jnp.zeros_like(column)
    speeds = []
    for start in chunks(levels):
        picked = []
        for g in range(FIELDS):
            values = {
                point: state[pl.ds((g * levels + start) * POINTS + point, ROWS, stride=POINTS), :]
                for point in RIM_POINTS
            }
            picked.append(pick(values, masks, flip))
        for k in range(NODES):
            rows = [picked[g][k] for g in range(FIELDS)]
            changed = [rows[f] + sign * along(fluxes, 0, f, rows) for f in range(FIELDS)]
            for place, f in enumerate(LATE_FIELDS):
                at = (place * levels + start) * NODES + k
                late[pl.ds(at, ROWS, stride=NODES), :] = changed[f]
            column[k, pl.ds(ROWS + start, ROWS), :] = changed[4]
            speeds.append(changed[3])
    for piece, start in enumerate(chunks(levels)):
        for k in range(NODES):
            upper = column[k, pl.ds(ROWS + start + 1, ROWS), :]
            lower = column[k, pl.ds(ROWS + start - 1, ROWS), :]
            source[pl.ds(start * NODES + k, ROWS, stride=NODES), :] = speeds[
                NODES * piece + k
            ] - gravity_couple * (upper - lower)
    for extra, level in ((0, 0), (1, levels - 1)):
        for k in range(NODES):
            at = (levels + extra) * NODES + k
            source[at : at + 1, :] = column[k, ROWS + level : ROWS + level + 1, :]
    half[...] = base[...]
    for start in chunks(levels + 2):
        picked = [source[pl.ds(start * NODES + k, ROWS, stride=NODES), :] for k in range(NODES)]
        add_first_side(0, start, picked, half, base, metric)


def face_kernel(partner, state, received, fluxes, *rest):
    lanes = state.shape[1]
    levels = state.shape[0] // (FIELDS * POINTS)
    at = (levels + 2) * len(RIM_POINTS)
    outs = rest[-2:]
    share = len(LATE_FIELDS) // len(outs)
    sign = side_sign(partner_side(partner))
    masks, flip = table_masks(
        received[at : at + 1, :].astype(jnp.int32),
        received[at + 1 : at + 2, :].astype(jnp.int32),
        lanes,
    )
    for start in chunks(levels):
        picked = []
        for g in range(FIELDS):
            values = {
                point: state[pl.ds((g * levels + start) * POINTS + point, ROWS, stride=POINTS), :]
                for point in RIM_POINTS
            }
            picked.append(pick(values, masks, flip))
        for place, f in enumerate(LATE_FIELDS):
            for k in range(NODES):
                normal = along(fluxes, 0, f, [picked[g][k] for g in range(FIELDS)])
                at = ((place % share) * levels + start) * NODES + k
                outs[place // share][pl.ds(at, ROWS, stride=NODES), :] = (
                    picked[f][k] + sign * normal
                )


def element_kernel(
    state,
    neighbour_face,
    orientation,
    metric,
    fluxes,
    tables,
    part,
    base,
    outer,
    operator_high,
    operator_low,
):
    levels = state.shape[0] // (FIELDS * POINTS)
    lanes = state.shape[1]
    lane = lax.broadcasted_iota(jnp.int32, (ROWS, lanes), 1)
    sides = []
    for side, (face, edge) in enumerate(((2, 0), (3, lanes - 1))):
        shift = 1 if side == 0 else lanes - 1
        row = jnp.broadcast_to(neighbour_face[face : face + 1, :], (ROWS, lanes))
        way = jnp.broadcast_to(orientation[face : face + 1, :], (ROWS, lanes))
        masks, flip = table_masks(
            pltpu.roll(row, lanes - shift, 1), pltpu.roll(way, lanes - shift, 1), lanes
        )
        sides.append((shift, edge, masks, flip))
    for f in range(FIELDS):
        for start in chunks(levels):
            q = f * levels + start
            values = {
                point: state[pl.ds(q * POINTS + point, ROWS, stride=POINTS), :]
                for point in RIM_POINTS
            }
            for side, (shift, edge, masks, flip) in enumerate(sides):
                for k, row in enumerate(pick(values, masks, flip)):
                    at = start * 8 * FIELDS + 8 * f + NODES * side + k
                    outer[pl.ds(at, ROWS, stride=8 * FIELDS), :] = jnp.where(
                        lane == edge, 0.0, pltpu.roll(row, shift, 1)
                    )
    index = lax.broadcasted_iota(jnp.int32, (1, lanes), 1)
    own_columns = FIELDS * POINTS
    owner = jnp.where(index < own_columns, index // POINTS, (index - own_columns) // 8)
    for f in range(FIELDS):
        first_row = jnp.zeros((1, lanes), jnp.float32)
        second_row = first_row
        for g in range(FIELDS):
            first, second = (flux_row(f, g, matrix) for matrix in range(2))
            first_row = jnp.where(owner == g, fluxes[first : first + 1, :], first_row)
            second_row = jnp.where(owner == g, fluxes[second : second + 1, :], second_row)
        block = (
            first_row * tables[0:POINTS, :]
            + second_row * tables[POINTS : 2 * POINTS, :]
            + tables[(2 + f) * POINTS : (3 + f) * POINTS, :]
        )
        high = block.astype(jnp.bfloat16)
        operator_high[f * POINTS : (f + 1) * POINTS, :] = high
        operator_low[f * POINTS : (f + 1) * POINTS, :] = (
            block - high.astype(jnp.float32)
        ).astype(jnp.bfloat16)
    high = operator_high[...]
    low = operator_low[...]
    scale = step_size * metric[...]
    blank = jnp.zeros((lanes - own_columns - 8 * FIELDS, lanes), jnp.float32)
    for pair in range(0, levels, 2):
        sides = []
        for level in (pair, pair + 1):
            rows = [
                state[pl.ds((f * levels + level) * POINTS, POINTS), :] for f in range(FIELDS)
            ]
            rows.append(outer[pl.ds(level * 8 * FIELDS, 8 * FIELDS), :])
            rows.append(blank)
            sides.append(jnp.concatenate(rows, axis=0))
        values = jnp.concatenate(sides, axis=1)
        top = values.astype(jnp.bfloat16)
        rest = (values - top.astype(jnp.float32)).astype(jnp.bfloat16)
        change = (
            jnp.dot(high, top, preferred_element_type=jnp.float32)
            + jnp.dot(high, rest, preferred_element_type=jnp.float32)
            + jnp.dot(low, top, preferred_element_type=jnp.float32)
        )
        for place, level in enumerate((pair, pair + 1)):
            for f in range(FIELDS):
                at = pl.ds((f * levels + level) * POINTS, POINTS)
                part[at, :] = (
                    state[at, :]
                    + scale
                    * change[
                        f * POINTS : (f + 1) * POINTS, place * lanes : (place + 1) * lanes
                    ]
                )
    for level in range(levels):
        speed = part[pl.ds((3 * levels + level) * POINTS, POINTS), :]
        upper = part[pl.ds((4 * levels + level + 1) * POINTS, POINTS), :] if level < levels - 1 else 0.0
        lower = part[pl.ds((4 * levels + level - 1) * POINTS, POINTS), :] if level else 0.0
        value = speed - gravity_couple * (upper - lower)
        for j in range(NODES):
            base[j, level * NODES : (level + 1) * NODES, :] = value[NODES * j : NODES * (j + 1)]
    for extra, level in ((0, 0), (1, levels - 1)):
        value = part[pl.ds((4 * levels + level) * POINTS, POINTS), :]
        at = (levels + extra) * NODES
        for j in range(NODES):
            base[j, at : at + NODES, :] = value[NODES * j : NODES * (j + 1)]


def side_corrections(received, side, fluxes, fields, pieces):
    lanes = received.shape[1]
    sign = 1.0 if side == 0 else -1.0
    result = [[] for _ in fields]
    for piece in range(pieces):
        rows = []
        for g in range(FIELDS):
            block, at = side_rows(g, piece)
            rows.append(
                pltpu.roll(
                    received[block * ROWS : (block + 1) * ROWS, :], (lanes - at - side) % lanes, 1
                )
            )
        for place, f in enumerate(fields):
            result[place].append(rows[f] + sign * along(fluxes, 1, f, rows))
    return result


def spread(value, edge, masks, flip):
    lanes = value.shape[1]
    values = {
        point: pltpu.roll(value, (edge - 2 * place) % lanes, 1)
        for place, point in enumerate(RIM_POINTS)
    }
    return pick(values, masks, flip)


def add_first_side(partner, start, picked, send, base, metric):
    weight = 0.5 * lift_weight * step_size
    i = (NODES - 1) * partner_side(partner)
    for j, row in enumerate(picked):
        at = pl.ds(start * NODES + i, ROWS, stride=NODES)
        scale = weight * metric[pl.ds(NODES * j + i, 1), :]
        send[j, at, :] = base[j, at, :] + scale * row


def pack_kernel(half, from_other, neighbour_face, orientation, metric, *rest):
    sends, (send,) = rest[:NODES], rest[NODES:]
    me = lax.axis_index("vz")
    send[...] = half[...]
    rows, lanes = half.shape[1:]
    width = len(RIM_POINTS)
    face = partner_side(1)
    masks, flip = table_masks(
        neighbour_face[pl.ds(face, 1), :], orientation[pl.ds(face, 1), :], lanes
    )
    for start in chunks(rows // NODES):
        values = {
            point: from_other[pl.ds(start * width + place, ROWS, stride=width), :]
            for place, point in enumerate(RIM_POINTS)
        }
        add_first_side(1, start, pick(values, masks, flip), send, half, metric)
    for out, way in zip(sends, WAYS):
        out[...] = send[me ^ way]


def half_pack_kernel(
    base,
    from_down,
    from_up,
    neighbour_face,
    orientation,
    metric,
    fluxes,
    factored,
    half,
    send,
    column,
    mixed,
):
    rows, lanes = base.shape[1:]
    levels = rows // NODES - 2
    width = len(RIM_POINTS)
    weight = 0.5 * lift_weight * step_size
    send[:, 0:rows, :] = base[...]
    send[:, rows:, :] = jnp.zeros((NODES, send.shape[1] - rows, lanes), jnp.float32)
    column[...] = jnp.zeros_like(column)
    mixed[...] = jnp.zeros_like(mixed)
    lane = lax.broadcasted_iota(jnp.int32, (ROWS, lanes), 1)
    for side, (received, edge, j) in enumerate(
        ((from_down, 0, 0), (from_up, lanes - 1, NODES - 1))
    ):
        face = 2 + side
        masks, flip = table_masks(
            neighbour_face[face : face + 1, :], orientation[face : face + 1, :], lanes
        )
        speed, heat = side_corrections(received, side, fluxes, (3, 4), len(chunks(levels)))
        for start, value in zip(chunks(levels), heat):
            column[pl.ds(ROWS + start, ROWS), :] = value
        for start, value in zip(chunks(levels), speed):
            upper = column[pl.ds(ROWS + start + 1, ROWS), :]
            lower = column[pl.ds(ROWS + start - 1, ROWS), :]
            mixed[pl.ds(start, ROWS), :] = value - gravity_couple * (upper - lower)
        mixed[levels : levels + 1, :] = column[ROWS : ROWS + 1, :]
        mixed[levels + 1 : levels + 2, :] = column[ROWS + levels - 1 : ROWS + levels, :]
        for start in ends(levels + 2):
            picked = spread(mixed[start : start + ROWS, :], edge, masks, flip)
            for k, row in enumerate(picked):
                point = NODES * j + k
                at = pl.ds(start * NODES + k, ROWS, stride=NODES)
                scale = weight * metric[point : point + 1, :]
                send[j, at, :] += jnp.where(lane == edge, scale * row, 0.0)
    half[...] = send[:, 0:rows, :]


def finish_section_kernel(
    part,
    near,
    other_early,
    other_late,
    from_down,
    from_up,
    neighbour_face,
    orientation,
    metric,
    fluxes,
    out,
    done,
    final,
    semaphore,
):
    levels = part.shape[0] // (FIELDS * POINTS)
    lanes = part.shape[1]
    size = levels * POINTS
    weight = 0.5 * lift_weight * step_size
    scale = weight * metric[...]
    lane = lax.broadcasted_iota(jnp.int32, (ROWS, lanes), 1)
    tables = []
    edges = []
    for side, received in enumerate((from_down, from_up)):
        face = 2 + side
        tables.append(
            table_masks(
                neighbour_face[face : face + 1, :], orientation[face : face + 1, :], lanes
            )
        )
        edges.append(
            side_corrections(received, side, fluxes, LATE_FIELDS, len(chunks(levels)))
        )
    copy = pltpu.make_async_copy(final, out.at[1:3], semaphore)
    sources = ((near,), (other_early, other_late))
    for place, f in ((1, 1), (2, 2), (0, 0), (3, 4)):
        target = final.at[f - 1] if f in (1, 2) else done.at[min(f, 1)]
        target[...] = part[f * size : (f + 1) * size, :]
        for piece, start in enumerate(chunks(levels)):
            for j in range(NODES):
                for partner, source in enumerate(sources):
                    point = NODES * j + (NODES - 1) * partner_side(partner)
                    share = len(LATE_FIELDS) // len(source)
                    rows = source[place // share][
                        pl.ds(((place % share) * levels + start) * NODES + j, ROWS, stride=NODES),
                        :,
                    ]
                    at = pl.ds(start * POINTS + point, ROWS, stride=POINTS)
                    target[at, :] = (
                        part[pl.ds(f * size + start * POINTS + point, ROWS, stride=POINTS), :]
                        + weight * metric[pl.ds(point, 1), :] * rows
                    )
        for piece, start in enumerate(chunks(levels)):
            row_index = lax.broadcasted_iota(jnp.int32, (ROWS, lanes), 0)
            fresh = row_index >= (-start) % ROWS
            for side, (edge, j) in enumerate(((0, 0), (lanes - 1, NODES - 1))):
                picked = spread(edges[side][place][piece], edge, *tables[side])
                for k, row in enumerate(picked):
                    point = NODES * j + k
                    at = pl.ds(start * POINTS + point, ROWS, stride=POINTS)
                    target[at, :] += jnp.where(
                        (lane == edge) & fresh, scale[point : point + 1, :] * row, 0.0
                    )
        if f == 2:
            copy.start()
    copy.wait()


def factor_kernel(coupling, damping, far, near, inverse, ratio, second):
    levels = coupling.shape[1]
    shape = coupling.shape[2:]
    blank = jnp.zeros(shape, jnp.float32)
    far_ratio, far_second, near_ratio, near_second = (blank,) * 4
    extra = damping[...]
    for level in range(levels):
        a, b, d, e = (coupling[entry, level] for entry in range(4))
        centre = a + b + d + e + extra
        reduced = -b + a * far_ratio
        pivot = centre + a * far_second - reduced * near_ratio
        scaled = 1.0 / pivot
        upper_ratio = (-d - reduced * near_second) * scaled
        second_ratio = -e * scaled
        far[level] = a * scaled
        near[level] = reduced * scaled
        inverse[level] = scaled
        ratio[level] = upper_ratio
        second[level] = second_ratio
        far_ratio, far_second = near_ratio, near_second
        near_ratio, near_second = upper_ratio, second_ratio


def solve_kernel(far, near, inverse, ratio, second, *rest):
    ways = NODES
    received, sends, (source, heat, speed) = rest[:ways], rest[ways : 2 * ways], rest[2 * ways :]
    levels = far.shape[0]
    here = levels // ways
    me = lax.axis_index("vz")
    for values, way in zip(received, WAYS):
        block = me ^ way
        source[pl.ds(block * here, here)] = values[0:here]
        heat[block] = values[here : here + 2]
    for block in range(ways - 1):
        last = block * here + here - 1
        source[last] = source[last] - gravity_couple * heat[block + 1, 0]
        source[last + 1] = source[last + 1] + gravity_couple * heat[block, 1]
    blank = jnp.zeros(far.shape[1:], jnp.float32)
    before_two, before_one = blank, blank
    for level in range(levels):
        value = source[level] * inverse[level]
        value = value + far[level] * before_two
        value = value - near[level] * before_one
        source[level] = value
        before_two, before_one = before_one, value
    speed[0] = blank
    speed[levels + 1] = blank
    next_one, next_two = blank, blank
    for level in range(levels - 1, -1, -1):
        value = source[level] - second[level] * next_two
        value = value - ratio[level] * next_one
        speed[level + 1] = value
        next_two, next_one = next_one, value
    for send, way in zip(sends, BACK_WAYS):
        send[...] = speed[pl.ds((me ^ way) * here, here + 2)]


def update_kernel(*refs):
    ways = NODES
    received, (done, earlier, out, speed, final, semaphores) = refs[:ways], refs[ways:]
    levels = done.shape[1] // POINTS
    me = lax.axis_index("vz")
    for values, way in zip(received, BACK_WAYS):
        speed[me ^ way] = values[...]
    lanes = done.shape[2]
    half = levels // 2
    low = lax.broadcasted_iota(jnp.int32, (ROWS, lanes), 0) < NODES
    copies = []
    for pair in range(half):
        lower = [speed[j, pair * ROWS : (pair + 1) * ROWS, :] for j in range(NODES)]
        upper = [speed[j, (pair + 1) * ROWS : (pair + 2) * ROWS, :] for j in range(NODES)]
        jump = [above - below for above, below in zip(upper, lower)]
        value = [jnp.where(low, above, below) for above, below in zip(upper, lower)]
        for h in range(2):
            a, b = 2 * h, 2 * h + 1
            for odd in range(2):
                at = pl.ds((2 * pair + odd) * POINTS + ROWS * h, ROWS)
                jumps = side_by_side(jump[a], jump[b], odd, low)
                final[0, at, :] = done[0, at, :] - density_couple * jumps
                final[1, at, :] = side_by_side(value[a], value[b], 1 - odd, low)
                final[2, at, :] = done[1, at, :] - theta_couple * jumps
        if pair in (half // 2 - 1, half - 1):
            first = 0 if pair < half - 1 else half // 2
            rows = pl.ds(first * 2 * POINTS, (pair + 1 - first) * 2 * POINTS)
            for place, f in enumerate((0, 3, 4)):
                copies.append(
                    pltpu.make_async_copy(
                        final.at[place, rows, :], out.at[f, rows, :], semaphores.at[len(copies)]
                    )
                )
                copies[-1].start()
    for copy in copies:
        copy.wait()


def side_by_side(first, second, upper, low):
    if upper:
        return jnp.where(low, pltpu.roll(first, NODES, 0), second)
    return jnp.where(low, first, pltpu.roll(second, NODES, 0))


VMEM = pl.BlockSpec(memory_space=pltpu.VMEM)
HBM = pl.BlockSpec(memory_space=pltpu.HBM)
ANY = pl.BlockSpec(memory_space=pl.ANY)


def call(kernel, outs, in_specs, scratch=(), cost=0, name=None):
    kinds = [x if hasattr(x, "dtype") else pltpu.VMEM(x, jnp.float32) for x in outs]
    return pl.pallas_call(
        kernel,
        out_shape=kinds,
        in_specs=in_specs,
        out_specs=[VMEM] * len(outs),
        scratch_shapes=list(scratch),
        compiler_params=pltpu.CompilerParams(vmem_limit_bytes=24 * 1024 * 1024),
        cost_estimate=pl.CostEstimate(flops=cost, bytes_accessed=cost, transcendentals=0),
        name=name,
    )


def per_device(
    prognostic, metric, first_flux, second_flux, neighbour_face, orientation, coupling, damping
):
    fields, levels = prognostic.shape[:2]
    lanes = prognostic.shape[-1]
    whole = (fields, levels * POINTS, lanes)
    metric = metric.reshape(POINTS, lanes)
    neighbour_face = neighbour_face.reshape(4, lanes)
    orientation = orientation.reshape(4, lanes)
    coupling = coupling.reshape(4, coupling.shape[1], NODES, lanes)
    damping = damping.reshape(NODES, lanes)
    tables, _ = operator_tables(lanes)

    def shifts(axis):
        size = lax.axis_size(axis)
        up = [(i, (i + 1) % size) for i in range(size)]
        return up, [(j, i) for i, j in up]

    def exchange(arrays, ways):
        size = lax.axis_size("vz")
        return [
            lax.ppermute(x, "vz", [(i, i ^ way) for i in range(size)]) if way else x
            for x, way in zip(arrays, ways)
        ]

    count = lax.axis_size("hy")
    near = [(i, i ^ 1) for i in range(count)]
    other = [(i, (i + 1 if i % 2 else i - 1) % count) for i in range(count)]
    second_up, second_down = shifts("hx")
    width = len(RIM_POINTS)
    message = (-(-((levels + 2) * width + 2) // ROWS) * ROWS, lanes)
    sides = (-(-fields * len(chunks(levels)) // 4) * ROWS, lanes)
    padded = levels + 2 * ROWS
    table = pltpu.VMEM((4, lanes), jnp.int32)
    inputs = (
        prognostic.reshape(whole),
        neighbour_face,
        orientation,
        metric,
        jnp.asarray(tables),
        first_flux,
        second_flux,
    )
    (
        to_other,
        state,
        neighbour_face,
        orientation,
        metric,
        tables,
        fluxes,
    ) = call(
        rim_kernel,
        [
            message,
            whole,
            table,
            table,
            (POINTS, lanes),
            tables.shape,
            (-(-2 * fields * fields // ROWS) * ROWS, lanes),
        ],
        [HBM] * len(inputs),
        [
            pltpu.VMEM((width, padded, lanes), jnp.float32),
            pltpu.VMEM((width, padded, lanes), jnp.float32),
            pltpu.SMEM((fields, fields), jnp.float32),
            pltpu.SMEM((fields, fields), jnp.float32),
            pltpu.SemaphoreType.DMA((6 + fields * -(-levels // ROWS),)),
        ],
        cost=1000,
        name="rim",
    )(*(pltpu.with_memory_space_constraint(x, pltpu.HBM) for x in inputs))
    state = state.reshape(fields * levels * POINTS, lanes)
    from_other = lax.ppermute(to_other, "hy", other)
    from_near = lax.ppermute(state, "hy", near)
    (to_sides,) = call(edge_kernel, [sides], [VMEM], cost=1000, name="edge")(state)
    from_down = lax.ppermute(to_sides, "hx", second_up)
    from_up = from_down
    if lax.axis_size("hx") > 2:
        from_up = lax.ppermute(to_sides, "hx", second_down)

    column = (coupling.shape[1], NODES, lanes)
    factors = call(factor_kernel, [column] * 5, [VMEM] * 2, cost=4000000, name="factor")(
        coupling, damping
    )
    block = ((levels + 2) * NODES, lanes)
    part, base = call(
        element_kernel,
        [state.shape, (NODES,) + block],
        [VMEM] * 6,
        [
            pltpu.VMEM((levels * 8 * fields, lanes), jnp.float32),
            pltpu.VMEM((fields * POINTS, lanes), jnp.bfloat16),
            pltpu.VMEM((fields * POINTS, lanes), jnp.bfloat16),
        ],
        cost=4000000,
        name="element",
    )(
        state,
        neighbour_face,
        orientation,
        metric,
        fluxes,
        tables,
    )
    late = levels * NODES * len(LATE_FIELDS)
    base, near_late = call(
        near_kernel,
        [(NODES,) + block, (late, lanes)],
        [VMEM] * 6,
        [pltpu.VMEM((NODES, padded, lanes), jnp.float32), pltpu.VMEM(block, jnp.float32)],
        cost=1000,
        name="near",
    )(from_near, neighbour_face, orientation, fluxes, base, metric)
    count = -(-(levels + 2) // ROWS) * ROWS
    (half,) = call(
        half_pack_kernel,
        [(NODES,) + block],
        [VMEM] * 7 + [ANY],
        [
            pltpu.VMEM((NODES, count * NODES, lanes), jnp.float32),
            pltpu.VMEM((padded, lanes), jnp.float32),
            pltpu.VMEM((count, lanes), jnp.float32),
        ],
        cost=1000,
        name="half_pack",
    )(
        base,
        from_down,
        from_up,
        neighbour_face,
        orientation,
        metric,
        fluxes,
        factors[0],
    )
    sends = call(
        pack_kernel,
        [block] * NODES,
        [VMEM] * 5,
        [pltpu.VMEM((NODES,) + block, jnp.float32)],
        cost=1000,
        name="pack",
    )(half, from_other, neighbour_face, orientation, metric)
    received = exchange(sends, WAYS)

    other_face = call(
        functools.partial(face_kernel, 1),
        [(late // 2, lanes)] * 2,
        [VMEM] * 3 + [ANY],
        cost=1000,
        name="other_face",
    )(state, from_other, fluxes, sends[-1])
    other_face = [lax.ppermute(x, "hy", other) for x in other_face]

    cube = (levels + 2, NODES, lanes)
    speeds = call(
        solve_kernel,
        [cube] * NODES,
        [VMEM] * (5 + NODES),
        [
            pltpu.VMEM(column, jnp.float32),
            pltpu.VMEM((NODES, 2, NODES, lanes), jnp.float32),
            pltpu.VMEM((column[0] + 2,) + column[1:], jnp.float32),
        ],
        cost=1000,
        name="solve",
    )(*factors, *[x.reshape(cube) for x in received])
    returned = exchange([x.reshape(block) for x in speeds], BACK_WAYS)
    size = levels * POINTS
    limits = pltpu.CompilerParams(vmem_limit_bytes=24 * 1024 * 1024)
    earlier, done = pl.pallas_call(
        finish_section_kernel,
        out_shape=[
            jax.ShapeDtypeStruct(whole, jnp.float32),
            pltpu.VMEM((2, size, lanes), jnp.float32),
        ],
        in_specs=[VMEM] * 10,
        out_specs=[HBM, VMEM],
        scratch_shapes=[
            pltpu.VMEM((2, size, lanes), jnp.float32),
            pltpu.SemaphoreType.DMA,
        ],
        compiler_params=limits,
        cost_estimate=pl.CostEstimate(flops=4000000, bytes_accessed=4000000, transcendentals=0),
        name="finish",
    )(
        part, near_late, *other_face, from_down, from_up, neighbour_face, orientation, metric, fluxes
    )
    updated = pl.pallas_call(
        update_kernel,
        out_shape=jax.ShapeDtypeStruct(whole, jnp.float32),
        in_specs=[VMEM] * (1 + NODES) + [HBM],
        out_specs=HBM,
        input_output_aliases={1 + NODES: 0},
        scratch_shapes=[
            pltpu.VMEM((NODES,) + block, jnp.float32),
            pltpu.VMEM((3, size, lanes), jnp.float32),
            pltpu.SemaphoreType.DMA((6,)),
        ],
        compiler_params=limits,
        name="update",
    )(*returned, done, earlier)
    return updated.reshape(prognostic.shape)


def solution(mesh):
    placed = (
        P(None, "vz", None, None, "hy", "hx"),
        P(None, None, "hy", "hx"),
        P(),
        P(),
        P(None, "hy", "hx"),
        P(None, "hy", "hx"),
        P(None, None, "vz", None, "hy", "hx"),
        P("vz", None, "hy", "hx"),
    )
    return jax.shard_map(
        per_device,
        mesh=mesh,
        in_specs=placed,
        out_specs=P(None, "vz", None, None, "hy", "hx"),
        check_vma=False,
    )
```

```python
import functools

import jax
import jax.numpy as jnp
import numpy as np
from jax import lax
from jax.experimental import pallas as pl
from jax.experimental.pallas import tpu as pltpu
from jax.sharding import PartitionSpec as P

step_size = 0.05
lift_weight = 6.0
gravity_couple = 0.5
density_couple = 0.3
theta_couple = 0.4

NODES = 4
POINTS = NODES * NODES
FIELDS = 5
FACE_POINTS = ((0, 4, 8, 12), (3, 7, 11, 15), (0, 1, 2, 3), (12, 13, 14, 15))
RIM_POINTS = tuple(sorted(set(sum(FACE_POINTS, ()))))
ROWS = 8
LATE_FIELDS = (0, 1, 2, 4)
WAYS = ((2, 1), (3, 2), (1, 3), (0, 0))


def derivative_table():
    points = np.array([-1.0, -1.0 / np.sqrt(5.0), 1.0 / np.sqrt(5.0), 1.0])
    number = points.shape[0]
    barycentric = np.ones(number)
    for source in range(number):
        for another in range(number):
            if another != source:
                barycentric[source] = barycentric[source] / (points[source] - points[another])
    matrix = np.zeros((number, number))
    for target in range(number):
        for source in range(number):
            if target != source:
                matrix[target, source] = (
                    barycentric[source] / barycentric[target] / (points[target] - points[source])
                )
        matrix[target, target] = -np.sum(matrix[target])
    return matrix


def operator_tables(lanes):
    weight = 0.5 * lift_weight
    table = derivative_table()
    table[0, 0] += weight
    table[-1, -1] -= weight
    eye = np.eye(NODES)
    along_first = np.kron(eye, table)
    along_second = np.kron(table, eye)
    ends = np.zeros(NODES)
    ends[0] = ends[-1] = 1.0
    faces = np.diag(np.kron(np.ones(NODES), ends) + np.kron(ends, np.ones(NODES)))
    first = np.zeros((POINTS, lanes))
    second = np.zeros((POINTS, lanes))
    same = np.zeros((FIELDS, POINTS, lanes))
    owner = np.full((lanes,), -1)
    for g in range(FIELDS):
        own = slice(POINTS * g, POINTS * (g + 1))
        first[:, own] = -along_first
        second[:, own] = -along_second
        same[g, :, own] = -weight * faces
        owner[own] = g
        for k in range(NODES):
            south = FIELDS * POINTS + 2 * NODES * g + k
            north = south + NODES
            second[FACE_POINTS[2][k], south] = weight
            second[FACE_POINTS[3][k], north] = -weight
            same[g, FACE_POINTS[2][k], south] = weight
            same[g, FACE_POINTS[3][k], north] = weight
            owner[south] = owner[north] = g
    tables = np.concatenate([first, second, same.reshape(FIELDS * POINTS, lanes)])
    return tables.astype(np.float32), owner


def chunks(total):
    return [min(start, total - ROWS) for start in range(0, total, ROWS)]


def partner_block(ways):
    odd = lax.rem(lax.axis_index("hy"), 2)
    return lax.axis_index("vz") ^ jnp.where(odd == 1, ways[1], ways[0])


def partner_side(partner):
    odd = lax.rem(lax.axis_index("hy"), 2)
    return odd if partner else 1 - odd


def side_sign(side):
    return (2 * side - 1).astype(jnp.float32)


def ends(total):
    return list(range(0, total, ROWS))


def pick(values, masks, flip):
    chosen = []
    for k in range(NODES):
        row = values[FACE_POINTS[0][k]]
        for option in range(1, 4):
            row = jnp.where(masks[option], values[FACE_POINTS[option][k]], row)
        chosen.append(row)
    return [jnp.where(flip, chosen[NODES - 1 - k], chosen[k]) for k in range(NODES)]


def table_masks(face_row, flip_row, lanes):
    face = jnp.broadcast_to(face_row, (ROWS, lanes))
    flip = jnp.broadcast_to(flip_row, (ROWS, lanes))
    return [face == option for option in range(4)], flip == 1


def flux_row(f, g, matrix):
    return (matrix * FIELDS + f) * FIELDS + g


def along(fluxes, matrix, f, rows):
    total = None
    for g in range(FIELDS):
        at = flux_row(f, g, matrix)
        term = fluxes[at : at + 1, :] * rows[g]
        total = term if total is None else total + term
    return total


def side_rows(f, piece):
    number = 3 * f + piece
    return number // 4, 32 * (number % 4)


def rim_kernel(
    state_hbm,
    face_hbm,
    way_hbm,
    metric_hbm,
    tables_hbm,
    flux_hbm,
    second_hbm,
    to_other,
    state,
    neighbour_face,
    orientation,
    metric,
    tables,
    fluxes,
    column,
    speed,
    flux,
    second_flux,
    semaphores,
):
    levels = state.shape[1] // POINTS
    face = partner_side(1)
    sign = side_sign(face)
    lanes = state.shape[2]
    width = len(RIM_POINTS)
    groups = [(start, min(start + ROWS, levels)) for start in range(0, levels, ROWS)]
    small = [
        pltpu.make_async_copy(source, target, semaphores.at[place])
        for place, (source, target) in enumerate(
            (
                (flux_hbm, flux),
                (face_hbm, neighbour_face),
                (way_hbm, orientation),
                (metric_hbm, metric),
                (tables_hbm, tables),
                (second_hbm, second_flux),
            )
        )
    ]
    large = []
    for place, (low, high) in enumerate(groups):
        rows = pl.ds(low * POINTS, (high - low) * POINTS)
        large.append(
            pltpu.make_async_copy(
                state_hbm.at[:, rows, :], state.at[:, rows, :], semaphores.at[len(small) + place]
            )
        )
    for copy in small[:1] + large + small[1:]:
        copy.start()
    column[...] = jnp.zeros_like(column)
    small[0].wait()
    arrived = 0
    for piece, start in enumerate(chunks(levels)):
        while arrived < len(groups) and groups[arrived][0] < start + ROWS:
            large[arrived].wait()
            arrived += 1
        for place, point in enumerate(RIM_POINTS):
            rows = [
                state[g, pl.ds(start * POINTS + point, ROWS, stride=POINTS), :]
                for g in range(FIELDS)
            ]
            for f, out in ((3, speed), (4, column)):
                normal = (sign * flux[f, 0]) * rows[0]
                for g in range(1, FIELDS):
                    normal = normal + (sign * flux[f, g]) * rows[g]
                out[place, pl.ds(ROWS + start, ROWS), :] = rows[f] + normal
    small[1].wait()
    small[2].wait()
    end = (levels + 2) * width
    for place in range(width):
        for start in chunks(levels):
            upper = column[place, pl.ds(ROWS + start + 1, ROWS), :]
            lower = column[place, pl.ds(ROWS + start - 1, ROWS), :]
            to_other[pl.ds(start * width + place, ROWS, stride=width), :] = speed[
                place, pl.ds(ROWS + start, ROWS), :
            ] - gravity_couple * (upper - lower)
        for extra, level in ((0, 0), (1, levels - 1)):
            at = (levels + extra) * width + place
            to_other[at : at + 1, :] = column[place, ROWS + level : ROWS + level + 1, :]
    to_other[end : end + 1, :] = neighbour_face[pl.ds(face, 1), :].astype(jnp.float32)
    to_other[end + 1 : end + 2, :] = orientation[pl.ds(face, 1), :].astype(jnp.float32)
    left = to_other.shape[0] - end - 2
    to_other[end + 2 :, :] = jnp.zeros((left, lanes), jnp.float32)
    small[3].wait()
    small[4].wait()
    small[5].wait()
    for place, source in enumerate((flux, second_flux)):
        for f in range(FIELDS):
            for g in range(FIELDS):
                at = flux_row(f, g, place)
                fluxes[at : at + 1, :] = jnp.full((1, lanes), source[f, g])


def edge_kernel(state, to_sides):
    lanes = state.shape[1]
    levels = state.shape[0] // (FIELDS * POINTS)
    lane = lax.broadcasted_iota(jnp.int32, (ROWS, lanes), 1)
    packed = [jnp.zeros((ROWS, lanes), jnp.float32) for _ in range(to_sides.shape[0] // ROWS)]
    for f in range(FIELDS):
        for piece, start in enumerate(chunks(levels)):
            block, at = side_rows(f, piece)
            for place, point in enumerate(RIM_POINTS):
                row = state[pl.ds((f * levels + start) * POINTS + point, ROWS, stride=POINTS), :]
                first = at + 2 * place
                packed[block] = jnp.where(
                    lane // 2 == first // 2, pltpu.roll(row, first + 1, 1), packed[block]
                )
    for block, value in enumerate(packed):
        to_sides[block * ROWS : (block + 1) * ROWS, :] = value


def near_kernel(
    state, neighbour_face, orientation, fluxes, base, metric, half, late, column, source
):
    lanes = state.shape[1]
    levels = state.shape[0] // (FIELDS * POINTS)
    face = partner_side(0)
    sign = -side_sign(face)
    masks, flip = table_masks(
        neighbour_face[pl.ds(face, 1), :], orientation[pl.ds(face, 1), :], lanes
    )
    column[...] = jnp.zeros_like(column)
    speeds = []
    for start in chunks(levels):
        picked = []
        for g in range(FIELDS):
            values = {
                point: state[pl.ds((g * levels + start) * POINTS + point, ROWS, stride=POINTS), :]
                for point in RIM_POINTS
            }
            picked.append(pick(values, masks, flip))
        for k in range(NODES):
            rows = [picked[g][k] for g in range(FIELDS)]
            changed = [rows[f] + sign * along(fluxes, 0, f, rows) for f in range(FIELDS)]
            for place, f in enumerate(LATE_FIELDS):
                at = (place * levels + start) * NODES + k
                late[pl.ds(at, ROWS, stride=NODES), :] = changed[f]
            column[k, pl.ds(ROWS + start, ROWS), :] = changed[4]
            speeds.append(changed[3])
    for piece, start in enumerate(chunks(levels)):
        for k in range(NODES):
            upper = column[k, pl.ds(ROWS + start + 1, ROWS), :]
            lower = column[k, pl.ds(ROWS + start - 1, ROWS), :]
            source[pl.ds(start * NODES + k, ROWS, stride=NODES), :] = speeds[
                NODES * piece + k
            ] - gravity_couple * (upper - lower)
    for extra, level in ((0, 0), (1, levels - 1)):
        for k in range(NODES):
            at = (levels + extra) * NODES + k
            source[at : at + 1, :] = column[k, ROWS + level : ROWS + level + 1, :]
    half[...] = base[...]
    for start in chunks(levels + 2):
        picked = [source[pl.ds(start * NODES + k, ROWS, stride=NODES), :] for k in range(NODES)]
        add_first_side(0, start, picked, half, base, metric)


def face_kernel(partner, state, received, fluxes, *rest):
    lanes = state.shape[1]
    levels = state.shape[0] // (FIELDS * POINTS)
    at = (levels + 2) * len(RIM_POINTS)
    outs = rest[-2:]
    share = len(LATE_FIELDS) // len(outs)
    sign = side_sign(partner_side(partner))
    masks, flip = table_masks(
        received[at : at + 1, :].astype(jnp.int32),
        received[at + 1 : at + 2, :].astype(jnp.int32),
        lanes,
    )
    for start in chunks(levels):
        picked = []
        for g in range(FIELDS):
            values = {
                point: state[pl.ds((g * levels + start) * POINTS + point, ROWS, stride=POINTS), :]
                for point in RIM_POINTS
            }
            picked.append(pick(values, masks, flip))
        for place, f in enumerate(LATE_FIELDS):
            for k in range(NODES):
                normal = along(fluxes, 0, f, [picked[g][k] for g in range(FIELDS)])
                at = ((place % share) * levels + start) * NODES + k
                outs[place // share][pl.ds(at, ROWS, stride=NODES), :] = (
                    picked[f][k] + sign * normal
                )


def element_kernel(
    state,
    neighbour_face,
    orientation,
    metric,
    fluxes,
    tables,
    part,
    base,
    outer,
    operator_high,
    operator_low,
):
    levels = state.shape[0] // (FIELDS * POINTS)
    lanes = state.shape[1]
    lane = lax.broadcasted_iota(jnp.int32, (ROWS, lanes), 1)
    sides = []
    for side, (face, edge) in enumerate(((2, 0), (3, lanes - 1))):
        shift = 1 if side == 0 else lanes - 1
        row = jnp.broadcast_to(neighbour_face[face : face + 1, :], (ROWS, lanes))
        way = jnp.broadcast_to(orientation[face : face + 1, :], (ROWS, lanes))
        masks, flip = table_masks(
            pltpu.roll(row, lanes - shift, 1), pltpu.roll(way, lanes - shift, 1), lanes
        )
        sides.append((shift, edge, masks, flip))
    for f in range(FIELDS):
        for start in chunks(levels):
            q = f * levels + start
            values = {
                point: state[pl.ds(q * POINTS + point, ROWS, stride=POINTS), :]
                for point in RIM_POINTS
            }
            for side, (shift, edge, masks, flip) in enumerate(sides):
                for k, row in enumerate(pick(values, masks, flip)):
                    at = start * 8 * FIELDS + 8 * f + NODES * side + k
                    outer[pl.ds(at, ROWS, stride=8 * FIELDS), :] = jnp.where(
                        lane == edge, 0.0, pltpu.roll(row, shift, 1)
                    )
    index = lax.broadcasted_iota(jnp.int32, (1, lanes), 1)
    own_columns = FIELDS * POINTS
    owner = jnp.where(index < own_columns, index // POINTS, (index - own_columns) // 8)
    for f in range(FIELDS):
        first_row = jnp.zeros((1, lanes), jnp.float32)
        second_row = first_row
        for g in range(FIELDS):
            first, second = (flux_row(f, g, matrix) for matrix in range(2))
            first_row = jnp.where(owner == g, fluxes[first : first + 1, :], first_row)
            second_row = jnp.where(owner == g, fluxes[second : second + 1, :], second_row)
        block = (
            first_row * tables[0:POINTS, :]
            + second_row * tables[POINTS : 2 * POINTS, :]
            + tables[(2 + f) * POINTS : (3 + f) * POINTS, :]
        )
        high = block.astype(jnp.bfloat16)
        operator_high[f * POINTS : (f + 1) * POINTS, :] = high
        operator_low[f * POINTS : (f + 1) * POINTS, :] = (
            block - high.astype(jnp.float32)
        ).astype(jnp.bfloat16)
    high = operator_high[...]
    low = operator_low[...]
    scale = step_size * metric[...]
    blank = jnp.zeros((lanes - own_columns - 8 * FIELDS, lanes), jnp.float32)
    for pair in range(0, levels, 2):
        sides = []
        for level in (pair, pair + 1):
            rows = [
                state[pl.ds((f * levels + level) * POINTS, POINTS), :] for f in range(FIELDS)
            ]
            rows.append(outer[pl.ds(level * 8 * FIELDS, 8 * FIELDS), :])
            rows.append(blank)
            sides.append(jnp.concatenate(rows, axis=0))
        values = jnp.concatenate(sides, axis=1)
        top = values.astype(jnp.bfloat16)
        rest = (values - top.astype(jnp.float32)).astype(jnp.bfloat16)
        change = (
            jnp.dot(high, top, preferred_element_type=jnp.float32)
            + jnp.dot(high, rest, preferred_element_type=jnp.float32)
            + jnp.dot(low, top, preferred_element_type=jnp.float32)
        )
        for place, level in enumerate((pair, pair + 1)):
            for f in range(FIELDS):
                at = pl.ds((f * levels + level) * POINTS, POINTS)
                part[at, :] = (
                    state[at, :]
                    + scale
                    * change[
                        f * POINTS : (f + 1) * POINTS, place * lanes : (place + 1) * lanes
                    ]
                )
    for level in range(levels):
        speed = part[pl.ds((3 * levels + level) * POINTS, POINTS), :]
        upper = part[pl.ds((4 * levels + level + 1) * POINTS, POINTS), :] if level < levels - 1 else 0.0
        lower = part[pl.ds((4 * levels + level - 1) * POINTS, POINTS), :] if level else 0.0
        value = speed - gravity_couple * (upper - lower)
        for j in range(NODES):
            base[j, level * NODES : (level + 1) * NODES, :] = value[NODES * j : NODES * (j + 1)]
    for extra, level in ((0, 0), (1, levels - 1)):
        value = part[pl.ds((4 * levels + level) * POINTS, POINTS), :]
        at = (levels + extra) * NODES
        for j in range(NODES):
            base[j, at : at + NODES, :] = value[NODES * j : NODES * (j + 1)]


def side_corrections(received, side, fluxes, fields, pieces):
    lanes = received.shape[1]
    sign = 1.0 if side == 0 else -1.0
    result = [[] for _ in fields]
    for piece in range(pieces):
        rows = []
        for g in range(FIELDS):
            block, at = side_rows(g, piece)
            rows.append(
                pltpu.roll(
                    received[block * ROWS : (block + 1) * ROWS, :], (lanes - at - side) % lanes, 1
                )
            )
        for place, f in enumerate(fields):
            result[place].append(rows[f] + sign * along(fluxes, 1, f, rows))
    return result


def spread(value, edge, masks, flip):
    lanes = value.shape[1]
    values = {
        point: pltpu.roll(value, (edge - 2 * place) % lanes, 1)
        for place, point in enumerate(RIM_POINTS)
    }
    return pick(values, masks, flip)


def add_first_side(partner, start, picked, send, base, metric):
    weight = 0.5 * lift_weight * step_size
    i = (NODES - 1) * partner_side(partner)
    for j, row in enumerate(picked):
        at = pl.ds(start * NODES + i, ROWS, stride=NODES)
        scale = weight * metric[pl.ds(NODES * j + i, 1), :]
        send[j, at, :] = base[j, at, :] + scale * row


def pack_kernel(half, from_other, neighbour_face, orientation, metric, *rest):
    sends, (send,) = rest[:NODES], rest[NODES:]
    send[...] = half[...]
    rows, lanes = half.shape[1:]
    width = len(RIM_POINTS)
    face = partner_side(1)
    masks, flip = table_masks(
        neighbour_face[pl.ds(face, 1), :], orientation[pl.ds(face, 1), :], lanes
    )
    for start in chunks(rows // NODES):
        values = {
            point: from_other[pl.ds(start * width + place, ROWS, stride=width), :]
            for place, point in enumerate(RIM_POINTS)
        }
        add_first_side(1, start, pick(values, masks, flip), send, half, metric)
    for out, ways in zip(sends, WAYS):
        out[...] = send[partner_block(ways)]


def half_pack_kernel(
    base,
    from_down,
    from_up,
    neighbour_face,
    orientation,
    metric,
    fluxes,
    factored,
    half,
    send,
    column,
    mixed,
):
    rows, lanes = base.shape[1:]
    levels = rows // NODES - 2
    width = len(RIM_POINTS)
    weight = 0.5 * lift_weight * step_size
    send[:, 0:rows, :] = base[...]
    send[:, rows:, :] = jnp.zeros((NODES, send.shape[1] - rows, lanes), jnp.float32)
    column[...] = jnp.zeros_like(column)
    mixed[...] = jnp.zeros_like(mixed)
    lane = lax.broadcasted_iota(jnp.int32, (ROWS, lanes), 1)
    for side, (received, edge, j) in enumerate(
        ((from_down, 0, 0), (from_up, lanes - 1, NODES - 1))
    ):
        face = 2 + side
        masks, flip = table_masks(
            neighbour_face[face : face + 1, :], orientation[face : face + 1, :], lanes
        )
        speed, heat = side_corrections(received, side, fluxes, (3, 4), len(chunks(levels)))
        for start, value in zip(chunks(levels), heat):
            column[pl.ds(ROWS + start, ROWS), :] = value
        for start, value in zip(chunks(levels), speed):
            upper = column[pl.ds(ROWS + start + 1, ROWS), :]
            lower = column[pl.ds(ROWS + start - 1, ROWS), :]
            mixed[pl.ds(start, ROWS), :] = value - gravity_couple * (upper - lower)
        mixed[levels : levels + 1, :] = column[ROWS : ROWS + 1, :]
        mixed[levels + 1 : levels + 2, :] = column[ROWS + levels - 1 : ROWS + levels, :]
        for start in ends(levels + 2):
            picked = spread(mixed[start : start + ROWS, :], edge, masks, flip)
            for k, row in enumerate(picked):
                point = NODES * j + k
                at = pl.ds(start * NODES + k, ROWS, stride=NODES)
                scale = weight * metric[point : point + 1, :]
                send[j, at, :] += jnp.where(lane == edge, scale * row, 0.0)
    half[...] = send[:, 0:rows, :]


def finish_section_kernel(
    part,
    near,
    other_early,
    other_late,
    from_down,
    from_up,
    neighbour_face,
    orientation,
    metric,
    fluxes,
    out,
    done,
    final,
    semaphore,
):
    levels = part.shape[0] // (FIELDS * POINTS)
    lanes = part.shape[1]
    size = levels * POINTS
    weight = 0.5 * lift_weight * step_size
    scale = weight * metric[...]
    lane = lax.broadcasted_iota(jnp.int32, (ROWS, lanes), 1)
    tables = []
    edges = []
    for side, received in enumerate((from_down, from_up)):
        face = 2 + side
        tables.append(
            table_masks(
                neighbour_face[face : face + 1, :], orientation[face : face + 1, :], lanes
            )
        )
        edges.append(
            side_corrections(received, side, fluxes, LATE_FIELDS, len(chunks(levels)))
        )
    copy = pltpu.make_async_copy(final, out.at[1:3], semaphore)
    sources = ((near,), (other_early, other_late))
    for place, f in ((1, 1), (2, 2), (0, 0), (3, 4)):
        target = final.at[f - 1] if f in (1, 2) else done.at[min(f, 1)]
        target[...] = part[f * size : (f + 1) * size, :]
        for piece, start in enumerate(chunks(levels)):
            for j in range(NODES):
                for partner, source in enumerate(sources):
                    point = NODES * j + (NODES - 1) * partner_side(partner)
                    share = len(LATE_FIELDS) // len(source)
                    rows = source[place // share][
                        pl.ds(((place % share) * levels + start) * NODES + j, ROWS, stride=NODES),
                        :,
                    ]
                    at = pl.ds(start * POINTS + point, ROWS, stride=POINTS)
                    target[at, :] = (
                        part[pl.ds(f * size + start * POINTS + point, ROWS, stride=POINTS), :]
                        + weight * metric[pl.ds(point, 1), :] * rows
                    )
        for piece, start in enumerate(chunks(levels)):
            row_index = lax.broadcasted_iota(jnp.int32, (ROWS, lanes), 0)
            fresh = row_index >= (-start) % ROWS
            for side, (edge, j) in enumerate(((0, 0), (lanes - 1, NODES - 1))):
                picked = spread(edges[side][place][piece], edge, *tables[side])
                for k, row in enumerate(picked):
                    point = NODES * j + k
                    at = pl.ds(start * POINTS + point, ROWS, stride=POINTS)
                    target[at, :] += jnp.where(
                        (lane == edge) & fresh, scale[point : point + 1, :] * row, 0.0
                    )
        if f == 2:
            copy.start()
    copy.wait()


def factor_kernel(coupling, damping, far, near, inverse, ratio, second):
    levels = coupling.shape[1]
    shape = coupling.shape[2:]
    blank = jnp.zeros(shape, jnp.float32)
    far_ratio, far_second, near_ratio, near_second = (blank,) * 4
    extra = damping[...]
    for level in range(levels):
        a, b, d, e = (coupling[entry, level] for entry in range(4))
        centre = a + b + d + e + extra
        reduced = -b + a * far_ratio
        pivot = centre + a * far_second - reduced * near_ratio
        scaled = 1.0 / pivot
        upper_ratio = (-d - reduced * near_second) * scaled
        second_ratio = -e * scaled
        far[level] = a * scaled
        near[level] = reduced * scaled
        inverse[level] = scaled
        ratio[level] = upper_ratio
        second[level] = second_ratio
        far_ratio, far_second = near_ratio, near_second
        near_ratio, near_second = upper_ratio, second_ratio


def solve_kernel(far, near, inverse, ratio, second, *rest):
    ways = NODES
    received, sends, (source, heat, speed) = rest[:ways], rest[ways : 2 * ways], rest[2 * ways :]
    levels = far.shape[0]
    here = levels // ways
    for values, step in zip(received, WAYS):
        block = partner_block(step)
        source[pl.ds(block * here, here)] = values[0:here]
        heat[block] = values[here : here + 2]
    for block in range(ways - 1):
        last = block * here + here - 1
        source[last] = source[last] - gravity_couple * heat[block + 1, 0]
        source[last + 1] = source[last + 1] + gravity_couple * heat[block, 1]
    blank = jnp.zeros(far.shape[1:], jnp.float32)
    before_two, before_one = blank, blank
    for level in range(levels):
        value = source[level] * inverse[level]
        value = value + far[level] * before_two
        value = value - near[level] * before_one
        source[level] = value
        before_two, before_one = before_one, value
    speed[0] = blank
    speed[levels + 1] = blank
    next_one, next_two = blank, blank
    for level in range(levels - 1, -1, -1):
        value = source[level] - second[level] * next_two
        value = value - ratio[level] * next_one
        speed[level + 1] = value
        next_two, next_one = next_one, value
    for send, step in zip(sends, WAYS):
        send[...] = speed[pl.ds(partner_block(step) * here, here + 2)]


def update_kernel(*refs):
    ways = NODES
    received, (done, earlier, out, speed, final, semaphores) = refs[:ways], refs[ways:]
    levels = done.shape[1] // POINTS
    for values, step in zip(received, WAYS):
        speed[partner_block(step)] = values[...]
    lanes = done.shape[2]
    half = levels // 2
    low = lax.broadcasted_iota(jnp.int32, (ROWS, lanes), 0) < NODES
    copies = []
    for pair in range(half):
        lower = [speed[j, pair * ROWS : (pair + 1) * ROWS, :] for j in range(NODES)]
        upper = [speed[j, (pair + 1) * ROWS : (pair + 2) * ROWS, :] for j in range(NODES)]
        jump = [above - below for above, below in zip(upper, lower)]
        value = [jnp.where(low, above, below) for above, below in zip(upper, lower)]
        for h in range(2):
            a, b = 2 * h, 2 * h + 1
            for odd in range(2):
                at = pl.ds((2 * pair + odd) * POINTS + ROWS * h, ROWS)
                jumps = side_by_side(jump[a], jump[b], odd, low)
                final[0, at, :] = done[0, at, :] - density_couple * jumps
                final[1, at, :] = side_by_side(value[a], value[b], 1 - odd, low)
                final[2, at, :] = done[1, at, :] - theta_couple * jumps
        if pair in (half // 2 - 1, half - 1):
            first = 0 if pair < half - 1 else half // 2
            rows = pl.ds(first * 2 * POINTS, (pair + 1 - first) * 2 * POINTS)
            for place, f in enumerate((0, 3, 4)):
                copies.append(
                    pltpu.make_async_copy(
                        final.at[place, rows, :], out.at[f, rows, :], semaphores.at[len(copies)]
                    )
                )
                copies[-1].start()
    for copy in copies:
        copy.wait()


def side_by_side(first, second, upper, low):
    if upper:
        return jnp.where(low, pltpu.roll(first, NODES, 0), second)
    return jnp.where(low, first, pltpu.roll(second, NODES, 0))


VMEM = pl.BlockSpec(memory_space=pltpu.VMEM)
HBM = pl.BlockSpec(memory_space=pltpu.HBM)
ANY = pl.BlockSpec(memory_space=pl.ANY)


def call(kernel, outs, in_specs, scratch=(), cost=0, name=None):
    kinds = [x if hasattr(x, "dtype") else pltpu.VMEM(x, jnp.float32) for x in outs]
    return pl.pallas_call(
        kernel,
        out_shape=kinds,
        in_specs=in_specs,
        out_specs=[VMEM] * len(outs),
        scratch_shapes=list(scratch),
        compiler_params=pltpu.CompilerParams(vmem_limit_bytes=24 * 1024 * 1024),
        cost_estimate=pl.CostEstimate(flops=cost, bytes_accessed=cost, transcendentals=0),
        name=name,
    )


def per_device(
    prognostic, metric, first_flux, second_flux, neighbour_face, orientation, coupling, damping
):
    fields, levels = prognostic.shape[:2]
    lanes = prognostic.shape[-1]
    whole = (fields, levels * POINTS, lanes)
    metric = metric.reshape(POINTS, lanes)
    neighbour_face = neighbour_face.reshape(4, lanes)
    orientation = orientation.reshape(4, lanes)
    coupling = coupling.reshape(4, coupling.shape[1], NODES, lanes)
    damping = damping.reshape(NODES, lanes)
    tables, _ = operator_tables(lanes)

    def shifts(axis):
        size = lax.axis_size(axis)
        up = [(i, (i + 1) % size) for i in range(size)]
        return up, [(j, i) for i, j in up]

    def exchange(arrays):
        rows, size = lax.axis_size("hy"), lax.axis_size("vz")
        moved = []
        for x, ways in zip(arrays, WAYS):
            pairs = [
                (row * size + i, row * size + (i ^ ways[row % 2]))
                for row in range(rows)
                for i in range(size)
            ]
            moved.append(lax.ppermute(x, ("hy", "vz"), pairs) if any(ways) else x)
        return moved

    count = lax.axis_size("hy")
    near = [(i, i ^ 1) for i in range(count)]
    other = [(i, (i + 1 if i % 2 else i - 1) % count) for i in range(count)]
    second_up, second_down = shifts("hx")
    width = len(RIM_POINTS)
    message = (-(-((levels + 2) * width + 2) // ROWS) * ROWS, lanes)
    sides = (-(-fields * len(chunks(levels)) // 4) * ROWS, lanes)
    padded = levels + 2 * ROWS
    table = pltpu.VMEM((4, lanes), jnp.int32)
    inputs = (
        prognostic.reshape(whole),
        neighbour_face,
        orientation,
        metric,
        jnp.asarray(tables),
        first_flux,
        second_flux,
    )
    (
        to_other,
        state,
        neighbour_face,
        orientation,
        metric,
        tables,
        fluxes,
    ) = call(
        rim_kernel,
        [
            message,
            whole,
            table,
            table,
            (POINTS, lanes),
            tables.shape,
            (-(-2 * fields * fields // ROWS) * ROWS, lanes),
        ],
        [HBM] * len(inputs),
        [
            pltpu.VMEM((width, padded, lanes), jnp.float32),
            pltpu.VMEM((width, padded, lanes), jnp.float32),
            pltpu.SMEM((fields, fields), jnp.float32),
            pltpu.SMEM((fields, fields), jnp.float32),
            pltpu.SemaphoreType.DMA((6 + -(-levels // ROWS),)),
        ],
        cost=1000,
        name="rim",
    )(*(pltpu.with_memory_space_constraint(x, pltpu.HBM) for x in inputs))
    state = state.reshape(fields * levels * POINTS, lanes)
    from_other = lax.ppermute(to_other, "hy", other)
    from_near = lax.ppermute(state, "hy", near)
    (to_sides,) = call(edge_kernel, [sides], [VMEM], cost=1000, name="edge")(state)
    from_down = lax.ppermute(to_sides, "hx", second_up)
    from_up = from_down
    if lax.axis_size("hx") > 2:
        from_up = lax.ppermute(to_sides, "hx", second_down)

    column = (coupling.shape[1], NODES, lanes)
    factors = call(factor_kernel, [column] * 5, [VMEM] * 2, cost=4000000, name="factor")(
        coupling, damping
    )
    block = ((levels + 2) * NODES, lanes)
    part, base = call(
        element_kernel,
        [state.shape, (NODES,) + block],
        [VMEM] * 6,
        [
            pltpu.VMEM((levels * 8 * fields, lanes), jnp.float32),
            pltpu.VMEM((fields * POINTS, lanes), jnp.bfloat16),
            pltpu.VMEM((fields * POINTS, lanes), jnp.bfloat16),
        ],
        cost=4000000,
        name="element",
    )(
        state,
        neighbour_face,
        orientation,
        metric,
        fluxes,
        tables,
    )
    late = levels * NODES * len(LATE_FIELDS)
    base, near_late = call(
        near_kernel,
        [(NODES,) + block, (late, lanes)],
        [VMEM] * 6,
        [pltpu.VMEM((NODES, padded, lanes), jnp.float32), pltpu.VMEM(block, jnp.float32)],
        cost=1000,
        name="near",
    )(from_near, neighbour_face, orientation, fluxes, base, metric)
    count = -(-(levels + 2) // ROWS) * ROWS
    (half,) = call(
        half_pack_kernel,
        [(NODES,) + block],
        [VMEM] * 7 + [ANY],
        [
            pltpu.VMEM((NODES, count * NODES, lanes), jnp.float32),
            pltpu.VMEM((padded, lanes), jnp.float32),
            pltpu.VMEM((count, lanes), jnp.float32),
        ],
        cost=1000,
        name="half_pack",
    )(
        base,
        from_down,
        from_up,
        neighbour_face,
        orientation,
        metric,
        fluxes,
        factors[0],
    )
    sends = call(
        pack_kernel,
        [block] * NODES,
        [VMEM] * 5,
        [pltpu.VMEM((NODES,) + block, jnp.float32)],
        cost=1000,
        name="pack",
    )(half, from_other, neighbour_face, orientation, metric)
    received = exchange(sends)

    other_face = call(
        functools.partial(face_kernel, 1),
        [(late // 2, lanes)] * 2,
        [VMEM] * 3 + [ANY],
        cost=1000,
        name="other_face",
    )(state, from_other, fluxes, sends[-1])
    other_face = [lax.ppermute(x, "hy", other) for x in other_face]

    cube = (levels + 2, NODES, lanes)
    speeds = call(
        solve_kernel,
        [cube] * NODES,
        [VMEM] * (5 + NODES),
        [
            pltpu.VMEM(column, jnp.float32),
            pltpu.VMEM((NODES, 2, NODES, lanes), jnp.float32),
            pltpu.VMEM((column[0] + 2,) + column[1:], jnp.float32),
        ],
        cost=1000,
        name="solve",
    )(*factors, *[x.reshape(cube) for x in received])
    returned = exchange([x.reshape(block) for x in speeds])
    size = levels * POINTS
    limits = pltpu.CompilerParams(vmem_limit_bytes=24 * 1024 * 1024)
    earlier, done = pl.pallas_call(
        finish_section_kernel,
        out_shape=[
            jax.ShapeDtypeStruct(whole, jnp.float32),
            pltpu.VMEM((2, size, lanes), jnp.float32),
        ],
        in_specs=[VMEM] * 10,
        out_specs=[HBM, VMEM],
        scratch_shapes=[
            pltpu.VMEM((2, size, lanes), jnp.float32),
            pltpu.SemaphoreType.DMA,
        ],
        compiler_params=limits,
        cost_estimate=pl.CostEstimate(flops=4000000, bytes_accessed=4000000, transcendentals=0),
        name="finish",
    )(
        part, near_late, *other_face, from_down, from_up, neighbour_face, orientation, metric, fluxes
    )
    updated = pl.pallas_call(
        update_kernel,
        out_shape=jax.ShapeDtypeStruct(whole, jnp.float32),
        in_specs=[VMEM] * (1 + NODES) + [HBM],
        out_specs=HBM,
        input_output_aliases={1 + NODES: 0},
        scratch_shapes=[
            pltpu.VMEM((NODES,) + block, jnp.float32),
            pltpu.VMEM((3, size, lanes), jnp.float32),
            pltpu.SemaphoreType.DMA((6,)),
        ],
        compiler_params=limits,
        name="update",
    )(*returned, done, earlier)
    return updated.reshape(prognostic.shape)


def solution(mesh):
    placed = (
        P(None, "vz", None, None, "hy", "hx"),
        P(None, None, "hy", "hx"),
        P(),
        P(),
        P(None, "hy", "hx"),
        P(None, "hy", "hx"),
        P(None, None, "vz", None, "hy", "hx"),
        P("vz", None, "hy", "hx"),
    )
    return jax.shard_map(
        per_device,
        mesh=mesh,
        in_specs=placed,
        out_specs=P(None, "vz", None, None, "hy", "hx"),
        check_vma=False,
    )
```

```python
import functools

import jax
import jax.numpy as jnp
import numpy as np
from jax import lax
from jax.experimental import pallas as pl
from jax.experimental.pallas import tpu as pltpu
from jax.sharding import PartitionSpec as P

step_size = 0.05
lift_weight = 6.0
gravity_couple = 0.5
density_couple = 0.3
theta_couple = 0.4

NODES = 4
POINTS = NODES * NODES
FIELDS = 5
FACE_POINTS = ((0, 4, 8, 12), (3, 7, 11, 15), (0, 1, 2, 3), (12, 13, 14, 15))
RIM_POINTS = tuple(sorted(set(sum(FACE_POINTS, ()))))
ROWS = 8
LATE_FIELDS = (0, 1, 2, 4)
WAYS = (2, 3, 1, 0)
BACK_WAYS = (2, 3, 1, 0)


def derivative_table():
    points = np.array([-1.0, -1.0 / np.sqrt(5.0), 1.0 / np.sqrt(5.0), 1.0])
    number = points.shape[0]
    barycentric = np.ones(number)
    for source in range(number):
        for another in range(number):
            if another != source:
                barycentric[source] = barycentric[source] / (points[source] - points[another])
    matrix = np.zeros((number, number))
    for target in range(number):
        for source in range(number):
            if target != source:
                matrix[target, source] = (
                    barycentric[source] / barycentric[target] / (points[target] - points[source])
                )
        matrix[target, target] = -np.sum(matrix[target])
    return matrix


def operator_tables(lanes):
    weight = 0.5 * lift_weight
    table = derivative_table()
    table[0, 0] += weight
    table[-1, -1] -= weight
    eye = np.eye(NODES)
    along_first = np.kron(eye, table)
    along_second = np.kron(table, eye)
    ends = np.zeros(NODES)
    ends[0] = ends[-1] = 1.0
    faces = np.diag(np.kron(np.ones(NODES), ends) + np.kron(ends, np.ones(NODES)))
    first = np.zeros((POINTS, lanes))
    second = np.zeros((POINTS, lanes))
    same = np.zeros((FIELDS, POINTS, lanes))
    owner = np.full((lanes,), -1)
    for g in range(FIELDS):
        own = slice(POINTS * g, POINTS * (g + 1))
        first[:, own] = -along_first
        second[:, own] = -along_second
        same[g, :, own] = -weight * faces
        owner[own] = g
        for k in range(NODES):
            south = FIELDS * POINTS + 2 * NODES * g + k
            north = south + NODES
            second[FACE_POINTS[2][k], south] = weight
            second[FACE_POINTS[3][k], north] = -weight
            same[g, FACE_POINTS[2][k], south] = weight
            same[g, FACE_POINTS[3][k], north] = weight
            owner[south] = owner[north] = g
    tables = np.concatenate([first, second, same.reshape(FIELDS * POINTS, lanes)])
    return tables.astype(np.float32), owner


def chunks(total):
    return [min(start, total - ROWS) for start in range(0, total, ROWS)]


def partner_side(partner):
    odd = lax.rem(lax.axis_index("hy"), 2)
    return odd if partner else 1 - odd


def side_sign(side):
    return (2 * side - 1).astype(jnp.float32)


def ends(total):
    return list(range(0, total, ROWS))


def pick(values, masks, flip):
    chosen = []
    for k in range(NODES):
        row = values[FACE_POINTS[0][k]]
        for option in range(1, 4):
            row = jnp.where(masks[option], values[FACE_POINTS[option][k]], row)
        chosen.append(row)
    return [jnp.where(flip, chosen[NODES - 1 - k], chosen[k]) for k in range(NODES)]


def table_masks(face_row, flip_row, lanes):
    face = jnp.broadcast_to(face_row, (ROWS, lanes))
    flip = jnp.broadcast_to(flip_row, (ROWS, lanes))
    return [face == option for option in range(4)], flip == 1


def flux_row(f, g, matrix):
    return (matrix * FIELDS + f) * FIELDS + g


def along(fluxes, matrix, f, rows):
    total = None
    for g in range(FIELDS):
        at = flux_row(f, g, matrix)
        term = fluxes[at : at + 1, :] * rows[g]
        total = term if total is None else total + term
    return total


def side_rows(f, piece):
    number = 3 * f + piece
    return number // 4, 32 * (number % 4)


def rim_kernel(
    state_hbm,
    face_hbm,
    way_hbm,
    metric_hbm,
    tables_hbm,
    flux_hbm,
    second_hbm,
    to_other,
    state,
    neighbour_face,
    orientation,
    metric,
    tables,
    fluxes,
    column,
    speed,
    flux,
    second_flux,
    semaphores,
):
    levels = state.shape[1] // POINTS
    face = partner_side(1)
    sign = side_sign(face)
    lanes = state.shape[2]
    width = len(RIM_POINTS)
    small = [
        pltpu.make_async_copy(source, target, semaphores.at[place])
        for place, (source, target) in enumerate(
            (
                (flux_hbm, flux),
                (face_hbm, neighbour_face),
                (way_hbm, orientation),
                (metric_hbm, metric),
                (tables_hbm, tables),
                (second_hbm, second_flux),
            )
        )
    ]
    large = pltpu.make_async_copy(state_hbm, state, semaphores.at[len(small)])
    for copy in small[:1] + [large] + small[1:]:
        copy.start()
    column[...] = jnp.zeros_like(column)
    small[0].wait()
    large.wait()
    for start in chunks(levels):
        for place, point in enumerate(RIM_POINTS):
            rows = [
                state[g, pl.ds(start * POINTS + point, ROWS, stride=POINTS), :]
                for g in range(FIELDS)
            ]
            for f, out in ((3, speed), (4, column)):
                normal = (sign * flux[f, 0]) * rows[0]
                for g in range(1, FIELDS):
                    normal = normal + (sign * flux[f, g]) * rows[g]
                out[place, pl.ds(ROWS + start, ROWS), :] = rows[f] + normal
    small[1].wait()
    small[2].wait()
    end = (levels + 2) * width
    for place in range(width):
        for start in chunks(levels):
            upper = column[place, pl.ds(ROWS + start + 1, ROWS), :]
            lower = column[place, pl.ds(ROWS + start - 1, ROWS), :]
            to_other[pl.ds(start * width + place, ROWS, stride=width), :] = speed[
                place, pl.ds(ROWS + start, ROWS), :
            ] - gravity_couple * (upper - lower)
        for extra, level in ((0, 0), (1, levels - 1)):
            at = (levels + extra) * width + place
            to_other[at : at + 1, :] = column[place, ROWS + level : ROWS + level + 1, :]
    to_other[end : end + 1, :] = neighbour_face[pl.ds(face, 1), :].astype(jnp.float32)
    to_other[end + 1 : end + 2, :] = orientation[pl.ds(face, 1), :].astype(jnp.float32)
    left = to_other.shape[0] - end - 2
    to_other[end + 2 :, :] = jnp.zeros((left, lanes), jnp.float32)
    small[3].wait()
    small[4].wait()
    small[5].wait()
    for place, source in enumerate((flux, second_flux)):
        for f in range(FIELDS):
            for g in range(FIELDS):
                at = flux_row(f, g, place)
                fluxes[at : at + 1, :] = jnp.full((1, lanes), source[f, g])


def edge_kernel(state, to_sides):
    lanes = state.shape[1]
    levels = state.shape[0] // (FIELDS * POINTS)
    lane = lax.broadcasted_iota(jnp.int32, (ROWS, lanes), 1)
    packed = [jnp.zeros((ROWS, lanes), jnp.float32) for _ in range(to_sides.shape[0] // ROWS)]
    for f in range(FIELDS):
        for piece, start in enumerate(chunks(levels)):
            block, at = side_rows(f, piece)
            for place, point in enumerate(RIM_POINTS):
                row = state[pl.ds((f * levels + start) * POINTS + point, ROWS, stride=POINTS), :]
                first = at + 2 * place
                packed[block] = jnp.where(
                    lane // 2 == first // 2, pltpu.roll(row, first + 1, 1), packed[block]
                )
    for block, value in enumerate(packed):
        to_sides[block * ROWS : (block + 1) * ROWS, :] = value


def near_kernel(
    state, neighbour_face, orientation, fluxes, base, metric, half, late, column, source
):
    lanes = state.shape[1]
    levels = state.shape[0] // (FIELDS * POINTS)
    face = partner_side(0)
    sign = -side_sign(face)
    masks, flip = table_masks(
        neighbour_face[pl.ds(face, 1), :], orientation[pl.ds(face, 1), :], lanes
    )
    column[...] = jnp.zeros_like(column)
    speeds = []
    for start in chunks(levels):
        picked = []
        for g in range(FIELDS):
            values = {
                point: state[pl.ds((g * levels + start) * POINTS + point, ROWS, stride=POINTS), :]
                for point in RIM_POINTS
            }
            picked.append(pick(values, masks, flip))
        for k in range(NODES):
            rows = [picked[g][k] for g in range(FIELDS)]
            changed = [rows[f] + sign * along(fluxes, 0, f, rows) for f in range(FIELDS)]
            for place, f in enumerate(LATE_FIELDS):
                at = (place * levels + start) * NODES + k
                late[pl.ds(at, ROWS, stride=NODES), :] = changed[f]
            column[k, pl.ds(ROWS + start, ROWS), :] = changed[4]
            speeds.append(changed[3])
    for piece, start in enumerate(chunks(levels)):
        for k in range(NODES):
            upper = column[k, pl.ds(ROWS + start + 1, ROWS), :]
            lower = column[k, pl.ds(ROWS + start - 1, ROWS), :]
            source[pl.ds(start * NODES + k, ROWS, stride=NODES), :] = speeds[
                NODES * piece + k
            ] - gravity_couple * (upper - lower)
    for extra, level in ((0, 0), (1, levels - 1)):
        for k in range(NODES):
            at = (levels + extra) * NODES + k
            source[at : at + 1, :] = column[k, ROWS + level : ROWS + level + 1, :]
    half[...] = base[...]
    for start in chunks(levels + 2):
        picked = [source[pl.ds(start * NODES + k, ROWS, stride=NODES), :] for k in range(NODES)]
        add_first_side(0, start, picked, half, base, metric)


def face_kernel(partner, state, received, fluxes, *rest):
    lanes = state.shape[1]
    levels = state.shape[0] // (FIELDS * POINTS)
    at = (levels + 2) * len(RIM_POINTS)
    outs = rest[-2:]
    share = len(LATE_FIELDS) // len(outs)
    sign = side_sign(partner_side(partner))
    masks, flip = table_masks(
        received[at : at + 1, :].astype(jnp.int32),
        received[at + 1 : at + 2, :].astype(jnp.int32),
        lanes,
    )
    for start in chunks(levels):
        picked = []
        for g in range(FIELDS):
            values = {
                point: state[pl.ds((g * levels + start) * POINTS + point, ROWS, stride=POINTS), :]
                for point in RIM_POINTS
            }
            picked.append(pick(values, masks, flip))
        for place, f in enumerate(LATE_FIELDS):
            for k in range(NODES):
                normal = along(fluxes, 0, f, [picked[g][k] for g in range(FIELDS)])
                at = ((place % share) * levels + start) * NODES + k
                outs[place // share][pl.ds(at, ROWS, stride=NODES), :] = (
                    picked[f][k] + sign * normal
                )


def element_kernel(
    state,
    neighbour_face,
    orientation,
    metric,
    fluxes,
    tables,
    part,
    base,
    outer,
    operator_high,
    operator_low,
):
    levels = state.shape[0] // (FIELDS * POINTS)
    lanes = state.shape[1]
    lane = lax.broadcasted_iota(jnp.int32, (ROWS, lanes), 1)
    sides = []
    for side, (face, edge) in enumerate(((2, 0), (3, lanes - 1))):
        shift = 1 if side == 0 else lanes - 1
        row = jnp.broadcast_to(neighbour_face[face : face + 1, :], (ROWS, lanes))
        way = jnp.broadcast_to(orientation[face : face + 1, :], (ROWS, lanes))
        masks, flip = table_masks(
            pltpu.roll(row, lanes - shift, 1), pltpu.roll(way, lanes - shift, 1), lanes
        )
        sides.append((shift, edge, masks, flip))
    for f in range(FIELDS):
        for start in chunks(levels):
            q = f * levels + start
            values = {
                point: state[pl.ds(q * POINTS + point, ROWS, stride=POINTS), :]
                for point in RIM_POINTS
            }
            for side, (shift, edge, masks, flip) in enumerate(sides):
                for k, row in enumerate(pick(values, masks, flip)):
                    at = start * 8 * FIELDS + 8 * f + NODES * side + k
                    outer[pl.ds(at, ROWS, stride=8 * FIELDS), :] = jnp.where(
                        lane == edge, 0.0, pltpu.roll(row, shift, 1)
                    )
    index = lax.broadcasted_iota(jnp.int32, (1, lanes), 1)
    own_columns = FIELDS * POINTS
    owner = jnp.where(index < own_columns, index // POINTS, (index - own_columns) // 8)
    for f in range(FIELDS):
        first_row = jnp.zeros((1, lanes), jnp.float32)
        second_row = first_row
        for g in range(FIELDS):
            first, second = (flux_row(f, g, matrix) for matrix in range(2))
            first_row = jnp.where(owner == g, fluxes[first : first + 1, :], first_row)
            second_row = jnp.where(owner == g, fluxes[second : second + 1, :], second_row)
        block = (
            first_row * tables[0:POINTS, :]
            + second_row * tables[POINTS : 2 * POINTS, :]
            + tables[(2 + f) * POINTS : (3 + f) * POINTS, :]
        )
        high = block.astype(jnp.bfloat16)
        operator_high[f * POINTS : (f + 1) * POINTS, :] = high
        operator_low[f * POINTS : (f + 1) * POINTS, :] = (
            block - high.astype(jnp.float32)
        ).astype(jnp.bfloat16)
    high = operator_high[...]
    low = operator_low[...]
    scale = step_size * metric[...]
    blank = jnp.zeros((lanes - own_columns - 8 * FIELDS, lanes), jnp.float32)
    for pair in range(0, levels, 2):
        sides = []
        for level in (pair, pair + 1):
            rows = [
                state[pl.ds((f * levels + level) * POINTS, POINTS), :] for f in range(FIELDS)
            ]
            rows.append(outer[pl.ds(level * 8 * FIELDS, 8 * FIELDS), :])
            rows.append(blank)
            sides.append(jnp.concatenate(rows, axis=0))
        values = jnp.concatenate(sides, axis=1)
        top = values.astype(jnp.bfloat16)
        rest = (values - top.astype(jnp.float32)).astype(jnp.bfloat16)
        change = (
            jnp.dot(high, top, preferred_element_type=jnp.float32)
            + jnp.dot(high, rest, preferred_element_type=jnp.float32)
            + jnp.dot(low, top, preferred_element_type=jnp.float32)
        )
        for place, level in enumerate((pair, pair + 1)):
            for f in range(FIELDS):
                at = pl.ds((f * levels + level) * POINTS, POINTS)
                part[at, :] = (
                    state[at, :]
                    + scale
                    * change[
                        f * POINTS : (f + 1) * POINTS, place * lanes : (place + 1) * lanes
                    ]
                )
    for level in range(levels):
        speed = part[pl.ds((3 * levels + level) * POINTS, POINTS), :]
        upper = part[pl.ds((4 * levels + level + 1) * POINTS, POINTS), :] if level < levels - 1 else 0.0
        lower = part[pl.ds((4 * levels + level - 1) * POINTS, POINTS), :] if level else 0.0
        value = speed - gravity_couple * (upper - lower)
        for j in range(NODES):
            base[j, level * NODES : (level + 1) * NODES, :] = value[NODES * j : NODES * (j + 1)]
    for extra, level in ((0, 0), (1, levels - 1)):
        value = part[pl.ds((4 * levels + level) * POINTS, POINTS), :]
        at = (levels + extra) * NODES
        for j in range(NODES):
            base[j, at : at + NODES, :] = value[NODES * j : NODES * (j + 1)]


def side_corrections(received, side, fluxes, fields, pieces):
    lanes = received.shape[1]
    sign = 1.0 if side == 0 else -1.0
    result = [[] for _ in fields]
    for piece in range(pieces):
        rows = []
        for g in range(FIELDS):
            block, at = side_rows(g, piece)
            rows.append(
                pltpu.roll(
                    received[block * ROWS : (block + 1) * ROWS, :], (lanes - at - side) % lanes, 1
                )
            )
        for place, f in enumerate(fields):
            result[place].append(rows[f] + sign * along(fluxes, 1, f, rows))
    return result


def spread(value, edge, masks, flip):
    lanes = value.shape[1]
    values = {
        point: pltpu.roll(value, (edge - 2 * place) % lanes, 1)
        for place, point in enumerate(RIM_POINTS)
    }
    return pick(values, masks, flip)


def add_first_side(partner, start, picked, send, base, metric):
    weight = 0.5 * lift_weight * step_size
    i = (NODES - 1) * partner_side(partner)
    for j, row in enumerate(picked):
        at = pl.ds(start * NODES + i, ROWS, stride=NODES)
        scale = weight * metric[pl.ds(NODES * j + i, 1), :]
        send[j, at, :] = base[j, at, :] + scale * row


def pack_kernel(half, from_other, neighbour_face, orientation, metric, *rest):
    sends, (send,) = rest[:NODES], rest[NODES:]
    me = lax.axis_index("vz")
    send[...] = half[...]
    rows, lanes = half.shape[1:]
    width = len(RIM_POINTS)
    face = partner_side(1)
    masks, flip = table_masks(
        neighbour_face[pl.ds(face, 1), :], orientation[pl.ds(face, 1), :], lanes
    )
    for start in chunks(rows // NODES):
        values = {
            point: from_other[pl.ds(start * width + place, ROWS, stride=width), :]
            for place, point in enumerate(RIM_POINTS)
        }
        add_first_side(1, start, pick(values, masks, flip), send, half, metric)
    for out, way in zip(sends, WAYS):
        out[...] = send[me ^ way]


def half_pack_kernel(
    base,
    from_down,
    from_up,
    neighbour_face,
    orientation,
    metric,
    fluxes,
    factored,
    half,
    send,
    column,
    mixed,
):
    rows, lanes = base.shape[1:]
    levels = rows // NODES - 2
    width = len(RIM_POINTS)
    weight = 0.5 * lift_weight * step_size
    send[:, 0:rows, :] = base[...]
    send[:, rows:, :] = jnp.zeros((NODES, send.shape[1] - rows, lanes), jnp.float32)
    column[...] = jnp.zeros_like(column)
    mixed[...] = jnp.zeros_like(mixed)
    lane = lax.broadcasted_iota(jnp.int32, (ROWS, lanes), 1)
    for side, (received, edge, j) in enumerate(
        ((from_down, 0, 0), (from_up, lanes - 1, NODES - 1))
    ):
        face = 2 + side
        masks, flip = table_masks(
            neighbour_face[face : face + 1, :], orientation[face : face + 1, :], lanes
        )
        speed, heat = side_corrections(received, side, fluxes, (3, 4), len(chunks(levels)))
        for start, value in zip(chunks(levels), heat):
            column[pl.ds(ROWS + start, ROWS), :] = value
        for start, value in zip(chunks(levels), speed):
            upper = column[pl.ds(ROWS + start + 1, ROWS), :]
            lower = column[pl.ds(ROWS + start - 1, ROWS), :]
            mixed[pl.ds(start, ROWS), :] = value - gravity_couple * (upper - lower)
        mixed[levels : levels + 1, :] = column[ROWS : ROWS + 1, :]
        mixed[levels + 1 : levels + 2, :] = column[ROWS + levels - 1 : ROWS + levels, :]
        for start in ends(levels + 2):
            picked = spread(mixed[start : start + ROWS, :], edge, masks, flip)
            for k, row in enumerate(picked):
                point = NODES * j + k
                at = pl.ds(start * NODES + k, ROWS, stride=NODES)
                scale = weight * metric[point : point + 1, :]
                send[j, at, :] += jnp.where(lane == edge, scale * row, 0.0)
    half[...] = send[:, 0:rows, :]


def finish_section_kernel(
    part,
    near,
    other_early,
    other_late,
    from_down,
    from_up,
    neighbour_face,
    orientation,
    metric,
    fluxes,
    out,
    done,
    final,
    semaphore,
):
    levels = part.shape[0] // (FIELDS * POINTS)
    lanes = part.shape[1]
    size = levels * POINTS
    weight = 0.5 * lift_weight * step_size
    scale = weight * metric[...]
    lane = lax.broadcasted_iota(jnp.int32, (ROWS, lanes), 1)
    tables = []
    edges = []
    for side, received in enumerate((from_down, from_up)):
        face = 2 + side
        tables.append(
            table_masks(
                neighbour_face[face : face + 1, :], orientation[face : face + 1, :], lanes
            )
        )
        edges.append(
            side_corrections(received, side, fluxes, LATE_FIELDS, len(chunks(levels)))
        )
    copy = pltpu.make_async_copy(final, out.at[1:3], semaphore)
    sources = ((near,), (other_early, other_late))
    for place, f in ((1, 1), (2, 2), (0, 0), (3, 4)):
        target = final.at[f - 1] if f in (1, 2) else done.at[min(f, 1)]
        target[...] = part[f * size : (f + 1) * size, :]
        for piece, start in enumerate(chunks(levels)):
            for j in range(NODES):
                for partner, source in enumerate(sources):
                    point = NODES * j + (NODES - 1) * partner_side(partner)
                    share = len(LATE_FIELDS) // len(source)
                    rows = source[place // share][
                        pl.ds(((place % share) * levels + start) * NODES + j, ROWS, stride=NODES),
                        :,
                    ]
                    at = pl.ds(start * POINTS + point, ROWS, stride=POINTS)
                    target[at, :] = (
                        part[pl.ds(f * size + start * POINTS + point, ROWS, stride=POINTS), :]
                        + weight * metric[pl.ds(point, 1), :] * rows
                    )
        for piece, start in enumerate(chunks(levels)):
            row_index = lax.broadcasted_iota(jnp.int32, (ROWS, lanes), 0)
            fresh = row_index >= (-start) % ROWS
            for side, (edge, j) in enumerate(((0, 0), (lanes - 1, NODES - 1))):
                picked = spread(edges[side][place][piece], edge, *tables[side])
                for k, row in enumerate(picked):
                    point = NODES * j + k
                    at = pl.ds(start * POINTS + point, ROWS, stride=POINTS)
                    target[at, :] += jnp.where(
                        (lane == edge) & fresh, scale[point : point + 1, :] * row, 0.0
                    )
        if f == 2:
            copy.start()
    copy.wait()


def factor_kernel(coupling, damping, far, near, inverse, ratio, second):
    levels = coupling.shape[1]
    shape = coupling.shape[2:]
    blank = jnp.zeros(shape, jnp.float32)
    far_ratio, far_second, near_ratio, near_second = (blank,) * 4
    extra = damping[...]
    for level in range(levels):
        a, b, d, e = (coupling[entry, level] for entry in range(4))
        centre = a + b + d + e + extra
        reduced = -b + a * far_ratio
        pivot = centre + a * far_second - reduced * near_ratio
        scaled = 1.0 / pivot
        upper_ratio = (-d - reduced * near_second) * scaled
        second_ratio = -e * scaled
        far[level] = a * scaled
        near[level] = reduced * scaled
        inverse[level] = scaled
        ratio[level] = upper_ratio
        second[level] = second_ratio
        far_ratio, far_second = near_ratio, near_second
        near_ratio, near_second = upper_ratio, second_ratio


def solve_kernel(far, near, inverse, ratio, second, *rest):
    ways = NODES
    received, sends, (source, heat, speed) = rest[:ways], rest[ways : 2 * ways], rest[2 * ways :]
    levels = far.shape[0]
    here = levels // ways
    me = lax.axis_index("vz")
    for values, way in zip(received, WAYS):
        block = me ^ way
        source[pl.ds(block * here, here)] = values[0:here]
        heat[block] = values[here : here + 2]
    for block in range(ways - 1):
        last = block * here + here - 1
        source[last] = source[last] - gravity_couple * heat[block + 1, 0]
        source[last + 1] = source[last + 1] + gravity_couple * heat[block, 1]
    blank = jnp.zeros(far.shape[1:], jnp.float32)
    before_two, before_one = blank, blank
    for level in range(levels):
        value = source[level] * inverse[level]
        value = value + far[level] * before_two
        value = value - near[level] * before_one
        source[level] = value
        before_two, before_one = before_one, value
    speed[0] = blank
    speed[levels + 1] = blank
    next_one, next_two = blank, blank
    for level in range(levels - 1, -1, -1):
        value = source[level] - second[level] * next_two
        value = value - ratio[level] * next_one
        speed[level + 1] = value
        next_two, next_one = next_one, value
    for send, way in zip(sends, BACK_WAYS):
        send[...] = speed[pl.ds((me ^ way) * here, here + 2)]


def update_kernel(*refs):
    ways = NODES
    received, (done, earlier, out, speed, final, semaphores) = refs[:ways], refs[ways:]
    levels = done.shape[1] // POINTS
    me = lax.axis_index("vz")
    for values, way in zip(received, BACK_WAYS):
        speed[me ^ way] = values[...]
    lanes = done.shape[2]
    half = levels // 2
    low = lax.broadcasted_iota(jnp.int32, (ROWS, lanes), 0) < NODES
    copies = []
    for pair in range(half):
        lower = [speed[j, pair * ROWS : (pair + 1) * ROWS, :] for j in range(NODES)]
        upper = [speed[j, (pair + 1) * ROWS : (pair + 2) * ROWS, :] for j in range(NODES)]
        jump = [above - below for above, below in zip(upper, lower)]
        value = [jnp.where(low, above, below) for above, below in zip(upper, lower)]
        for h in range(2):
            a, b = 2 * h, 2 * h + 1
            for odd in range(2):
                at = pl.ds((2 * pair + odd) * POINTS + ROWS * h, ROWS)
                jumps = side_by_side(jump[a], jump[b], odd, low)
                final[0, at, :] = done[0, at, :] - density_couple * jumps
                final[1, at, :] = side_by_side(value[a], value[b], 1 - odd, low)
                final[2, at, :] = done[1, at, :] - theta_couple * jumps
        if pair in (half // 2 - 1, half - 1):
            first = 0 if pair < half - 1 else half // 2
            rows = pl.ds(first * 2 * POINTS, (pair + 1 - first) * 2 * POINTS)
            for place, f in enumerate((0, 3, 4)):
                copies.append(
                    pltpu.make_async_copy(
                        final.at[place, rows, :], out.at[f, rows, :], semaphores.at[len(copies)]
                    )
                )
                copies[-1].start()
    for copy in copies:
        copy.wait()


def side_by_side(first, second, upper, low):
    if upper:
        return jnp.where(low, pltpu.roll(first, NODES, 0), second)
    return jnp.where(low, first, pltpu.roll(second, NODES, 0))


VMEM = pl.BlockSpec(memory_space=pltpu.VMEM)
HBM = pl.BlockSpec(memory_space=pltpu.HBM)
ANY = pl.BlockSpec(memory_space=pl.ANY)


def call(kernel, outs, in_specs, scratch=(), cost=0, name=None):
    kinds = [x if hasattr(x, "dtype") else pltpu.VMEM(x, jnp.float32) for x in outs]
    return pl.pallas_call(
        kernel,
        out_shape=kinds,
        in_specs=in_specs,
        out_specs=[VMEM] * len(outs),
        scratch_shapes=list(scratch),
        compiler_params=pltpu.CompilerParams(vmem_limit_bytes=24 * 1024 * 1024),
        cost_estimate=pl.CostEstimate(flops=cost, bytes_accessed=cost, transcendentals=0),
        name=name,
    )


def per_device(
    prognostic, metric, first_flux, second_flux, neighbour_face, orientation, coupling, damping
):
    fields, levels = prognostic.shape[:2]
    lanes = prognostic.shape[-1]
    whole = (fields, levels * POINTS, lanes)
    metric = metric.reshape(POINTS, lanes)
    neighbour_face = neighbour_face.reshape(4, lanes)
    orientation = orientation.reshape(4, lanes)
    coupling = coupling.reshape(4, coupling.shape[1], NODES, lanes)
    damping = damping.reshape(NODES, lanes)
    tables, _ = operator_tables(lanes)

    def shifts(axis):
        size = lax.axis_size(axis)
        up = [(i, (i + 1) % size) for i in range(size)]
        return up, [(j, i) for i, j in up]

    def exchange(arrays, ways):
        size = lax.axis_size("vz")
        return [
            lax.ppermute(x, "vz", [(i, i ^ way) for i in range(size)]) if way else x
            for x, way in zip(arrays, ways)
        ]

    count = lax.axis_size("hy")
    near = [(i, i ^ 1) for i in range(count)]
    other = [(i, (i + 1 if i % 2 else i - 1) % count) for i in range(count)]
    second_up, second_down = shifts("hx")
    width = len(RIM_POINTS)
    message = (-(-((levels + 2) * width + 2) // ROWS) * ROWS, lanes)
    sides = (-(-fields * len(chunks(levels)) // 4) * ROWS, lanes)
    padded = levels + 2 * ROWS
    table = pltpu.VMEM((4, lanes), jnp.int32)
    inputs = (
        prognostic.reshape(whole),
        neighbour_face,
        orientation,
        metric,
        jnp.asarray(tables),
        first_flux,
        second_flux,
    )
    (
        to_other,
        state,
        neighbour_face,
        orientation,
        metric,
        tables,
        fluxes,
    ) = call(
        rim_kernel,
        [
            message,
            whole,
            table,
            table,
            (POINTS, lanes),
            tables.shape,
            (-(-2 * fields * fields // ROWS) * ROWS, lanes),
        ],
        [HBM] * len(inputs),
        [
            pltpu.VMEM((width, padded, lanes), jnp.float32),
            pltpu.VMEM((width, padded, lanes), jnp.float32),
            pltpu.SMEM((fields, fields), jnp.float32),
            pltpu.SMEM((fields, fields), jnp.float32),
            pltpu.SemaphoreType.DMA((7,)),
        ],
        cost=1000,
        name="rim",
    )(*(pltpu.with_memory_space_constraint(x, pltpu.HBM) for x in inputs))
    state = state.reshape(fields * levels * POINTS, lanes)
    from_other = lax.ppermute(to_other, "hy", other)
    from_near = lax.ppermute(state, "hy", near)
    (to_sides,) = call(edge_kernel, [sides], [VMEM], cost=1000, name="edge")(state)
    from_down = lax.ppermute(to_sides, "hx", second_up)
    from_up = from_down
    if lax.axis_size("hx") > 2:
        from_up = lax.ppermute(to_sides, "hx", second_down)

    column = (coupling.shape[1], NODES, lanes)
    factors = call(factor_kernel, [column] * 5, [VMEM] * 2, cost=4000000, name="factor")(
        coupling, damping
    )
    block = ((levels + 2) * NODES, lanes)
    part, base = call(
        element_kernel,
        [state.shape, (NODES,) + block],
        [VMEM] * 6,
        [
            pltpu.VMEM((levels * 8 * fields, lanes), jnp.float32),
            pltpu.VMEM((fields * POINTS, lanes), jnp.bfloat16),
            pltpu.VMEM((fields * POINTS, lanes), jnp.bfloat16),
        ],
        cost=4000000,
        name="element",
    )(
        state,
        neighbour_face,
        orientation,
        metric,
        fluxes,
        tables,
    )
    late = levels * NODES * len(LATE_FIELDS)
    base, near_late = call(
        near_kernel,
        [(NODES,) + block, (late, lanes)],
        [VMEM] * 6,
        [pltpu.VMEM((NODES, padded, lanes), jnp.float32), pltpu.VMEM(block, jnp.float32)],
        cost=1000,
        name="near",
    )(from_near, neighbour_face, orientation, fluxes, base, metric)
    count = -(-(levels + 2) // ROWS) * ROWS
    (half,) = call(
        half_pack_kernel,
        [(NODES,) + block],
        [VMEM] * 7 + [ANY],
        [
            pltpu.VMEM((NODES, count * NODES, lanes), jnp.float32),
            pltpu.VMEM((padded, lanes), jnp.float32),
            pltpu.VMEM((count, lanes), jnp.float32),
        ],
        cost=1000,
        name="half_pack",
    )(
        base,
        from_down,
        from_up,
        neighbour_face,
        orientation,
        metric,
        fluxes,
        factors[0],
    )
    sends = call(
        pack_kernel,
        [block] * NODES,
        [VMEM] * 5,
        [pltpu.VMEM((NODES,) + block, jnp.float32)],
        cost=1000,
        name="pack",
    )(half, from_other, neighbour_face, orientation, metric)
    received = exchange(sends, WAYS)

    other_face = call(
        functools.partial(face_kernel, 1),
        [(late // 2, lanes)] * 2,
        [VMEM] * 3 + [ANY],
        cost=1000,
        name="other_face",
    )(state, from_other, fluxes, sends[-1])
    other_face = [lax.ppermute(x, "hy", other) for x in other_face]

    cube = (levels + 2, NODES, lanes)
    speeds = call(
        solve_kernel,
        [cube] * NODES,
        [VMEM] * (5 + NODES),
        [
            pltpu.VMEM(column, jnp.float32),
            pltpu.VMEM((NODES, 2, NODES, lanes), jnp.float32),
            pltpu.VMEM((column[0] + 2,) + column[1:], jnp.float32),
        ],
        cost=1000,
        name="solve",
    )(*factors, *[x.reshape(cube) for x in received])
    returned = exchange([x.reshape(block) for x in speeds], BACK_WAYS)
    size = levels * POINTS
    limits = pltpu.CompilerParams(vmem_limit_bytes=24 * 1024 * 1024)
    earlier, done = pl.pallas_call(
        finish_section_kernel,
        out_shape=[
            jax.ShapeDtypeStruct(whole, jnp.float32),
            pltpu.VMEM((2, size, lanes), jnp.float32),
        ],
        in_specs=[VMEM] * 10,
        out_specs=[HBM, VMEM],
        scratch_shapes=[
            pltpu.VMEM((2, size, lanes), jnp.float32),
            pltpu.SemaphoreType.DMA,
        ],
        compiler_params=limits,
        cost_estimate=pl.CostEstimate(flops=4000000, bytes_accessed=4000000, transcendentals=0),
        name="finish",
    )(
        part, near_late, *other_face, from_down, from_up, neighbour_face, orientation, metric, fluxes
    )
    updated = pl.pallas_call(
        update_kernel,
        out_shape=jax.ShapeDtypeStruct(whole, jnp.float32),
        in_specs=[VMEM] * (1 + NODES) + [HBM],
        out_specs=HBM,
        input_output_aliases={1 + NODES: 0},
        scratch_shapes=[
            pltpu.VMEM((NODES,) + block, jnp.float32),
            pltpu.VMEM((3, size, lanes), jnp.float32),
            pltpu.SemaphoreType.DMA((6,)),
        ],
        compiler_params=limits,
        name="update",
    )(*returned, done, earlier)
    return updated.reshape(prognostic.shape)


def solution(mesh):
    placed = (
        P(None, "vz", None, None, "hy", "hx"),
        P(None, None, "hy", "hx"),
        P(),
        P(),
        P(None, "hy", "hx"),
        P(None, "hy", "hx"),
        P(None, None, "vz", None, "hy", "hx"),
        P("vz", None, "hy", "hx"),
    )
    return jax.shard_map(
        per_device,
        mesh=mesh,
        in_specs=placed,
        out_specs=P(None, "vz", None, None, "hy", "hx"),
        check_vma=False,
    )
```

```python
import functools

import jax
import jax.numpy as jnp
import numpy as np
from jax import lax
from jax.experimental import pallas as pl
from jax.experimental.pallas import tpu as pltpu
from jax.sharding import PartitionSpec as P

step_size = 0.05
lift_weight = 6.0
gravity_couple = 0.5
density_couple = 0.3
theta_couple = 0.4

NODES = 4
POINTS = NODES * NODES
FIELDS = 5
FACE_POINTS = ((0, 4, 8, 12), (3, 7, 11, 15), (0, 1, 2, 3), (12, 13, 14, 15))
RIM_POINTS = tuple(sorted(set(sum(FACE_POINTS, ()))))
ROWS = 8
LATE_FIELDS = (0, 1, 2, 4)
WAYS = (2, 3, 1, 0)
BACK_WAYS = (3, 2, 1, 0)


def derivative_table():
    points = np.array([-1.0, -1.0 / np.sqrt(5.0), 1.0 / np.sqrt(5.0), 1.0])
    number = points.shape[0]
    barycentric = np.ones(number)
    for source in range(number):
        for another in range(number):
            if another != source:
                barycentric[source] = barycentric[source] / (points[source] - points[another])
    matrix = np.zeros((number, number))
    for target in range(number):
        for source in range(number):
            if target != source:
                matrix[target, source] = (
                    barycentric[source] / barycentric[target] / (points[target] - points[source])
                )
        matrix[target, target] = -np.sum(matrix[target])
    return matrix


def operator_tables(lanes):
    weight = 0.5 * lift_weight
    table = derivative_table()
    table[0, 0] += weight
    table[-1, -1] -= weight
    eye = np.eye(NODES)
    along_first = np.kron(eye, table)
    along_second = np.kron(table, eye)
    ends = np.zeros(NODES)
    ends[0] = ends[-1] = 1.0
    faces = np.diag(np.kron(np.ones(NODES), ends) + np.kron(ends, np.ones(NODES)))
    first = np.zeros((POINTS, lanes))
    second = np.zeros((POINTS, lanes))
    same = np.zeros((FIELDS, POINTS, lanes))
    owner = np.full((lanes,), -1)
    for g in range(FIELDS):
        own = slice(POINTS * g, POINTS * (g + 1))
        first[:, own] = -along_first
        second[:, own] = -along_second
        same[g, :, own] = -weight * faces
        owner[own] = g
        for k in range(NODES):
            south = FIELDS * POINTS + 2 * NODES * g + k
            north = south + NODES
            second[FACE_POINTS[2][k], south] = weight
            second[FACE_POINTS[3][k], north] = -weight
            same[g, FACE_POINTS[2][k], south] = weight
            same[g, FACE_POINTS[3][k], north] = weight
            owner[south] = owner[north] = g
    tables = np.concatenate([first, second, same.reshape(FIELDS * POINTS, lanes)])
    return tables.astype(np.float32), owner


def chunks(total):
    return [min(start, total - ROWS) for start in range(0, total, ROWS)]


def partner_side(partner):
    odd = lax.rem(lax.axis_index("hy"), 2)
    return odd if partner else 1 - odd


def side_sign(side):
    return (2 * side - 1).astype(jnp.float32)


def ends(total):
    return list(range(0, total, ROWS))


def pick(values, masks, flip):
    chosen = []
    for k in range(NODES):
        row = values[FACE_POINTS[0][k]]
        for option in range(1, 4):
            row = jnp.where(masks[option], values[FACE_POINTS[option][k]], row)
        chosen.append(row)
    return [jnp.where(flip, chosen[NODES - 1 - k], chosen[k]) for k in range(NODES)]


def table_masks(face_row, flip_row, lanes):
    face = jnp.broadcast_to(face_row, (ROWS, lanes))
    flip = jnp.broadcast_to(flip_row, (ROWS, lanes))
    return [face == option for option in range(4)], flip == 1


def flux_row(f, g, matrix):
    return (matrix * FIELDS + f) * FIELDS + g


def along(fluxes, matrix, f, rows):
    total = None
    for g in range(FIELDS):
        at = flux_row(f, g, matrix)
        term = fluxes[at : at + 1, :] * rows[g]
        total = term if total is None else total + term
    return total


def side_rows(f, piece):
    number = 3 * f + piece
    return number // 4, 32 * (number % 4)


def rim_kernel(
    state_hbm,
    face_hbm,
    way_hbm,
    metric_hbm,
    tables_hbm,
    flux_hbm,
    second_hbm,
    to_other,
    state,
    neighbour_face,
    orientation,
    metric,
    tables,
    fluxes,
    column,
    speed,
    flux,
    second_flux,
    semaphores,
):
    levels = state.shape[1] // POINTS
    face = partner_side(1)
    sign = side_sign(face)
    lanes = state.shape[2]
    width = len(RIM_POINTS)
    groups = [(start, min(start + ROWS, levels)) for start in range(0, levels, ROWS)]
    small = [
        pltpu.make_async_copy(source, target, semaphores.at[place])
        for place, (source, target) in enumerate(
            (
                (flux_hbm, flux),
                (face_hbm, neighbour_face),
                (way_hbm, orientation),
                (metric_hbm, metric),
                (tables_hbm, tables),
                (second_hbm, second_flux),
            )
        )
    ]
    large = []
    for place, (low, high) in enumerate(groups):
        rows = pl.ds(low * POINTS, (high - low) * POINTS)
        large.append(
            pltpu.make_async_copy(
                state_hbm.at[:, rows, :], state.at[:, rows, :], semaphores.at[len(small) + place]
            )
        )
    for copy in small[:1] + large + small[1:]:
        copy.start()
    column[...] = jnp.zeros_like(column)
    small[0].wait()
    arrived = 0
    for piece, start in enumerate(chunks(levels)):
        while arrived < len(groups) and groups[arrived][0] < start + ROWS:
            large[arrived].wait()
            arrived += 1
        for place, point in enumerate(RIM_POINTS):
            rows = [
                state[g, pl.ds(start * POINTS + point, ROWS, stride=POINTS), :]
                for g in range(FIELDS)
            ]
            for f, out in ((3, speed), (4, column)):
                normal = (sign * flux[f, 0]) * rows[0]
                for g in range(1, FIELDS):
                    normal = normal + (sign * flux[f, g]) * rows[g]
                out[place, pl.ds(ROWS + start, ROWS), :] = rows[f] + normal
    small[1].wait()
    small[2].wait()
    end = (levels + 2) * width
    for place in range(width):
        for start in chunks(levels):
            upper = column[place, pl.ds(ROWS + start + 1, ROWS), :]
            lower = column[place, pl.ds(ROWS + start - 1, ROWS), :]
            to_other[pl.ds(start * width + place, ROWS, stride=width), :] = speed[
                place, pl.ds(ROWS + start, ROWS), :
            ] - gravity_couple * (upper - lower)
        for extra, level in ((0, 0), (1, levels - 1)):
            at = (levels + extra) * width + place
            to_other[at : at + 1, :] = column[place, ROWS + level : ROWS + level + 1, :]
    to_other[end : end + 1, :] = neighbour_face[pl.ds(face, 1), :].astype(jnp.float32)
    to_other[end + 1 : end + 2, :] = orientation[pl.ds(face, 1), :].astype(jnp.float32)
    left = to_other.shape[0] - end - 2
    to_other[end + 2 :, :] = jnp.zeros((left, lanes), jnp.float32)
    small[3].wait()
    small[4].wait()
    small[5].wait()
    for place, source in enumerate((flux, second_flux)):
        for f in range(FIELDS):
            for g in range(FIELDS):
                at = flux_row(f, g, place)
                fluxes[at : at + 1, :] = jnp.full((1, lanes), source[f, g])


def edge_kernel(state, to_sides):
    lanes = state.shape[1]
    levels = state.shape[0] // (FIELDS * POINTS)
    lane = lax.broadcasted_iota(jnp.int32, (ROWS, lanes), 1)
    packed = [jnp.zeros((ROWS, lanes), jnp.float32) for _ in range(to_sides.shape[0] // ROWS)]
    for f in range(FIELDS):
        for piece, start in enumerate(chunks(levels)):
            block, at = side_rows(f, piece)
            for place, point in enumerate(RIM_POINTS):
                row = state[pl.ds((f * levels + start) * POINTS + point, ROWS, stride=POINTS), :]
                first = at + 2 * place
                packed[block] = jnp.where(
                    lane // 2 == first // 2, pltpu.roll(row, first + 1, 1), packed[block]
                )
    for block, value in enumerate(packed):
        to_sides[block * ROWS : (block + 1) * ROWS, :] = value


def near_kernel(
    state, neighbour_face, orientation, fluxes, base, metric, half, late, column, source
):
    lanes = state.shape[1]
    levels = state.shape[0] // (FIELDS * POINTS)
    face = partner_side(0)
    sign = -side_sign(face)
    masks, flip = table_masks(
        neighbour_face[pl.ds(face, 1), :], orientation[pl.ds(face, 1), :], lanes
    )
    column[...] = jnp.zeros_like(column)
    speeds = []
    for start in chunks(levels):
        picked = []
        for g in range(FIELDS):
            values = {
                point: state[pl.ds((g * levels + start) * POINTS + point, ROWS, stride=POINTS), :]
                for point in RIM_POINTS
            }
            picked.append(pick(values, masks, flip))
        for k in range(NODES):
            rows = [picked[g][k] for g in range(FIELDS)]
            changed = [rows[f] + sign * along(fluxes, 0, f, rows) for f in range(FIELDS)]
            for place, f in enumerate(LATE_FIELDS):
                at = (place * levels + start) * NODES + k
                late[pl.ds(at, ROWS, stride=NODES), :] = changed[f]
            column[k, pl.ds(ROWS + start, ROWS), :] = changed[4]
            speeds.append(changed[3])
    for piece, start in enumerate(chunks(levels)):
        for k in range(NODES):
            upper = column[k, pl.ds(ROWS + start + 1, ROWS), :]
            lower = column[k, pl.ds(ROWS + start - 1, ROWS), :]
            source[pl.ds(start * NODES + k, ROWS, stride=NODES), :] = speeds[
                NODES * piece + k
            ] - gravity_couple * (upper - lower)
    for extra, level in ((0, 0), (1, levels - 1)):
        for k in range(NODES):
            at = (levels + extra) * NODES + k
            source[at : at + 1, :] = column[k, ROWS + level : ROWS + level + 1, :]
    half[...] = base[...]
    for start in chunks(levels + 2):
        picked = [source[pl.ds(start * NODES + k, ROWS, stride=NODES), :] for k in range(NODES)]
        add_first_side(0, start, picked, half, base, metric)


def face_kernel(partner, state, received, fluxes, *rest):
    lanes = state.shape[1]
    levels = state.shape[0] // (FIELDS * POINTS)
    at = (levels + 2) * len(RIM_POINTS)
    outs = rest[-2:]
    share = len(LATE_FIELDS) // len(outs)
    sign = side_sign(partner_side(partner))
    masks, flip = table_masks(
        received[at : at + 1, :].astype(jnp.int32),
        received[at + 1 : at + 2, :].astype(jnp.int32),
        lanes,
    )
    for start in chunks(levels):
        picked = []
        for g in range(FIELDS):
            values = {
                point: state[pl.ds((g * levels + start) * POINTS + point, ROWS, stride=POINTS), :]
                for point in RIM_POINTS
            }
            picked.append(pick(values, masks, flip))
        for place, f in enumerate(LATE_FIELDS):
            for k in range(NODES):
                normal = along(fluxes, 0, f, [picked[g][k] for g in range(FIELDS)])
                at = ((place % share) * levels + start) * NODES + k
                outs[place // share][pl.ds(at, ROWS, stride=NODES), :] = (
                    picked[f][k] + sign * normal
                )


def element_kernel(
    state,
    neighbour_face,
    orientation,
    metric,
    fluxes,
    tables,
    part,
    base,
    outer,
    operator_high,
    operator_low,
):
    levels = state.shape[0] // (FIELDS * POINTS)
    lanes = state.shape[1]
    lane = lax.broadcasted_iota(jnp.int32, (ROWS, lanes), 1)
    sides = []
    for side, (face, edge) in enumerate(((2, 0), (3, lanes - 1))):
        shift = 1 if side == 0 else lanes - 1
        row = jnp.broadcast_to(neighbour_face[face : face + 1, :], (ROWS, lanes))
        way = jnp.broadcast_to(orientation[face : face + 1, :], (ROWS, lanes))
        masks, flip = table_masks(
            pltpu.roll(row, lanes - shift, 1), pltpu.roll(way, lanes - shift, 1), lanes
        )
        sides.append((shift, edge, masks, flip))
    for f in range(FIELDS):
        for start in chunks(levels):
            q = f * levels + start
            values = {
                point: state[pl.ds(q * POINTS + point, ROWS, stride=POINTS), :]
                for point in RIM_POINTS
            }
            for side, (shift, edge, masks, flip) in enumerate(sides):
                for k, row in enumerate(pick(values, masks, flip)):
                    at = start * 8 * FIELDS + 8 * f + NODES * side + k
                    outer[pl.ds(at, ROWS, stride=8 * FIELDS), :] = jnp.where(
                        lane == edge, 0.0, pltpu.roll(row, shift, 1)
                    )
    index = lax.broadcasted_iota(jnp.int32, (1, lanes), 1)
    own_columns = FIELDS * POINTS
    owner = jnp.where(index < own_columns, index // POINTS, (index - own_columns) // 8)
    for f in range(FIELDS):
        first_row = jnp.zeros((1, lanes), jnp.float32)
        second_row = first_row
        for g in range(FIELDS):
            first, second = (flux_row(f, g, matrix) for matrix in range(2))
            first_row = jnp.where(owner == g, fluxes[first : first + 1, :], first_row)
            second_row = jnp.where(owner == g, fluxes[second : second + 1, :], second_row)
        block = (
            first_row * tables[0:POINTS, :]
            + second_row * tables[POINTS : 2 * POINTS, :]
            + tables[(2 + f) * POINTS : (3 + f) * POINTS, :]
        )
        high = block.astype(jnp.bfloat16)
        operator_high[f * POINTS : (f + 1) * POINTS, :] = high
        operator_low[f * POINTS : (f + 1) * POINTS, :] = (
            block - high.astype(jnp.float32)
        ).astype(jnp.bfloat16)
    high = operator_high[...]
    low = operator_low[...]
    scale = step_size * metric[...]
    blank = jnp.zeros((lanes - own_columns - 8 * FIELDS, lanes), jnp.float32)
    for pair in range(0, levels, 2):
        sides = []
        for level in (pair, pair + 1):
            rows = [
                state[pl.ds((f * levels + level) * POINTS, POINTS), :] for f in range(FIELDS)
            ]
            rows.append(outer[pl.ds(level * 8 * FIELDS, 8 * FIELDS), :])
            rows.append(blank)
            sides.append(jnp.concatenate(rows, axis=0))
        values = jnp.concatenate(sides, axis=1)
        top = values.astype(jnp.bfloat16)
        rest = (values - top.astype(jnp.float32)).astype(jnp.bfloat16)
        change = (
            jnp.dot(high, top, preferred_element_type=jnp.float32)
            + jnp.dot(high, rest, preferred_element_type=jnp.float32)
            + jnp.dot(low, top, preferred_element_type=jnp.float32)
        )
        for place, level in enumerate((pair, pair + 1)):
            for f in range(FIELDS):
                at = pl.ds((f * levels + level) * POINTS, POINTS)
                part[at, :] = (
                    state[at, :]
                    + scale
                    * change[
                        f * POINTS : (f + 1) * POINTS, place * lanes : (place + 1) * lanes
                    ]
                )
    for level in range(levels):
        speed = part[pl.ds((3 * levels + level) * POINTS, POINTS), :]
        upper = part[pl.ds((4 * levels + level + 1) * POINTS, POINTS), :] if level < levels - 1 else 0.0
        lower = part[pl.ds((4 * levels + level - 1) * POINTS, POINTS), :] if level else 0.0
        value = speed - gravity_couple * (upper - lower)
        for j in range(NODES):
            base[j, level * NODES : (level + 1) * NODES, :] = value[NODES * j : NODES * (j + 1)]
    for extra, level in ((0, 0), (1, levels - 1)):
        value = part[pl.ds((4 * levels + level) * POINTS, POINTS), :]
        at = (levels + extra) * NODES
        for j in range(NODES):
            base[j, at : at + NODES, :] = value[NODES * j : NODES * (j + 1)]


def side_corrections(received, side, fluxes, fields, pieces):
    lanes = received.shape[1]
    sign = 1.0 if side == 0 else -1.0
    result = [[] for _ in fields]
    for piece in range(pieces):
        rows = []
        for g in range(FIELDS):
            block, at = side_rows(g, piece)
            rows.append(
                pltpu.roll(
                    received[block * ROWS : (block + 1) * ROWS, :], (lanes - at - side) % lanes, 1
                )
            )
        for place, f in enumerate(fields):
            result[place].append(rows[f] + sign * along(fluxes, 1, f, rows))
    return result


def spread(value, edge, masks, flip):
    lanes = value.shape[1]
    values = {
        point: pltpu.roll(value, (edge - 2 * place) % lanes, 1)
        for place, point in enumerate(RIM_POINTS)
    }
    return pick(values, masks, flip)


def add_first_side(partner, start, picked, send, base, metric):
    weight = 0.5 * lift_weight * step_size
    i = (NODES - 1) * partner_side(partner)
    for j, row in enumerate(picked):
        at = pl.ds(start * NODES + i, ROWS, stride=NODES)
        scale = weight * metric[pl.ds(NODES * j + i, 1), :]
        send[j, at, :] = base[j, at, :] + scale * row


def pack_kernel(half, from_other, neighbour_face, orientation, metric, *rest):
    sends, (send,) = rest[:NODES], rest[NODES:]
    me = lax.axis_index("vz")
    send[...] = half[...]
    rows, lanes = half.shape[1:]
    width = len(RIM_POINTS)
    face = partner_side(1)
    masks, flip = table_masks(
        neighbour_face[pl.ds(face, 1), :], orientation[pl.ds(face, 1), :], lanes
    )
    for start in chunks(rows // NODES):
        values = {
            point: from_other[pl.ds(start * width + place, ROWS, stride=width), :]
            for place, point in enumerate(RIM_POINTS)
        }
        add_first_side(1, start, pick(values, masks, flip), send, half, metric)
    for out, way in zip(sends, WAYS):
        out[...] = send[me ^ way]


def half_pack_kernel(
    base,
    from_down,
    from_up,
    neighbour_face,
    orientation,
    metric,
    fluxes,
    factored,
    half,
    send,
    column,
    mixed,
):
    rows, lanes = base.shape[1:]
    levels = rows // NODES - 2
    width = len(RIM_POINTS)
    weight = 0.5 * lift_weight * step_size
    send[:, 0:rows, :] = base[...]
    send[:, rows:, :] = jnp.zeros((NODES, send.shape[1] - rows, lanes), jnp.float32)
    column[...] = jnp.zeros_like(column)
    mixed[...] = jnp.zeros_like(mixed)
    lane = lax.broadcasted_iota(jnp.int32, (ROWS, lanes), 1)
    for side, (received, edge, j) in enumerate(
        ((from_down, 0, 0), (from_up, lanes - 1, NODES - 1))
    ):
        face = 2 + side
        masks, flip = table_masks(
            neighbour_face[face : face + 1, :], orientation[face : face + 1, :], lanes
        )
        speed, heat = side_corrections(received, side, fluxes, (3, 4), len(chunks(levels)))
        for start, value in zip(chunks(levels), heat):
            column[pl.ds(ROWS + start, ROWS), :] = value
        for start, value in zip(chunks(levels), speed):
            upper = column[pl.ds(ROWS + start + 1, ROWS), :]
            lower = column[pl.ds(ROWS + start - 1, ROWS), :]
            mixed[pl.ds(start, ROWS), :] = value - gravity_couple * (upper - lower)
        mixed[levels : levels + 1, :] = column[ROWS : ROWS + 1, :]
        mixed[levels + 1 : levels + 2, :] = column[ROWS + levels - 1 : ROWS + levels, :]
        for start in ends(levels + 2):
            picked = spread(mixed[start : start + ROWS, :], edge, masks, flip)
            for k, row in enumerate(picked):
                point = NODES * j + k
                at = pl.ds(start * NODES + k, ROWS, stride=NODES)
                scale = weight * metric[point : point + 1, :]
                send[j, at, :] += jnp.where(lane == edge, scale * row, 0.0)
    half[...] = send[:, 0:rows, :]


def finish_section_kernel(
    part,
    near,
    other_early,
    other_late,
    from_down,
    from_up,
    neighbour_face,
    orientation,
    metric,
    fluxes,
    out,
    done,
    final,
    semaphore,
):
    levels = part.shape[0] // (FIELDS * POINTS)
    lanes = part.shape[1]
    size = levels * POINTS
    weight = 0.5 * lift_weight * step_size
    scale = weight * metric[...]
    lane = lax.broadcasted_iota(jnp.int32, (ROWS, lanes), 1)
    tables = []
    edges = []
    for side, received in enumerate((from_down, from_up)):
        face = 2 + side
        tables.append(
            table_masks(
                neighbour_face[face : face + 1, :], orientation[face : face + 1, :], lanes
            )
        )
        edges.append(
            side_corrections(received, side, fluxes, LATE_FIELDS, len(chunks(levels)))
        )
    copy = pltpu.make_async_copy(final, out.at[1:3], semaphore)
    sources = ((near,), (other_early, other_late))
    for place, f in ((1, 1), (2, 2), (0, 0), (3, 4)):
        target = final.at[f - 1] if f in (1, 2) else done.at[min(f, 1)]
        target[...] = part[f * size : (f + 1) * size, :]
        for piece, start in enumerate(chunks(levels)):
            for j in range(NODES):
                for partner, source in enumerate(sources):
                    point = NODES * j + (NODES - 1) * partner_side(partner)
                    share = len(LATE_FIELDS) // len(source)
                    rows = source[place // share][
                        pl.ds(((place % share) * levels + start) * NODES + j, ROWS, stride=NODES),
                        :,
                    ]
                    at = pl.ds(start * POINTS + point, ROWS, stride=POINTS)
                    target[at, :] = (
                        part[pl.ds(f * size + start * POINTS + point, ROWS, stride=POINTS), :]
                        + weight * metric[pl.ds(point, 1), :] * rows
                    )
        for piece, start in enumerate(chunks(levels)):
            row_index = lax.broadcasted_iota(jnp.int32, (ROWS, lanes), 0)
            fresh = row_index >= (-start) % ROWS
            for side, (edge, j) in enumerate(((0, 0), (lanes - 1, NODES - 1))):
                picked = spread(edges[side][place][piece], edge, *tables[side])
                for k, row in enumerate(picked):
                    point = NODES * j + k
                    at = pl.ds(start * POINTS + point, ROWS, stride=POINTS)
                    target[at, :] += jnp.where(
                        (lane == edge) & fresh, scale[point : point + 1, :] * row, 0.0
                    )
        if f == 2:
            copy.start()
    copy.wait()


def factor_kernel(coupling, damping, inverse, near, far_two, far_three, ratio, next_two, next_three):
    levels = coupling.shape[1]
    blank = jnp.zeros(coupling.shape[2:], jnp.float32)
    far_ratio, far_second, near_ratio, near_second = (blank,) * 4
    far_before, near_before = blank, blank
    extra = damping[...]
    for level in range(levels):
        a, b, d, e = (coupling[entry, level] for entry in range(4))
        centre = a + b + d + e + extra
        reduced = -b + a * far_ratio
        pivot = centre + a * far_second - reduced * near_ratio
        scaled = 1.0 / pivot
        upper_ratio = (-d - reduced * near_second) * scaled
        second_ratio = -e * scaled
        far_here, near_here = a * scaled, reduced * scaled
        inverse[level] = scaled
        near[level] = near_here
        far_two[level] = far_here + near_here * near_before
        far_three[level] = near_here * far_before
        ratio[level] = upper_ratio
        if level:
            next_two[level - 1] = near_ratio * upper_ratio - near_second
            next_three[level - 1] = near_ratio * second_ratio
        far_before, near_before = far_here, near_here
        far_ratio, far_second = near_ratio, near_second
        near_ratio, near_second = upper_ratio, second_ratio
    next_two[levels - 1] = -near_second
    next_three[levels - 1] = blank


def solve_kernel(inverse, near, far_two, far_three, ratio, next_two, next_three, *rest):
    ways = NODES
    received, sends, (source, heat, speed) = rest[:ways], rest[ways : 2 * ways], rest[2 * ways :]
    levels = near.shape[0]
    here = levels // ways
    me = lax.axis_index("vz")
    for values, way in zip(received, WAYS):
        block = me ^ way
        source[pl.ds(block * here, here)] = values[0:here]
        heat[block] = values[here : here + 2]
    for block in range(ways - 1):
        last = block * here + here - 1
        source[last] = source[last] - gravity_couple * heat[block + 1, 0]
        source[last + 1] = source[last + 1] + gravity_couple * heat[block, 1]
    blank = jnp.zeros(near.shape[1:], jnp.float32)
    scaled = blank
    known = [blank, blank, blank]
    for level in range(levels):
        before, scaled = scaled, source[level] * inverse[level]
        value = scaled - near[level] * before - far_three[level] * known[-3]
        value = value + far_two[level] * known[-2]
        source[level] = value
        known = [*known[1:], value]
    speed[0] = blank
    speed[levels + 1] = blank
    known = [blank, blank, blank]
    above = blank
    for level in range(levels - 1, -1, -1):
        here_value = source[level]
        value = here_value - ratio[level] * above + next_three[level] * known[-3]
        value = value + next_two[level] * known[-2]
        speed[level + 1] = value
        above = here_value
        known = [*known[1:], value]
    for send, way in zip(sends, BACK_WAYS):
        send[...] = speed[pl.ds((me ^ way) * here, here + 2)]


def update_kernel(*refs):
    ways = NODES
    received, (done, earlier, out, speed, final, semaphores) = refs[:ways], refs[ways:]
    levels = done.shape[1] // POINTS
    me = lax.axis_index("vz")
    for values, way in zip(received, BACK_WAYS):
        speed[me ^ way] = values[...]
    lanes = done.shape[2]
    half = levels // 2
    low = lax.broadcasted_iota(jnp.int32, (ROWS, lanes), 0) < NODES
    copies = []
    for pair in range(half):
        lower = [speed[j, pair * ROWS : (pair + 1) * ROWS, :] for j in range(NODES)]
        upper = [speed[j, (pair + 1) * ROWS : (pair + 2) * ROWS, :] for j in range(NODES)]
        jump = [above - below for above, below in zip(upper, lower)]
        value = [jnp.where(low, above, below) for above, below in zip(upper, lower)]
        for h in range(2):
            a, b = 2 * h, 2 * h + 1
            for odd in range(2):
                at = pl.ds((2 * pair + odd) * POINTS + ROWS * h, ROWS)
                jumps = side_by_side(jump[a], jump[b], odd, low)
                final[0, at, :] = done[0, at, :] - density_couple * jumps
                final[1, at, :] = side_by_side(value[a], value[b], 1 - odd, low)
                final[2, at, :] = done[1, at, :] - theta_couple * jumps
        if pair in (half // 2 - 1, half - 1):
            first = 0 if pair < half - 1 else half // 2
            rows = pl.ds(first * 2 * POINTS, (pair + 1 - first) * 2 * POINTS)
            for place, f in enumerate((0, 3, 4)):
                copies.append(
                    pltpu.make_async_copy(
                        final.at[place, rows, :], out.at[f, rows, :], semaphores.at[len(copies)]
                    )
                )
                copies[-1].start()
    for copy in copies:
        copy.wait()


def side_by_side(first, second, upper, low):
    if upper:
        return jnp.where(low, pltpu.roll(first, NODES, 0), second)
    return jnp.where(low, first, pltpu.roll(second, NODES, 0))


VMEM = pl.BlockSpec(memory_space=pltpu.VMEM)
HBM = pl.BlockSpec(memory_space=pltpu.HBM)
ANY = pl.BlockSpec(memory_space=pl.ANY)


def call(kernel, outs, in_specs, scratch=(), cost=0, name=None):
    kinds = [x if hasattr(x, "dtype") else pltpu.VMEM(x, jnp.float32) for x in outs]
    return pl.pallas_call(
        kernel,
        out_shape=kinds,
        in_specs=in_specs,
        out_specs=[VMEM] * len(outs),
        scratch_shapes=list(scratch),
        compiler_params=pltpu.CompilerParams(vmem_limit_bytes=24 * 1024 * 1024),
        cost_estimate=pl.CostEstimate(flops=cost, bytes_accessed=cost, transcendentals=0),
        name=name,
    )


def per_device(
    prognostic, metric, first_flux, second_flux, neighbour_face, orientation, coupling, damping
):
    fields, levels = prognostic.shape[:2]
    lanes = prognostic.shape[-1]
    whole = (fields, levels * POINTS, lanes)
    metric = metric.reshape(POINTS, lanes)
    neighbour_face = neighbour_face.reshape(4, lanes)
    orientation = orientation.reshape(4, lanes)
    coupling = coupling.reshape(4, coupling.shape[1], NODES, lanes)
    damping = damping.reshape(NODES, lanes)
    tables, _ = operator_tables(lanes)

    def shifts(axis):
        size = lax.axis_size(axis)
        up = [(i, (i + 1) % size) for i in range(size)]
        return up, [(j, i) for i, j in up]

    def exchange(arrays, ways):
        size = lax.axis_size("vz")
        return [
            lax.ppermute(x, "vz", [(i, i ^ way) for i in range(size)]) if way else x
            for x, way in zip(arrays, ways)
        ]

    count = lax.axis_size("hy")
    near = [(i, i ^ 1) for i in range(count)]
    other = [(i, (i + 1 if i % 2 else i - 1) % count) for i in range(count)]
    second_up, second_down = shifts("hx")
    width = len(RIM_POINTS)
    message = (-(-((levels + 2) * width + 2) // ROWS) * ROWS, lanes)
    sides = (-(-fields * len(chunks(levels)) // 4) * ROWS, lanes)
    padded = levels + 2 * ROWS
    table = pltpu.VMEM((4, lanes), jnp.int32)
    inputs = (
        prognostic.reshape(whole),
        neighbour_face,
        orientation,
        metric,
        jnp.asarray(tables),
        first_flux,
        second_flux,
    )
    (
        to_other,
        state,
        neighbour_face,
        orientation,
        metric,
        tables,
        fluxes,
    ) = call(
        rim_kernel,
        [
            message,
            whole,
            table,
            table,
            (POINTS, lanes),
            tables.shape,
            (-(-2 * fields * fields // ROWS) * ROWS, lanes),
        ],
        [HBM] * len(inputs),
        [
            pltpu.VMEM((width, padded, lanes), jnp.float32),
            pltpu.VMEM((width, padded, lanes), jnp.float32),
            pltpu.SMEM((fields, fields), jnp.float32),
            pltpu.SMEM((fields, fields), jnp.float32),
            pltpu.SemaphoreType.DMA((6 + -(-levels // ROWS),)),
        ],
        cost=1000,
        name="rim",
    )(*(pltpu.with_memory_space_constraint(x, pltpu.HBM) for x in inputs))
    state = state.reshape(fields * levels * POINTS, lanes)
    from_other = lax.ppermute(to_other, "hy", other)
    from_near = lax.ppermute(state, "hy", near)
    (to_sides,) = call(edge_kernel, [sides], [VMEM], cost=1000, name="edge")(state)
    from_down = lax.ppermute(to_sides, "hx", second_up)
    from_up = from_down
    if lax.axis_size("hx") > 2:
        from_up = lax.ppermute(to_sides, "hx", second_down)

    column = (coupling.shape[1], NODES, lanes)
    factors = call(factor_kernel, [column] * 7, [VMEM] * 2, cost=4000000, name="factor")(
        coupling, damping
    )
    block = ((levels + 2) * NODES, lanes)
    part, base = call(
        element_kernel,
        [state.shape, (NODES,) + block],
        [VMEM] * 6,
        [
            pltpu.VMEM((levels * 8 * fields, lanes), jnp.float32),
            pltpu.VMEM((fields * POINTS, lanes), jnp.bfloat16),
            pltpu.VMEM((fields * POINTS, lanes), jnp.bfloat16),
        ],
        cost=4000000,
        name="element",
    )(
        state,
        neighbour_face,
        orientation,
        metric,
        fluxes,
        tables,
    )
    late = levels * NODES * len(LATE_FIELDS)
    base, near_late = call(
        near_kernel,
        [(NODES,) + block, (late, lanes)],
        [VMEM] * 6,
        [pltpu.VMEM((NODES, padded, lanes), jnp.float32), pltpu.VMEM(block, jnp.float32)],
        cost=1000,
        name="near",
    )(from_near, neighbour_face, orientation, fluxes, base, metric)
    count = -(-(levels + 2) // ROWS) * ROWS
    (half,) = call(
        half_pack_kernel,
        [(NODES,) + block],
        [VMEM] * 7 + [ANY],
        [
            pltpu.VMEM((NODES, count * NODES, lanes), jnp.float32),
            pltpu.VMEM((padded, lanes), jnp.float32),
            pltpu.VMEM((count, lanes), jnp.float32),
        ],
        cost=1000,
        name="half_pack",
    )(
        base,
        from_down,
        from_up,
        neighbour_face,
        orientation,
        metric,
        fluxes,
        factors[0],
    )
    sends = call(
        pack_kernel,
        [block] * NODES,
        [VMEM] * 5,
        [pltpu.VMEM((NODES,) + block, jnp.float32)],
        cost=1000,
        name="pack",
    )(half, from_other, neighbour_face, orientation, metric)
    received = exchange(sends, WAYS)

    other_face = call(
        functools.partial(face_kernel, 1),
        [(late // 2, lanes)] * 2,
        [VMEM] * 3 + [ANY],
        cost=1000,
        name="other_face",
    )(state, from_other, fluxes, sends[-1])
    other_face = [lax.ppermute(x, "hy", other) for x in other_face]

    cube = (levels + 2, NODES, lanes)
    speeds = call(
        solve_kernel,
        [cube] * NODES,
        [VMEM] * (7 + NODES),
        [
            pltpu.VMEM(column, jnp.float32),
            pltpu.VMEM((NODES, 2, NODES, lanes), jnp.float32),
            pltpu.VMEM((column[0] + 2,) + column[1:], jnp.float32),
        ],
        cost=1000,
        name="solve",
    )(*factors, *[x.reshape(cube) for x in received])
    returned = exchange([x.reshape(block) for x in speeds], BACK_WAYS)
    size = levels * POINTS
    limits = pltpu.CompilerParams(vmem_limit_bytes=24 * 1024 * 1024)
    earlier, done = pl.pallas_call(
        finish_section_kernel,
        out_shape=[
            jax.ShapeDtypeStruct(whole, jnp.float32),
            pltpu.VMEM((2, size, lanes), jnp.float32),
        ],
        in_specs=[VMEM] * 10,
        out_specs=[HBM, VMEM],
        scratch_shapes=[
            pltpu.VMEM((2, size, lanes), jnp.float32),
            pltpu.SemaphoreType.DMA,
        ],
        compiler_params=limits,
        cost_estimate=pl.CostEstimate(flops=4000000, bytes_accessed=4000000, transcendentals=0),
        name="finish",
    )(
        part, near_late, *other_face, from_down, from_up, neighbour_face, orientation, metric, fluxes
    )
    updated = pl.pallas_call(
        update_kernel,
        out_shape=jax.ShapeDtypeStruct(whole, jnp.float32),
        in_specs=[VMEM] * (1 + NODES) + [HBM],
        out_specs=HBM,
        input_output_aliases={1 + NODES: 0},
        scratch_shapes=[
            pltpu.VMEM((NODES,) + block, jnp.float32),
            pltpu.VMEM((3, size, lanes), jnp.float32),
            pltpu.SemaphoreType.DMA((6,)),
        ],
        compiler_params=limits,
        name="update",
    )(*returned, done, earlier)
    return updated.reshape(prognostic.shape)


def solution(mesh):
    placed = (
        P(None, "vz", None, None, "hy", "hx"),
        P(None, None, "hy", "hx"),
        P(),
        P(),
        P(None, "hy", "hx"),
        P(None, "hy", "hx"),
        P(None, None, "vz", None, "hy", "hx"),
        P("vz", None, "hy", "hx"),
    )
    return jax.shard_map(
        per_device,
        mesh=mesh,
        in_specs=placed,
        out_specs=P(None, "vz", None, None, "hy", "hx"),
        check_vma=False,
    )
```

```python
import functools

import jax
import jax.numpy as jnp
import numpy as np
from jax import lax
from jax.experimental import pallas as pl
from jax.experimental.pallas import tpu as pltpu
from jax.sharding import PartitionSpec as P

step_size = 0.05
lift_weight = 6.0
gravity_couple = 0.5
density_couple = 0.3
theta_couple = 0.4

NODES = 4
POINTS = NODES * NODES
FIELDS = 5
FACE_POINTS = ((0, 4, 8, 12), (3, 7, 11, 15), (0, 1, 2, 3), (12, 13, 14, 15))
RIM_POINTS = tuple(sorted(set(sum(FACE_POINTS, ()))))
ROWS = 8
LATE_FIELDS = (0, 1, 2, 4)
WAYS = (3, 3, 2, 1, 0)
FORWARD_ROOM = (0, 2, 2, 2, 0)
BACK_WAYS = (3, 2, 1, 0)


def derivative_table():
    points = np.array([-1.0, -1.0 / np.sqrt(5.0), 1.0 / np.sqrt(5.0), 1.0])
    number = points.shape[0]
    barycentric = np.ones(number)
    for source in range(number):
        for another in range(number):
            if another != source:
                barycentric[source] = barycentric[source] / (points[source] - points[another])
    matrix = np.zeros((number, number))
    for target in range(number):
        for source in range(number):
            if target != source:
                matrix[target, source] = (
                    barycentric[source] / barycentric[target] / (points[target] - points[source])
                )
        matrix[target, target] = -np.sum(matrix[target])
    return matrix


def operator_tables(lanes):
    weight = 0.5 * lift_weight
    table = derivative_table()
    table[0, 0] += weight
    table[-1, -1] -= weight
    eye = np.eye(NODES)
    along_first = np.kron(eye, table)
    along_second = np.kron(table, eye)
    ends = np.zeros(NODES)
    ends[0] = ends[-1] = 1.0
    faces = np.diag(np.kron(np.ones(NODES), ends) + np.kron(ends, np.ones(NODES)))
    first = np.zeros((POINTS, lanes))
    second = np.zeros((POINTS, lanes))
    same = np.zeros((FIELDS, POINTS, lanes))
    owner = np.full((lanes,), -1)
    for g in range(FIELDS):
        own = slice(POINTS * g, POINTS * (g + 1))
        first[:, own] = -along_first
        second[:, own] = -along_second
        same[g, :, own] = -weight * faces
        owner[own] = g
        for k in range(NODES):
            south = FIELDS * POINTS + 2 * NODES * g + k
            north = south + NODES
            second[FACE_POINTS[2][k], south] = weight
            second[FACE_POINTS[3][k], north] = -weight
            same[g, FACE_POINTS[2][k], south] = weight
            same[g, FACE_POINTS[3][k], north] = weight
            owner[south] = owner[north] = g
    tables = np.concatenate([first, second, same.reshape(FIELDS * POINTS, lanes)])
    return tables.astype(np.float32), owner


def chunks(total):
    return [min(start, total - ROWS) for start in range(0, total, ROWS)]


def partner_side(partner):
    odd = lax.rem(lax.axis_index("hy"), 2)
    return odd if partner else 1 - odd


def side_sign(side):
    return (2 * side - 1).astype(jnp.float32)


def ends(total):
    return list(range(0, total, ROWS))


def pick(values, masks, flip):
    chosen = []
    for k in range(NODES):
        row = values[FACE_POINTS[0][k]]
        for option in range(1, 4):
            row = jnp.where(masks[option], values[FACE_POINTS[option][k]], row)
        chosen.append(row)
    return [jnp.where(flip, chosen[NODES - 1 - k], chosen[k]) for k in range(NODES)]


def table_masks(face_row, flip_row, lanes):
    face = jnp.broadcast_to(face_row, (ROWS, lanes))
    flip = jnp.broadcast_to(flip_row, (ROWS, lanes))
    return [face == option for option in range(4)], flip == 1


def flux_row(f, g, matrix):
    return (matrix * FIELDS + f) * FIELDS + g


def along(fluxes, matrix, f, rows):
    total = None
    for g in range(FIELDS):
        at = flux_row(f, g, matrix)
        term = fluxes[at : at + 1, :] * rows[g]
        total = term if total is None else total + term
    return total


def side_rows(f, piece):
    number = 3 * f + piece
    return number // 4, 32 * (number % 4)


def rim_kernel(
    state_hbm,
    face_hbm,
    way_hbm,
    metric_hbm,
    tables_hbm,
    flux_hbm,
    second_hbm,
    to_other,
    state,
    neighbour_face,
    orientation,
    metric,
    tables,
    fluxes,
    column,
    speed,
    flux,
    second_flux,
    semaphores,
):
    levels = state.shape[1] // POINTS
    face = partner_side(1)
    sign = side_sign(face)
    lanes = state.shape[2]
    width = len(RIM_POINTS)
    groups = [(start, min(start + ROWS, levels)) for start in range(0, levels, ROWS)]
    small = [
        pltpu.make_async_copy(source, target, semaphores.at[place])
        for place, (source, target) in enumerate(
            (
                (flux_hbm, flux),
                (face_hbm, neighbour_face),
                (way_hbm, orientation),
                (metric_hbm, metric),
                (tables_hbm, tables),
                (second_hbm, second_flux),
            )
        )
    ]
    large = []
    for place, (low, high) in enumerate(groups):
        rows = pl.ds(low * POINTS, (high - low) * POINTS)
        large.append(
            pltpu.make_async_copy(
                state_hbm.at[:, rows, :], state.at[:, rows, :], semaphores.at[len(small) + place]
            )
        )
    for copy in small[:1] + large + small[1:]:
        copy.start()
    column[...] = jnp.zeros_like(column)
    small[0].wait()
    arrived = 0
    for piece, start in enumerate(chunks(levels)):
        while arrived < len(groups) and groups[arrived][0] < start + ROWS:
            large[arrived].wait()
            arrived += 1
        for place, point in enumerate(RIM_POINTS):
            rows = [
                state[g, pl.ds(start * POINTS + point, ROWS, stride=POINTS), :]
                for g in range(FIELDS)
            ]
            for f, out in ((3, speed), (4, column)):
                normal = (sign * flux[f, 0]) * rows[0]
                for g in range(1, FIELDS):
                    normal = normal + (sign * flux[f, g]) * rows[g]
                out[place, pl.ds(ROWS + start, ROWS), :] = rows[f] + normal
    small[1].wait()
    small[2].wait()
    end = (levels + 2) * width
    for place in range(width):
        for start in chunks(levels):
            upper = column[place, pl.ds(ROWS + start + 1, ROWS), :]
            lower = column[place, pl.ds(ROWS + start - 1, ROWS), :]
            to_other[pl.ds(start * width + place, ROWS, stride=width), :] = speed[
                place, pl.ds(ROWS + start, ROWS), :
            ] - gravity_couple * (upper - lower)
        for extra, level in ((0, 0), (1, levels - 1)):
            at = (levels + extra) * width + place
            to_other[at : at + 1, :] = column[place, ROWS + level : ROWS + level + 1, :]
    to_other[end : end + 1, :] = neighbour_face[pl.ds(face, 1), :].astype(jnp.float32)
    to_other[end + 1 : end + 2, :] = orientation[pl.ds(face, 1), :].astype(jnp.float32)
    left = to_other.shape[0] - end - 2
    to_other[end + 2 :, :] = jnp.zeros((left, lanes), jnp.float32)
    small[3].wait()
    small[4].wait()
    small[5].wait()
    for place, source in enumerate((flux, second_flux)):
        for f in range(FIELDS):
            for g in range(FIELDS):
                at = flux_row(f, g, place)
                fluxes[at : at + 1, :] = jnp.full((1, lanes), source[f, g])


def edge_kernel(state, to_sides):
    lanes = state.shape[1]
    levels = state.shape[0] // (FIELDS * POINTS)
    lane = lax.broadcasted_iota(jnp.int32, (ROWS, lanes), 1)
    packed = [jnp.zeros((ROWS, lanes), jnp.float32) for _ in range(to_sides.shape[0] // ROWS)]
    for f in range(FIELDS):
        for piece, start in enumerate(chunks(levels)):
            block, at = side_rows(f, piece)
            for place, point in enumerate(RIM_POINTS):
                row = state[pl.ds((f * levels + start) * POINTS + point, ROWS, stride=POINTS), :]
                first = at + 2 * place
                packed[block] = jnp.where(
                    lane // 2 == first // 2, pltpu.roll(row, first + 1, 1), packed[block]
                )
    for block, value in enumerate(packed):
        to_sides[block * ROWS : (block + 1) * ROWS, :] = value


def near_kernel(
    state, neighbour_face, orientation, fluxes, base, metric, half, late, column, source
):
    lanes = state.shape[1]
    levels = state.shape[0] // (FIELDS * POINTS)
    face = partner_side(0)
    sign = -side_sign(face)
    masks, flip = table_masks(
        neighbour_face[pl.ds(face, 1), :], orientation[pl.ds(face, 1), :], lanes
    )
    column[...] = jnp.zeros_like(column)
    speeds = []
    for start in chunks(levels):
        picked = []
        for g in range(FIELDS):
            values = {
                point: state[pl.ds((g * levels + start) * POINTS + point, ROWS, stride=POINTS), :]
                for point in RIM_POINTS
            }
            picked.append(pick(values, masks, flip))
        for k in range(NODES):
            rows = [picked[g][k] for g in range(FIELDS)]
            changed = [rows[f] + sign * along(fluxes, 0, f, rows) for f in range(FIELDS)]
            for place, f in enumerate(LATE_FIELDS):
                at = (place * levels + start) * NODES + k
                late[pl.ds(at, ROWS, stride=NODES), :] = changed[f]
            column[k, pl.ds(ROWS + start, ROWS), :] = changed[4]
            speeds.append(changed[3])
    for piece, start in enumerate(chunks(levels)):
        for k in range(NODES):
            upper = column[k, pl.ds(ROWS + start + 1, ROWS), :]
            lower = column[k, pl.ds(ROWS + start - 1, ROWS), :]
            source[pl.ds(start * NODES + k, ROWS, stride=NODES), :] = speeds[
                NODES * piece + k
            ] - gravity_couple * (upper - lower)
    for extra, level in ((0, 0), (1, levels - 1)):
        for k in range(NODES):
            at = (levels + extra) * NODES + k
            source[at : at + 1, :] = column[k, ROWS + level : ROWS + level + 1, :]
    half[...] = base[...]
    for start in chunks(levels + 2):
        picked = [source[pl.ds(start * NODES + k, ROWS, stride=NODES), :] for k in range(NODES)]
        add_first_side(0, start, picked, half, base, metric)


def face_kernel(partner, state, received, fluxes, *rest):
    lanes = state.shape[1]
    levels = state.shape[0] // (FIELDS * POINTS)
    at = (levels + 2) * len(RIM_POINTS)
    outs = rest[-2:]
    share = len(LATE_FIELDS) // len(outs)
    sign = side_sign(partner_side(partner))
    masks, flip = table_masks(
        received[at : at + 1, :].astype(jnp.int32),
        received[at + 1 : at + 2, :].astype(jnp.int32),
        lanes,
    )
    for start in chunks(levels):
        picked = []
        for g in range(FIELDS):
            values = {
                point: state[pl.ds((g * levels + start) * POINTS + point, ROWS, stride=POINTS), :]
                for point in RIM_POINTS
            }
            picked.append(pick(values, masks, flip))
        for place, f in enumerate(LATE_FIELDS):
            for k in range(NODES):
                normal = along(fluxes, 0, f, [picked[g][k] for g in range(FIELDS)])
                at = ((place % share) * levels + start) * NODES + k
                outs[place // share][pl.ds(at, ROWS, stride=NODES), :] = (
                    picked[f][k] + sign * normal
                )


def element_kernel(
    state,
    neighbour_face,
    orientation,
    metric,
    fluxes,
    tables,
    part,
    base,
    outer,
    operator_high,
    operator_low,
):
    levels = state.shape[0] // (FIELDS * POINTS)
    lanes = state.shape[1]
    lane = lax.broadcasted_iota(jnp.int32, (ROWS, lanes), 1)
    sides = []
    for side, (face, edge) in enumerate(((2, 0), (3, lanes - 1))):
        shift = 1 if side == 0 else lanes - 1
        row = jnp.broadcast_to(neighbour_face[face : face + 1, :], (ROWS, lanes))
        way = jnp.broadcast_to(orientation[face : face + 1, :], (ROWS, lanes))
        masks, flip = table_masks(
            pltpu.roll(row, lanes - shift, 1), pltpu.roll(way, lanes - shift, 1), lanes
        )
        sides.append((shift, edge, masks, flip))
    for f in range(FIELDS):
        for start in chunks(levels):
            q = f * levels + start
            values = {
                point: state[pl.ds(q * POINTS + point, ROWS, stride=POINTS), :]
                for point in RIM_POINTS
            }
            for side, (shift, edge, masks, flip) in enumerate(sides):
                for k, row in enumerate(pick(values, masks, flip)):
                    at = start * 8 * FIELDS + 8 * f + NODES * side + k
                    outer[pl.ds(at, ROWS, stride=8 * FIELDS), :] = jnp.where(
                        lane == edge, 0.0, pltpu.roll(row, shift, 1)
                    )
    index = lax.broadcasted_iota(jnp.int32, (1, lanes), 1)
    own_columns = FIELDS * POINTS
    owner = jnp.where(index < own_columns, index // POINTS, (index - own_columns) // 8)
    for f in range(FIELDS):
        first_row = jnp.zeros((1, lanes), jnp.float32)
        second_row = first_row
        for g in range(FIELDS):
            first, second = (flux_row(f, g, matrix) for matrix in range(2))
            first_row = jnp.where(owner == g, fluxes[first : first + 1, :], first_row)
            second_row = jnp.where(owner == g, fluxes[second : second + 1, :], second_row)
        block = (
            first_row * tables[0:POINTS, :]
            + second_row * tables[POINTS : 2 * POINTS, :]
            + tables[(2 + f) * POINTS : (3 + f) * POINTS, :]
        )
        high = block.astype(jnp.bfloat16)
        operator_high[f * POINTS : (f + 1) * POINTS, :] = high
        operator_low[f * POINTS : (f + 1) * POINTS, :] = (
            block - high.astype(jnp.float32)
        ).astype(jnp.bfloat16)
    high = operator_high[...]
    low = operator_low[...]
    scale = step_size * metric[...]
    blank = jnp.zeros((lanes - own_columns - 8 * FIELDS, lanes), jnp.float32)
    for pair in range(0, levels, 2):
        sides = []
        for level in (pair, pair + 1):
            rows = [
                state[pl.ds((f * levels + level) * POINTS, POINTS), :] for f in range(FIELDS)
            ]
            rows.append(outer[pl.ds(level * 8 * FIELDS, 8 * FIELDS), :])
            rows.append(blank)
            sides.append(jnp.concatenate(rows, axis=0))
        values = jnp.concatenate(sides, axis=1)
        top = values.astype(jnp.bfloat16)
        rest = (values - top.astype(jnp.float32)).astype(jnp.bfloat16)
        change = (
            jnp.dot(high, top, preferred_element_type=jnp.float32)
            + jnp.dot(high, rest, preferred_element_type=jnp.float32)
            + jnp.dot(low, top, preferred_element_type=jnp.float32)
        )
        for place, level in enumerate((pair, pair + 1)):
            for f in range(FIELDS):
                at = pl.ds((f * levels + level) * POINTS, POINTS)
                part[at, :] = (
                    state[at, :]
                    + scale
                    * change[
                        f * POINTS : (f + 1) * POINTS, place * lanes : (place + 1) * lanes
                    ]
                )
    for level in range(levels):
        speed = part[pl.ds((3 * levels + level) * POINTS, POINTS), :]
        upper = part[pl.ds((4 * levels + level + 1) * POINTS, POINTS), :] if level < levels - 1 else 0.0
        lower = part[pl.ds((4 * levels + level - 1) * POINTS, POINTS), :] if level else 0.0
        value = speed - gravity_couple * (upper - lower)
        for j in range(NODES):
            base[j, level * NODES : (level + 1) * NODES, :] = value[NODES * j : NODES * (j + 1)]
    for extra, level in ((0, 0), (1, levels - 1)):
        value = part[pl.ds((4 * levels + level) * POINTS, POINTS), :]
        at = (levels + extra) * NODES
        for j in range(NODES):
            base[j, at : at + NODES, :] = value[NODES * j : NODES * (j + 1)]


def side_corrections(received, side, fluxes, fields, pieces):
    lanes = received.shape[1]
    sign = 1.0 if side == 0 else -1.0
    result = [[] for _ in fields]
    for piece in range(pieces):
        rows = []
        for g in range(FIELDS):
            block, at = side_rows(g, piece)
            rows.append(
                pltpu.roll(
                    received[block * ROWS : (block + 1) * ROWS, :], (lanes - at - side) % lanes, 1
                )
            )
        for place, f in enumerate(fields):
            result[place].append(rows[f] + sign * along(fluxes, 1, f, rows))
    return result


def spread(value, edge, masks, flip):
    lanes = value.shape[1]
    values = {
        point: pltpu.roll(value, (edge - 2 * place) % lanes, 1)
        for place, point in enumerate(RIM_POINTS)
    }
    return pick(values, masks, flip)


def add_first_side(partner, start, picked, send, base, metric):
    weight = 0.5 * lift_weight * step_size
    i = (NODES - 1) * partner_side(partner)
    for j, row in enumerate(picked):
        at = pl.ds(start * NODES + i, ROWS, stride=NODES)
        scale = weight * metric[pl.ds(NODES * j + i, 1), :]
        send[j, at, :] = base[j, at, :] + scale * row


def pack_kernel(half, from_other, neighbour_face, orientation, metric, *rest):
    sends, (send,) = rest[: NODES + 1], rest[NODES + 1 :]
    me = lax.axis_index("vz")
    send[...] = half[...]
    rows, lanes = half.shape[1:]
    width = len(RIM_POINTS)
    face = partner_side(1)
    masks, flip = table_masks(
        neighbour_face[pl.ds(face, 1), :], orientation[pl.ds(face, 1), :], lanes
    )
    for start in chunks(rows // NODES):
        values = {
            point: from_other[pl.ds(start * width + place, ROWS, stride=width), :]
            for place, point in enumerate(RIM_POINTS)
        }
        add_first_side(1, start, pick(values, masks, flip), send, half, metric)
    for out, way in zip(sends, WAYS):
        out[0:rows, :] = send[me ^ way]
        if out.shape[0] > rows:
            out[rows:, :] = jnp.zeros((out.shape[0] - rows, lanes), jnp.float32)


def half_pack_kernel(
    base,
    from_down,
    from_up,
    neighbour_face,
    orientation,
    metric,
    fluxes,
    factored,
    half,
    send,
    column,
    mixed,
):
    rows, lanes = base.shape[1:]
    levels = rows // NODES - 2
    width = len(RIM_POINTS)
    weight = 0.5 * lift_weight * step_size
    send[:, 0:rows, :] = base[...]
    send[:, rows:, :] = jnp.zeros((NODES, send.shape[1] - rows, lanes), jnp.float32)
    column[...] = jnp.zeros_like(column)
    mixed[...] = jnp.zeros_like(mixed)
    lane = lax.broadcasted_iota(jnp.int32, (ROWS, lanes), 1)
    for side, (received, edge, j) in enumerate(
        ((from_down, 0, 0), (from_up, lanes - 1, NODES - 1))
    ):
        face = 2 + side
        masks, flip = table_masks(
            neighbour_face[face : face + 1, :], orientation[face : face + 1, :], lanes
        )
        speed, heat = side_corrections(received, side, fluxes, (3, 4), len(chunks(levels)))
        for start, value in zip(chunks(levels), heat):
            column[pl.ds(ROWS + start, ROWS), :] = value
        for start, value in zip(chunks(levels), speed):
            upper = column[pl.ds(ROWS + start + 1, ROWS), :]
            lower = column[pl.ds(ROWS + start - 1, ROWS), :]
            mixed[pl.ds(start, ROWS), :] = value - gravity_couple * (upper - lower)
        mixed[levels : levels + 1, :] = column[ROWS : ROWS + 1, :]
        mixed[levels + 1 : levels + 2, :] = column[ROWS + levels - 1 : ROWS + levels, :]
        for start in ends(levels + 2):
            picked = spread(mixed[start : start + ROWS, :], edge, masks, flip)
            for k, row in enumerate(picked):
                point = NODES * j + k
                at = pl.ds(start * NODES + k, ROWS, stride=NODES)
                scale = weight * metric[point : point + 1, :]
                send[j, at, :] += jnp.where(lane == edge, scale * row, 0.0)
    half[...] = send[:, 0:rows, :]


def finish_section_kernel(
    part,
    near,
    other_early,
    other_late,
    from_down,
    from_up,
    neighbour_face,
    orientation,
    metric,
    fluxes,
    out,
    done,
    final,
    semaphore,
):
    levels = part.shape[0] // (FIELDS * POINTS)
    lanes = part.shape[1]
    size = levels * POINTS
    weight = 0.5 * lift_weight * step_size
    scale = weight * metric[...]
    lane = lax.broadcasted_iota(jnp.int32, (ROWS, lanes), 1)
    tables = []
    edges = []
    for side, received in enumerate((from_down, from_up)):
        face = 2 + side
        tables.append(
            table_masks(
                neighbour_face[face : face + 1, :], orientation[face : face + 1, :], lanes
            )
        )
        edges.append(
            side_corrections(received, side, fluxes, LATE_FIELDS, len(chunks(levels)))
        )
    copy = pltpu.make_async_copy(final, out.at[1:3], semaphore)
    sources = ((near,), (other_early, other_late))
    for place, f in ((1, 1), (2, 2), (0, 0), (3, 4)):
        target = final.at[f - 1] if f in (1, 2) else done.at[min(f, 1)]
        target[...] = part[f * size : (f + 1) * size, :]
        for piece, start in enumerate(chunks(levels)):
            for j in range(NODES):
                for partner, source in enumerate(sources):
                    point = NODES * j + (NODES - 1) * partner_side(partner)
                    share = len(LATE_FIELDS) // len(source)
                    rows = source[place // share][
                        pl.ds(((place % share) * levels + start) * NODES + j, ROWS, stride=NODES),
                        :,
                    ]
                    at = pl.ds(start * POINTS + point, ROWS, stride=POINTS)
                    target[at, :] = (
                        part[pl.ds(f * size + start * POINTS + point, ROWS, stride=POINTS), :]
                        + weight * metric[pl.ds(point, 1), :] * rows
                    )
        for piece, start in enumerate(chunks(levels)):
            row_index = lax.broadcasted_iota(jnp.int32, (ROWS, lanes), 0)
            fresh = row_index >= (-start) % ROWS
            for side, (edge, j) in enumerate(((0, 0), (lanes - 1, NODES - 1))):
                picked = spread(edges[side][place][piece], edge, *tables[side])
                for k, row in enumerate(picked):
                    point = NODES * j + k
                    at = pl.ds(start * POINTS + point, ROWS, stride=POINTS)
                    target[at, :] += jnp.where(
                        (lane == edge) & fresh, scale[point : point + 1, :] * row, 0.0
                    )
        if f == 2:
            copy.start()
    copy.wait()


def factor_kernel(coupling, damping, inverse, near, far_two, far_three, ratio, next_two, next_three):
    levels = coupling.shape[1]
    blank = jnp.zeros(coupling.shape[2:], jnp.float32)
    far_ratio, far_second, near_ratio, near_second = (blank,) * 4
    far_before, near_before = blank, blank
    extra = damping[...]
    for level in range(levels):
        a, b, d, e = (coupling[entry, level] for entry in range(4))
        centre = a + b + d + e + extra
        reduced = -b + a * far_ratio
        pivot = centre + a * far_second - reduced * near_ratio
        scaled = 1.0 / pivot
        upper_ratio = (-d - reduced * near_second) * scaled
        second_ratio = -e * scaled
        far_here, near_here = a * scaled, reduced * scaled
        inverse[level] = scaled
        near[level] = near_here
        far_two[level] = far_here + near_here * near_before
        far_three[level] = near_here * far_before
        ratio[level] = upper_ratio
        if level:
            next_two[level - 1] = near_ratio * upper_ratio - near_second
            next_three[level - 1] = near_ratio * second_ratio
        far_before, near_before = far_here, near_here
        far_ratio, far_second = near_ratio, near_second
        near_ratio, near_second = upper_ratio, second_ratio
    next_two[levels - 1] = -near_second
    next_three[levels - 1] = blank


def solve_kernel(inverse, near, far_two, far_three, ratio, next_two, next_three, *rest):
    ways = NODES
    fallen, middle, risen, beside, own = rest[: ways + 1]
    sends, (source, heat, speed) = rest[ways + 1 : 2 * ways + 1], rest[2 * ways + 1 :]
    levels = near.shape[0]
    here = levels // ways
    me = lax.axis_index("vz")
    far = jnp.where(me < ways // 2, fallen[0 : here + 2], risen[0 : here + 2])
    for values, way in ((far, 3), (middle, 2), (beside, 1), (own, 0)):
        block = me ^ way
        source[pl.ds(block * here, here)] = values[0:here]
        heat[block] = values[here : here + 2]
    for block in range(ways - 1):
        last = block * here + here - 1
        source[last] = source[last] - gravity_couple * heat[block + 1, 0]
        source[last + 1] = source[last + 1] + gravity_couple * heat[block, 1]
    blank = jnp.zeros(near.shape[1:], jnp.float32)
    scaled = blank
    known = [blank, blank, blank]
    for level in range(levels):
        before, scaled = scaled, source[level] * inverse[level]
        value = scaled - near[level] * before - far_three[level] * known[-3]
        value = value + far_two[level] * known[-2]
        source[level] = value
        known = [*known[1:], value]
    speed[0] = blank
    speed[levels + 1] = blank
    known = [blank, blank, blank]
    above = blank
    for level in range(levels - 1, -1, -1):
        here_value = source[level]
        value = here_value - ratio[level] * above + next_three[level] * known[-3]
        value = value + next_two[level] * known[-2]
        speed[level + 1] = value
        above = here_value
        known = [*known[1:], value]
    for send, way in zip(sends, BACK_WAYS):
        send[...] = speed[pl.ds((me ^ way) * here, here + 2)]


def update_kernel(*refs):
    ways = NODES
    received, (done, earlier, out, speed, final, semaphores) = refs[:ways], refs[ways:]
    levels = done.shape[1] // POINTS
    me = lax.axis_index("vz")
    for values, way in zip(received, BACK_WAYS):
        speed[me ^ way] = values[...]
    lanes = done.shape[2]
    half = levels // 2
    low = lax.broadcasted_iota(jnp.int32, (ROWS, lanes), 0) < NODES
    copies = []
    for pair in range(half):
        lower = [speed[j, pair * ROWS : (pair + 1) * ROWS, :] for j in range(NODES)]
        upper = [speed[j, (pair + 1) * ROWS : (pair + 2) * ROWS, :] for j in range(NODES)]
        jump = [above - below for above, below in zip(upper, lower)]
        value = [jnp.where(low, above, below) for above, below in zip(upper, lower)]
        for h in range(2):
            a, b = 2 * h, 2 * h + 1
            for odd in range(2):
                at = pl.ds((2 * pair + odd) * POINTS + ROWS * h, ROWS)
                jumps = side_by_side(jump[a], jump[b], odd, low)
                final[0, at, :] = done[0, at, :] - density_couple * jumps
                final[1, at, :] = side_by_side(value[a], value[b], 1 - odd, low)
                final[2, at, :] = done[1, at, :] - theta_couple * jumps
        if pair in (half // 2 - 1, half - 1):
            first = 0 if pair < half - 1 else half // 2
            rows = pl.ds(first * 2 * POINTS, (pair + 1 - first) * 2 * POINTS)
            for place, f in enumerate((0, 3, 4)):
                copies.append(
                    pltpu.make_async_copy(
                        final.at[place, rows, :], out.at[f, rows, :], semaphores.at[len(copies)]
                    )
                )
                copies[-1].start()
    for copy in copies:
        copy.wait()


def side_by_side(first, second, upper, low):
    if upper:
        return jnp.where(low, pltpu.roll(first, NODES, 0), second)
    return jnp.where(low, first, pltpu.roll(second, NODES, 0))


VMEM = pl.BlockSpec(memory_space=pltpu.VMEM)
HBM = pl.BlockSpec(memory_space=pltpu.HBM)
ANY = pl.BlockSpec(memory_space=pl.ANY)


def call(kernel, outs, in_specs, scratch=(), cost=0, name=None):
    kinds = [x if hasattr(x, "dtype") else pltpu.VMEM(x, jnp.float32) for x in outs]
    return pl.pallas_call(
        kernel,
        out_shape=kinds,
        in_specs=in_specs,
        out_specs=[VMEM] * len(outs),
        scratch_shapes=list(scratch),
        compiler_params=pltpu.CompilerParams(vmem_limit_bytes=24 * 1024 * 1024),
        cost_estimate=pl.CostEstimate(flops=cost, bytes_accessed=cost, transcendentals=0),
        name=name,
    )


def per_device(
    prognostic, metric, first_flux, second_flux, neighbour_face, orientation, coupling, damping
):
    fields, levels = prognostic.shape[:2]
    lanes = prognostic.shape[-1]
    whole = (fields, levels * POINTS, lanes)
    metric = metric.reshape(POINTS, lanes)
    neighbour_face = neighbour_face.reshape(4, lanes)
    orientation = orientation.reshape(4, lanes)
    coupling = coupling.reshape(4, coupling.shape[1], NODES, lanes)
    damping = damping.reshape(NODES, lanes)
    tables, _ = operator_tables(lanes)

    def shifts(axis):
        size = lax.axis_size(axis)
        up = [(i, (i + 1) % size) for i in range(size)]
        return up, [(j, i) for i, j in up]

    def exchange(arrays, ways):
        size = lax.axis_size("vz")
        return [
            lax.ppermute(x, "vz", [(i, i ^ way) for i in range(size)]) if way else x
            for x, way in zip(arrays, ways)
        ]

    count = lax.axis_size("hy")
    near = [(i, i ^ 1) for i in range(count)]
    other = [(i, (i + 1 if i % 2 else i - 1) % count) for i in range(count)]
    second_up, second_down = shifts("hx")
    width = len(RIM_POINTS)
    message = (-(-((levels + 2) * width + 2) // ROWS) * ROWS, lanes)
    sides = (-(-fields * len(chunks(levels)) // 4) * ROWS, lanes)
    padded = levels + 2 * ROWS
    table = pltpu.VMEM((4, lanes), jnp.int32)
    inputs = (
        prognostic.reshape(whole),
        neighbour_face,
        orientation,
        metric,
        jnp.asarray(tables),
        first_flux,
        second_flux,
    )
    (
        to_other,
        state,
        neighbour_face,
        orientation,
        metric,
        tables,
        fluxes,
    ) = call(
        rim_kernel,
        [
            message,
            whole,
            table,
            table,
            (POINTS, lanes),
            tables.shape,
            (-(-2 * fields * fields // ROWS) * ROWS, lanes),
        ],
        [HBM] * len(inputs),
        [
            pltpu.VMEM((width, padded, lanes), jnp.float32),
            pltpu.VMEM((width, padded, lanes), jnp.float32),
            pltpu.SMEM((fields, fields), jnp.float32),
            pltpu.SMEM((fields, fields), jnp.float32),
            pltpu.SemaphoreType.DMA((6 + -(-levels // ROWS),)),
        ],
        cost=1000,
        name="rim",
    )(*(pltpu.with_memory_space_constraint(x, pltpu.HBM) for x in inputs))
    state = state.reshape(fields * levels * POINTS, lanes)
    from_other = lax.ppermute(to_other, "hy", other)
    from_near = lax.ppermute(state, "hy", near)
    (to_sides,) = call(edge_kernel, [sides], [VMEM], cost=1000, name="edge")(state)
    from_down = lax.ppermute(to_sides, "hx", second_up)
    from_up = from_down
    if lax.axis_size("hx") > 2:
        from_up = lax.ppermute(to_sides, "hx", second_down)

    column = (coupling.shape[1], NODES, lanes)
    factors = call(factor_kernel, [column] * 7, [VMEM] * 2, cost=4000000, name="factor")(
        coupling, damping
    )
    block = ((levels + 2) * NODES, lanes)
    part, base = call(
        element_kernel,
        [state.shape, (NODES,) + block],
        [VMEM] * 6,
        [
            pltpu.VMEM((levels * 8 * fields, lanes), jnp.float32),
            pltpu.VMEM((fields * POINTS, lanes), jnp.bfloat16),
            pltpu.VMEM((fields * POINTS, lanes), jnp.bfloat16),
        ],
        cost=4000000,
        name="element",
    )(
        state,
        neighbour_face,
        orientation,
        metric,
        fluxes,
        tables,
    )
    late = levels * NODES * len(LATE_FIELDS)
    base, near_late = call(
        near_kernel,
        [(NODES,) + block, (late, lanes)],
        [VMEM] * 6,
        [pltpu.VMEM((NODES, padded, lanes), jnp.float32), pltpu.VMEM(block, jnp.float32)],
        cost=1000,
        name="near",
    )(from_near, neighbour_face, orientation, fluxes, base, metric)
    count = -(-(levels + 2) // ROWS) * ROWS
    (half,) = call(
        half_pack_kernel,
        [(NODES,) + block],
        [VMEM] * 7 + [ANY],
        [
            pltpu.VMEM((NODES, count * NODES, lanes), jnp.float32),
            pltpu.VMEM((padded, lanes), jnp.float32),
            pltpu.VMEM((count, lanes), jnp.float32),
        ],
        cost=1000,
        name="half_pack",
    )(
        base,
        from_down,
        from_up,
        neighbour_face,
        orientation,
        metric,
        fluxes,
        factors[0],
    )
    sends = call(
        pack_kernel,
        [((levels + 2 + more) * NODES, lanes) for more in FORWARD_ROOM],
        [VMEM] * 5,
        [pltpu.VMEM((NODES,) + block, jnp.float32)],
        cost=1000,
        name="pack",
    )(half, from_other, neighbour_face, orientation, metric)
    size = lax.axis_size("vz")
    falls = [(i, i ^ 3) for i in range(size) if i > i ^ 3]
    rises = [(j, i) for i, j in falls]
    fallen = lax.ppermute(sends[0], "vz", falls)
    risen = lax.ppermute(sends[1], "vz", rises)
    middle, beside, own = exchange(sends[2:], WAYS[2:])
    received = [fallen, middle, risen, beside, own]

    other_face = call(
        functools.partial(face_kernel, 1),
        [(late // 2, lanes)] * 2,
        [VMEM] * 3 + [ANY],
        cost=1000,
        name="other_face",
    )(state, from_other, fluxes, sends[-1])
    other_face = [lax.ppermute(x, "hy", other) for x in other_face]

    cube = (levels + 2, NODES, lanes)
    speeds = call(
        solve_kernel,
        [cube] * NODES,
        [VMEM] * (7 + 1 + NODES),
        [
            pltpu.VMEM(column, jnp.float32),
            pltpu.VMEM((NODES, 2, NODES, lanes), jnp.float32),
            pltpu.VMEM((column[0] + 2,) + column[1:], jnp.float32),
        ],
        cost=1000,
        name="solve",
    )(*factors, *[x.reshape(-1, NODES, lanes) for x in received])
    returned = exchange([x.reshape(block) for x in speeds], BACK_WAYS)
    size = levels * POINTS
    limits = pltpu.CompilerParams(vmem_limit_bytes=24 * 1024 * 1024)
    earlier, done = pl.pallas_call(
        finish_section_kernel,
        out_shape=[
            jax.ShapeDtypeStruct(whole, jnp.float32),
            pltpu.VMEM((2, size, lanes), jnp.float32),
        ],
        in_specs=[VMEM] * 10,
        out_specs=[HBM, VMEM],
        scratch_shapes=[
            pltpu.VMEM((2, size, lanes), jnp.float32),
            pltpu.SemaphoreType.DMA,
        ],
        compiler_params=limits,
        cost_estimate=pl.CostEstimate(flops=4000000, bytes_accessed=4000000, transcendentals=0),
        name="finish",
    )(
        part, near_late, *other_face, from_down, from_up, neighbour_face, orientation, metric, fluxes
    )
    updated = pl.pallas_call(
        update_kernel,
        out_shape=jax.ShapeDtypeStruct(whole, jnp.float32),
        in_specs=[VMEM] * (1 + NODES) + [HBM],
        out_specs=HBM,
        input_output_aliases={1 + NODES: 0},
        scratch_shapes=[
            pltpu.VMEM((NODES,) + block, jnp.float32),
            pltpu.VMEM((3, size, lanes), jnp.float32),
            pltpu.SemaphoreType.DMA((6,)),
        ],
        compiler_params=limits,
        name="update",
    )(*returned, done, earlier)
    return updated.reshape(prognostic.shape)


def solution(mesh):
    placed = (
        P(None, "vz", None, None, "hy", "hx"),
        P(None, None, "hy", "hx"),
        P(),
        P(),
        P(None, "hy", "hx"),
        P(None, "hy", "hx"),
        P(None, None, "vz", None, "hy", "hx"),
        P("vz", None, "hy", "hx"),
    )
    return jax.shard_map(
        per_device,
        mesh=mesh,
        in_specs=placed,
        out_specs=P(None, "vz", None, None, "hy", "hx"),
        check_vma=False,
    )
```

```python
import functools

import jax
import jax.numpy as jnp
import numpy as np
from jax import lax
from jax.experimental import pallas as pl
from jax.experimental.pallas import tpu as pltpu
from jax.sharding import PartitionSpec as P

step_size = 0.05
lift_weight = 6.0
gravity_couple = 0.5
density_couple = 0.3
theta_couple = 0.4

NODES = 4
POINTS = NODES * NODES
FIELDS = 5
FACE_POINTS = ((0, 4, 8, 12), (3, 7, 11, 15), (0, 1, 2, 3), (12, 13, 14, 15))
RIM_POINTS = tuple(sorted(set(sum(FACE_POINTS, ()))))
ROWS = 8
LATE_FIELDS = (0, 1, 2, 4)
WAYS = (2, 3, 1, 0)
BACK_WAYS = (3, 2, 1, 0)


def derivative_table():
    points = np.array([-1.0, -1.0 / np.sqrt(5.0), 1.0 / np.sqrt(5.0), 1.0])
    number = points.shape[0]
    barycentric = np.ones(number)
    for source in range(number):
        for another in range(number):
            if another != source:
                barycentric[source] = barycentric[source] / (points[source] - points[another])
    matrix = np.zeros((number, number))
    for target in range(number):
        for source in range(number):
            if target != source:
                matrix[target, source] = (
                    barycentric[source] / barycentric[target] / (points[target] - points[source])
                )
        matrix[target, target] = -np.sum(matrix[target])
    return matrix


def operator_tables(lanes):
    weight = 0.5 * lift_weight
    table = derivative_table()
    table[0, 0] += weight
    table[-1, -1] -= weight
    eye = np.eye(NODES)
    along_first = np.kron(eye, table)
    along_second = np.kron(table, eye)
    ends = np.zeros(NODES)
    ends[0] = ends[-1] = 1.0
    faces = np.diag(np.kron(np.ones(NODES), ends) + np.kron(ends, np.ones(NODES)))
    first = np.zeros((POINTS, lanes))
    second = np.zeros((POINTS, lanes))
    same = np.zeros((FIELDS, POINTS, lanes))
    owner = np.full((lanes,), -1)
    for g in range(FIELDS):
        own = slice(POINTS * g, POINTS * (g + 1))
        first[:, own] = -along_first
        second[:, own] = -along_second
        same[g, :, own] = -weight * faces
        owner[own] = g
        for k in range(NODES):
            south = FIELDS * POINTS + 2 * NODES * g + k
            north = south + NODES
            second[FACE_POINTS[2][k], south] = weight
            second[FACE_POINTS[3][k], north] = -weight
            same[g, FACE_POINTS[2][k], south] = weight
            same[g, FACE_POINTS[3][k], north] = weight
            owner[south] = owner[north] = g
    tables = np.concatenate([first, second, same.reshape(FIELDS * POINTS, lanes)])
    return tables.astype(np.float32), owner


def chunks(total):
    return [min(start, total - ROWS) for start in range(0, total, ROWS)]


def partner_side(partner):
    odd = lax.rem(lax.axis_index("hy"), 2)
    return odd if partner else 1 - odd


def side_sign(side):
    return (2 * side - 1).astype(jnp.float32)


def pick(values, masks, flip):
    chosen = []
    for k in range(NODES):
        row = values[FACE_POINTS[0][k]]
        for option in range(1, 4):
            row = jnp.where(masks[option], values[FACE_POINTS[option][k]], row)
        chosen.append(row)
    return [jnp.where(flip, chosen[NODES - 1 - k], chosen[k]) for k in range(NODES)]


def table_masks(face_row, flip_row, lanes):
    face = jnp.broadcast_to(face_row, (ROWS, lanes))
    flip = jnp.broadcast_to(flip_row, (ROWS, lanes))
    return [face == option for option in range(4)], flip == 1


def flux_row(f, g, matrix):
    return (matrix * FIELDS + f) * FIELDS + g


def along(fluxes, matrix, f, rows):
    total = None
    for g in range(FIELDS):
        at = flux_row(f, g, matrix)
        term = fluxes[at : at + 1, :] * rows[g]
        total = term if total is None else total + term
    return total


def side_rows(f, piece):
    number = 3 * f + piece
    return number // 4, 32 * (number % 4)


def rim_kernel(
    state_hbm,
    face_hbm,
    way_hbm,
    metric_hbm,
    tables_hbm,
    flux_hbm,
    second_hbm,
    to_other,
    state,
    neighbour_face,
    orientation,
    metric,
    tables,
    fluxes,
    column,
    speed,
    flux,
    second_flux,
    semaphores,
):
    levels = state.shape[1] // POINTS
    face = partner_side(1)
    sign = side_sign(face)
    lanes = state.shape[2]
    width = len(RIM_POINTS)
    groups = [(start, min(start + ROWS, levels)) for start in range(0, levels, ROWS)]
    small = [
        pltpu.make_async_copy(source, target, semaphores.at[place])
        for place, (source, target) in enumerate(
            (
                (flux_hbm, flux),
                (face_hbm, neighbour_face),
                (way_hbm, orientation),
                (metric_hbm, metric),
                (tables_hbm, tables),
                (second_hbm, second_flux),
            )
        )
    ]
    large = []
    for place, (low, high) in enumerate(groups):
        rows = pl.ds(low * POINTS, (high - low) * POINTS)
        large.append(
            pltpu.make_async_copy(
                state_hbm.at[:, rows, :], state.at[:, rows, :], semaphores.at[len(small) + place]
            )
        )
    for copy in (small[0], small[5], *large, *small[1:5]):
        copy.start()
    column[...] = jnp.zeros_like(column)
    small[0].wait()
    small[5].wait()
    for place, source in enumerate((flux, second_flux)):
        for f in range(FIELDS):
            for g in range(FIELDS):
                at = flux_row(f, g, place)
                fluxes[at : at + 1, :] = jnp.full((1, lanes), source[f, g])
    arrived = 0
    for piece, start in enumerate(chunks(levels)):
        while arrived < len(groups) and groups[arrived][0] < start + ROWS:
            large[arrived].wait()
            arrived += 1
        for place, point in enumerate(RIM_POINTS):
            rows = [
                state[g, pl.ds(start * POINTS + point, ROWS, stride=POINTS), :]
                for g in range(FIELDS)
            ]
            for f, out in ((3, speed), (4, column)):
                normal = (sign * flux[f, 0]) * rows[0]
                for g in range(1, FIELDS):
                    normal = normal + (sign * flux[f, g]) * rows[g]
                out[place, pl.ds(ROWS + start, ROWS), :] = rows[f] + normal
    small[1].wait()
    small[2].wait()
    end = (levels + 2) * width
    for place in range(width):
        for start in chunks(levels):
            upper = column[place, pl.ds(ROWS + start + 1, ROWS), :]
            lower = column[place, pl.ds(ROWS + start - 1, ROWS), :]
            to_other[pl.ds(start * width + place, ROWS, stride=width), :] = speed[
                place, pl.ds(ROWS + start, ROWS), :
            ] - gravity_couple * (upper - lower)
        for extra, level in ((0, 0), (1, levels - 1)):
            at = (levels + extra) * width + place
            to_other[at : at + 1, :] = column[place, ROWS + level : ROWS + level + 1, :]
    to_other[end : end + 1, :] = neighbour_face[pl.ds(face, 1), :].astype(jnp.float32)
    to_other[end + 1 : end + 2, :] = orientation[pl.ds(face, 1), :].astype(jnp.float32)
    left = to_other.shape[0] - end - 2
    to_other[end + 2 :, :] = jnp.zeros((left, lanes), jnp.float32)
    small[3].wait()
    small[4].wait()


def edge_kernel(state, to_sides):
    lanes = state.shape[1]
    levels = state.shape[0] // (FIELDS * POINTS)
    lane = lax.broadcasted_iota(jnp.int32, (ROWS, lanes), 1)
    packed = [jnp.zeros((ROWS, lanes), jnp.float32) for _ in range(to_sides.shape[0] // ROWS)]
    for f in range(FIELDS):
        for piece, start in enumerate(chunks(levels)):
            block, at = side_rows(f, piece)
            for place, point in enumerate(RIM_POINTS):
                row = state[pl.ds((f * levels + start) * POINTS + point, ROWS, stride=POINTS), :]
                first = at + 2 * place
                packed[block] = jnp.where(
                    lane // 2 == first // 2, pltpu.roll(row, first + 1, 1), packed[block]
                )
    for block, value in enumerate(packed):
        to_sides[block * ROWS : (block + 1) * ROWS, :] = value


def near_kernel(
    state, neighbour_face, orientation, fluxes, base, metric, half, late, column, source
):
    lanes = state.shape[1]
    levels = state.shape[0] // (FIELDS * POINTS)
    face = partner_side(0)
    sign = -side_sign(face)
    masks, flip = table_masks(
        neighbour_face[pl.ds(face, 1), :], orientation[pl.ds(face, 1), :], lanes
    )
    column[...] = jnp.zeros_like(column)
    speeds = []
    for start in chunks(levels):
        picked = []
        for g in range(FIELDS):
            values = {
                point: state[pl.ds((g * levels + start) * POINTS + point, ROWS, stride=POINTS), :]
                for point in RIM_POINTS
            }
            picked.append(pick(values, masks, flip))
        for k in range(NODES):
            rows = [picked[g][k] for g in range(FIELDS)]
            changed = [rows[f] + sign * along(fluxes, 0, f, rows) for f in range(FIELDS)]
            for place, f in enumerate(LATE_FIELDS):
                at = (place * levels + start) * NODES + k
                late[pl.ds(at, ROWS, stride=NODES), :] = changed[f]
            column[k, pl.ds(ROWS + start, ROWS), :] = changed[4]
            speeds.append(changed[3])
    for piece, start in enumerate(chunks(levels)):
        for k in range(NODES):
            upper = column[k, pl.ds(ROWS + start + 1, ROWS), :]
            lower = column[k, pl.ds(ROWS + start - 1, ROWS), :]
            source[pl.ds(start * NODES + k, ROWS, stride=NODES), :] = speeds[
                NODES * piece + k
            ] - gravity_couple * (upper - lower)
    for extra, level in ((0, 0), (1, levels - 1)):
        for k in range(NODES):
            at = (levels + extra) * NODES + k
            source[at : at + 1, :] = column[k, ROWS + level : ROWS + level + 1, :]
    for start in chunks(levels + 2):
        picked = [source[pl.ds(start * NODES + k, ROWS, stride=NODES), :] for k in range(NODES)]
        add_first_side(0, start, picked, half, metric)


def face_kernel(partner, state, received, fluxes, *rest):
    lanes = state.shape[1]
    levels = state.shape[0] // (FIELDS * POINTS)
    at = (levels + 2) * len(RIM_POINTS)
    outs = rest[-2:]
    share = len(LATE_FIELDS) // len(outs)
    sign = side_sign(partner_side(partner))
    masks, flip = table_masks(
        received[at : at + 1, :].astype(jnp.int32),
        received[at + 1 : at + 2, :].astype(jnp.int32),
        lanes,
    )
    for start in chunks(levels):
        picked = []
        for g in range(FIELDS):
            values = {
                point: state[pl.ds((g * levels + start) * POINTS + point, ROWS, stride=POINTS), :]
                for point in RIM_POINTS
            }
            picked.append(pick(values, masks, flip))
        for place, f in enumerate(LATE_FIELDS):
            for k in range(NODES):
                normal = along(fluxes, 0, f, [picked[g][k] for g in range(FIELDS)])
                at = ((place % share) * levels + start) * NODES + k
                outs[place // share][pl.ds(at, ROWS, stride=NODES), :] = (
                    picked[f][k] + sign * normal
                )


def element_kernel(
    state,
    neighbour_face,
    orientation,
    metric,
    fluxes,
    tables,
    part,
    base,
    outer,
    operator_high,
    operator_low,
):
    levels = state.shape[0] // (FIELDS * POINTS)
    lanes = state.shape[1]
    lane = lax.broadcasted_iota(jnp.int32, (ROWS, lanes), 1)
    sides = []
    for side, (face, edge) in enumerate(((2, 0), (3, lanes - 1))):
        shift = 1 if side == 0 else lanes - 1
        row = jnp.broadcast_to(neighbour_face[face : face + 1, :], (ROWS, lanes))
        way = jnp.broadcast_to(orientation[face : face + 1, :], (ROWS, lanes))
        masks, flip = table_masks(
            pltpu.roll(row, lanes - shift, 1), pltpu.roll(way, lanes - shift, 1), lanes
        )
        sides.append((shift, edge, masks, flip))
    for f in range(FIELDS):
        for start in chunks(levels):
            q = f * levels + start
            values = {
                point: state[pl.ds(q * POINTS + point, ROWS, stride=POINTS), :]
                for point in RIM_POINTS
            }
            for side, (shift, edge, masks, flip) in enumerate(sides):
                for k, row in enumerate(pick(values, masks, flip)):
                    at = start * 8 * FIELDS + 8 * f + NODES * side + k
                    outer[pl.ds(at, ROWS, stride=8 * FIELDS), :] = jnp.where(
                        lane == edge, 0.0, pltpu.roll(row, shift, 1)
                    )
    index = lax.broadcasted_iota(jnp.int32, (1, lanes), 1)
    own_columns = FIELDS * POINTS
    owner = jnp.where(index < own_columns, index // POINTS, (index - own_columns) // 8)
    for f in range(FIELDS):
        first_row = jnp.zeros((1, lanes), jnp.float32)
        second_row = first_row
        for g in range(FIELDS):
            first, second = (flux_row(f, g, matrix) for matrix in range(2))
            first_row = jnp.where(owner == g, fluxes[first : first + 1, :], first_row)
            second_row = jnp.where(owner == g, fluxes[second : second + 1, :], second_row)
        block = (
            first_row * tables[0:POINTS, :]
            + second_row * tables[POINTS : 2 * POINTS, :]
            + tables[(2 + f) * POINTS : (3 + f) * POINTS, :]
        )
        high = block.astype(jnp.bfloat16)
        operator_high[f * POINTS : (f + 1) * POINTS, :] = high
        operator_low[f * POINTS : (f + 1) * POINTS, :] = (
            block - high.astype(jnp.float32)
        ).astype(jnp.bfloat16)
    high = operator_high[...]
    low = operator_low[...]
    scale = step_size * metric[...]
    blank = jnp.zeros((lanes - own_columns - 8 * FIELDS, lanes), jnp.float32)
    for pair in range(0, levels, 2):
        sides = []
        for level in (pair, pair + 1):
            rows = [
                state[pl.ds((f * levels + level) * POINTS, POINTS), :] for f in range(FIELDS)
            ]
            rows.append(outer[pl.ds(level * 8 * FIELDS, 8 * FIELDS), :])
            rows.append(blank)
            sides.append(jnp.concatenate(rows, axis=0))
        values = jnp.concatenate(sides, axis=1)
        top = values.astype(jnp.bfloat16)
        rest = (values - top.astype(jnp.float32)).astype(jnp.bfloat16)
        change = (
            jnp.dot(high, top, preferred_element_type=jnp.float32)
            + jnp.dot(high, rest, preferred_element_type=jnp.float32)
            + jnp.dot(low, top, preferred_element_type=jnp.float32)
        )
        for place, level in enumerate((pair, pair + 1)):
            for f in range(FIELDS):
                at = pl.ds((f * levels + level) * POINTS, POINTS)
                part[at, :] = (
                    state[at, :]
                    + scale
                    * change[
                        f * POINTS : (f + 1) * POINTS, place * lanes : (place + 1) * lanes
                    ]
                )
    for level in range(levels):
        speed = part[pl.ds((3 * levels + level) * POINTS, POINTS), :]
        upper = part[pl.ds((4 * levels + level + 1) * POINTS, POINTS), :] if level < levels - 1 else 0.0
        lower = part[pl.ds((4 * levels + level - 1) * POINTS, POINTS), :] if level else 0.0
        value = speed - gravity_couple * (upper - lower)
        for j in range(NODES):
            base[j, level * NODES : (level + 1) * NODES, :] = value[NODES * j : NODES * (j + 1)]
    for extra, level in ((0, 0), (1, levels - 1)):
        value = part[pl.ds((4 * levels + level) * POINTS, POINTS), :]
        at = (levels + extra) * NODES
        for j in range(NODES):
            base[j, at : at + NODES, :] = value[NODES * j : NODES * (j + 1)]


def side_corrections(received, side, fluxes, fields, pieces):
    lanes = received.shape[1]
    sign = 1.0 if side == 0 else -1.0
    result = [[] for _ in fields]
    for piece in range(pieces):
        rows = []
        for g in range(FIELDS):
            block, at = side_rows(g, piece)
            rows.append(
                pltpu.roll(
                    received[block * ROWS : (block + 1) * ROWS, :], (lanes - at - side) % lanes, 1
                )
            )
        for place, f in enumerate(fields):
            result[place].append(rows[f] + sign * along(fluxes, 1, f, rows))
    return result


def spread(value, edge, masks, flip):
    lanes = value.shape[1]
    values = {
        point: pltpu.roll(value, (edge - 2 * place) % lanes, 1)
        for place, point in enumerate(RIM_POINTS)
    }
    return pick(values, masks, flip)


def add_first_side(partner, start, picked, send, metric):
    weight = 0.5 * lift_weight * step_size
    i = (NODES - 1) * partner_side(partner)
    fresh = fresh_rows(start, picked[0].shape)
    for j, row in enumerate(picked):
        at = pl.ds(start * NODES + i, ROWS, stride=NODES)
        scale = weight * metric[pl.ds(NODES * j + i, 1), :]
        send[j, at, :] += jnp.where(fresh, scale * row, 0.0)


def fresh_rows(start, shape):
    return lax.broadcasted_iota(jnp.int32, shape, 0) >= (-start) % ROWS


def pack_kernel(half, from_other, neighbour_face, orientation, metric, *rest):
    sends, (send,) = rest[:NODES], rest[NODES:]
    me = lax.axis_index("vz")
    send[...] = half[...]
    rows, lanes = half.shape[1:]
    width = len(RIM_POINTS)
    face = partner_side(1)
    masks, flip = table_masks(
        neighbour_face[pl.ds(face, 1), :], orientation[pl.ds(face, 1), :], lanes
    )
    for start in chunks(rows // NODES):
        values = {
            point: from_other[pl.ds(start * width + place, ROWS, stride=width), :]
            for place, point in enumerate(RIM_POINTS)
        }
        add_first_side(1, start, pick(values, masks, flip), send, metric)
    for out, way in zip(sends, WAYS):
        out[...] = send[me ^ way]


def half_pack_kernel(
    base,
    from_down,
    from_up,
    neighbour_face,
    orientation,
    metric,
    fluxes,
    factored,
    half,
    column,
    mixed,
):
    rows, lanes = base.shape[1:]
    levels = rows // NODES - 2
    width = len(RIM_POINTS)
    weight = 0.5 * lift_weight * step_size
    column[...] = jnp.zeros_like(column)
    mixed[...] = jnp.zeros_like(mixed)
    lane = lax.broadcasted_iota(jnp.int32, (ROWS, lanes), 1)
    for side, (received, edge, j) in enumerate(
        ((from_down, 0, 0), (from_up, lanes - 1, NODES - 1))
    ):
        face = 2 + side
        masks, flip = table_masks(
            neighbour_face[face : face + 1, :], orientation[face : face + 1, :], lanes
        )
        speed, heat = side_corrections(received, side, fluxes, (3, 4), len(chunks(levels)))
        for start, value in zip(chunks(levels), heat):
            column[pl.ds(ROWS + start, ROWS), :] = value
        for start, value in zip(chunks(levels), speed):
            upper = column[pl.ds(ROWS + start + 1, ROWS), :]
            lower = column[pl.ds(ROWS + start - 1, ROWS), :]
            mixed[pl.ds(start, ROWS), :] = value - gravity_couple * (upper - lower)
        mixed[levels : levels + 1, :] = column[ROWS : ROWS + 1, :]
        mixed[levels + 1 : levels + 2, :] = column[ROWS + levels - 1 : ROWS + levels, :]
        for start in chunks(levels + 2):
            fresh = (lane == edge) & fresh_rows(start, lane.shape)
            picked = spread(mixed[start : start + ROWS, :], edge, masks, flip)
            for k, row in enumerate(picked):
                point = NODES * j + k
                at = pl.ds(start * NODES + k, ROWS, stride=NODES)
                scale = weight * metric[point : point + 1, :]
                half[j, at, :] += jnp.where(fresh, scale * row, 0.0)


def finish_section_kernel(
    part,
    near,
    other_early,
    other_late,
    from_down,
    from_up,
    neighbour_face,
    orientation,
    metric,
    fluxes,
    out,
    done,
    final,
    semaphore,
):
    levels = part.shape[0] // (FIELDS * POINTS)
    lanes = part.shape[1]
    size = levels * POINTS
    weight = 0.5 * lift_weight * step_size
    scale = weight * metric[...]
    lane = lax.broadcasted_iota(jnp.int32, (ROWS, lanes), 1)
    tables = []
    edges = []
    for side, received in enumerate((from_down, from_up)):
        face = 2 + side
        tables.append(
            table_masks(
                neighbour_face[face : face + 1, :], orientation[face : face + 1, :], lanes
            )
        )
        edges.append(
            side_corrections(received, side, fluxes, LATE_FIELDS, len(chunks(levels)))
        )
    copy = pltpu.make_async_copy(final, out.at[1:3], semaphore)
    sources = ((near,), (other_early, other_late))
    for place, f in ((1, 1), (2, 2), (0, 0), (3, 4)):
        target = final.at[f - 1] if f in (1, 2) else done.at[min(f, 1)]
        target[...] = part[f * size : (f + 1) * size, :]
        for piece, start in enumerate(chunks(levels)):
            for j in range(NODES):
                for partner, source in enumerate(sources):
                    point = NODES * j + (NODES - 1) * partner_side(partner)
                    share = len(LATE_FIELDS) // len(source)
                    rows = source[place // share][
                        pl.ds(((place % share) * levels + start) * NODES + j, ROWS, stride=NODES),
                        :,
                    ]
                    at = pl.ds(start * POINTS + point, ROWS, stride=POINTS)
                    target[at, :] = (
                        part[pl.ds(f * size + start * POINTS + point, ROWS, stride=POINTS), :]
                        + weight * metric[pl.ds(point, 1), :] * rows
                    )
        for piece, start in enumerate(chunks(levels)):
            row_index = lax.broadcasted_iota(jnp.int32, (ROWS, lanes), 0)
            fresh = row_index >= (-start) % ROWS
            for side, (edge, j) in enumerate(((0, 0), (lanes - 1, NODES - 1))):
                picked = spread(edges[side][place][piece], edge, *tables[side])
                for k, row in enumerate(picked):
                    point = NODES * j + k
                    at = pl.ds(start * POINTS + point, ROWS, stride=POINTS)
                    target[at, :] += jnp.where(
                        (lane == edge) & fresh, scale[point : point + 1, :] * row, 0.0
                    )
        if f == 2:
            copy.start()
    copy.wait()


def factor_kernel(coupling, damping, inverse, near, far_two, far_three, ratio, next_two, next_three):
    levels = coupling.shape[1]
    blank = jnp.zeros(coupling.shape[2:], jnp.float32)
    far_ratio, far_second, near_ratio, near_second = (blank,) * 4
    far_before, near_before = blank, blank
    extra = damping[...]
    for level in range(levels):
        a, b, d, e = (coupling[entry, level] for entry in range(4))
        centre = a + b + d + e + extra
        reduced = -b + a * far_ratio
        pivot = centre + a * far_second - reduced * near_ratio
        scaled = 1.0 / pivot
        upper_ratio = (-d - reduced * near_second) * scaled
        second_ratio = -e * scaled
        far_here, near_here = a * scaled, reduced * scaled
        inverse[level] = scaled
        near[level] = near_here
        far_two[level] = far_here + near_here * near_before
        far_three[level] = near_here * far_before
        ratio[level] = upper_ratio
        if level:
            next_two[level - 1] = near_ratio * upper_ratio - near_second
            next_three[level - 1] = near_ratio * second_ratio
        far_before, near_before = far_here, near_here
        far_ratio, far_second = near_ratio, near_second
        near_ratio, near_second = upper_ratio, second_ratio
    next_two[levels - 1] = -near_second
    next_three[levels - 1] = blank


def solve_kernel(inverse, near, far_two, far_three, ratio, next_two, next_three, *rest):
    ways = NODES
    received, sends, (source, heat, speed) = rest[:ways], rest[ways : 2 * ways], rest[2 * ways :]
    levels = near.shape[0]
    here = levels // ways
    me = lax.axis_index("vz")
    for values, way in zip(received, WAYS):
        block = me ^ way
        source[pl.ds(block * here, here)] = values[0:here]
        heat[block] = values[here : here + 2]
    for block in range(ways - 1):
        last = block * here + here - 1
        source[last] = source[last] - gravity_couple * heat[block + 1, 0]
        source[last + 1] = source[last + 1] + gravity_couple * heat[block, 1]
    blank = jnp.zeros(near.shape[1:], jnp.float32)
    scaled = blank
    known = [blank, blank, blank]
    for level in range(levels):
        before, scaled = scaled, source[level] * inverse[level]
        value = scaled - near[level] * before - far_three[level] * known[-3]
        value = value + far_two[level] * known[-2]
        source[level] = value
        known = [*known[1:], value]
    speed[0] = blank
    speed[levels + 1] = blank
    known = [blank, blank, blank]
    above = blank
    for level in range(levels - 1, -1, -1):
        here_value = source[level]
        value = here_value - ratio[level] * above + next_three[level] * known[-3]
        value = value + next_two[level] * known[-2]
        speed[level + 1] = value
        above = here_value
        known = [*known[1:], value]
    for send, way in zip(sends, BACK_WAYS):
        send[...] = speed[pl.ds((me ^ way) * here, here + 2)]


def update_kernel(*refs):
    ways = NODES
    received, (done, earlier, out, speed, final, semaphores) = refs[:ways], refs[ways:]
    levels = done.shape[1] // POINTS
    me = lax.axis_index("vz")
    for values, way in zip(received, BACK_WAYS):
        speed[me ^ way] = values[...]
    lanes = done.shape[2]
    half = levels // 2
    low = lax.broadcasted_iota(jnp.int32, (ROWS, lanes), 0) < NODES
    copies = []
    for pair in range(half):
        lower = [speed[j, pair * ROWS : (pair + 1) * ROWS, :] for j in range(NODES)]
        upper = [speed[j, (pair + 1) * ROWS : (pair + 2) * ROWS, :] for j in range(NODES)]
        jump = [above - below for above, below in zip(upper, lower)]
        value = [jnp.where(low, above, below) for above, below in zip(upper, lower)]
        for h in range(2):
            a, b = 2 * h, 2 * h + 1
            for odd in range(2):
                at = pl.ds((2 * pair + odd) * POINTS + ROWS * h, ROWS)
                jumps = side_by_side(jump[a], jump[b], odd, low)
                final[0, at, :] = done[0, at, :] - density_couple * jumps
                final[1, at, :] = side_by_side(value[a], value[b], 1 - odd, low)
                final[2, at, :] = done[1, at, :] - theta_couple * jumps
        if pair in (half // 2 - 1, half - 1):
            first = 0 if pair < half - 1 else half // 2
            rows = pl.ds(first * 2 * POINTS, (pair + 1 - first) * 2 * POINTS)
            for place, f in enumerate((0, 3, 4)):
                copies.append(
                    pltpu.make_async_copy(
                        final.at[place, rows, :], out.at[f, rows, :], semaphores.at[len(copies)]
                    )
                )
                copies[-1].start()
    for copy in copies:
        copy.wait()


def side_by_side(first, second, upper, low):
    if upper:
        return jnp.where(low, pltpu.roll(first, NODES, 0), second)
    return jnp.where(low, first, pltpu.roll(second, NODES, 0))


VMEM = pl.BlockSpec(memory_space=pltpu.VMEM)
HBM = pl.BlockSpec(memory_space=pltpu.HBM)
ANY = pl.BlockSpec(memory_space=pl.ANY)


def call(kernel, outs, in_specs, scratch=(), cost=0, name=None, aliases=None):
    kinds = [x if hasattr(x, "dtype") else pltpu.VMEM(x, jnp.float32) for x in outs]
    return pl.pallas_call(
        kernel,
        out_shape=kinds,
        in_specs=in_specs,
        out_specs=[VMEM] * len(outs),
        scratch_shapes=list(scratch),
        input_output_aliases=aliases or {},
        compiler_params=pltpu.CompilerParams(vmem_limit_bytes=24 * 1024 * 1024),
        cost_estimate=pl.CostEstimate(flops=cost, bytes_accessed=cost, transcendentals=0),
        name=name,
    )


def per_device(
    prognostic, metric, first_flux, second_flux, neighbour_face, orientation, coupling, damping
):
    fields, levels = prognostic.shape[:2]
    lanes = prognostic.shape[-1]
    whole = (fields, levels * POINTS, lanes)
    metric = metric.reshape(POINTS, lanes)
    neighbour_face = neighbour_face.reshape(4, lanes)
    orientation = orientation.reshape(4, lanes)
    coupling = coupling.reshape(4, coupling.shape[1], NODES, lanes)
    damping = damping.reshape(NODES, lanes)
    tables, _ = operator_tables(lanes)

    def shifts(axis):
        size = lax.axis_size(axis)
        up = [(i, (i + 1) % size) for i in range(size)]
        return up, [(j, i) for i, j in up]

    def exchange(arrays, ways):
        size = lax.axis_size("vz")
        return [
            lax.ppermute(x, "vz", [(i, i ^ way) for i in range(size)]) if way else x
            for x, way in zip(arrays, ways)
        ]

    count = lax.axis_size("hy")
    near = [(i, i ^ 1) for i in range(count)]
    other = [(i, (i + 1 if i % 2 else i - 1) % count) for i in range(count)]
    second_up, second_down = shifts("hx")
    width = len(RIM_POINTS)
    message = (-(-((levels + 2) * width + 2) // ROWS) * ROWS, lanes)
    sides = (-(-fields * len(chunks(levels)) // 4) * ROWS, lanes)
    padded = levels + 2 * ROWS
    table = pltpu.VMEM((4, lanes), jnp.int32)
    inputs = (
        prognostic.reshape(whole),
        neighbour_face,
        orientation,
        metric,
        jnp.asarray(tables),
        first_flux,
        second_flux,
    )
    (
        to_other,
        state,
        neighbour_face,
        orientation,
        metric,
        tables,
        fluxes,
    ) = call(
        rim_kernel,
        [
            message,
            whole,
            table,
            table,
            (POINTS, lanes),
            tables.shape,
            (-(-2 * fields * fields // ROWS) * ROWS, lanes),
        ],
        [HBM] * len(inputs),
        [
            pltpu.VMEM((width, padded, lanes), jnp.float32),
            pltpu.VMEM((width, padded, lanes), jnp.float32),
            pltpu.SMEM((fields, fields), jnp.float32),
            pltpu.SMEM((fields, fields), jnp.float32),
            pltpu.SemaphoreType.DMA((6 + -(-levels // ROWS),)),
        ],
        cost=1000,
        name="rim",
    )(*(pltpu.with_memory_space_constraint(x, pltpu.HBM) for x in inputs))
    state = state.reshape(fields * levels * POINTS, lanes)
    from_other = lax.ppermute(to_other, "hy", other)
    from_near = lax.ppermute(state, "hy", near)
    (to_sides,) = call(edge_kernel, [sides], [VMEM], cost=1000, name="edge")(state)
    from_down = lax.ppermute(to_sides, "hx", second_up)
    from_up = from_down
    if lax.axis_size("hx") > 2:
        from_up = lax.ppermute(to_sides, "hx", second_down)

    column = (coupling.shape[1], NODES, lanes)
    factors = call(factor_kernel, [column] * 7, [VMEM] * 2, cost=4000000, name="factor")(
        coupling, damping
    )
    block = ((levels + 2) * NODES, lanes)
    part, base = call(
        element_kernel,
        [state.shape, (NODES,) + block],
        [VMEM] * 6,
        [
            pltpu.VMEM((levels * 8 * fields, lanes), jnp.float32),
            pltpu.VMEM((fields * POINTS, lanes), jnp.bfloat16),
            pltpu.VMEM((fields * POINTS, lanes), jnp.bfloat16),
        ],
        cost=4000000,
        name="element",
    )(
        state,
        neighbour_face,
        orientation,
        metric,
        fluxes,
        tables,
    )
    late = levels * NODES * len(LATE_FIELDS)
    base, near_late = call(
        near_kernel,
        [(NODES,) + block, (late, lanes)],
        [VMEM] * 6,
        [pltpu.VMEM((NODES, padded, lanes), jnp.float32), pltpu.VMEM(block, jnp.float32)],
        cost=1000,
        name="near",
        aliases={4: 0},
    )(from_near, neighbour_face, orientation, fluxes, base, metric)
    count = -(-(levels + 2) // ROWS) * ROWS
    (half,) = call(
        half_pack_kernel,
        [(NODES,) + block],
        [VMEM] * 7 + [ANY],
        [
            pltpu.VMEM((padded, lanes), jnp.float32),
            pltpu.VMEM((count, lanes), jnp.float32),
        ],
        cost=1000,
        name="half_pack",
        aliases={0: 0},
    )(
        base,
        from_down,
        from_up,
        neighbour_face,
        orientation,
        metric,
        fluxes,
        factors[0],
    )
    sends = call(
        pack_kernel,
        [block] * NODES,
        [VMEM] * 5,
        [pltpu.VMEM((NODES,) + block, jnp.float32)],
        cost=1000,
        name="pack",
    )(half, from_other, neighbour_face, orientation, metric)
    received = exchange(sends, WAYS)

    other_face = call(
        functools.partial(face_kernel, 1),
        [(late // 2, lanes)] * 2,
        [VMEM] * 3 + [ANY],
        cost=1000,
        name="other_face",
    )(state, from_other, fluxes, sends[-1])
    other_face = [lax.ppermute(x, "hy", other) for x in other_face]

    cube = (levels + 2, NODES, lanes)
    speeds = call(
        solve_kernel,
        [cube] * NODES,
        [VMEM] * (7 + NODES),
        [
            pltpu.VMEM(column, jnp.float32),
            pltpu.VMEM((NODES, 2, NODES, lanes), jnp.float32),
            pltpu.VMEM((column[0] + 2,) + column[1:], jnp.float32),
        ],
        cost=1000,
        name="solve",
    )(*factors, *[x.reshape(cube) for x in received])
    returned = exchange([x.reshape(block) for x in speeds], BACK_WAYS)
    size = levels * POINTS
    limits = pltpu.CompilerParams(vmem_limit_bytes=24 * 1024 * 1024)
    earlier, done = pl.pallas_call(
        finish_section_kernel,
        out_shape=[
            jax.ShapeDtypeStruct(whole, jnp.float32),
            pltpu.VMEM((2, size, lanes), jnp.float32),
        ],
        in_specs=[VMEM] * 10,
        out_specs=[HBM, VMEM],
        scratch_shapes=[
            pltpu.VMEM((2, size, lanes), jnp.float32),
            pltpu.SemaphoreType.DMA,
        ],
        compiler_params=limits,
        cost_estimate=pl.CostEstimate(flops=4000000, bytes_accessed=4000000, transcendentals=0),
        name="finish",
    )(
        part, near_late, *other_face, from_down, from_up, neighbour_face, orientation, metric, fluxes
    )
    updated = pl.pallas_call(
        update_kernel,
        out_shape=jax.ShapeDtypeStruct(whole, jnp.float32),
        in_specs=[VMEM] * (1 + NODES) + [HBM],
        out_specs=HBM,
        input_output_aliases={1 + NODES: 0},
        scratch_shapes=[
            pltpu.VMEM((NODES,) + block, jnp.float32),
            pltpu.VMEM((3, size, lanes), jnp.float32),
            pltpu.SemaphoreType.DMA((6,)),
        ],
        compiler_params=limits,
        name="update",
    )(*returned, done, earlier)
    return updated.reshape(prognostic.shape)


def solution(mesh):
    placed = (
        P(None, "vz", None, None, "hy", "hx"),
        P(None, None, "hy", "hx"),
        P(),
        P(),
        P(None, "hy", "hx"),
        P(None, "hy", "hx"),
        P(None, None, "vz", None, "hy", "hx"),
        P("vz", None, "hy", "hx"),
    )
    return jax.shard_map(
        per_device,
        mesh=mesh,
        in_specs=placed,
        out_specs=P(None, "vz", None, None, "hy", "hx"),
        check_vma=False,
    )
```

```python
import functools

import jax
import jax.numpy as jnp
import numpy as np
from jax import lax
from jax.experimental import pallas as pl
from jax.experimental.pallas import tpu as pltpu
from jax.sharding import PartitionSpec as P

step_size = 0.05
lift_weight = 6.0
gravity_couple = 0.5
density_couple = 0.3
theta_couple = 0.4

NODES = 4
POINTS = NODES * NODES
FIELDS = 5
FACE_POINTS = ((0, 4, 8, 12), (3, 7, 11, 15), (0, 1, 2, 3), (12, 13, 14, 15))
RIM_POINTS = tuple(sorted(set(sum(FACE_POINTS, ()))))
ROWS = 8
LATE_FIELDS = (0, 1, 2, 4)
WAYS = (2, 3, 1, 0)
BACK_WAYS = (2, 3, 1, 0)


def derivative_table():
    points = np.array([-1.0, -1.0 / np.sqrt(5.0), 1.0 / np.sqrt(5.0), 1.0])
    number = points.shape[0]
    barycentric = np.ones(number)
    for source in range(number):
        for another in range(number):
            if another != source:
                barycentric[source] = barycentric[source] / (points[source] - points[another])
    matrix = np.zeros((number, number))
    for target in range(number):
        for source in range(number):
            if target != source:
                matrix[target, source] = (
                    barycentric[source] / barycentric[target] / (points[target] - points[source])
                )
        matrix[target, target] = -np.sum(matrix[target])
    return matrix


def operator_tables(lanes):
    weight = 0.5 * lift_weight
    table = derivative_table()
    table[0, 0] += weight
    table[-1, -1] -= weight
    eye = np.eye(NODES)
    along_first = np.kron(eye, table)
    along_second = np.kron(table, eye)
    ends = np.zeros(NODES)
    ends[0] = ends[-1] = 1.0
    faces = np.diag(np.kron(np.ones(NODES), ends) + np.kron(ends, np.ones(NODES)))
    first = np.zeros((POINTS, lanes))
    second = np.zeros((POINTS, lanes))
    same = np.zeros((FIELDS, POINTS, lanes))
    owner = np.full((lanes,), -1)
    for g in range(FIELDS):
        own = slice(POINTS * g, POINTS * (g + 1))
        first[:, own] = -along_first
        second[:, own] = -along_second
        same[g, :, own] = -weight * faces
        owner[own] = g
        for k in range(NODES):
            south = FIELDS * POINTS + 2 * NODES * g + k
            north = south + NODES
            second[FACE_POINTS[2][k], south] = weight
            second[FACE_POINTS[3][k], north] = -weight
            same[g, FACE_POINTS[2][k], south] = weight
            same[g, FACE_POINTS[3][k], north] = weight
            owner[south] = owner[north] = g
    tables = np.concatenate([first, second, same.reshape(FIELDS * POINTS, lanes)])
    return tables.astype(np.float32), owner


def chunks(total):
    return [min(start, total - ROWS) for start in range(0, total, ROWS)]


def partner_side(partner):
    odd = lax.rem(lax.axis_index("hy"), 2)
    return odd if partner else 1 - odd


def side_sign(side):
    return (2 * side - 1).astype(jnp.float32)


def ends(total):
    return list(range(0, total, ROWS))


def pick(values, masks, flip):
    chosen = []
    for k in range(NODES):
        row = values[FACE_POINTS[0][k]]
        for option in range(1, 4):
            row = jnp.where(masks[option], values[FACE_POINTS[option][k]], row)
        chosen.append(row)
    return [jnp.where(flip, chosen[NODES - 1 - k], chosen[k]) for k in range(NODES)]


def table_masks(face_row, flip_row, lanes):
    face = jnp.broadcast_to(face_row, (ROWS, lanes))
    flip = jnp.broadcast_to(flip_row, (ROWS, lanes))
    return [face == option for option in range(4)], flip == 1


def flux_row(f, g, matrix):
    return (matrix * FIELDS + f) * FIELDS + g


def along(fluxes, matrix, f, rows):
    total = None
    for g in range(FIELDS):
        at = flux_row(f, g, matrix)
        term = fluxes[at : at + 1, :] * rows[g]
        total = term if total is None else total + term
    return total


def side_rows(f, piece):
    number = 3 * f + piece
    return number // 4, 32 * (number % 4)


def rim_kernel(
    state_hbm,
    face_hbm,
    way_hbm,
    metric_hbm,
    tables_hbm,
    flux_hbm,
    second_hbm,
    to_other,
    state,
    neighbour_face,
    orientation,
    metric,
    tables,
    fluxes,
    column,
    speed,
    flux,
    second_flux,
    semaphores,
):
    levels = state.shape[1] // POINTS
    face = partner_side(1)
    sign = side_sign(face)
    lanes = state.shape[2]
    width = len(RIM_POINTS)
    groups = [(start, min(start + ROWS, levels)) for start in range(0, levels, ROWS)]
    small = [
        pltpu.make_async_copy(source, target, semaphores.at[place])
        for place, (source, target) in enumerate(
            (
                (flux_hbm, flux),
                (face_hbm, neighbour_face),
                (way_hbm, orientation),
                (metric_hbm, metric),
                (tables_hbm, tables),
                (second_hbm, second_flux),
            )
        )
    ]
    large = []
    for place, (low, high) in enumerate(groups):
        rows = pl.ds(low * POINTS, (high - low) * POINTS)
        large.append(
            pltpu.make_async_copy(
                state_hbm.at[:, rows, :], state.at[:, rows, :], semaphores.at[len(small) + place]
            )
        )
    for copy in small[:1] + large + small[1:]:
        copy.start()
    column[...] = jnp.zeros_like(column)
    small[0].wait()
    arrived = 0
    for piece, start in enumerate(chunks(levels)):
        while arrived < len(groups) and groups[arrived][0] < start + ROWS:
            large[arrived].wait()
            arrived += 1
        for place, point in enumerate(RIM_POINTS):
            rows = [
                state[g, pl.ds(start * POINTS + point, ROWS, stride=POINTS), :]
                for g in range(FIELDS)
            ]
            for f, out in ((3, speed), (4, column)):
                normal = (sign * flux[f, 0]) * rows[0]
                for g in range(1, FIELDS):
                    normal = normal + (sign * flux[f, g]) * rows[g]
                out[place, pl.ds(ROWS + start, ROWS), :] = rows[f] + normal
    small[1].wait()
    small[2].wait()
    end = (levels + 2) * width
    for place in range(width):
        for start in chunks(levels):
            upper = column[place, pl.ds(ROWS + start + 1, ROWS), :]
            lower = column[place, pl.ds(ROWS + start - 1, ROWS), :]
            to_other[pl.ds(start * width + place, ROWS, stride=width), :] = speed[
                place, pl.ds(ROWS + start, ROWS), :
            ] - gravity_couple * (upper - lower)
        for extra, level in ((0, 0), (1, levels - 1)):
            at = (levels + extra) * width + place
            to_other[at : at + 1, :] = column[place, ROWS + level : ROWS + level + 1, :]
    to_other[end : end + 1, :] = neighbour_face[pl.ds(face, 1), :].astype(jnp.float32)
    to_other[end + 1 : end + 2, :] = orientation[pl.ds(face, 1), :].astype(jnp.float32)
    left = to_other.shape[0] - end - 2
    to_other[end + 2 :, :] = jnp.zeros((left, lanes), jnp.float32)
    small[3].wait()
    small[4].wait()
    small[5].wait()
    for place, source in enumerate((flux, second_flux)):
        for f in range(FIELDS):
            for g in range(FIELDS):
                at = flux_row(f, g, place)
                fluxes[at : at + 1, :] = jnp.full((1, lanes), source[f, g])


def edge_kernel(state, to_sides):
    lanes = state.shape[1]
    levels = state.shape[0] // (FIELDS * POINTS)
    lane = lax.broadcasted_iota(jnp.int32, (ROWS, lanes), 1)
    packed = [jnp.zeros((ROWS, lanes), jnp.float32) for _ in range(to_sides.shape[0] // ROWS)]
    for f in range(FIELDS):
        for piece, start in enumerate(chunks(levels)):
            block, at = side_rows(f, piece)
            for place, point in enumerate(RIM_POINTS):
                row = state[pl.ds((f * levels + start) * POINTS + point, ROWS, stride=POINTS), :]
                first = at + 2 * place
                packed[block] = jnp.where(
                    lane // 2 == first // 2, pltpu.roll(row, first + 1, 1), packed[block]
                )
    for block, value in enumerate(packed):
        to_sides[block * ROWS : (block + 1) * ROWS, :] = value


def near_kernel(
    state, neighbour_face, orientation, fluxes, base, metric, half, late, column, source
):
    lanes = state.shape[1]
    levels = state.shape[0] // (FIELDS * POINTS)
    face = partner_side(0)
    sign = -side_sign(face)
    masks, flip = table_masks(
        neighbour_face[pl.ds(face, 1), :], orientation[pl.ds(face, 1), :], lanes
    )
    column[...] = jnp.zeros_like(column)
    speeds = []
    for start in chunks(levels):
        picked = []
        for g in range(FIELDS):
            values = {
                point: state[pl.ds((g * levels + start) * POINTS + point, ROWS, stride=POINTS), :]
                for point in RIM_POINTS
            }
            picked.append(pick(values, masks, flip))
        for k in range(NODES):
            rows = [picked[g][k] for g in range(FIELDS)]
            changed = [rows[f] + sign * along(fluxes, 0, f, rows) for f in range(FIELDS)]
            for place, f in enumerate(LATE_FIELDS):
                at = (place * levels + start) * NODES + k
                late[pl.ds(at, ROWS, stride=NODES), :] = changed[f]
            column[k, pl.ds(ROWS + start, ROWS), :] = changed[4]
            speeds.append(changed[3])
    for piece, start in enumerate(chunks(levels)):
        for k in range(NODES):
            upper = column[k, pl.ds(ROWS + start + 1, ROWS), :]
            lower = column[k, pl.ds(ROWS + start - 1, ROWS), :]
            source[pl.ds(start * NODES + k, ROWS, stride=NODES), :] = speeds[
                NODES * piece + k
            ] - gravity_couple * (upper - lower)
    for extra, level in ((0, 0), (1, levels - 1)):
        for k in range(NODES):
            at = (levels + extra) * NODES + k
            source[at : at + 1, :] = column[k, ROWS + level : ROWS + level + 1, :]
    half[...] = base[...]
    for start in chunks(levels + 2):
        picked = [source[pl.ds(start * NODES + k, ROWS, stride=NODES), :] for k in range(NODES)]
        add_first_side(0, start, picked, half, base, metric)


def face_kernel(partner, state, received, fluxes, *rest):
    lanes = state.shape[1]
    levels = state.shape[0] // (FIELDS * POINTS)
    at = (levels + 2) * len(RIM_POINTS)
    outs = rest[-2:]
    share = len(LATE_FIELDS) // len(outs)
    sign = side_sign(partner_side(partner))
    masks, flip = table_masks(
        received[at : at + 1, :].astype(jnp.int32),
        received[at + 1 : at + 2, :].astype(jnp.int32),
        lanes,
    )
    for start in chunks(levels):
        picked = []
        for g in range(FIELDS):
            values = {
                point: state[pl.ds((g * levels + start) * POINTS + point, ROWS, stride=POINTS), :]
                for point in RIM_POINTS
            }
            picked.append(pick(values, masks, flip))
        for place, f in enumerate(LATE_FIELDS):
            for k in range(NODES):
                normal = along(fluxes, 0, f, [picked[g][k] for g in range(FIELDS)])
                at = ((place % share) * levels + start) * NODES + k
                outs[place // share][pl.ds(at, ROWS, stride=NODES), :] = (
                    picked[f][k] + sign * normal
                )


def element_kernel(
    state,
    neighbour_face,
    orientation,
    metric,
    fluxes,
    tables,
    part,
    base,
    outer,
    operator_high,
    operator_low,
):
    levels = state.shape[0] // (FIELDS * POINTS)
    lanes = state.shape[1]
    lane = lax.broadcasted_iota(jnp.int32, (ROWS, lanes), 1)
    sides = []
    for side, (face, edge) in enumerate(((2, 0), (3, lanes - 1))):
        shift = 1 if side == 0 else lanes - 1
        row = jnp.broadcast_to(neighbour_face[face : face + 1, :], (ROWS, lanes))
        way = jnp.broadcast_to(orientation[face : face + 1, :], (ROWS, lanes))
        masks, flip = table_masks(
            pltpu.roll(row, lanes - shift, 1), pltpu.roll(way, lanes - shift, 1), lanes
        )
        sides.append((shift, edge, masks, flip))
    for f in range(FIELDS):
        for start in chunks(levels):
            q = f * levels + start
            values = {
                point: state[pl.ds(q * POINTS + point, ROWS, stride=POINTS), :]
                for point in RIM_POINTS
            }
            for side, (shift, edge, masks, flip) in enumerate(sides):
                for k, row in enumerate(pick(values, masks, flip)):
                    at = start * 8 * FIELDS + 8 * f + NODES * side + k
                    outer[pl.ds(at, ROWS, stride=8 * FIELDS), :] = jnp.where(
                        lane == edge, 0.0, pltpu.roll(row, shift, 1)
                    )
    index = lax.broadcasted_iota(jnp.int32, (1, lanes), 1)
    own_columns = FIELDS * POINTS
    owner = jnp.where(index < own_columns, index // POINTS, (index - own_columns) // 8)
    for f in range(FIELDS):
        first_row = jnp.zeros((1, lanes), jnp.float32)
        second_row = first_row
        for g in range(FIELDS):
            first, second = (flux_row(f, g, matrix) for matrix in range(2))
            first_row = jnp.where(owner == g, fluxes[first : first + 1, :], first_row)
            second_row = jnp.where(owner == g, fluxes[second : second + 1, :], second_row)
        block = (
            first_row * tables[0:POINTS, :]
            + second_row * tables[POINTS : 2 * POINTS, :]
            + tables[(2 + f) * POINTS : (3 + f) * POINTS, :]
        )
        high = block.astype(jnp.bfloat16)
        operator_high[f * POINTS : (f + 1) * POINTS, :] = high
        operator_low[f * POINTS : (f + 1) * POINTS, :] = (
            block - high.astype(jnp.float32)
        ).astype(jnp.bfloat16)
    high = operator_high[...]
    low = operator_low[...]
    scale = step_size * metric[...]
    blank = jnp.zeros((lanes - own_columns - 8 * FIELDS, lanes), jnp.float32)
    for pair in range(0, levels, 2):
        sides = []
        for level in (pair, pair + 1):
            rows = [
                state[pl.ds((f * levels + level) * POINTS, POINTS), :] for f in range(FIELDS)
            ]
            rows.append(outer[pl.ds(level * 8 * FIELDS, 8 * FIELDS), :])
            rows.append(blank)
            sides.append(jnp.concatenate(rows, axis=0))
        values = jnp.concatenate(sides, axis=1)
        top = values.astype(jnp.bfloat16)
        rest = (values - top.astype(jnp.float32)).astype(jnp.bfloat16)
        change = (
            jnp.dot(high, top, preferred_element_type=jnp.float32)
            + jnp.dot(high, rest, preferred_element_type=jnp.float32)
            + jnp.dot(low, top, preferred_element_type=jnp.float32)
        )
        for place, level in enumerate((pair, pair + 1)):
            for f in range(FIELDS):
                at = pl.ds((f * levels + level) * POINTS, POINTS)
                part[at, :] = (
                    state[at, :]
                    + scale
                    * change[
                        f * POINTS : (f + 1) * POINTS, place * lanes : (place + 1) * lanes
                    ]
                )
    for level in range(levels):
        speed = part[pl.ds((3 * levels + level) * POINTS, POINTS), :]
        upper = part[pl.ds((4 * levels + level + 1) * POINTS, POINTS), :] if level < levels - 1 else 0.0
        lower = part[pl.ds((4 * levels + level - 1) * POINTS, POINTS), :] if level else 0.0
        value = speed - gravity_couple * (upper - lower)
        for j in range(NODES):
            base[j, level * NODES : (level + 1) * NODES, :] = value[NODES * j : NODES * (j + 1)]
    for extra, level in ((0, 0), (1, levels - 1)):
        value = part[pl.ds((4 * levels + level) * POINTS, POINTS), :]
        at = (levels + extra) * NODES
        for j in range(NODES):
            base[j, at : at + NODES, :] = value[NODES * j : NODES * (j + 1)]


def side_corrections(received, side, fluxes, fields, pieces):
    lanes = received.shape[1]
    sign = 1.0 if side == 0 else -1.0
    result = [[] for _ in fields]
    for piece in range(pieces):
        rows = []
        for g in range(FIELDS):
            block, at = side_rows(g, piece)
            rows.append(
                pltpu.roll(
                    received[block * ROWS : (block + 1) * ROWS, :], (lanes - at - side) % lanes, 1
                )
            )
        for place, f in enumerate(fields):
            result[place].append(rows[f] + sign * along(fluxes, 1, f, rows))
    return result


def spread(value, edge, masks, flip):
    lanes = value.shape[1]
    values = {
        point: pltpu.roll(value, (edge - 2 * place) % lanes, 1)
        for place, point in enumerate(RIM_POINTS)
    }
    return pick(values, masks, flip)


def add_first_side(partner, start, picked, send, base, metric):
    weight = 0.5 * lift_weight * step_size
    i = (NODES - 1) * partner_side(partner)
    for j, row in enumerate(picked):
        at = pl.ds(start * NODES + i, ROWS, stride=NODES)
        scale = weight * metric[pl.ds(NODES * j + i, 1), :]
        send[j, at, :] = base[j, at, :] + scale * row


def pack_kernel(half, from_other, neighbour_face, orientation, metric, *rest):
    sends, (send,) = rest[:NODES], rest[NODES:]
    me = lax.axis_index("vz")
    send[...] = half[...]
    rows, lanes = half.shape[1:]
    width = len(RIM_POINTS)
    face = partner_side(1)
    masks, flip = table_masks(
        neighbour_face[pl.ds(face, 1), :], orientation[pl.ds(face, 1), :], lanes
    )
    for start in chunks(rows // NODES):
        values = {
            point: from_other[pl.ds(start * width + place, ROWS, stride=width), :]
            for place, point in enumerate(RIM_POINTS)
        }
        add_first_side(1, start, pick(values, masks, flip), send, half, metric)
    for out, way in zip(sends, WAYS):
        out[...] = send[me ^ way]


def half_pack_kernel(
    base,
    from_down,
    from_up,
    neighbour_face,
    orientation,
    metric,
    fluxes,
    factored,
    half,
    send,
    column,
    mixed,
):
    rows, lanes = base.shape[1:]
    levels = rows // NODES - 2
    width = len(RIM_POINTS)
    weight = 0.5 * lift_weight * step_size
    send[:, 0:rows, :] = base[...]
    send[:, rows:, :] = jnp.zeros((NODES, send.shape[1] - rows, lanes), jnp.float32)
    column[...] = jnp.zeros_like(column)
    mixed[...] = jnp.zeros_like(mixed)
    lane = lax.broadcasted_iota(jnp.int32, (ROWS, lanes), 1)
    for side, (received, edge, j) in enumerate(
        ((from_down, 0, 0), (from_up, lanes - 1, NODES - 1))
    ):
        face = 2 + side
        masks, flip = table_masks(
            neighbour_face[face : face + 1, :], orientation[face : face + 1, :], lanes
        )
        speed, heat = side_corrections(received, side, fluxes, (3, 4), len(chunks(levels)))
        for start, value in zip(chunks(levels), heat):
            column[pl.ds(ROWS + start, ROWS), :] = value
        for start, value in zip(chunks(levels), speed):
            upper = column[pl.ds(ROWS + start + 1, ROWS), :]
            lower = column[pl.ds(ROWS + start - 1, ROWS), :]
            mixed[pl.ds(start, ROWS), :] = value - gravity_couple * (upper - lower)
        mixed[levels : levels + 1, :] = column[ROWS : ROWS + 1, :]
        mixed[levels + 1 : levels + 2, :] = column[ROWS + levels - 1 : ROWS + levels, :]
        for start in ends(levels + 2):
            picked = spread(mixed[start : start + ROWS, :], edge, masks, flip)
            for k, row in enumerate(picked):
                point = NODES * j + k
                at = pl.ds(start * NODES + k, ROWS, stride=NODES)
                scale = weight * metric[point : point + 1, :]
                send[j, at, :] += jnp.where(lane == edge, scale * row, 0.0)
    half[...] = send[:, 0:rows, :]


def finish_section_kernel(
    part,
    near,
    other_early,
    other_late,
    from_down,
    from_up,
    neighbour_face,
    orientation,
    metric,
    fluxes,
    out,
    done,
    final,
    semaphore,
):
    levels = part.shape[0] // (FIELDS * POINTS)
    lanes = part.shape[1]
    size = levels * POINTS
    weight = 0.5 * lift_weight * step_size
    scale = weight * metric[...]
    lane = lax.broadcasted_iota(jnp.int32, (ROWS, lanes), 1)
    tables = []
    edges = []
    for side, received in enumerate((from_down, from_up)):
        face = 2 + side
        tables.append(
            table_masks(
                neighbour_face[face : face + 1, :], orientation[face : face + 1, :], lanes
            )
        )
        edges.append(
            side_corrections(received, side, fluxes, LATE_FIELDS, len(chunks(levels)))
        )
    copy = pltpu.make_async_copy(final, out.at[1:3], semaphore)
    sources = ((near,), (other_early, other_late))
    for place, f in ((1, 1), (2, 2), (0, 0), (3, 4)):
        target = final.at[f - 1] if f in (1, 2) else done.at[min(f, 1)]
        target[...] = part[f * size : (f + 1) * size, :]
        for piece, start in enumerate(chunks(levels)):
            for j in range(NODES):
                for partner, source in enumerate(sources):
                    point = NODES * j + (NODES - 1) * partner_side(partner)
                    share = len(LATE_FIELDS) // len(source)
                    rows = source[place // share][
                        pl.ds(((place % share) * levels + start) * NODES + j, ROWS, stride=NODES),
                        :,
                    ]
                    at = pl.ds(start * POINTS + point, ROWS, stride=POINTS)
                    target[at, :] = (
                        part[pl.ds(f * size + start * POINTS + point, ROWS, stride=POINTS), :]
                        + weight * metric[pl.ds(point, 1), :] * rows
                    )
        for piece, start in enumerate(chunks(levels)):
            row_index = lax.broadcasted_iota(jnp.int32, (ROWS, lanes), 0)
            fresh = row_index >= (-start) % ROWS
            for side, (edge, j) in enumerate(((0, 0), (lanes - 1, NODES - 1))):
                picked = spread(edges[side][place][piece], edge, *tables[side])
                for k, row in enumerate(picked):
                    point = NODES * j + k
                    at = pl.ds(start * POINTS + point, ROWS, stride=POINTS)
                    target[at, :] += jnp.where(
                        (lane == edge) & fresh, scale[point : point + 1, :] * row, 0.0
                    )
        if f == 2:
            copy.start()
    copy.wait()


def factor_kernel(coupling, damping, inverse, near, far_two, far_three, ratio, next_two, next_three):
    levels = coupling.shape[1]
    blank = jnp.zeros(coupling.shape[2:], jnp.float32)
    far_ratio, far_second, near_ratio, near_second = (blank,) * 4
    far_before, near_before = blank, blank
    extra = damping[...]
    for level in range(levels):
        a, b, d, e = (coupling[entry, level] for entry in range(4))
        centre = a + b + d + e + extra
        reduced = -b + a * far_ratio
        pivot = centre + a * far_second - reduced * near_ratio
        scaled = 1.0 / pivot
        upper_ratio = (-d - reduced * near_second) * scaled
        second_ratio = -e * scaled
        far_here, near_here = a * scaled, reduced * scaled
        inverse[level] = scaled
        near[level] = near_here
        far_two[level] = far_here + near_here * near_before
        far_three[level] = near_here * far_before
        ratio[level] = upper_ratio
        if level:
            next_two[level - 1] = near_ratio * upper_ratio - near_second
            next_three[level - 1] = near_ratio * second_ratio
        far_before, near_before = far_here, near_here
        far_ratio, far_second = near_ratio, near_second
        near_ratio, near_second = upper_ratio, second_ratio
    next_two[levels - 1] = -near_second
    next_three[levels - 1] = blank


def solve_kernel(inverse, near, far_two, far_three, ratio, next_two, next_three, *rest):
    ways = NODES
    received, sends, (source, heat, speed) = rest[:ways], rest[ways : 2 * ways], rest[2 * ways :]
    levels = near.shape[0]
    here = levels // ways
    me = lax.axis_index("vz")
    for values, way in zip(received, WAYS):
        block = me ^ way
        source[pl.ds(block * here, here)] = values[0:here]
        heat[block] = values[here : here + 2]
    for block in range(ways - 1):
        last = block * here + here - 1
        source[last] = source[last] - gravity_couple * heat[block + 1, 0]
        source[last + 1] = source[last + 1] + gravity_couple * heat[block, 1]
    blank = jnp.zeros(near.shape[1:], jnp.float32)
    scaled = blank
    known = [blank, blank, blank]
    for level in range(levels):
        before, scaled = scaled, source[level] * inverse[level]
        value = scaled - near[level] * before - far_three[level] * known[-3]
        value = value + far_two[level] * known[-2]
        source[level] = value
        known = [*known[1:], value]
    speed[0] = blank
    speed[levels + 1] = blank
    known = [blank, blank, blank]
    above = blank
    for level in range(levels - 1, -1, -1):
        here_value = source[level]
        value = here_value - ratio[level] * above + next_three[level] * known[-3]
        value = value + next_two[level] * known[-2]
        speed[level + 1] = value
        above = here_value
        known = [*known[1:], value]
    for send, way in zip(sends, BACK_WAYS):
        send[...] = speed[pl.ds((me ^ way) * here, here + 2)]


def update_kernel(*refs):
    ways = NODES
    received, (done, earlier, out, speed, final, semaphores) = refs[:ways], refs[ways:]
    levels = done.shape[1] // POINTS
    me = lax.axis_index("vz")
    for values, way in zip(received, BACK_WAYS):
        speed[me ^ way] = values[...]
    lanes = done.shape[2]
    half = levels // 2
    low = lax.broadcasted_iota(jnp.int32, (ROWS, lanes), 0) < NODES
    copies = []
    for pair in range(half):
        lower = [speed[j, pair * ROWS : (pair + 1) * ROWS, :] for j in range(NODES)]
        upper = [speed[j, (pair + 1) * ROWS : (pair + 2) * ROWS, :] for j in range(NODES)]
        jump = [above - below for above, below in zip(upper, lower)]
        value = [jnp.where(low, above, below) for above, below in zip(upper, lower)]
        for h in range(2):
            a, b = 2 * h, 2 * h + 1
            for odd in range(2):
                at = pl.ds((2 * pair + odd) * POINTS + ROWS * h, ROWS)
                jumps = side_by_side(jump[a], jump[b], odd, low)
                final[0, at, :] = done[0, at, :] - density_couple * jumps
                final[1, at, :] = side_by_side(value[a], value[b], 1 - odd, low)
                final[2, at, :] = done[1, at, :] - theta_couple * jumps
        if pair in (half // 2 - 1, half - 1):
            first = 0 if pair < half - 1 else half // 2
            rows = pl.ds(first * 2 * POINTS, (pair + 1 - first) * 2 * POINTS)
            for place, f in enumerate((0, 3, 4)):
                copies.append(
                    pltpu.make_async_copy(
                        final.at[place, rows, :], out.at[f, rows, :], semaphores.at[len(copies)]
                    )
                )
                copies[-1].start()
    for copy in copies:
        copy.wait()


def side_by_side(first, second, upper, low):
    if upper:
        return jnp.where(low, pltpu.roll(first, NODES, 0), second)
    return jnp.where(low, first, pltpu.roll(second, NODES, 0))


VMEM = pl.BlockSpec(memory_space=pltpu.VMEM)
HBM = pl.BlockSpec(memory_space=pltpu.HBM)
ANY = pl.BlockSpec(memory_space=pl.ANY)


def call(kernel, outs, in_specs, scratch=(), cost=0, name=None):
    kinds = [x if hasattr(x, "dtype") else pltpu.VMEM(x, jnp.float32) for x in outs]
    return pl.pallas_call(
        kernel,
        out_shape=kinds,
        in_specs=in_specs,
        out_specs=[VMEM] * len(outs),
        scratch_shapes=list(scratch),
        compiler_params=pltpu.CompilerParams(vmem_limit_bytes=24 * 1024 * 1024),
        cost_estimate=pl.CostEstimate(flops=cost, bytes_accessed=cost, transcendentals=0),
        name=name,
    )


def per_device(
    prognostic, metric, first_flux, second_flux, neighbour_face, orientation, coupling, damping
):
    fields, levels = prognostic.shape[:2]
    lanes = prognostic.shape[-1]
    whole = (fields, levels * POINTS, lanes)
    metric = metric.reshape(POINTS, lanes)
    neighbour_face = neighbour_face.reshape(4, lanes)
    orientation = orientation.reshape(4, lanes)
    coupling = coupling.reshape(4, coupling.shape[1], NODES, lanes)
    damping = damping.reshape(NODES, lanes)
    tables, _ = operator_tables(lanes)

    def shifts(axis):
        size = lax.axis_size(axis)
        up = [(i, (i + 1) % size) for i in range(size)]
        return up, [(j, i) for i, j in up]

    def exchange(arrays, ways):
        size = lax.axis_size("vz")
        return [
            lax.ppermute(x, "vz", [(i, i ^ way) for i in range(size)]) if way else x
            for x, way in zip(arrays, ways)
        ]

    count = lax.axis_size("hy")
    near = [(i, i ^ 1) for i in range(count)]
    other = [(i, (i + 1 if i % 2 else i - 1) % count) for i in range(count)]
    second_up, second_down = shifts("hx")
    width = len(RIM_POINTS)
    message = (-(-((levels + 2) * width + 2) // ROWS) * ROWS, lanes)
    sides = (-(-fields * len(chunks(levels)) // 4) * ROWS, lanes)
    padded = levels + 2 * ROWS
    table = pltpu.VMEM((4, lanes), jnp.int32)
    inputs = (
        prognostic.reshape(whole),
        neighbour_face,
        orientation,
        metric,
        jnp.asarray(tables),
        first_flux,
        second_flux,
    )
    (
        to_other,
        state,
        neighbour_face,
        orientation,
        metric,
        tables,
        fluxes,
    ) = call(
        rim_kernel,
        [
            message,
            whole,
            table,
            table,
            (POINTS, lanes),
            tables.shape,
            (-(-2 * fields * fields // ROWS) * ROWS, lanes),
        ],
        [HBM] * len(inputs),
        [
            pltpu.VMEM((width, padded, lanes), jnp.float32),
            pltpu.VMEM((width, padded, lanes), jnp.float32),
            pltpu.SMEM((fields, fields), jnp.float32),
            pltpu.SMEM((fields, fields), jnp.float32),
            pltpu.SemaphoreType.DMA((6 + -(-levels // ROWS),)),
        ],
        cost=1000,
        name="rim",
    )(*(pltpu.with_memory_space_constraint(x, pltpu.HBM) for x in inputs))
    state = state.reshape(fields * levels * POINTS, lanes)
    from_other = lax.ppermute(to_other, "hy", other)
    from_near = lax.ppermute(state, "hy", near)
    (to_sides,) = call(edge_kernel, [sides], [VMEM], cost=1000, name="edge")(state)
    from_down = lax.ppermute(to_sides, "hx", second_up)
    from_up = from_down
    if lax.axis_size("hx") > 2:
        from_up = lax.ppermute(to_sides, "hx", second_down)

    column = (coupling.shape[1], NODES, lanes)
    factors = call(factor_kernel, [column] * 7, [VMEM] * 2, cost=4000000, name="factor")(
        coupling, damping
    )
    block = ((levels + 2) * NODES, lanes)
    part, base = call(
        element_kernel,
        [state.shape, (NODES,) + block],
        [VMEM] * 6,
        [
            pltpu.VMEM((levels * 8 * fields, lanes), jnp.float32),
            pltpu.VMEM((fields * POINTS, lanes), jnp.bfloat16),
            pltpu.VMEM((fields * POINTS, lanes), jnp.bfloat16),
        ],
        cost=4000000,
        name="element",
    )(
        state,
        neighbour_face,
        orientation,
        metric,
        fluxes,
        tables,
    )
    late = levels * NODES * len(LATE_FIELDS)
    base, near_late = call(
        near_kernel,
        [(NODES,) + block, (late, lanes)],
        [VMEM] * 6,
        [pltpu.VMEM((NODES, padded, lanes), jnp.float32), pltpu.VMEM(block, jnp.float32)],
        cost=1000,
        name="near",
    )(from_near, neighbour_face, orientation, fluxes, base, metric)
    count = -(-(levels + 2) // ROWS) * ROWS
    (half,) = call(
        half_pack_kernel,
        [(NODES,) + block],
        [VMEM] * 7 + [ANY],
        [
            pltpu.VMEM((NODES, count * NODES, lanes), jnp.float32),
            pltpu.VMEM((padded, lanes), jnp.float32),
            pltpu.VMEM((count, lanes), jnp.float32),
        ],
        cost=1000,
        name="half_pack",
    )(
        base,
        from_down,
        from_up,
        neighbour_face,
        orientation,
        metric,
        fluxes,
        factors[0],
    )
    sends = call(
        pack_kernel,
        [block] * NODES,
        [VMEM] * 5,
        [pltpu.VMEM((NODES,) + block, jnp.float32)],
        cost=1000,
        name="pack",
    )(half, from_other, neighbour_face, orientation, metric)
    received = exchange(sends, WAYS)

    other_face = call(
        functools.partial(face_kernel, 1),
        [(late // 2, lanes)] * 2,
        [VMEM] * 3 + [ANY],
        cost=1000,
        name="other_face",
    )(state, from_other, fluxes, sends[-1])
    other_face = [lax.ppermute(x, "hy", other) for x in other_face]

    cube = (levels + 2, NODES, lanes)
    speeds = call(
        solve_kernel,
        [cube] * NODES,
        [VMEM] * (7 + NODES),
        [
            pltpu.VMEM(column, jnp.float32),
            pltpu.VMEM((NODES, 2, NODES, lanes), jnp.float32),
            pltpu.VMEM((column[0] + 2,) + column[1:], jnp.float32),
        ],
        cost=1000,
        name="solve",
    )(*factors, *[x.reshape(cube) for x in received])
    returned = exchange([x.reshape(block) for x in speeds], BACK_WAYS)
    size = levels * POINTS
    limits = pltpu.CompilerParams(vmem_limit_bytes=24 * 1024 * 1024)
    earlier, done = pl.pallas_call(
        finish_section_kernel,
        out_shape=[
            jax.ShapeDtypeStruct(whole, jnp.float32),
            pltpu.VMEM((2, size, lanes), jnp.float32),
        ],
        in_specs=[VMEM] * 10,
        out_specs=[HBM, VMEM],
        scratch_shapes=[
            pltpu.VMEM((2, size, lanes), jnp.float32),
            pltpu.SemaphoreType.DMA,
        ],
        compiler_params=limits,
        cost_estimate=pl.CostEstimate(flops=4000000, bytes_accessed=4000000, transcendentals=0),
        name="finish",
    )(
        part, near_late, *other_face, from_down, from_up, neighbour_face, orientation, metric, fluxes
    )
    updated = pl.pallas_call(
        update_kernel,
        out_shape=jax.ShapeDtypeStruct(whole, jnp.float32),
        in_specs=[VMEM] * (1 + NODES) + [HBM],
        out_specs=HBM,
        input_output_aliases={1 + NODES: 0},
        scratch_shapes=[
            pltpu.VMEM((NODES,) + block, jnp.float32),
            pltpu.VMEM((3, size, lanes), jnp.float32),
            pltpu.SemaphoreType.DMA((6,)),
        ],
        compiler_params=limits,
        name="update",
    )(*returned, done, earlier)
    return updated.reshape(prognostic.shape)


def solution(mesh):
    placed = (
        P(None, "vz", None, None, "hy", "hx"),
        P(None, None, "hy", "hx"),
        P(),
        P(),
        P(None, "hy", "hx"),
        P(None, "hy", "hx"),
        P(None, None, "vz", None, "hy", "hx"),
        P("vz", None, "hy", "hx"),
    )
    return jax.shard_map(
        per_device,
        mesh=mesh,
        in_specs=placed,
        out_specs=P(None, "vz", None, None, "hy", "hx"),
        check_vma=False,
    )
```

```python
import functools

import jax
import jax.numpy as jnp
import numpy as np
from jax import lax
from jax.experimental import pallas as pl
from jax.experimental.pallas import tpu as pltpu
from jax.sharding import PartitionSpec as P

step_size = 0.05
lift_weight = 6.0
gravity_couple = 0.5
density_couple = 0.3
theta_couple = 0.4

NODES = 4
POINTS = NODES * NODES
FIELDS = 5
FACE_POINTS = ((0, 4, 8, 12), (3, 7, 11, 15), (0, 1, 2, 3), (12, 13, 14, 15))
RIM_POINTS = tuple(sorted(set(sum(FACE_POINTS, ()))))
ROWS = 8
LATE_FIELDS = (0, 1, 2, 4)
WAYS = (2, 3, 1, 0)
BACK_WAYS = (3, 2, 1, 0)


def derivative_table():
    points = np.array([-1.0, -1.0 / np.sqrt(5.0), 1.0 / np.sqrt(5.0), 1.0])
    number = points.shape[0]
    barycentric = np.ones(number)
    for source in range(number):
        for another in range(number):
            if another != source:
                barycentric[source] = barycentric[source] / (points[source] - points[another])
    matrix = np.zeros((number, number))
    for target in range(number):
        for source in range(number):
            if target != source:
                matrix[target, source] = (
                    barycentric[source] / barycentric[target] / (points[target] - points[source])
                )
        matrix[target, target] = -np.sum(matrix[target])
    return matrix


def operator_tables(lanes):
    weight = 0.5 * lift_weight
    table = derivative_table()
    table[0, 0] += weight
    table[-1, -1] -= weight
    eye = np.eye(NODES)
    along_first = np.kron(eye, table)
    along_second = np.kron(table, eye)
    ends = np.zeros(NODES)
    ends[0] = ends[-1] = 1.0
    faces = np.diag(np.kron(np.ones(NODES), ends) + np.kron(ends, np.ones(NODES)))
    first = np.zeros((POINTS, lanes))
    second = np.zeros((POINTS, lanes))
    same = np.zeros((FIELDS, POINTS, lanes))
    owner = np.full((lanes,), -1)
    for g in range(FIELDS):
        own = slice(POINTS * g, POINTS * (g + 1))
        first[:, own] = -along_first
        second[:, own] = -along_second
        same[g, :, own] = -weight * faces
        owner[own] = g
        for k in range(NODES):
            south = FIELDS * POINTS + 2 * NODES * g + k
            north = south + NODES
            second[FACE_POINTS[2][k], south] = weight
            second[FACE_POINTS[3][k], north] = -weight
            same[g, FACE_POINTS[2][k], south] = weight
            same[g, FACE_POINTS[3][k], north] = weight
            owner[south] = owner[north] = g
    tables = np.concatenate([first, second, same.reshape(FIELDS * POINTS, lanes)])
    return tables.astype(np.float32), owner


def chunks(total):
    return [min(start, total - ROWS) for start in range(0, total, ROWS)]


def partner_side(partner):
    odd = lax.rem(lax.axis_index("hy"), 2)
    return odd if partner else 1 - odd


def side_sign(side):
    return (2 * side - 1).astype(jnp.float32)


def ends(total):
    return list(range(0, total, ROWS))


def pick(values, masks, flip):
    chosen = []
    for k in range(NODES):
        row = values[FACE_POINTS[0][k]]
        for option in range(1, 4):
            row = jnp.where(masks[option], values[FACE_POINTS[option][k]], row)
        chosen.append(row)
    return [jnp.where(flip, chosen[NODES - 1 - k], chosen[k]) for k in range(NODES)]


def table_masks(face_row, flip_row, lanes):
    face = jnp.broadcast_to(face_row, (ROWS, lanes))
    flip = jnp.broadcast_to(flip_row, (ROWS, lanes))
    return [face == option for option in range(4)], flip == 1


def flux_row(f, g, matrix):
    return (matrix * FIELDS + f) * FIELDS + g


def along(fluxes, matrix, f, rows):
    total = None
    for g in range(FIELDS):
        at = flux_row(f, g, matrix)
        term = fluxes[at : at + 1, :] * rows[g]
        total = term if total is None else total + term
    return total


def side_rows(f, piece):
    number = 3 * f + piece
    return number // 4, 32 * (number % 4)


def rim_kernel(
    state_hbm,
    face_hbm,
    way_hbm,
    metric_hbm,
    tables_hbm,
    flux_hbm,
    second_hbm,
    to_other,
    state,
    neighbour_face,
    orientation,
    metric,
    tables,
    fluxes,
    column,
    speed,
    flux,
    second_flux,
    semaphores,
):
    levels = state.shape[1] // POINTS
    face = partner_side(1)
    sign = side_sign(face)
    lanes = state.shape[2]
    width = len(RIM_POINTS)
    groups = [(start, min(start + ROWS, levels)) for start in range(0, levels, ROWS)]
    small = [
        pltpu.make_async_copy(source, target, semaphores.at[place])
        for place, (source, target) in enumerate(
            (
                (flux_hbm, flux),
                (face_hbm, neighbour_face),
                (way_hbm, orientation),
                (metric_hbm, metric),
                (tables_hbm, tables),
                (second_hbm, second_flux),
            )
        )
    ]
    large = []
    for place, (low, high) in enumerate(groups):
        rows = pl.ds(low * POINTS, (high - low) * POINTS)
        large.append(
            pltpu.make_async_copy(
                state_hbm.at[:, rows, :], state.at[:, rows, :], semaphores.at[len(small) + place]
            )
        )
    for copy in small[:1] + large + small[1:]:
        copy.start()
    column[...] = jnp.zeros_like(column)
    small[0].wait()
    arrived = 0
    for piece, start in enumerate(chunks(levels)):
        while arrived < len(groups) and groups[arrived][0] < start + ROWS:
            large[arrived].wait()
            arrived += 1
        for place, point in enumerate(RIM_POINTS):
            rows = [
                state[g, pl.ds(start * POINTS + point, ROWS, stride=POINTS), :]
                for g in range(FIELDS)
            ]
            for f, out in ((3, speed), (4, column)):
                normal = (sign * flux[f, 0]) * rows[0]
                for g in range(1, FIELDS):
                    normal = normal + (sign * flux[f, g]) * rows[g]
                out[place, pl.ds(ROWS + start, ROWS), :] = rows[f] + normal
    small[1].wait()
    small[2].wait()
    end = (levels + 2) * width
    for place in range(width):
        for start in chunks(levels):
            upper = column[place, pl.ds(ROWS + start + 1, ROWS), :]
            lower = column[place, pl.ds(ROWS + start - 1, ROWS), :]
            to_other[pl.ds(start * width + place, ROWS, stride=width), :] = speed[
                place, pl.ds(ROWS + start, ROWS), :
            ] - gravity_couple * (upper - lower)
        for extra, level in ((0, 0), (1, levels - 1)):
            at = (levels + extra) * width + place
            to_other[at : at + 1, :] = column[place, ROWS + level : ROWS + level + 1, :]
    to_other[end : end + 1, :] = neighbour_face[pl.ds(face, 1), :].astype(jnp.float32)
    to_other[end + 1 : end + 2, :] = orientation[pl.ds(face, 1), :].astype(jnp.float32)
    left = to_other.shape[0] - end - 2
    to_other[end + 2 :, :] = jnp.zeros((left, lanes), jnp.float32)
    small[3].wait()
    small[4].wait()
    small[5].wait()
    for place, source in enumerate((flux, second_flux)):
        for f in range(FIELDS):
            for g in range(FIELDS):
                at = flux_row(f, g, place)
                fluxes[at : at + 1, :] = jnp.full((1, lanes), source[f, g])


def edge_kernel(state, to_sides):
    lanes = state.shape[1]
    levels = state.shape[0] // (FIELDS * POINTS)
    lane = lax.broadcasted_iota(jnp.int32, (ROWS, lanes), 1)
    packed = [jnp.zeros((ROWS, lanes), jnp.float32) for _ in range(to_sides.shape[0] // ROWS)]
    for f in range(FIELDS):
        for piece, start in enumerate(chunks(levels)):
            block, at = side_rows(f, piece)
            for place, point in enumerate(RIM_POINTS):
                row = state[pl.ds((f * levels + start) * POINTS + point, ROWS, stride=POINTS), :]
                first = at + 2 * place
                packed[block] = jnp.where(
                    lane // 2 == first // 2, pltpu.roll(row, first + 1, 1), packed[block]
                )
    for block, value in enumerate(packed):
        to_sides[block * ROWS : (block + 1) * ROWS, :] = value


def near_kernel(
    state, neighbour_face, orientation, fluxes, base, metric, half, late, column, source
):
    lanes = state.shape[1]
    levels = state.shape[0] // (FIELDS * POINTS)
    face = partner_side(0)
    sign = -side_sign(face)
    masks, flip = table_masks(
        neighbour_face[pl.ds(face, 1), :], orientation[pl.ds(face, 1), :], lanes
    )
    column[...] = jnp.zeros_like(column)
    speeds = []
    for start in chunks(levels):
        picked = []
        for g in range(FIELDS):
            values = {
                point: state[pl.ds((g * levels + start) * POINTS + point, ROWS, stride=POINTS), :]
                for point in RIM_POINTS
            }
            picked.append(pick(values, masks, flip))
        for k in range(NODES):
            rows = [picked[g][k] for g in range(FIELDS)]
            changed = [rows[f] + sign * along(fluxes, 0, f, rows) for f in range(FIELDS)]
            for place, f in enumerate(LATE_FIELDS):
                at = (place * levels + start) * NODES + k
                late[pl.ds(at, ROWS, stride=NODES), :] = changed[f]
            column[k, pl.ds(ROWS + start, ROWS), :] = changed[4]
            speeds.append(changed[3])
    for piece, start in enumerate(chunks(levels)):
        for k in range(NODES):
            upper = column[k, pl.ds(ROWS + start + 1, ROWS), :]
            lower = column[k, pl.ds(ROWS + start - 1, ROWS), :]
            source[pl.ds(start * NODES + k, ROWS, stride=NODES), :] = speeds[
                NODES * piece + k
            ] - gravity_couple * (upper - lower)
    for extra, level in ((0, 0), (1, levels - 1)):
        for k in range(NODES):
            at = (levels + extra) * NODES + k
            source[at : at + 1, :] = column[k, ROWS + level : ROWS + level + 1, :]
    half[...] = base[...]
    for start in chunks(levels + 2):
        picked = [source[pl.ds(start * NODES + k, ROWS, stride=NODES), :] for k in range(NODES)]
        add_first_side(0, start, picked, half, base, metric)


def face_kernel(partner, state, received, fluxes, *rest):
    lanes = state.shape[1]
    levels = state.shape[0] // (FIELDS * POINTS)
    at = (levels + 2) * len(RIM_POINTS)
    outs = rest[-2:]
    share = len(LATE_FIELDS) // len(outs)
    sign = side_sign(partner_side(partner))
    masks, flip = table_masks(
        received[at : at + 1, :].astype(jnp.int32),
        received[at + 1 : at + 2, :].astype(jnp.int32),
        lanes,
    )
    for start in chunks(levels):
        picked = []
        for g in range(FIELDS):
            values = {
                point: state[pl.ds((g * levels + start) * POINTS + point, ROWS, stride=POINTS), :]
                for point in RIM_POINTS
            }
            picked.append(pick(values, masks, flip))
        for place, f in enumerate(LATE_FIELDS):
            for k in range(NODES):
                normal = along(fluxes, 0, f, [picked[g][k] for g in range(FIELDS)])
                at = ((place % share) * levels + start) * NODES + k
                outs[place // share][pl.ds(at, ROWS, stride=NODES), :] = (
                    picked[f][k] + sign * normal
                )


def element_kernel(
    state,
    neighbour_face,
    orientation,
    metric,
    fluxes,
    tables,
    part,
    base,
    outer,
    operator_high,
    operator_low,
):
    levels = state.shape[0] // (FIELDS * POINTS)
    lanes = state.shape[1]
    lane = lax.broadcasted_iota(jnp.int32, (ROWS, lanes), 1)
    sides = []
    for side, (face, edge) in enumerate(((2, 0), (3, lanes - 1))):
        shift = 1 if side == 0 else lanes - 1
        row = jnp.broadcast_to(neighbour_face[face : face + 1, :], (ROWS, lanes))
        way = jnp.broadcast_to(orientation[face : face + 1, :], (ROWS, lanes))
        masks, flip = table_masks(
            pltpu.roll(row, lanes - shift, 1), pltpu.roll(way, lanes - shift, 1), lanes
        )
        sides.append((shift, edge, masks, flip))
    for f in range(FIELDS):
        for start in chunks(levels):
            q = f * levels + start
            values = {
                point: state[pl.ds(q * POINTS + point, ROWS, stride=POINTS), :]
                for point in RIM_POINTS
            }
            for side, (shift, edge, masks, flip) in enumerate(sides):
                for k, row in enumerate(pick(values, masks, flip)):
                    at = start * 8 * FIELDS + 8 * f + NODES * side + k
                    outer[pl.ds(at, ROWS, stride=8 * FIELDS), :] = jnp.where(
                        lane == edge, 0.0, pltpu.roll(row, shift, 1)
                    )
    index = lax.broadcasted_iota(jnp.int32, (1, lanes), 1)
    own_columns = FIELDS * POINTS
    owner = jnp.where(index < own_columns, index // POINTS, (index - own_columns) // 8)
    for f in range(FIELDS):
        first_row = jnp.zeros((1, lanes), jnp.float32)
        second_row = first_row
        for g in range(FIELDS):
            first, second = (flux_row(f, g, matrix) for matrix in range(2))
            first_row = jnp.where(owner == g, fluxes[first : first + 1, :], first_row)
            second_row = jnp.where(owner == g, fluxes[second : second + 1, :], second_row)
        block = (
            first_row * tables[0:POINTS, :]
            + second_row * tables[POINTS : 2 * POINTS, :]
            + tables[(2 + f) * POINTS : (3 + f) * POINTS, :]
        )
        high = block.astype(jnp.bfloat16)
        operator_high[f * POINTS : (f + 1) * POINTS, :] = high
        operator_low[f * POINTS : (f + 1) * POINTS, :] = (
            block - high.astype(jnp.float32)
        ).astype(jnp.bfloat16)
    high = operator_high[...]
    low = operator_low[...]
    scale = step_size * metric[...]
    blank = jnp.zeros((lanes - own_columns - 8 * FIELDS, lanes), jnp.float32)
    for pair in range(0, levels, 2):
        sides = []
        for level in (pair, pair + 1):
            rows = [
                state[pl.ds((f * levels + level) * POINTS, POINTS), :] for f in range(FIELDS)
            ]
            rows.append(outer[pl.ds(level * 8 * FIELDS, 8 * FIELDS), :])
            rows.append(blank)
            sides.append(jnp.concatenate(rows, axis=0))
        values = jnp.concatenate(sides, axis=1)
        top = values.astype(jnp.bfloat16)
        rest = (values - top.astype(jnp.float32)).astype(jnp.bfloat16)
        change = (
            jnp.dot(high, top, preferred_element_type=jnp.float32)
            + jnp.dot(high, rest, preferred_element_type=jnp.float32)
            + jnp.dot(low, top, preferred_element_type=jnp.float32)
        )
        for place, level in enumerate((pair, pair + 1)):
            for f in range(FIELDS):
                at = pl.ds((f * levels + level) * POINTS, POINTS)
                part[at, :] = (
                    state[at, :]
                    + scale
                    * change[
                        f * POINTS : (f + 1) * POINTS, place * lanes : (place + 1) * lanes
                    ]
                )
    for level in range(levels):
        speed = part[pl.ds((3 * levels + level) * POINTS, POINTS), :]
        upper = part[pl.ds((4 * levels + level + 1) * POINTS, POINTS), :] if level < levels - 1 else 0.0
        lower = part[pl.ds((4 * levels + level - 1) * POINTS, POINTS), :] if level else 0.0
        value = speed - gravity_couple * (upper - lower)
        for j in range(NODES):
            base[j, level * NODES : (level + 1) * NODES, :] = value[NODES * j : NODES * (j + 1)]
    for extra, level in ((0, 0), (1, levels - 1)):
        value = part[pl.ds((4 * levels + level) * POINTS, POINTS), :]
        at = (levels + extra) * NODES
        for j in range(NODES):
            base[j, at : at + NODES, :] = value[NODES * j : NODES * (j + 1)]


def side_corrections(received, side, fluxes, fields, pieces):
    lanes = received.shape[1]
    sign = 1.0 if side == 0 else -1.0
    result = [[] for _ in fields]
    for piece in range(pieces):
        rows = []
        for g in range(FIELDS):
            block, at = side_rows(g, piece)
            rows.append(
                pltpu.roll(
                    received[block * ROWS : (block + 1) * ROWS, :], (lanes - at - side) % lanes, 1
                )
            )
        for place, f in enumerate(fields):
            result[place].append(rows[f] + sign * along(fluxes, 1, f, rows))
    return result


def spread(value, edge, masks, flip):
    lanes = value.shape[1]
    values = {
        point: pltpu.roll(value, (edge - 2 * place) % lanes, 1)
        for place, point in enumerate(RIM_POINTS)
    }
    return pick(values, masks, flip)


def add_first_side(partner, start, picked, send, base, metric):
    weight = 0.5 * lift_weight * step_size
    i = (NODES - 1) * partner_side(partner)
    for j, row in enumerate(picked):
        at = pl.ds(start * NODES + i, ROWS, stride=NODES)
        scale = weight * metric[pl.ds(NODES * j + i, 1), :]
        send[j, at, :] = base[j, at, :] + scale * row


def pack_kernel(half, from_other, neighbour_face, orientation, metric, *rest):
    sends, (send,) = rest[:NODES], rest[NODES:]
    me = lax.axis_index("vz")
    send[...] = half[...]
    rows, lanes = half.shape[1:]
    width = len(RIM_POINTS)
    face = partner_side(1)
    masks, flip = table_masks(
        neighbour_face[pl.ds(face, 1), :], orientation[pl.ds(face, 1), :], lanes
    )
    for start in chunks(rows // NODES):
        values = {
            point: from_other[pl.ds(start * width + place, ROWS, stride=width), :]
            for place, point in enumerate(RIM_POINTS)
        }
        add_first_side(1, start, pick(values, masks, flip), send, half, metric)
    for out, way in zip(sends, WAYS):
        out[...] = send[me ^ way]


def half_pack_kernel(
    base,
    from_down,
    from_up,
    neighbour_face,
    orientation,
    metric,
    fluxes,
    factored,
    half,
    send,
    column,
    mixed,
):
    rows, lanes = base.shape[1:]
    levels = rows // NODES - 2
    width = len(RIM_POINTS)
    weight = 0.5 * lift_weight * step_size
    send[:, 0:rows, :] = base[...]
    send[:, rows:, :] = jnp.zeros((NODES, send.shape[1] - rows, lanes), jnp.float32)
    column[...] = jnp.zeros_like(column)
    mixed[...] = jnp.zeros_like(mixed)
    lane = lax.broadcasted_iota(jnp.int32, (ROWS, lanes), 1)
    for side, (received, edge, j) in enumerate(
        ((from_down, 0, 0), (from_up, lanes - 1, NODES - 1))
    ):
        face = 2 + side
        masks, flip = table_masks(
            neighbour_face[face : face + 1, :], orientation[face : face + 1, :], lanes
        )
        speed, heat = side_corrections(received, side, fluxes, (3, 4), len(chunks(levels)))
        for start, value in zip(chunks(levels), heat):
            column[pl.ds(ROWS + start, ROWS), :] = value
        for start, value in zip(chunks(levels), speed):
            upper = column[pl.ds(ROWS + start + 1, ROWS), :]
            lower = column[pl.ds(ROWS + start - 1, ROWS), :]
            mixed[pl.ds(start, ROWS), :] = value - gravity_couple * (upper - lower)
        mixed[levels : levels + 1, :] = column[ROWS : ROWS + 1, :]
        mixed[levels + 1 : levels + 2, :] = column[ROWS + levels - 1 : ROWS + levels, :]
        for start in ends(levels + 2):
            picked = spread(mixed[start : start + ROWS, :], edge, masks, flip)
            for k, row in enumerate(picked):
                point = NODES * j + k
                at = pl.ds(start * NODES + k, ROWS, stride=NODES)
                scale = weight * metric[point : point + 1, :]
                send[j, at, :] += jnp.where(lane == edge, scale * row, 0.0)
    half[...] = send[:, 0:rows, :]


def finish_section_kernel(
    part,
    near,
    other_early,
    other_late,
    from_down,
    from_up,
    neighbour_face,
    orientation,
    metric,
    fluxes,
    out,
    done,
    final,
    semaphore,
):
    levels = part.shape[0] // (FIELDS * POINTS)
    lanes = part.shape[1]
    size = levels * POINTS
    weight = 0.5 * lift_weight * step_size
    scale = weight * metric[...]
    lane = lax.broadcasted_iota(jnp.int32, (ROWS, lanes), 1)
    tables = []
    edges = []
    for side, received in enumerate((from_down, from_up)):
        face = 2 + side
        tables.append(
            table_masks(
                neighbour_face[face : face + 1, :], orientation[face : face + 1, :], lanes
            )
        )
        edges.append(
            side_corrections(received, side, fluxes, LATE_FIELDS, len(chunks(levels)))
        )
    copy = pltpu.make_async_copy(final, out.at[1:3], semaphore)
    sources = ((near,), (other_early, other_late))
    for place, f in ((1, 1), (2, 2), (0, 0), (3, 4)):
        target = final.at[f - 1] if f in (1, 2) else done.at[min(f, 1)]
        target[...] = part[f * size : (f + 1) * size, :]
        for piece, start in enumerate(chunks(levels)):
            for j in range(NODES):
                for partner, source in enumerate(sources):
                    point = NODES * j + (NODES - 1) * partner_side(partner)
                    share = len(LATE_FIELDS) // len(source)
                    rows = source[place // share][
                        pl.ds(((place % share) * levels + start) * NODES + j, ROWS, stride=NODES),
                        :,
                    ]
                    at = pl.ds(start * POINTS + point, ROWS, stride=POINTS)
                    target[at, :] = (
                        part[pl.ds(f * size + start * POINTS + point, ROWS, stride=POINTS), :]
                        + weight * metric[pl.ds(point, 1), :] * rows
                    )
        for piece, start in enumerate(chunks(levels)):
            row_index = lax.broadcasted_iota(jnp.int32, (ROWS, lanes), 0)
            fresh = row_index >= (-start) % ROWS
            for side, (edge, j) in enumerate(((0, 0), (lanes - 1, NODES - 1))):
                picked = spread(edges[side][place][piece], edge, *tables[side])
                for k, row in enumerate(picked):
                    point = NODES * j + k
                    at = pl.ds(start * POINTS + point, ROWS, stride=POINTS)
                    target[at, :] += jnp.where(
                        (lane == edge) & fresh, scale[point : point + 1, :] * row, 0.0
                    )
        if f == 2:
            copy.start()
    copy.wait()


def factor_kernel(coupling, damping, inverse, near, far_two, far_three, ratio, next_two, next_three):
    levels = coupling.shape[1]
    blank = jnp.zeros(coupling.shape[2:], jnp.float32)
    far_ratio, far_second, near_ratio, near_second = (blank,) * 4
    far_before, near_before = blank, blank
    extra = damping[...]
    for level in range(levels):
        a, b, d, e = (coupling[entry, level] for entry in range(4))
        centre = a + b + d + e + extra
        reduced = -b + a * far_ratio
        pivot = centre + a * far_second - reduced * near_ratio
        scaled = 1.0 / pivot
        upper_ratio = (-d - reduced * near_second) * scaled
        second_ratio = -e * scaled
        far_here, near_here = a * scaled, reduced * scaled
        inverse[level] = scaled
        near[level] = near_here
        far_two[level] = far_here + near_here * near_before
        far_three[level] = near_here * far_before
        ratio[level] = upper_ratio
        if level:
            next_two[level - 1] = near_ratio * upper_ratio - near_second
            next_three[level - 1] = near_ratio * second_ratio
        far_before, near_before = far_here, near_here
        far_ratio, far_second = near_ratio, near_second
        near_ratio, near_second = upper_ratio, second_ratio
    next_two[levels - 1] = -near_second
    next_three[levels - 1] = blank


def solve_kernel(inverse, near, far_two, far_three, ratio, next_two, next_three, *rest):
    ways = NODES
    received, sends, (source, heat, speed) = rest[:ways], rest[ways : 2 * ways], rest[2 * ways :]
    levels = near.shape[0]
    here = levels // ways
    me = lax.axis_index("vz")
    for values, way in zip(received, WAYS):
        block = me ^ way
        source[pl.ds(block * here, here)] = values[0:here]
        heat[block] = values[here : here + 2]
    for block in range(ways - 1):
        last = block * here + here - 1
        source[last] = source[last] - gravity_couple * heat[block + 1, 0]
        source[last + 1] = source[last + 1] + gravity_couple * heat[block, 1]
    blank = jnp.zeros(near.shape[1:], jnp.float32)
    scaled = blank
    known = [blank, blank, blank]
    for level in range(levels):
        before, scaled = scaled, source[level] * inverse[level]
        value = scaled - near[level] * before - far_three[level] * known[-3]
        value = value + far_two[level] * known[-2]
        source[level] = value
        known = [*known[1:], value]
    speed[0] = blank
    speed[levels + 1] = blank
    known = [blank, blank, blank]
    above = blank
    for level in range(levels - 1, -1, -1):
        here_value = source[level]
        value = here_value - ratio[level] * above + next_three[level] * known[-3]
        value = value + next_two[level] * known[-2]
        speed[level + 1] = value
        above = here_value
        known = [*known[1:], value]
    for send, way in zip(sends, BACK_WAYS):
        send[...] = speed[pl.ds((me ^ way) * here, here + 2)]


def update_kernel(*refs):
    ways = NODES
    received, (done, earlier, out, speed, final, semaphores) = refs[:ways], refs[ways:]
    levels = done.shape[1] // POINTS
    me = lax.axis_index("vz")
    for values, way in zip(received, BACK_WAYS):
        speed[me ^ way] = values[...]
    lanes = done.shape[2]
    half = levels // 2
    early = (7 * half) // 10
    low = lax.broadcasted_iota(jnp.int32, (ROWS, lanes), 0) < NODES
    copies = []
    for pair in range(half):
        lower = [speed[j, pair * ROWS : (pair + 1) * ROWS, :] for j in range(NODES)]
        upper = [speed[j, (pair + 1) * ROWS : (pair + 2) * ROWS, :] for j in range(NODES)]
        jump = [above - below for above, below in zip(upper, lower)]
        value = [jnp.where(low, above, below) for above, below in zip(upper, lower)]
        for h in range(2):
            a, b = 2 * h, 2 * h + 1
            for odd in range(2):
                at = pl.ds((2 * pair + odd) * POINTS + ROWS * h, ROWS)
                jumps = side_by_side(jump[a], jump[b], odd, low)
                final[0, at, :] = done[0, at, :] - density_couple * jumps
                final[1, at, :] = side_by_side(value[a], value[b], 1 - odd, low)
                final[2, at, :] = done[1, at, :] - theta_couple * jumps
        if pair in (early - 1, half - 1):
            first = 0 if pair < half - 1 else early
            rows = pl.ds(first * 2 * POINTS, (pair + 1 - first) * 2 * POINTS)
            for place, f, count in ((1, 3, 2), (0, 0, 1)):
                copies.append(
                    pltpu.make_async_copy(
                        final.at[place : place + count, rows, :],
                        out.at[f : f + count, rows, :],
                        semaphores.at[len(copies)],
                    )
                )
                copies[-1].start()
    for copy in copies:
        copy.wait()


def side_by_side(first, second, upper, low):
    if upper:
        return jnp.where(low, pltpu.roll(first, NODES, 0), second)
    return jnp.where(low, first, pltpu.roll(second, NODES, 0))


VMEM = pl.BlockSpec(memory_space=pltpu.VMEM)
HBM = pl.BlockSpec(memory_space=pltpu.HBM)
ANY = pl.BlockSpec(memory_space=pl.ANY)


def call(kernel, outs, in_specs, scratch=(), cost=0, name=None):
    kinds = [x if hasattr(x, "dtype") else pltpu.VMEM(x, jnp.float32) for x in outs]
    return pl.pallas_call(
        kernel,
        out_shape=kinds,
        in_specs=in_specs,
        out_specs=[VMEM] * len(outs),
        scratch_shapes=list(scratch),
        compiler_params=pltpu.CompilerParams(vmem_limit_bytes=24 * 1024 * 1024),
        cost_estimate=pl.CostEstimate(flops=cost, bytes_accessed=cost, transcendentals=0),
        name=name,
    )


def per_device(
    prognostic, metric, first_flux, second_flux, neighbour_face, orientation, coupling, damping
):
    fields, levels = prognostic.shape[:2]
    lanes = prognostic.shape[-1]
    whole = (fields, levels * POINTS, lanes)
    metric = metric.reshape(POINTS, lanes)
    neighbour_face = neighbour_face.reshape(4, lanes)
    orientation = orientation.reshape(4, lanes)
    coupling = coupling.reshape(4, coupling.shape[1], NODES, lanes)
    damping = damping.reshape(NODES, lanes)
    tables, _ = operator_tables(lanes)

    def shifts(axis):
        size = lax.axis_size(axis)
        up = [(i, (i + 1) % size) for i in range(size)]
        return up, [(j, i) for i, j in up]

    def exchange(arrays, ways):
        size = lax.axis_size("vz")
        return [
            lax.ppermute(x, "vz", [(i, i ^ way) for i in range(size)]) if way else x
            for x, way in zip(arrays, ways)
        ]

    count = lax.axis_size("hy")
    near = [(i, i ^ 1) for i in range(count)]
    other = [(i, (i + 1 if i % 2 else i - 1) % count) for i in range(count)]
    second_up, second_down = shifts("hx")
    width = len(RIM_POINTS)
    message = (-(-((levels + 2) * width + 2) // ROWS) * ROWS, lanes)
    sides = (-(-fields * len(chunks(levels)) // 4) * ROWS, lanes)
    padded = levels + 2 * ROWS
    table = pltpu.VMEM((4, lanes), jnp.int32)
    inputs = (
        prognostic.reshape(whole),
        neighbour_face,
        orientation,
        metric,
        jnp.asarray(tables),
        first_flux,
        second_flux,
    )
    (
        to_other,
        state,
        neighbour_face,
        orientation,
        metric,
        tables,
        fluxes,
    ) = call(
        rim_kernel,
        [
            message,
            whole,
            table,
            table,
            (POINTS, lanes),
            tables.shape,
            (-(-2 * fields * fields // ROWS) * ROWS, lanes),
        ],
        [HBM] * len(inputs),
        [
            pltpu.VMEM((width, padded, lanes), jnp.float32),
            pltpu.VMEM((width, padded, lanes), jnp.float32),
            pltpu.SMEM((fields, fields), jnp.float32),
            pltpu.SMEM((fields, fields), jnp.float32),
            pltpu.SemaphoreType.DMA((6 + -(-levels // ROWS),)),
        ],
        cost=1000,
        name="rim",
    )(*(pltpu.with_memory_space_constraint(x, pltpu.HBM) for x in inputs))
    state = state.reshape(fields * levels * POINTS, lanes)
    from_other = lax.ppermute(to_other, "hy", other)
    from_near = lax.ppermute(state, "hy", near)
    (to_sides,) = call(edge_kernel, [sides], [VMEM], cost=1000, name="edge")(state)
    from_down = lax.ppermute(to_sides, "hx", second_up)
    from_up = from_down
    if lax.axis_size("hx") > 2:
        from_up = lax.ppermute(to_sides, "hx", second_down)

    column = (coupling.shape[1], NODES, lanes)
    factors = call(factor_kernel, [column] * 7, [VMEM] * 2, cost=4000000, name="factor")(
        coupling, damping
    )
    block = ((levels + 2) * NODES, lanes)
    part, base = call(
        element_kernel,
        [state.shape, (NODES,) + block],
        [VMEM] * 6,
        [
            pltpu.VMEM((levels * 8 * fields, lanes), jnp.float32),
            pltpu.VMEM((fields * POINTS, lanes), jnp.bfloat16),
            pltpu.VMEM((fields * POINTS, lanes), jnp.bfloat16),
        ],
        cost=4000000,
        name="element",
    )(
        state,
        neighbour_face,
        orientation,
        metric,
        fluxes,
        tables,
    )
    late = levels * NODES * len(LATE_FIELDS)
    base, near_late = call(
        near_kernel,
        [(NODES,) + block, (late, lanes)],
        [VMEM] * 6,
        [pltpu.VMEM((NODES, padded, lanes), jnp.float32), pltpu.VMEM(block, jnp.float32)],
        cost=1000,
        name="near",
    )(from_near, neighbour_face, orientation, fluxes, base, metric)
    count = -(-(levels + 2) // ROWS) * ROWS
    (half,) = call(
        half_pack_kernel,
        [(NODES,) + block],
        [VMEM] * 7 + [ANY],
        [
            pltpu.VMEM((NODES, count * NODES, lanes), jnp.float32),
            pltpu.VMEM((padded, lanes), jnp.float32),
            pltpu.VMEM((count, lanes), jnp.float32),
        ],
        cost=1000,
        name="half_pack",
    )(
        base,
        from_down,
        from_up,
        neighbour_face,
        orientation,
        metric,
        fluxes,
        factors[0],
    )
    sends = call(
        pack_kernel,
        [block] * NODES,
        [VMEM] * 5,
        [pltpu.VMEM((NODES,) + block, jnp.float32)],
        cost=1000,
        name="pack",
    )(half, from_other, neighbour_face, orientation, metric)
    received = exchange(sends, WAYS)

    other_face = call(
        functools.partial(face_kernel, 1),
        [(late // 2, lanes)] * 2,
        [VMEM] * 3 + [ANY],
        cost=1000,
        name="other_face",
    )(state, from_other, fluxes, sends[-1])
    other_face = [lax.ppermute(x, "hy", other) for x in other_face]

    cube = (levels + 2, NODES, lanes)
    speeds = call(
        solve_kernel,
        [cube] * NODES,
        [VMEM] * (7 + NODES),
        [
            pltpu.VMEM(column, jnp.float32),
            pltpu.VMEM((NODES, 2, NODES, lanes), jnp.float32),
            pltpu.VMEM((column[0] + 2,) + column[1:], jnp.float32),
        ],
        cost=1000,
        name="solve",
    )(*factors, *[x.reshape(cube) for x in received])
    returned = exchange([x.reshape(block) for x in speeds], BACK_WAYS)
    size = levels * POINTS
    limits = pltpu.CompilerParams(vmem_limit_bytes=24 * 1024 * 1024)
    earlier, done = pl.pallas_call(
        finish_section_kernel,
        out_shape=[
            jax.ShapeDtypeStruct(whole, jnp.float32),
            pltpu.VMEM((2, size, lanes), jnp.float32),
        ],
        in_specs=[VMEM] * 10,
        out_specs=[HBM, VMEM],
        scratch_shapes=[
            pltpu.VMEM((2, size, lanes), jnp.float32),
            pltpu.SemaphoreType.DMA,
        ],
        compiler_params=limits,
        cost_estimate=pl.CostEstimate(flops=4000000, bytes_accessed=4000000, transcendentals=0),
        name="finish",
    )(
        part, near_late, *other_face, from_down, from_up, neighbour_face, orientation, metric, fluxes
    )
    updated = pl.pallas_call(
        update_kernel,
        out_shape=jax.ShapeDtypeStruct(whole, jnp.float32),
        in_specs=[VMEM] * (1 + NODES) + [HBM],
        out_specs=HBM,
        input_output_aliases={1 + NODES: 0},
        scratch_shapes=[
            pltpu.VMEM((NODES,) + block, jnp.float32),
            pltpu.VMEM((3, size, lanes), jnp.float32),
            pltpu.SemaphoreType.DMA((4,)),
        ],
        compiler_params=limits,
        name="update",
    )(*returned, done, earlier)
    return updated.reshape(prognostic.shape)


def solution(mesh):
    placed = (
        P(None, "vz", None, None, "hy", "hx"),
        P(None, None, "hy", "hx"),
        P(),
        P(),
        P(None, "hy", "hx"),
        P(None, "hy", "hx"),
        P(None, None, "vz", None, "hy", "hx"),
        P("vz", None, "hy", "hx"),
    )
    return jax.shard_map(
        per_device,
        mesh=mesh,
        in_specs=placed,
        out_specs=P(None, "vz", None, None, "hy", "hx"),
        check_vma=False,
    )
```

```python
import functools

import jax
import jax.numpy as jnp
import numpy as np
from jax import lax
from jax.experimental import pallas as pl
from jax.experimental.pallas import tpu as pltpu
from jax.sharding import PartitionSpec as P

step_size = 0.05
lift_weight = 6.0
gravity_couple = 0.5
density_couple = 0.3
theta_couple = 0.4

NODES = 4
POINTS = NODES * NODES
FIELDS = 5
FACE_POINTS = ((0, 4, 8, 12), (3, 7, 11, 15), (0, 1, 2, 3), (12, 13, 14, 15))
RIM_POINTS = tuple(sorted(set(sum(FACE_POINTS, ()))))
ROWS = 8
LATE_FIELDS = (0, 1, 2, 4)
WAYS = (2, 3, 1, 0)
BACK_WAYS = (3, 2, 1, 0)


def derivative_table():
    points = np.array([-1.0, -1.0 / np.sqrt(5.0), 1.0 / np.sqrt(5.0), 1.0])
    number = points.shape[0]
    barycentric = np.ones(number)
    for source in range(number):
        for another in range(number):
            if another != source:
                barycentric[source] = barycentric[source] / (points[source] - points[another])
    matrix = np.zeros((number, number))
    for target in range(number):
        for source in range(number):
            if target != source:
                matrix[target, source] = (
                    barycentric[source] / barycentric[target] / (points[target] - points[source])
                )
        matrix[target, target] = -np.sum(matrix[target])
    return matrix


def operator_tables(lanes):
    weight = 0.5 * lift_weight
    table = derivative_table()
    table[0, 0] += weight
    table[-1, -1] -= weight
    eye = np.eye(NODES)
    along_first = np.kron(eye, table)
    along_second = np.kron(table, eye)
    ends = np.zeros(NODES)
    ends[0] = ends[-1] = 1.0
    faces = np.diag(np.kron(np.ones(NODES), ends) + np.kron(ends, np.ones(NODES)))
    first = np.zeros((POINTS, lanes))
    second = np.zeros((POINTS, lanes))
    same = np.zeros((FIELDS, POINTS, lanes))
    owner = np.full((lanes,), -1)
    for g in range(FIELDS):
        own = slice(POINTS * g, POINTS * (g + 1))
        first[:, own] = -along_first
        second[:, own] = -along_second
        same[g, :, own] = -weight * faces
        owner[own] = g
        for k in range(NODES):
            south = FIELDS * POINTS + 2 * NODES * g + k
            north = south + NODES
            second[FACE_POINTS[2][k], south] = weight
            second[FACE_POINTS[3][k], north] = -weight
            same[g, FACE_POINTS[2][k], south] = weight
            same[g, FACE_POINTS[3][k], north] = weight
            owner[south] = owner[north] = g
    tables = np.concatenate([first, second, same.reshape(FIELDS * POINTS, lanes)])
    return tables.astype(np.float32), owner


def chunks(total):
    return [min(start, total - ROWS) for start in range(0, total, ROWS)]


def partner_side(partner):
    odd = lax.rem(lax.axis_index("hy"), 2)
    return odd if partner else 1 - odd


def side_sign(side):
    return (2 * side - 1).astype(jnp.float32)


def ends(total):
    return list(range(0, total, ROWS))


def pick(values, masks, flip):
    chosen = []
    for k in range(NODES):
        row = values[FACE_POINTS[0][k]]
        for option in range(1, 4):
            row = jnp.where(masks[option], values[FACE_POINTS[option][k]], row)
        chosen.append(row)
    return [jnp.where(flip, chosen[NODES - 1 - k], chosen[k]) for k in range(NODES)]


def table_masks(face_row, flip_row, lanes):
    face = jnp.broadcast_to(face_row, (ROWS, lanes))
    flip = jnp.broadcast_to(flip_row, (ROWS, lanes))
    return [face == option for option in range(4)], flip == 1


def flux_row(f, g, matrix):
    return (matrix * FIELDS + f) * FIELDS + g


def along(fluxes, matrix, f, rows):
    total = None
    for g in range(FIELDS):
        at = flux_row(f, g, matrix)
        term = fluxes[at : at + 1, :] * rows[g]
        total = term if total is None else total + term
    return total


def side_rows(f, piece):
    number = 3 * f + piece
    return number // 4, 32 * (number % 4)


def rim_kernel(
    state_hbm,
    face_hbm,
    way_hbm,
    metric_hbm,
    tables_hbm,
    flux_hbm,
    second_hbm,
    to_other,
    state,
    neighbour_face,
    orientation,
    metric,
    tables,
    fluxes,
    column,
    speed,
    flux,
    second_flux,
    semaphores,
):
    levels = state.shape[1] // POINTS
    face = partner_side(1)
    sign = side_sign(face)
    lanes = state.shape[2]
    width = len(RIM_POINTS)
    groups = [(start, min(start + ROWS, levels)) for start in range(0, levels, ROWS)]
    small = [
        pltpu.make_async_copy(source, target, semaphores.at[place])
        for place, (source, target) in enumerate(
            (
                (flux_hbm, flux),
                (face_hbm, neighbour_face),
                (way_hbm, orientation),
                (metric_hbm, metric),
                (tables_hbm, tables),
                (second_hbm, second_flux),
            )
        )
    ]
    large = []
    for place, (low, high) in enumerate(groups):
        rows = pl.ds(low * POINTS, (high - low) * POINTS)
        large.append(
            pltpu.make_async_copy(
                state_hbm.at[:, rows, :], state.at[:, rows, :], semaphores.at[len(small) + place]
            )
        )
    for copy in small[:1] + large + small[1:]:
        copy.start()
    column[...] = jnp.zeros_like(column)
    small[0].wait()
    arrived = 0
    for piece, start in enumerate(chunks(levels)):
        while arrived < len(groups) and groups[arrived][0] < start + ROWS:
            large[arrived].wait()
            arrived += 1
        for place, point in enumerate(RIM_POINTS):
            rows = [
                state[g, pl.ds(start * POINTS + point, ROWS, stride=POINTS), :]
                for g in range(FIELDS)
            ]
            for f, out in ((3, speed), (4, column)):
                normal = (sign * flux[f, 0]) * rows[0]
                for g in range(1, FIELDS):
                    normal = normal + (sign * flux[f, g]) * rows[g]
                out[place, pl.ds(ROWS + start, ROWS), :] = rows[f] + normal
    small[1].wait()
    small[2].wait()
    end = (levels + 2) * width
    for place in range(width):
        for start in chunks(levels):
            upper = column[place, pl.ds(ROWS + start + 1, ROWS), :]
            lower = column[place, pl.ds(ROWS + start - 1, ROWS), :]
            to_other[pl.ds(start * width + place, ROWS, stride=width), :] = speed[
                place, pl.ds(ROWS + start, ROWS), :
            ] - gravity_couple * (upper - lower)
        for extra, level in ((0, 0), (1, levels - 1)):
            at = (levels + extra) * width + place
            to_other[at : at + 1, :] = column[place, ROWS + level : ROWS + level + 1, :]
    to_other[end : end + 1, :] = neighbour_face[pl.ds(face, 1), :].astype(jnp.float32)
    to_other[end + 1 : end + 2, :] = orientation[pl.ds(face, 1), :].astype(jnp.float32)
    left = to_other.shape[0] - end - 2
    to_other[end + 2 :, :] = jnp.zeros((left, lanes), jnp.float32)
    small[3].wait()
    small[4].wait()
    small[5].wait()
    for place, source in enumerate((flux, second_flux)):
        for f in range(FIELDS):
            for g in range(FIELDS):
                at = flux_row(f, g, place)
                fluxes[at : at + 1, :] = jnp.full((1, lanes), source[f, g])


def edge_kernel(state, to_sides):
    lanes = state.shape[1]
    levels = state.shape[0] // (FIELDS * POINTS)
    lane = lax.broadcasted_iota(jnp.int32, (ROWS, lanes), 1)
    packed = [jnp.zeros((ROWS, lanes), jnp.float32) for _ in range(to_sides.shape[0] // ROWS)]
    for f in range(FIELDS):
        for piece, start in enumerate(chunks(levels)):
            block, at = side_rows(f, piece)
            for place, point in enumerate(RIM_POINTS):
                row = state[pl.ds((f * levels + start) * POINTS + point, ROWS, stride=POINTS), :]
                first = at + 2 * place
                packed[block] = jnp.where(
                    lane // 2 == first // 2, pltpu.roll(row, first + 1, 1), packed[block]
                )
    for block, value in enumerate(packed):
        to_sides[block * ROWS : (block + 1) * ROWS, :] = value


def near_kernel(
    state, neighbour_face, orientation, fluxes, base, metric, half, late, column, source
):
    lanes = state.shape[1]
    levels = state.shape[0] // (FIELDS * POINTS)
    face = partner_side(0)
    sign = -side_sign(face)
    masks, flip = table_masks(
        neighbour_face[pl.ds(face, 1), :], orientation[pl.ds(face, 1), :], lanes
    )
    column[...] = jnp.zeros_like(column)
    speeds = []
    for start in chunks(levels):
        picked = []
        for g in range(FIELDS):
            values = {
                point: state[pl.ds((g * levels + start) * POINTS + point, ROWS, stride=POINTS), :]
                for point in RIM_POINTS
            }
            picked.append(pick(values, masks, flip))
        for k in range(NODES):
            rows = [picked[g][k] for g in range(FIELDS)]
            changed = [rows[f] + sign * along(fluxes, 0, f, rows) for f in range(FIELDS)]
            for place, f in enumerate(LATE_FIELDS):
                at = (place * levels + start) * NODES + k
                late[pl.ds(at, ROWS, stride=NODES), :] = changed[f]
            column[k, pl.ds(ROWS + start, ROWS), :] = changed[4]
            speeds.append(changed[3])
    for piece, start in enumerate(chunks(levels)):
        for k in range(NODES):
            upper = column[k, pl.ds(ROWS + start + 1, ROWS), :]
            lower = column[k, pl.ds(ROWS + start - 1, ROWS), :]
            source[pl.ds(start * NODES + k, ROWS, stride=NODES), :] = speeds[
                NODES * piece + k
            ] - gravity_couple * (upper - lower)
    for extra, level in ((0, 0), (1, levels - 1)):
        for k in range(NODES):
            at = (levels + extra) * NODES + k
            source[at : at + 1, :] = column[k, ROWS + level : ROWS + level + 1, :]
    half[...] = base[...]
    for start in chunks(levels + 2):
        picked = [source[pl.ds(start * NODES + k, ROWS, stride=NODES), :] for k in range(NODES)]
        add_first_side(0, start, picked, half, base, metric)


def face_kernel(partner, state, received, fluxes, *rest):
    lanes = state.shape[1]
    levels = state.shape[0] // (FIELDS * POINTS)
    at = (levels + 2) * len(RIM_POINTS)
    outs = rest[-2:]
    share = len(LATE_FIELDS) // len(outs)
    sign = side_sign(partner_side(partner))
    masks, flip = table_masks(
        received[at : at + 1, :].astype(jnp.int32),
        received[at + 1 : at + 2, :].astype(jnp.int32),
        lanes,
    )
    for start in chunks(levels):
        picked = []
        for g in range(FIELDS):
            values = {
                point: state[pl.ds((g * levels + start) * POINTS + point, ROWS, stride=POINTS), :]
                for point in RIM_POINTS
            }
            picked.append(pick(values, masks, flip))
        for place, f in enumerate(LATE_FIELDS):
            for k in range(NODES):
                normal = along(fluxes, 0, f, [picked[g][k] for g in range(FIELDS)])
                at = ((place % share) * levels + start) * NODES + k
                outs[place // share][pl.ds(at, ROWS, stride=NODES), :] = (
                    picked[f][k] + sign * normal
                )


def element_kernel(
    state,
    neighbour_face,
    orientation,
    metric,
    fluxes,
    tables,
    part,
    base,
    outer,
    operator_high,
    operator_low,
):
    levels = state.shape[0] // (FIELDS * POINTS)
    lanes = state.shape[1]
    lane = lax.broadcasted_iota(jnp.int32, (ROWS, lanes), 1)
    sides = []
    for side, (face, edge) in enumerate(((2, 0), (3, lanes - 1))):
        shift = 1 if side == 0 else lanes - 1
        row = jnp.broadcast_to(neighbour_face[face : face + 1, :], (ROWS, lanes))
        way = jnp.broadcast_to(orientation[face : face + 1, :], (ROWS, lanes))
        masks, flip = table_masks(
            pltpu.roll(row, lanes - shift, 1), pltpu.roll(way, lanes - shift, 1), lanes
        )
        sides.append((shift, edge, masks, flip))
    for f in range(FIELDS):
        for start in chunks(levels):
            q = f * levels + start
            values = {
                point: state[pl.ds(q * POINTS + point, ROWS, stride=POINTS), :]
                for point in RIM_POINTS
            }
            for side, (shift, edge, masks, flip) in enumerate(sides):
                for k, row in enumerate(pick(values, masks, flip)):
                    at = start * 8 * FIELDS + 8 * f + NODES * side + k
                    outer[pl.ds(at, ROWS, stride=8 * FIELDS), :] = jnp.where(
                        lane == edge, 0.0, pltpu.roll(row, shift, 1)
                    )
    index = lax.broadcasted_iota(jnp.int32, (1, lanes), 1)
    own_columns = FIELDS * POINTS
    owner = jnp.where(index < own_columns, index // POINTS, (index - own_columns) // 8)
    for f in range(FIELDS):
        first_row = jnp.zeros((1, lanes), jnp.float32)
        second_row = first_row
        for g in range(FIELDS):
            first, second = (flux_row(f, g, matrix) for matrix in range(2))
            first_row = jnp.where(owner == g, fluxes[first : first + 1, :], first_row)
            second_row = jnp.where(owner == g, fluxes[second : second + 1, :], second_row)
        block = (
            first_row * tables[0:POINTS, :]
            + second_row * tables[POINTS : 2 * POINTS, :]
            + tables[(2 + f) * POINTS : (3 + f) * POINTS, :]
        )
        high = block.astype(jnp.bfloat16)
        operator_high[f * POINTS : (f + 1) * POINTS, :] = high
        operator_low[f * POINTS : (f + 1) * POINTS, :] = (
            block - high.astype(jnp.float32)
        ).astype(jnp.bfloat16)
    high = operator_high[...]
    low = operator_low[...]
    scale = step_size * metric[...]
    blank = jnp.zeros((lanes - own_columns - 8 * FIELDS, lanes), jnp.float32)
    for pair in range(0, levels, 2):
        sides = []
        for level in (pair, pair + 1):
            rows = [
                state[pl.ds((f * levels + level) * POINTS, POINTS), :] for f in range(FIELDS)
            ]
            rows.append(outer[pl.ds(level * 8 * FIELDS, 8 * FIELDS), :])
            rows.append(blank)
            sides.append(jnp.concatenate(rows, axis=0))
        values = jnp.concatenate(sides, axis=1)
        top = values.astype(jnp.bfloat16)
        rest = (values - top.astype(jnp.float32)).astype(jnp.bfloat16)
        change = (
            jnp.dot(high, top, preferred_element_type=jnp.float32)
            + jnp.dot(high, rest, preferred_element_type=jnp.float32)
            + jnp.dot(low, top, preferred_element_type=jnp.float32)
        )
        for place, level in enumerate((pair, pair + 1)):
            for f in range(FIELDS):
                at = pl.ds((f * levels + level) * POINTS, POINTS)
                part[at, :] = (
                    state[at, :]
                    + scale
                    * change[
                        f * POINTS : (f + 1) * POINTS, place * lanes : (place + 1) * lanes
                    ]
                )
    for level in range(levels):
        speed = part[pl.ds((3 * levels + level) * POINTS, POINTS), :]
        upper = part[pl.ds((4 * levels + level + 1) * POINTS, POINTS), :] if level < levels - 1 else 0.0
        lower = part[pl.ds((4 * levels + level - 1) * POINTS, POINTS), :] if level else 0.0
        value = speed - gravity_couple * (upper - lower)
        for j in range(NODES):
            base[j, level * NODES : (level + 1) * NODES, :] = value[NODES * j : NODES * (j + 1)]
    for extra, level in ((0, 0), (1, levels - 1)):
        value = part[pl.ds((4 * levels + level) * POINTS, POINTS), :]
        at = (levels + extra) * NODES
        for j in range(NODES):
            base[j, at : at + NODES, :] = value[NODES * j : NODES * (j + 1)]


def side_corrections(received, side, fluxes, fields, pieces):
    lanes = received.shape[1]
    sign = 1.0 if side == 0 else -1.0
    result = [[] for _ in fields]
    for piece in range(pieces):
        rows = []
        for g in range(FIELDS):
            block, at = side_rows(g, piece)
            rows.append(
                pltpu.roll(
                    received[block * ROWS : (block + 1) * ROWS, :], (lanes - at - side) % lanes, 1
                )
            )
        for place, f in enumerate(fields):
            result[place].append(rows[f] + sign * along(fluxes, 1, f, rows))
    return result


def spread(value, edge, masks, flip):
    lanes = value.shape[1]
    values = {
        point: pltpu.roll(value, (edge - 2 * place) % lanes, 1)
        for place, point in enumerate(RIM_POINTS)
    }
    return pick(values, masks, flip)


def add_first_side(partner, start, picked, send, base, metric):
    weight = 0.5 * lift_weight * step_size
    i = (NODES - 1) * partner_side(partner)
    for j, row in enumerate(picked):
        at = pl.ds(start * NODES + i, ROWS, stride=NODES)
        scale = weight * metric[pl.ds(NODES * j + i, 1), :]
        send[j, at, :] = base[j, at, :] + scale * row


def pack_kernel(half, from_other, neighbour_face, orientation, metric, *rest):
    sends, (send,) = rest[:NODES], rest[NODES:]
    me = lax.axis_index("vz")
    send[...] = half[...]
    rows, lanes = half.shape[1:]
    width = len(RIM_POINTS)
    face = partner_side(1)
    masks, flip = table_masks(
        neighbour_face[pl.ds(face, 1), :], orientation[pl.ds(face, 1), :], lanes
    )
    for start in chunks(rows // NODES):
        values = {
            point: from_other[pl.ds(start * width + place, ROWS, stride=width), :]
            for place, point in enumerate(RIM_POINTS)
        }
        add_first_side(1, start, pick(values, masks, flip), send, half, metric)
    for out, way in zip(sends, WAYS):
        out[...] = send[me ^ way]


def half_pack_kernel(
    base,
    from_down,
    from_up,
    neighbour_face,
    orientation,
    metric,
    fluxes,
    factored,
    half,
    send,
    column,
    mixed,
):
    rows, lanes = base.shape[1:]
    levels = rows // NODES - 2
    width = len(RIM_POINTS)
    weight = 0.5 * lift_weight * step_size
    send[:, 0:rows, :] = base[...]
    send[:, rows:, :] = jnp.zeros((NODES, send.shape[1] - rows, lanes), jnp.float32)
    column[...] = jnp.zeros_like(column)
    mixed[...] = jnp.zeros_like(mixed)
    lane = lax.broadcasted_iota(jnp.int32, (ROWS, lanes), 1)
    for side, (received, edge, j) in enumerate(
        ((from_down, 0, 0), (from_up, lanes - 1, NODES - 1))
    ):
        face = 2 + side
        masks, flip = table_masks(
            neighbour_face[face : face + 1, :], orientation[face : face + 1, :], lanes
        )
        speed, heat = side_corrections(received, side, fluxes, (3, 4), len(chunks(levels)))
        for start, value in zip(chunks(levels), heat):
            column[pl.ds(ROWS + start, ROWS), :] = value
        for start, value in zip(chunks(levels), speed):
            upper = column[pl.ds(ROWS + start + 1, ROWS), :]
            lower = column[pl.ds(ROWS + start - 1, ROWS), :]
            mixed[pl.ds(start, ROWS), :] = value - gravity_couple * (upper - lower)
        mixed[levels : levels + 1, :] = column[ROWS : ROWS + 1, :]
        mixed[levels + 1 : levels + 2, :] = column[ROWS + levels - 1 : ROWS + levels, :]
        for start in ends(levels + 2):
            picked = spread(mixed[start : start + ROWS, :], edge, masks, flip)
            for k, row in enumerate(picked):
                point = NODES * j + k
                at = pl.ds(start * NODES + k, ROWS, stride=NODES)
                scale = weight * metric[point : point + 1, :]
                send[j, at, :] += jnp.where(lane == edge, scale * row, 0.0)
    half[...] = send[:, 0:rows, :]


def finish_section_kernel(
    part,
    near,
    other_early,
    other_late,
    from_down,
    from_up,
    neighbour_face,
    orientation,
    metric,
    fluxes,
    out,
    done,
    final,
    semaphore,
):
    levels = part.shape[0] // (FIELDS * POINTS)
    lanes = part.shape[1]
    size = levels * POINTS
    weight = 0.5 * lift_weight * step_size
    scale = weight * metric[...]
    lane = lax.broadcasted_iota(jnp.int32, (ROWS, lanes), 1)
    tables = []
    edges = []
    for side, received in enumerate((from_down, from_up)):
        face = 2 + side
        tables.append(
            table_masks(
                neighbour_face[face : face + 1, :], orientation[face : face + 1, :], lanes
            )
        )
        edges.append(
            side_corrections(received, side, fluxes, LATE_FIELDS, len(chunks(levels)))
        )
    copy = pltpu.make_async_copy(final, out.at[1:3], semaphore)
    sources = ((near,), (other_early, other_late))
    for place, f in ((1, 1), (2, 2), (0, 0), (3, 4)):
        target = final.at[f - 1] if f in (1, 2) else done.at[min(f, 1)]
        target[...] = part[f * size : (f + 1) * size, :]
        for piece, start in enumerate(chunks(levels)):
            for j in range(NODES):
                for partner, source in enumerate(sources):
                    point = NODES * j + (NODES - 1) * partner_side(partner)
                    share = len(LATE_FIELDS) // len(source)
                    rows = source[place // share][
                        pl.ds(((place % share) * levels + start) * NODES + j, ROWS, stride=NODES),
                        :,
                    ]
                    at = pl.ds(start * POINTS + point, ROWS, stride=POINTS)
                    target[at, :] = (
                        part[pl.ds(f * size + start * POINTS + point, ROWS, stride=POINTS), :]
                        + weight * metric[pl.ds(point, 1), :] * rows
                    )
        for piece, start in enumerate(chunks(levels)):
            row_index = lax.broadcasted_iota(jnp.int32, (ROWS, lanes), 0)
            fresh = row_index >= (-start) % ROWS
            for side, (edge, j) in enumerate(((0, 0), (lanes - 1, NODES - 1))):
                picked = spread(edges[side][place][piece], edge, *tables[side])
                for k, row in enumerate(picked):
                    point = NODES * j + k
                    at = pl.ds(start * POINTS + point, ROWS, stride=POINTS)
                    target[at, :] += jnp.where(
                        (lane == edge) & fresh, scale[point : point + 1, :] * row, 0.0
                    )
        if f == 2:
            copy.start()
    copy.wait()


def factor_kernel(coupling, damping, inverse, near, far_two, far_three, ratio, next_two, next_three):
    levels = coupling.shape[1]
    blank = jnp.zeros(coupling.shape[2:], jnp.float32)
    far_ratio, far_second, near_ratio, near_second = (blank,) * 4
    far_before, near_before = blank, blank
    extra = damping[...]
    for level in range(levels):
        a, b, d, e = (coupling[entry, level] for entry in range(4))
        centre = a + b + d + e + extra
        reduced = -b + a * far_ratio
        pivot = centre + a * far_second - reduced * near_ratio
        scaled = 1.0 / pivot
        upper_ratio = (-d - reduced * near_second) * scaled
        second_ratio = -e * scaled
        far_here, near_here = a * scaled, reduced * scaled
        inverse[level] = scaled
        near[level] = near_here
        far_two[level] = far_here + near_here * near_before
        far_three[level] = near_here * far_before
        ratio[level] = upper_ratio
        if level:
            next_two[level - 1] = near_ratio * upper_ratio - near_second
            next_three[level - 1] = near_ratio * second_ratio
        far_before, near_before = far_here, near_here
        far_ratio, far_second = near_ratio, near_second
        near_ratio, near_second = upper_ratio, second_ratio
    next_two[levels - 1] = -near_second
    next_three[levels - 1] = blank


def solve_kernel(inverse, near, far_two, far_three, ratio, next_two, next_three, *rest):
    ways = NODES
    received, sends, (source, heat, speed) = rest[:ways], rest[ways : 2 * ways], rest[2 * ways :]
    levels = near.shape[0]
    here = levels // ways
    me = lax.axis_index("vz")
    for values, way in zip(received, WAYS):
        block = me ^ way
        source[pl.ds(block * here, here)] = values[0:here]
        heat[block] = values[here : here + 2]
    for block in range(ways - 1):
        last = block * here + here - 1
        source[last] = source[last] - gravity_couple * heat[block + 1, 0]
        source[last + 1] = source[last + 1] + gravity_couple * heat[block, 1]
    blank = jnp.zeros(near.shape[1:], jnp.float32)
    scaled = blank
    known = [blank, blank, blank]
    for level in range(levels):
        before, scaled = scaled, source[level] * inverse[level]
        value = scaled - near[level] * before - far_three[level] * known[-3]
        value = value + far_two[level] * known[-2]
        source[level] = value
        known = [*known[1:], value]
    speed[0] = blank
    speed[levels + 1] = blank
    known = [blank, blank, blank]
    above = blank
    for level in range(levels - 1, -1, -1):
        here_value = source[level]
        value = here_value - ratio[level] * above + next_three[level] * known[-3]
        value = value + next_two[level] * known[-2]
        speed[level + 1] = value
        above = here_value
        known = [*known[1:], value]
    for send, way in zip(sends, BACK_WAYS):
        send[...] = speed[pl.ds((me ^ way) * here, here + 2)]


def update_kernel(*refs):
    ways = NODES
    received, (done, earlier, out, speed, final, semaphores) = refs[:ways], refs[ways:]
    levels = done.shape[1] // POINTS
    me = lax.axis_index("vz")
    for values, way in zip(received, BACK_WAYS):
        speed[me ^ way] = values[...]
    lanes = done.shape[2]
    half = levels // 2
    low = lax.broadcasted_iota(jnp.int32, (ROWS, lanes), 0) < NODES
    copies = []
    for pair in range(half):
        lower = [speed[j, pair * ROWS : (pair + 1) * ROWS, :] for j in range(NODES)]
        upper = [speed[j, (pair + 1) * ROWS : (pair + 2) * ROWS, :] for j in range(NODES)]
        jump = [above - below for above, below in zip(upper, lower)]
        value = [jnp.where(low, above, below) for above, below in zip(upper, lower)]
        for h in range(2):
            a, b = 2 * h, 2 * h + 1
            for odd in range(2):
                at = pl.ds((2 * pair + odd) * POINTS + ROWS * h, ROWS)
                jumps = side_by_side(jump[a], jump[b], odd, low)
                final[0, at, :] = done[0, at, :] - density_couple * jumps
                final[1, at, :] = side_by_side(value[a], value[b], 1 - odd, low)
                final[2, at, :] = done[1, at, :] - theta_couple * jumps
        if pair == half - 1:
            first = 0
            rows = pl.ds(first * 2 * POINTS, (pair + 1 - first) * 2 * POINTS)
            for place, f, count in ((1, 3, 2), (0, 0, 1)):
                copies.append(
                    pltpu.make_async_copy(
                        final.at[place : place + count, rows, :],
                        out.at[f : f + count, rows, :],
                        semaphores.at[len(copies)],
                    )
                )
                copies[-1].start()
    for copy in copies:
        copy.wait()


def side_by_side(first, second, upper, low):
    if upper:
        return jnp.where(low, pltpu.roll(first, NODES, 0), second)
    return jnp.where(low, first, pltpu.roll(second, NODES, 0))


VMEM = pl.BlockSpec(memory_space=pltpu.VMEM)
HBM = pl.BlockSpec(memory_space=pltpu.HBM)
ANY = pl.BlockSpec(memory_space=pl.ANY)


def call(kernel, outs, in_specs, scratch=(), cost=0, name=None):
    kinds = [x if hasattr(x, "dtype") else pltpu.VMEM(x, jnp.float32) for x in outs]
    return pl.pallas_call(
        kernel,
        out_shape=kinds,
        in_specs=in_specs,
        out_specs=[VMEM] * len(outs),
        scratch_shapes=list(scratch),
        compiler_params=pltpu.CompilerParams(vmem_limit_bytes=24 * 1024 * 1024),
        cost_estimate=pl.CostEstimate(flops=cost, bytes_accessed=cost, transcendentals=0),
        name=name,
    )


def per_device(
    prognostic, metric, first_flux, second_flux, neighbour_face, orientation, coupling, damping
):
    fields, levels = prognostic.shape[:2]
    lanes = prognostic.shape[-1]
    whole = (fields, levels * POINTS, lanes)
    metric = metric.reshape(POINTS, lanes)
    neighbour_face = neighbour_face.reshape(4, lanes)
    orientation = orientation.reshape(4, lanes)
    coupling = coupling.reshape(4, coupling.shape[1], NODES, lanes)
    damping = damping.reshape(NODES, lanes)
    tables, _ = operator_tables(lanes)

    def shifts(axis):
        size = lax.axis_size(axis)
        up = [(i, (i + 1) % size) for i in range(size)]
        return up, [(j, i) for i, j in up]

    def exchange(arrays, ways):
        size = lax.axis_size("vz")
        return [
            lax.ppermute(x, "vz", [(i, i ^ way) for i in range(size)]) if way else x
            for x, way in zip(arrays, ways)
        ]

    count = lax.axis_size("hy")
    near = [(i, i ^ 1) for i in range(count)]
    other = [(i, (i + 1 if i % 2 else i - 1) % count) for i in range(count)]
    second_up, second_down = shifts("hx")
    width = len(RIM_POINTS)
    message = (-(-((levels + 2) * width + 2) // ROWS) * ROWS, lanes)
    sides = (-(-fields * len(chunks(levels)) // 4) * ROWS, lanes)
    padded = levels + 2 * ROWS
    table = pltpu.VMEM((4, lanes), jnp.int32)
    inputs = (
        prognostic.reshape(whole),
        neighbour_face,
        orientation,
        metric,
        jnp.asarray(tables),
        first_flux,
        second_flux,
    )
    (
        to_other,
        state,
        neighbour_face,
        orientation,
        metric,
        tables,
        fluxes,
    ) = call(
        rim_kernel,
        [
            message,
            whole,
            table,
            table,
            (POINTS, lanes),
            tables.shape,
            (-(-2 * fields * fields // ROWS) * ROWS, lanes),
        ],
        [HBM] * len(inputs),
        [
            pltpu.VMEM((width, padded, lanes), jnp.float32),
            pltpu.VMEM((width, padded, lanes), jnp.float32),
            pltpu.SMEM((fields, fields), jnp.float32),
            pltpu.SMEM((fields, fields), jnp.float32),
            pltpu.SemaphoreType.DMA((6 + -(-levels // ROWS),)),
        ],
        cost=1000,
        name="rim",
    )(*(pltpu.with_memory_space_constraint(x, pltpu.HBM) for x in inputs))
    state = state.reshape(fields * levels * POINTS, lanes)
    from_other = lax.ppermute(to_other, "hy", other)
    from_near = lax.ppermute(state, "hy", near)
    (to_sides,) = call(edge_kernel, [sides], [VMEM], cost=1000, name="edge")(state)
    from_down = lax.ppermute(to_sides, "hx", second_up)
    from_up = from_down
    if lax.axis_size("hx") > 2:
        from_up = lax.ppermute(to_sides, "hx", second_down)

    column = (coupling.shape[1], NODES, lanes)
    factors = call(factor_kernel, [column] * 7, [VMEM] * 2, cost=4000000, name="factor")(
        coupling, damping
    )
    block = ((levels + 2) * NODES, lanes)
    part, base = call(
        element_kernel,
        [state.shape, (NODES,) + block],
        [VMEM] * 6,
        [
            pltpu.VMEM((levels * 8 * fields, lanes), jnp.float32),
            pltpu.VMEM((fields * POINTS, lanes), jnp.bfloat16),
            pltpu.VMEM((fields * POINTS, lanes), jnp.bfloat16),
        ],
        cost=4000000,
        name="element",
    )(
        state,
        neighbour_face,
        orientation,
        metric,
        fluxes,
        tables,
    )
    late = levels * NODES * len(LATE_FIELDS)
    base, near_late = call(
        near_kernel,
        [(NODES,) + block, (late, lanes)],
        [VMEM] * 6,
        [pltpu.VMEM((NODES, padded, lanes), jnp.float32), pltpu.VMEM(block, jnp.float32)],
        cost=1000,
        name="near",
    )(from_near, neighbour_face, orientation, fluxes, base, metric)
    count = -(-(levels + 2) // ROWS) * ROWS
    (half,) = call(
        half_pack_kernel,
        [(NODES,) + block],
        [VMEM] * 7 + [ANY],
        [
            pltpu.VMEM((NODES, count * NODES, lanes), jnp.float32),
            pltpu.VMEM((padded, lanes), jnp.float32),
            pltpu.VMEM((count, lanes), jnp.float32),
        ],
        cost=1000,
        name="half_pack",
    )(
        base,
        from_down,
        from_up,
        neighbour_face,
        orientation,
        metric,
        fluxes,
        factors[0],
    )
    sends = call(
        pack_kernel,
        [block] * NODES,
        [VMEM] * 5,
        [pltpu.VMEM((NODES,) + block, jnp.float32)],
        cost=1000,
        name="pack",
    )(half, from_other, neighbour_face, orientation, metric)
    received = exchange(sends, WAYS)

    other_face = call(
        functools.partial(face_kernel, 1),
        [(late // 2, lanes)] * 2,
        [VMEM] * 3 + [ANY],
        cost=1000,
        name="other_face",
    )(state, from_other, fluxes, sends[-1])
    other_face = [lax.ppermute(x, "hy", other) for x in other_face]

    cube = (levels + 2, NODES, lanes)
    speeds = call(
        solve_kernel,
        [cube] * NODES,
        [VMEM] * (7 + NODES),
        [
            pltpu.VMEM(column, jnp.float32),
            pltpu.VMEM((NODES, 2, NODES, lanes), jnp.float32),
            pltpu.VMEM((column[0] + 2,) + column[1:], jnp.float32),
        ],
        cost=1000,
        name="solve",
    )(*factors, *[x.reshape(cube) for x in received])
    returned = exchange([x.reshape(block) for x in speeds], BACK_WAYS)
    size = levels * POINTS
    limits = pltpu.CompilerParams(vmem_limit_bytes=24 * 1024 * 1024)
    earlier, done = pl.pallas_call(
        finish_section_kernel,
        out_shape=[
            jax.ShapeDtypeStruct(whole, jnp.float32),
            pltpu.VMEM((2, size, lanes), jnp.float32),
        ],
        in_specs=[VMEM] * 10,
        out_specs=[HBM, VMEM],
        scratch_shapes=[
            pltpu.VMEM((2, size, lanes), jnp.float32),
            pltpu.SemaphoreType.DMA,
        ],
        compiler_params=limits,
        cost_estimate=pl.CostEstimate(flops=4000000, bytes_accessed=4000000, transcendentals=0),
        name="finish",
    )(
        part, near_late, *other_face, from_down, from_up, neighbour_face, orientation, metric, fluxes
    )
    updated = pl.pallas_call(
        update_kernel,
        out_shape=jax.ShapeDtypeStruct(whole, jnp.float32),
        in_specs=[VMEM] * (1 + NODES) + [HBM],
        out_specs=HBM,
        input_output_aliases={1 + NODES: 0},
        scratch_shapes=[
            pltpu.VMEM((NODES,) + block, jnp.float32),
            pltpu.VMEM((3, size, lanes), jnp.float32),
            pltpu.SemaphoreType.DMA((2,)),
        ],
        compiler_params=limits,
        name="update",
    )(*returned, done, earlier)
    return updated.reshape(prognostic.shape)


def solution(mesh):
    placed = (
        P(None, "vz", None, None, "hy", "hx"),
        P(None, None, "hy", "hx"),
        P(),
        P(),
        P(None, "hy", "hx"),
        P(None, "hy", "hx"),
        P(None, None, "vz", None, "hy", "hx"),
        P("vz", None, "hy", "hx"),
    )
    return jax.shard_map(
        per_device,
        mesh=mesh,
        in_specs=placed,
        out_specs=P(None, "vz", None, None, "hy", "hx"),
        check_vma=False,
    )
```
